32 devices in a mesh: row: 8 (over z, y), col: 4 (over x, core).
Axes of the slice: x: 2, y: 2, z: 4, core: 2. Of those that a mesh axis runs over, the one named last changes fastest.
Arguments:
- block_cols: int32 [32, 8], replicated, may hold values from -1 to 31, as said below
- step_dir: bfloat16 [32, 8, 128, 128], P('row', 'col')
- intersection: bfloat16 [32, 8, 128, 128], P('row', 'col')
- density: bfloat16 [32, 8, 128, 128], P('row', 'col')
- kohn_sham: bfloat16 [32, 8, 128, 128], P('row', 'col')
Outputs:
- commutator: bfloat16 [32, 8, 128, 128], P('row', 'col')
- trace_value: float32 [], replicated
The draws below stay inside these ranges and needn't reach their ends.
Inputs may be any that keep to these rules, and one draw needn't show every extreme that they name: block_cols[i, s] is -1 or a block column of group s // 2, that is from (s // 2) * 8 to (s // 2 + 1) * 8 - 1; the live entries of one block row within one group are distinct; the pattern is symmetric (j is live in row i exactly when i is live in row j) and holds every diagonal block.
All inputs are finite; a program needn't handle non-finite values.
Results may differ from the reference program's by a relative error of at most 0.0057.
Values may be sent and summed in bfloat16 or wider, within the bound.
No kernel may reach another device: no remote copies, remote signals or barrier semaphores. Data moves between devices by JAX's collectives and lax.ppermute only.
A program may use at most 64 MiB of HBM per device.

```python
import jax
import jax.numpy as jnp
from jax import lax

BLK = 128
KS = 2
NB = 32
GROUP = 8
KT = 8


def build_pattern(key):
    tile_count = NB // GROUP
    perm_keys = jax.random.split(jax.random.fold_in(key, 1), tile_count * tile_count)
    permuted = jax.vmap(lambda sub_key: jax.random.permutation(sub_key, GROUP))(perm_keys).reshape(tile_count, tile_count, GROUP)
    keep_flags = jax.random.randint(jax.random.fold_in(key, 2), (NB, tile_count, KS), 0, 2)
    row_ids = jnp.arange(NB)
    tile_row = row_ids // GROUP
    local_row = row_ids % GROUP
    keep_flags = jnp.where(local_row[:, None, None] == 0, 1, keep_flags)
    shift_ids = jnp.arange(KS)
    shift_pos = (local_row[:, None] + shift_ids[None, :]) % GROUP
    targets = permuted[tile_row[:, None, None], jnp.arange(tile_count)[None, :, None], shift_pos[:, None, :]]
    hit_mask = (targets[..., None] == jnp.arange(GROUP)[None, None, None, :]) & (keep_flags[..., None] == 1)
    full_mask = jnp.any(hit_mask, axis=2).reshape(NB, NB)
    half_count = (KS - 1) // 2
    half_mask = jnp.any(hit_mask & (shift_ids[None, None, :, None] < half_count), axis=2).reshape(NB, NB)
    tile_left = tile_row[:, None]
    tile_right = tile_row[None, :]
    on_diagonal = row_ids[:, None] == row_ids[None, :]
    inner_mask = half_mask | half_mask.T | on_diagonal
    return jnp.where(tile_left < tile_right, full_mask, jnp.where(tile_left > tile_right, full_mask.T, inner_mask))


def draw_block_cols(key, part):
    sym_mask = build_pattern(jax.random.fold_in(key, 11))
    tile_count = NB // GROUP
    grouped = sym_mask.reshape(NB, tile_count, GROUP)
    local_ids = jnp.arange(GROUP, dtype=jnp.int32)
    scores = jnp.where(grouped, local_ids, GROUP + local_ids)
    slot_order = jnp.argsort(scores, axis=-1, stable=True)[..., :KS]
    is_live = jnp.take_along_axis(grouped, slot_order, axis=-1)
    column = jnp.arange(tile_count, dtype=jnp.int32)[None, :, None] * GROUP + slot_order
    return jnp.where(is_live, column, -1).reshape(NB, tile_count * KS).astype(jnp.int32)


def diagonal_blocks(key, part):
    pattern = draw_block_cols(key, part)
    on_diagonal = (pattern == jnp.arange(NB, dtype=jnp.int32)[:, None]).astype(jnp.float32)
    return on_diagonal[:, :, None, None] * jnp.eye(BLK, dtype=jnp.float32)[None, None, :, :]


def fock_unit(key):
    values = jnp.clip(jax.random.normal(jax.random.fold_in(key, 31), (NB, KT, BLK, BLK), jnp.float32), -3.0, 3.0)
    return values


def draw_kohn_sham(key, part):
    spread = (BLK * KT // 2) ** (-0.5)
    return (fock_unit(key) * spread).astype(jnp.bfloat16)


def draw_intersection(key, part):
    spread = (BLK * KT // 2) ** (-0.5)
    values = jnp.clip(jax.random.normal(jax.random.fold_in(key, 21), (NB, KT, BLK, BLK), jnp.float32), -4.0, 4.0)
    return (values * spread + diagonal_blocks(key, part)).astype(jnp.bfloat16)


def draw_density(key, part):
    spread = (BLK * KT // 2) ** (-0.5)
    values = jnp.clip(jax.random.normal(jax.random.fold_in(key, 22), (NB, KT, BLK, BLK), jnp.float32), -4.0, 4.0)
    return (values * spread + 0.5 * diagonal_blocks(key, part)).astype(jnp.bfloat16)


def draw_step_dir(key, part):
    row_ids = jnp.arange(NB).astype(jnp.float32)
    noise_vals = jnp.clip(jax.random.normal(jax.random.fold_in(key, 41), (NB, KT, BLK, BLK), jnp.float32), -3.0, 3.0)
    row_ramp = 1.0 + 2.0 * row_ids / (NB - 1)
    mixed = 0.6 * fock_unit(key) + 0.8 * noise_vals
    return (mixed * row_ramp[:, None, None, None]).astype(jnp.bfloat16)


def setup_inputs(seed: int = 0) -> dict:
    splits = jax.random.split(jax.random.key(seed), 6)
    return {
        "block_cols": draw_block_cols(jax.random.fold_in(splits[5], 71), 0),
        "step_dir": draw_step_dir(jax.random.fold_in(splits[5], 71), 0),
        "intersection": draw_intersection(jax.random.fold_in(splits[5], 71), 0),
        "density": draw_density(jax.random.fold_in(splits[5], 71), 0),
        "kohn_sham": draw_kohn_sham(jax.random.fold_in(splits[5], 71), 0),
    }


def product(left_blocks, right_blocks, block_cols):
    def one_row(row_args):
        row_cols, row_left = row_args
        target_rows = jnp.clip(row_cols, 0, NB - 1).astype(jnp.int32)
        right_rows = right_blocks[target_rows].astype(jnp.float32)
        right_cols = block_cols[target_rows]
        matched = (right_cols[:, None, :] == row_cols[None, :, None]) & (row_cols[None, :, None] >= 0) & (row_cols[:, None, None] >= 0)
        picked = jnp.einsum('tab,tbqr->taqr', matched.astype(jnp.float32), right_rows, precision=lax.Precision.HIGHEST)
        return jnp.einsum('apr,taqr->tpq', row_left.astype(jnp.float32), picked, precision=lax.Precision.HIGHEST)

    return lax.map(one_row, (block_cols, left_blocks))


def reference(block_cols, step_dir, intersection, density, kohn_sham):
    scaled_step = product(step_dir, intersection, block_cols).astype(jnp.bfloat16)
    summed = product(scaled_step, density, block_cols) + product(density, scaled_step, block_cols)
    change = (-summed).astype(jnp.bfloat16)
    difference = product(kohn_sham, change, block_cols) - product(change, kohn_sham, block_cols)
    commutator = difference.astype(jnp.bfloat16)
    trace_value = jnp.sum(change.astype(jnp.float32) * kohn_sham.astype(jnp.float32)) / (NB * BLK * BLK)
    return commutator, trace_value
```

```python
import functools

import jax
import jax.numpy as jnp
from jax import lax
from jax.experimental import pallas as pl
from jax.experimental.pallas import tpu as pltpu
from jax.sharding import PartitionSpec as P

CORES = 2


def row_major_perm(n_row, n_col, target):
    pairs = []
    for r in range(n_row):
        for c in range(n_col):
            to_r, to_c = target(r, c)
            pairs.append((r * n_col + c, to_r * n_col + to_c))
    return pairs


def load_blocks(pieces, scratch, sems):
    per_piece = pieces[0].shape[0]
    copies = []
    for index, piece in enumerate(pieces):
        copy = pltpu.make_async_copy(
            piece, scratch.at[pl.ds(index * per_piece, per_piece)], sems.at[index]
        )
        copy.start()
        copies.append(copy)
    last = scratch.shape[0] - 1
    scratch[last] = jnp.zeros(scratch.shape[1:], scratch.dtype)
    return copies


def multiply(index_ref, left_of, scratch, outs, rows, slots, contract):
    for i in range(rows):
        left = left_of(i)
        for h, out in enumerate(outs):
            for x in range(out.shape[0]):
                for s in range(slots):
                    base = (((h * out.shape[0] + x) * rows + i) * slots + s) * slots
                    right = jnp.concatenate(
                        [scratch[index_ref[base + a]] for a in range(slots)], axis=1
                    )
                    out[x, i * slots + s] = lax.dot_general(
                        right,
                        left,
                        (((1,), (contract,)), ((), ())),
                        preferred_element_type=jnp.float32,
                    ).astype(out.dtype)


def first_kernel(rows, slots, n_pieces, index_ref, left_ref, *refs):
    pieces, (keep, send), (scratch, sems) = refs[:n_pieces], refs[n_pieces:-2], refs[-2:]
    copies = load_blocks(pieces, scratch, sems)
    for copy in copies:
        copy.wait()

    def left_of(i):
        return jnp.concatenate([left_ref[i * slots + a] for a in range(slots)], axis=1)

    multiply(index_ref, left_of, scratch, (keep, send), rows, slots, 1)


def second_kernel(rows, slots, n_pieces, index_ref, total_ref, *refs):
    n_recv = len(refs) - n_pieces - 4
    received, refs = refs[:n_recv], refs[n_recv:]
    pieces, (keep, send), (scratch, sems) = refs[:n_pieces], refs[n_pieces:-2], refs[-2:]
    copies = load_blocks(pieces, scratch, sems)

    def left_of(i):
        blocks = []
        for a in range(slots):
            value = total_ref[i * slots + a]
            for part in received:
                value = value + part[i * slots + a].astype(jnp.float32)
            blocks.append(value.astype(jnp.bfloat16))
        return jnp.concatenate(blocks, axis=0)

    for copy in copies:
        copy.wait()
    multiply(index_ref, left_of, scratch, (keep, send), rows, slots, 0)


def third_kernel(rows, slots, n_pieces, n_mirror, index_ref, mirror_ref, total_ref, own_ref, *refs):
    mirrored, refs = refs[:n_mirror], refs[n_mirror:]
    pieces, refs = refs[:n_pieces], refs[n_pieces:]
    keep, send, trace, scratch, sems, mirror_scratch, mirror_sems, change = refs
    mirror_copies = load_blocks(mirrored, mirror_scratch, mirror_sems)
    copies = load_blocks(pieces, scratch, sems)
    for copy in mirror_copies:
        copy.wait()
    total_trace = jnp.zeros(trace.shape, jnp.float32)
    for b in range(rows * slots):
        other = mirror_scratch[mirror_ref[b]].astype(jnp.float32).T
        value = (-(total_ref[b] + other)).astype(jnp.bfloat16)
        change[b] = value
        product = value.astype(jnp.float32) * own_ref[b].astype(jnp.float32).T
        total_trace = total_trace + product.reshape((-1,) + trace.shape).sum(0)
    trace[...] = total_trace

    def left_of(i):
        return jnp.concatenate([change[i * slots + a] for a in range(slots)], axis=0)

    for copy in copies:
        copy.wait()
    multiply(index_ref, left_of, scratch, (keep, send), rows, slots, 0)


def last_kernel(n_mirror, mirror_ref, total_ref, *refs):
    mirrored, (out, mirror_scratch, mirror_sems) = refs[:n_mirror], refs[n_mirror:]
    copies = load_blocks(mirrored, mirror_scratch, mirror_sems)
    for copy in copies:
        copy.wait()
    for b in range(out.shape[0]):
        other = mirror_scratch[mirror_ref[b]].astype(jnp.float32)
        out[b] = (other - total_ref[b].T).astype(out.dtype)


def per_device(n_row, n_col, block_cols, step_dir, intersection, density, kohn_sham):
    rows, slots, side = step_dir.shape[:3]
    blocks = rows * slots
    blocks_total = block_cols.shape[0]
    n_chip = n_col // CORES
    inner = n_row // n_col
    outer = n_row // inner
    row_index = lax.axis_index("row")
    col_index = lax.axis_index("col")
    chip_index, core_index = col_index // CORES, col_index % CORES
    outer_index, inner_index = row_index // inner, row_index % inner
    bf16, f32 = jnp.bfloat16, jnp.float32

    by_group = block_cols.reshape(blocks_total, n_col, slots)
    own_rows = lax.dynamic_slice_in_dim(by_group, row_index * rows, rows, 0)
    own_cols = lax.dynamic_slice_in_dim(own_rows, col_index, 1, 1)[:, 0]
    group_cols = lax.dynamic_slice_in_dim(by_group, col_index, 1, 1)[:, 0]
    mirror_cols = lax.dynamic_slice_in_dim(by_group, outer_index, 1, 1)[:, 0]
    rel_core, rel_chip = jnp.meshgrid(jnp.arange(CORES), jnp.arange(n_chip), indexing="ij")
    rel_group = ((chip_index + rel_chip) % n_chip) * CORES + (core_index + rel_core) % CORES
    wanted = own_rows[:, rel_group].transpose(1, 2, 0, 3)
    safe = jnp.clip(wanted, 0, blocks_total - 1)
    right_cols = group_cols[safe]
    matched = (
        (right_cols[..., None, :] == own_cols[None, None, :, None, :, None])
        & (wanted >= 0)[..., None, None]
        & (own_cols >= 0)[None, None, :, None, :, None]
    )
    safe_dev = safe // rows
    piece = ((inner_index - safe_dev) % inner) * outer + (outer_index - safe_dev // inner) % outer
    place = (piece * rows + safe % rows) * slots
    index = jnp.where(
        matched.any(-1), place[..., None] + jnp.argmax(matched, axis=-1), n_row * blocks
    ).astype(jnp.int32).reshape(-1)

    own_ids = row_index * rows + jnp.arange(rows)
    safe_own = jnp.clip(own_cols, 0, blocks_total - 1)
    found = mirror_cols[safe_own] == own_ids[:, None, None]
    source = (inner_index - safe_own // rows) % inner
    mirror = jnp.where(
        own_cols >= 0,
        (source * rows + safe_own % rows) * slots + jnp.argmax(found, axis=-1),
        inner * blocks,
    ).astype(jnp.int32).reshape(-1)

    def shift_outer(k):
        return [
            (r, ((r // inner + k) % outer) * inner + r % inner) for r in range(n_row)
        ]

    def shift_inner(m):
        return [(r, (r // inner) * inner + (r % inner + m) % inner) for r in range(n_row)]

    def gather_rows(x):
        first = [x] + [lax.ppermute(x, "row", shift_outer(k)) for k in range(1, outer)]
        pieces = list(first)
        for m in range(1, inner):
            pieces += [lax.ppermute(p, "row", shift_inner(m)) for p in first]
        return first, pieces

    flip_core = [(c, (c // CORES) * CORES + (c + 1) % CORES) for c in range(n_col)]

    def shift_chip(d):
        return [(c, ((c // CORES + d) % n_chip) * CORES + c % CORES) for c in range(n_col)]

    def scatter_sum(keep, send):
        total = keep + lax.ppermute(send, "col", flip_core)
        sent = total[1:].astype(bf16)
        received = [lax.ppermute(sent[d - 1], "col", shift_chip(d)) for d in range(1, n_chip)]
        return total[0], received

    def mirror_send(x):
        out = []
        for m in range(inner):
            pairs = row_major_perm(
                n_row, n_col, lambda r, c: (inner * c + (r % inner + m) % inner, r // inner)
            )
            moved = lax.ppermute(x, ("row", "col"), pairs)
            out.append(moved)
        return out

    def add_up(total, received):
        value = total
        for part in received:
            value = value + part.astype(f32)
        return value

    smem = pl.BlockSpec(memory_space=pltpu.SMEM)
    vmem = pl.BlockSpec(memory_space=pltpu.VMEM)
    anywhere = pl.BlockSpec(memory_space=pl.ANY)
    partial_shape = jax.ShapeDtypeStruct((n_chip, blocks, side, side), f32)
    params = pltpu.CompilerParams(vmem_limit_bytes=32 * 2**20)
    right_scratch = [
        pltpu.VMEM((n_row * blocks + 1, side, side), bf16),
        pltpu.SemaphoreType.DMA((n_row,)),
    ]
    mirror_scratch = [
        pltpu.VMEM((inner * blocks + 1, side, side), bf16),
        pltpu.SemaphoreType.DMA((inner,)),
    ]
    product_flops = 2 * CORES * n_chip * blocks * slots * side**3
    cost = pl.CostEstimate(
        flops=product_flops, bytes_accessed=4 * 2**20, transcendentals=0
    )

    flat = lambda x: x.reshape(blocks, side, side)
    step, inter, dens, kohn = flat(step_dir), flat(intersection), flat(density), flat(kohn_sham)

    inter_first, inter_pieces = gather_rows(inter)
    dens_in, _ = lax.optimization_barrier((dens, tuple(inter_first)))
    dens_first, dens_pieces = gather_rows(dens_in)
    kohn_in, _ = lax.optimization_barrier((kohn, tuple(dens_first)))
    _, kohn_pieces = gather_rows(kohn_in)

    keep, send = pl.pallas_call(
        functools.partial(first_kernel, rows, slots, n_row),
        out_shape=(partial_shape, partial_shape),
        in_specs=[smem, vmem] + [anywhere] * n_row,
        out_specs=(vmem, vmem),
        scratch_shapes=right_scratch,
        compiler_params=params,
        cost_estimate=cost,
        name="scaled_step_product",
    )(index, step, *inter_pieces)
    total, received = scatter_sum(keep, send)

    keep, send = pl.pallas_call(
        functools.partial(second_kernel, rows, slots, n_row),
        out_shape=(partial_shape, partial_shape),
        in_specs=[smem, vmem] + [vmem] * len(received) + [anywhere] * n_row,
        out_specs=(vmem, vmem),
        scratch_shapes=right_scratch,
        compiler_params=params,
        cost_estimate=cost,
        name="change_product",
    )(index, total, *received, *dens_pieces)
    total = add_up(*scatter_sum(keep, send))
    mirrored = mirror_send(total.astype(bf16))

    keep, send, trace = pl.pallas_call(
        functools.partial(third_kernel, rows, slots, n_row, inner),
        out_shape=(partial_shape, partial_shape, jax.ShapeDtypeStruct((8, side), f32)),
        in_specs=[smem, smem, vmem, vmem] + [anywhere] * (inner + n_row),
        out_specs=(vmem, vmem, vmem),
        scratch_shapes=right_scratch + mirror_scratch + [pltpu.VMEM((blocks, side, side), bf16)],
        compiler_params=params,
        cost_estimate=cost,
        name="commutator_product",
    )(index, mirror, total, kohn, *mirrored, *kohn_pieces)
    traces = lax.all_gather(trace, ("row", "col"), axis=0, tiled=False)
    total = add_up(*scatter_sum(keep, send))
    mirrored = mirror_send(total.astype(bf16))

    commutator = pl.pallas_call(
        functools.partial(last_kernel, inner),
        out_shape=jax.ShapeDtypeStruct((blocks, side, side), bf16),
        in_specs=[smem, vmem] + [anywhere] * inner,
        out_specs=vmem,
        scratch_shapes=mirror_scratch,
        compiler_params=params,
        name="commutator_difference",
    )(mirror, total, *mirrored)
    trace_value = traces.sum() / (blocks_total * side * side)
    return commutator.reshape(step_dir.shape), trace_value


def solution(mesh):
    in_specs = (P(),) + (P("row", "col", None, None),) * 4
    out_specs = (P("row", "col", None, None), P())
    return jax.shard_map(
        functools.partial(per_device, mesh.shape["row"], mesh.shape["col"]),
        mesh=mesh,
        in_specs=in_specs,
        out_specs=out_specs,
        check_vma=False,
    )
```

```python
import functools

import jax
import jax.numpy as jnp
from jax import lax
from jax.experimental import pallas as pl
from jax.experimental.pallas import tpu as pltpu
from jax.sharding import PartitionSpec as P

CORES = 2


def row_major_perm(n_row, n_col, target):
    pairs = []
    for r in range(n_row):
        for c in range(n_col):
            to_r, to_c = target(r, c)
            pairs.append((r * n_col + c, to_r * n_col + to_c))
    return pairs


def load_blocks(pieces, scratch, sems):
    per_piece = pieces[0].shape[0]
    copies = []
    for index, piece in enumerate(pieces):
        copy = pltpu.make_async_copy(
            piece, scratch.at[pl.ds(index * per_piece, per_piece)], sems.at[index]
        )
        copy.start()
        copies.append(copy)
    last = scratch.shape[0] - 1
    scratch[last] = jnp.zeros(scratch.shape[1:], scratch.dtype)
    return copies


def multiply(index_ref, left_of, scratch, outs, rows, slots, contract):
    for i in range(rows):
        left = left_of(i)
        for h, out in enumerate(outs):
            for x in range(out.shape[0]):
                for s in range(slots):
                    base = (((h * out.shape[0] + x) * rows + i) * slots + s) * slots
                    right = jnp.concatenate(
                        [scratch[index_ref[base + a]] for a in range(slots)], axis=1
                    )
                    out[x, i * slots + s] = lax.dot_general(
                        right,
                        left,
                        (((1,), (contract,)), ((), ())),
                        preferred_element_type=jnp.float32,
                    ).astype(out.dtype)


def first_kernel(rows, slots, n_pieces, index_ref, left_ref, *refs):
    pieces, (keep, send, scratch, sems) = refs[:n_pieces], refs[-4:]
    copies = load_blocks(pieces, scratch, sems)
    for copy in copies:
        copy.wait()

    def left_of(i):
        return jnp.concatenate([left_ref[i * slots + a] for a in range(slots)], axis=1)

    multiply(index_ref, left_of, scratch, (keep, send), rows, slots, 1)


def second_kernel(rows, slots, n_pieces, n_recv, index_ref, total_ref, *refs):
    received, refs = refs[:n_recv], refs[n_recv:]
    pieces, (keep, send, scratch, sems) = refs[:n_pieces], refs[-4:]
    copies = load_blocks(pieces, scratch, sems)

    def left_of(i):
        blocks = []
        for a in range(slots):
            value = total_ref[i * slots + a]
            for part in received:
                value = value + part[i * slots + a].astype(jnp.float32)
            blocks.append(value.astype(jnp.bfloat16))
        return jnp.concatenate(blocks, axis=0)

    for copy in copies:
        copy.wait()
    multiply(index_ref, left_of, scratch, (keep, send), rows, slots, 0)


def third_kernel(rows, slots, n_pieces, n_mirror, index_ref, mirror_ref, total_ref, own_ref, *refs):
    mirrored, refs = refs[:n_mirror], refs[n_mirror:]
    pieces, refs = refs[:n_pieces], refs[n_pieces:]
    keep, send, trace, scratch, sems, mirror_scratch, mirror_sems, change = refs
    mirror_copies = load_blocks(mirrored, mirror_scratch, mirror_sems)
    copies = load_blocks(pieces, scratch, sems)
    for copy in mirror_copies:
        copy.wait()
    total_trace = jnp.zeros(trace.shape, jnp.float32)
    for b in range(rows * slots):
        other = mirror_scratch[mirror_ref[b]].astype(jnp.float32).T
        value = (-(total_ref[b] + other)).astype(jnp.bfloat16)
        change[b] = value
        product = value.astype(jnp.float32) * own_ref[b].astype(jnp.float32).T
        total_trace = total_trace + product.reshape((-1,) + trace.shape).sum(0)
    trace[...] = total_trace

    def left_of(i):
        return jnp.concatenate([change[i * slots + a] for a in range(slots)], axis=0)

    for copy in copies:
        copy.wait()
    multiply(index_ref, left_of, scratch, (keep, send), rows, slots, 0)


def last_kernel(n_mirror, mirror_ref, own_ref, *refs):
    mirrored, (out, mirror_scratch, mirror_sems) = refs[:n_mirror], refs[n_mirror:]
    copies = load_blocks(mirrored, mirror_scratch, mirror_sems)
    for copy in copies:
        copy.wait()
    for b in range(out.shape[0]):
        other = mirror_scratch[mirror_ref[b]].astype(jnp.float32)
        out[b] = (other - own_ref[b].astype(jnp.float32).T).astype(out.dtype)


def per_device(n_row, n_col, block_cols, step_dir, intersection, density, kohn_sham):
    rows, slots, side = step_dir.shape[:3]
    blocks = rows * slots
    blocks_total = block_cols.shape[0]
    n_chip = n_col // CORES
    inner = n_row // n_col
    outer = n_row // inner
    row_index = lax.axis_index("row")
    col_index = lax.axis_index("col")
    chip_index, core_index = col_index // CORES, col_index % CORES
    outer_index, inner_index = row_index // inner, row_index % inner
    bf16, f32 = jnp.bfloat16, jnp.float32

    def place_of(g):
        return (g % n_chip) * CORES + g // n_chip

    def group_of(c):
        return (c % CORES) * n_chip + c // CORES

    own_group = group_of(col_index)

    by_group = block_cols.reshape(blocks_total, n_col, slots)
    own_rows = lax.dynamic_slice_in_dim(by_group, row_index * rows, rows, 0)
    own_cols = lax.dynamic_slice_in_dim(own_rows, own_group, 1, 1)[:, 0]
    group_cols = lax.dynamic_slice_in_dim(by_group, own_group, 1, 1)[:, 0]
    mirror_cols = lax.dynamic_slice_in_dim(by_group, outer_index, 1, 1)[:, 0]
    rel_core, rel_chip = jnp.meshgrid(jnp.arange(CORES), jnp.arange(n_chip), indexing="ij")
    rel_group = ((core_index + rel_core) % CORES) * n_chip + (chip_index + rel_chip) % n_chip
    wanted = own_rows[:, rel_group].transpose(1, 2, 0, 3)
    safe = jnp.clip(wanted, 0, blocks_total - 1)
    right_cols = group_cols[safe]
    matched = (
        (right_cols[..., None, :] == own_cols[None, None, :, None, :, None])
        & (wanted >= 0)[..., None, None]
        & (own_cols >= 0)[None, None, :, None, :, None]
    )
    safe_dev = safe // rows
    piece = ((inner_index - safe_dev) % inner) * outer + (outer_index ^ (safe_dev // inner))
    place = (piece * rows + safe % rows) * slots
    index = jnp.where(
        matched.any(-1), place[..., None] + jnp.argmax(matched, axis=-1), n_row * blocks
    ).astype(jnp.int32).reshape(-1)

    own_ids = row_index * rows + jnp.arange(rows)

    def mirror_table(cols):
        safe_own = jnp.clip(cols, 0, blocks_total - 1)
        found = mirror_cols[safe_own] == own_ids[:, None, None]
        source = (inner_index - safe_own // rows) % inner
        return jnp.where(
            cols >= 0,
            (source * rows + safe_own % rows) * slots + jnp.argmax(found, axis=-1),
            inner * blocks,
        ).astype(jnp.int32).reshape(-1)

    out_cols = lax.dynamic_slice_in_dim(own_rows, col_index, 1, 1)[:, 0]
    mirror, out_mirror = mirror_table(own_cols), mirror_table(out_cols)

    def permute(x, target):
        return lax.ppermute(x, ("row", "col"), row_major_perm(n_row, n_col, target))

    def relayout(x, m=0, turn=0):
        def target(r, c):
            o, q = r // inner, r % inner
            return (o ^ m) * inner + (q + turn) % inner, place_of(c)

        return permute(x, target)

    def to_inner(x, turn):
        return permute(x, lambda r, c: ((r // inner) * inner + (r % inner + turn) % inner, c))

    def gather_first(x):
        far = {m: relayout(x, m) for m in range(2, outer, 2)}
        near = {1: relayout(x, 1), 0: relayout(x)}
        beside = [relayout(x, 0, turn) for turn in range(1, inner)]
        return far | near, beside

    def gather_rest(first, beside):
        for m in range(2, outer, 2):
            first[m + 1] = permute(first[m], lambda r, c: ((r // inner ^ 1) * inner + r % inner, c))
        pieces = [first[m] for m in range(outer)]
        for turn in range(1, inner):
            pieces += [beside[turn - 1]] + [to_inner(first[m], turn) for m in range(1, outer)]
        return pieces

    def scatter_sum(keep, send):
        def flip(c):
            return (c // CORES) * CORES + (c + 1) % CORES

        def shift(c, d):
            return ((c // CORES + d) % n_chip) * CORES + c % CORES

        total = keep + permute(send, lambda r, c: (r, flip(c))).astype(f32)
        sent = total[1:].astype(bf16)
        received = [
            permute(sent[d - 1], lambda r, c, d=d: (r, shift(c, d))) for d in range(1, n_chip)
        ]
        return total[0], received

    def mirror_send(x, landing):
        return [
            permute(
                x,
                lambda r, c, m=m: (
                    inner * group_of(c) + (r % inner + m) % inner,
                    landing(r // inner),
                ),
            )
            for m in range(inner)
        ]

    def add_up(total, received):
        value = total
        for part in received:
            value = value + part.astype(f32)
        return value

    def sum_over_devices(x):
        step = 1
        while step < n_col:
            x = x + permute(x, lambda r, c, step=step: (r, c ^ step))
            step *= 2
        step = 1
        while step < n_row:
            x = x + permute(x, lambda r, c, step=step: (r ^ step, c))
            step *= 2
        return x

    smem = pl.BlockSpec(memory_space=pltpu.SMEM)
    vmem = pl.BlockSpec(memory_space=pltpu.VMEM)
    anywhere = pl.BlockSpec(memory_space=pl.ANY)
    partial_shapes = tuple(
        jax.ShapeDtypeStruct((n_chip, blocks, side, side), dtype) for dtype in (f32, bf16)
    )
    params = pltpu.CompilerParams(vmem_limit_bytes=32 * 2**20)
    right_scratch = [
        pltpu.VMEM((n_row * blocks + 1, side, side), bf16),
        pltpu.SemaphoreType.DMA((n_row,)),
    ]
    mirror_scratch = [
        pltpu.VMEM((inner * blocks + 1, side, side), bf16),
        pltpu.SemaphoreType.DMA((inner,)),
    ]
    product_flops = 2 * CORES * n_chip * blocks * slots * side**3
    cost = pl.CostEstimate(
        flops=product_flops, bytes_accessed=4 * 2**20, transcendentals=0
    )

    flat = lambda x: x.reshape(blocks, side, side)
    step, inter, dens, kohn = flat(step_dir), flat(intersection), flat(density), flat(kohn_sham)

    inter_first, inter_beside = gather_first(inter)
    step = relayout(step)
    dens_in, _ = lax.optimization_barrier((dens, (inter_first[1], inter_first[2])))
    dens_first, dens_beside = gather_first(dens_in)
    kohn_in, _ = lax.optimization_barrier((kohn, (dens_first[1], dens_first[2])))
    kohn_first, kohn_beside = gather_first(kohn_in)
    dens_early = [dens_first[m] for m in sorted(dens_first)] + dens_beside
    kohn_early = [kohn_first[m] for m in sorted(kohn_first)] + kohn_beside
    inter_pieces = gather_rest(inter_first, inter_beside)
    dens_pieces = gather_rest(dens_first, dens_beside)
    kohn_pieces = gather_rest(kohn_first, kohn_beside)

    keep, send = pl.pallas_call(
        functools.partial(first_kernel, rows, slots, n_row),
        out_shape=partial_shapes,
        in_specs=[smem, vmem] + [anywhere] * (n_row + len(dens_early)),
        out_specs=(vmem, vmem),
        scratch_shapes=right_scratch,
        compiler_params=params,
        cost_estimate=cost,
        name="scaled_step_product",
    )(index, step, *inter_pieces, *dens_early)
    total, received = scatter_sum(keep, send)

    keep, send = pl.pallas_call(
        functools.partial(second_kernel, rows, slots, n_row, len(received)),
        out_shape=partial_shapes,
        in_specs=[smem, vmem] + [vmem] * len(received) + [anywhere] * (n_row + len(kohn_early)),
        out_specs=(vmem, vmem),
        scratch_shapes=right_scratch,
        compiler_params=params,
        cost_estimate=cost,
        name="change_product",
    )(index, total, *received, *dens_pieces, *kohn_early)
    total = add_up(*scatter_sum(keep, send))
    mirrored = mirror_send(total.astype(bf16), place_of)

    keep, send, trace = pl.pallas_call(
        functools.partial(third_kernel, rows, slots, n_row, inner),
        out_shape=partial_shapes + (jax.ShapeDtypeStruct((8, side), f32),),
        in_specs=[smem, smem, vmem, vmem] + [anywhere] * (inner + n_row),
        out_specs=(vmem, vmem, vmem),
        scratch_shapes=right_scratch + mirror_scratch + [pltpu.VMEM((blocks, side, side), bf16)],
        compiler_params=params,
        cost_estimate=cost,
        name="commutator_product",
    )(index, mirror, total, kohn_pieces[0], *mirrored, *kohn_pieces)
    trace = sum_over_devices(trace)
    total = add_up(*scatter_sum(keep, send)).astype(bf16)
    mirrored = mirror_send(total, lambda o: o)
    own = permute(total, lambda r, c: (r, group_of(c)))

    commutator = pl.pallas_call(
        functools.partial(last_kernel, inner),
        out_shape=jax.ShapeDtypeStruct((blocks, side, side), bf16),
        in_specs=[smem, vmem] + [anywhere] * inner,
        out_specs=vmem,
        scratch_shapes=mirror_scratch,
        compiler_params=params,
        name="commutator_difference",
    )(out_mirror, own, *mirrored)
    trace_value = trace.sum() / (blocks_total * side * side)
    return commutator.reshape(step_dir.shape), trace_value


def solution(mesh):
    in_specs = (P(),) + (P("row", "col", None, None),) * 4
    out_specs = (P("row", "col", None, None), P())
    return jax.shard_map(
        functools.partial(per_device, mesh.shape["row"], mesh.shape["col"]),
        mesh=mesh,
        in_specs=in_specs,
        out_specs=out_specs,
        check_vma=False,
    )
```

```python
import functools

import jax
import jax.numpy as jnp
from jax import lax
from jax.experimental import pallas as pl
from jax.experimental.pallas import tpu as pltpu
from jax.sharding import PartitionSpec as P

CORES = 2


def row_major_perm(n_row, n_col, target):
    pairs = []
    for r in range(n_row):
        for c in range(n_col):
            to_r, to_c = target(r, c)
            pairs.append((r * n_col + c, to_r * n_col + to_c))
    return pairs


def load_blocks(pieces, scratch, sems):
    per_piece = pieces[0].shape[0]
    copies = []
    for index, piece in enumerate(pieces):
        copy = pltpu.make_async_copy(
            piece, scratch.at[pl.ds(index * per_piece, per_piece)], sems.at[index]
        )
        copy.start()
        copies.append(copy)
    last = scratch.shape[0] - 1
    scratch[last] = jnp.zeros(scratch.shape[1:], scratch.dtype)
    return copies


def multiply(index_ref, left_of, scratch, own, away, cross, rows, slots, contract):
    n_chip = cross.shape[0]
    for i in range(rows):
        left = left_of(i)
        for h in range(CORES):
            for x in range(n_chip):
                out = cross.at[x] if h else (away.at[x - 1] if x else own)
                for s in range(slots):
                    base = (((h * n_chip + x) * rows + i) * slots + s) * slots
                    right = jnp.concatenate(
                        [scratch[index_ref[base + a]] for a in range(slots)], axis=1
                    )
                    out[i * slots + s] = lax.dot_general(
                        right,
                        left,
                        (((1,), (contract,)), ((), ())),
                        preferred_element_type=jnp.float32,
                    ).astype(out.dtype)


def summed(own, core, chips, block):
    value = own[block] + core[0, block].astype(jnp.float32)
    for part in chips:
        value = value + part[block].astype(jnp.float32)
    return value


def first_kernel(rows, slots, n_pieces, index_ref, left_ref, *refs):
    pieces, (own, away, cross, scratch, sems) = refs[:n_pieces], refs[n_pieces:]
    copies = load_blocks(pieces, scratch, sems)
    for copy in copies:
        copy.wait()

    def left_of(i):
        return jnp.concatenate([left_ref[i * slots + a] for a in range(slots)], axis=1)

    multiply(index_ref, left_of, scratch, own, away, cross, rows, slots, 1)


def second_kernel(rows, slots, index_ref, right_ref, own_in, core_in, *refs):
    chips_in, (own, away, cross, scratch, sems) = refs[:-5], refs[-5:]
    copies = load_blocks([right_ref], scratch, sems)

    def left_of(i):
        return jnp.concatenate(
            [
                summed(own_in, core_in, chips_in, i * slots + a).astype(jnp.bfloat16)
                for a in range(slots)
            ],
            axis=0,
        )

    for copy in copies:
        copy.wait()
    multiply(index_ref, left_of, scratch, own, away, cross, rows, slots, 0)


def third_kernel(rows, slots, n_mirror, index_ref, mirror_ref, kohn_ref, right_ref, own_in, core_in, *refs):
    refs, (own, away, cross, trace, scratch, sems, mirror_scratch, mirror_sems, change) = (
        refs[:-9],
        refs[-9:],
    )
    mirrored, chips_in = refs[:n_mirror], refs[n_mirror:]
    mirror_copies = load_blocks(mirrored, mirror_scratch, mirror_sems)
    copies = load_blocks([right_ref], scratch, sems)
    for copy in mirror_copies:
        copy.wait()
    total_trace = jnp.zeros(trace.shape, jnp.float32)
    for b in range(rows * slots):
        other = mirror_scratch[mirror_ref[b]].astype(jnp.float32).T
        value = (-(summed(own_in, core_in, chips_in, b) + other)).astype(jnp.bfloat16)
        change[b] = value
        product = value.astype(jnp.float32) * kohn_ref[b].astype(jnp.float32).T
        total_trace = total_trace + product.reshape((-1,) + trace.shape).sum(0)
    trace[...] = total_trace

    def left_of(i):
        return jnp.concatenate([change[i * slots + a] for a in range(slots)], axis=0)

    for copy in copies:
        copy.wait()
    multiply(index_ref, left_of, scratch, own, away, cross, rows, slots, 0)


def last_kernel(n_mirror, mirror_ref, own_ref, *refs):
    mirrored, (out, mirror_scratch, mirror_sems) = refs[:n_mirror], refs[n_mirror:]
    copies = load_blocks(mirrored, mirror_scratch, mirror_sems)
    for copy in copies:
        copy.wait()
    for b in range(out.shape[0]):
        other = mirror_scratch[mirror_ref[b]].astype(jnp.float32)
        out[b] = (other - own_ref[b].astype(jnp.float32).T).astype(out.dtype)


def per_device(n_row, n_col, block_cols, step_dir, intersection, density, kohn_sham):
    rows, slots, side = step_dir.shape[:3]
    blocks = rows * slots
    blocks_total = block_cols.shape[0]
    n_chip = n_col // CORES
    inner = n_row // n_col
    outer = n_row // inner
    row_index = lax.axis_index("row")
    col_index = lax.axis_index("col")
    chip_index, core_index = col_index // CORES, col_index % CORES
    outer_index, inner_index = row_index // inner, row_index % inner
    bf16, f32 = jnp.bfloat16, jnp.float32

    def place_of(g):
        return (g % n_chip) * CORES + g // n_chip

    def group_of(c):
        return (c % CORES) * n_chip + c // CORES

    own_group = group_of(col_index)

    by_group = block_cols.reshape(blocks_total, n_col, slots)
    own_rows = lax.dynamic_slice_in_dim(by_group, row_index * rows, rows, 0)
    own_cols = lax.dynamic_slice_in_dim(own_rows, own_group, 1, 1)[:, 0]
    group_cols = lax.dynamic_slice_in_dim(by_group, own_group, 1, 1)[:, 0]
    mirror_cols = lax.dynamic_slice_in_dim(by_group, outer_index, 1, 1)[:, 0]
    rel_core, rel_chip = jnp.meshgrid(jnp.arange(CORES), jnp.arange(n_chip), indexing="ij")
    rel_group = ((core_index + rel_core) % CORES) * n_chip + (chip_index + rel_chip) % n_chip
    wanted = own_rows[:, rel_group].transpose(1, 2, 0, 3)
    safe = jnp.clip(wanted, 0, blocks_total - 1)
    right_cols = group_cols[safe]
    matched = (
        (right_cols[..., None, :] == own_cols[None, None, :, None, :, None])
        & (wanted >= 0)[..., None, None]
        & (own_cols >= 0)[None, None, :, None, :, None]
    )
    safe_dev = safe // rows
    piece = ((inner_index - safe_dev) % inner) * outer + (outer_index ^ (safe_dev // inner))
    gathered = (safe_dev % inner) * outer + safe_dev // inner
    hit, which = matched.any(-1), jnp.argmax(matched, axis=-1)

    def index_table(piece):
        place = (piece * rows + safe % rows) * slots
        index = jnp.where(hit, place[..., None] + which, n_row * blocks)
        return index.astype(jnp.int32).reshape(-1)

    piece_index, index = index_table(piece), index_table(gathered)

    own_ids = row_index * rows + jnp.arange(rows)

    def mirror_table(cols):
        safe_own = jnp.clip(cols, 0, blocks_total - 1)
        found = mirror_cols[safe_own] == own_ids[:, None, None]
        source = (inner_index - safe_own // rows) % inner
        return jnp.where(
            cols >= 0,
            (source * rows + safe_own % rows) * slots + jnp.argmax(found, axis=-1),
            inner * blocks,
        ).astype(jnp.int32).reshape(-1)

    out_cols = lax.dynamic_slice_in_dim(own_rows, col_index, 1, 1)[:, 0]
    mirror, out_mirror = mirror_table(own_cols), mirror_table(out_cols)

    def permute(x, target):
        return lax.ppermute(x, ("row", "col"), row_major_perm(n_row, n_col, target))

    def relayout(x, m=0, turn=0):
        def target(r, c):
            o, q = r // inner, r % inner
            return (o ^ m) * inner + (q + turn) % inner, place_of(c)

        return permute(x, target)

    def to_inner(x, turn):
        return permute(x, lambda r, c: ((r // inner) * inner + (r % inner + turn) % inner, c))

    def gather_pieces(x, own):
        first = {m: relayout(x, m) for m in range(2, outer, 2)}
        first |= {1: relayout(x, 1), 0: own}
        beside = [relayout(x, 0, turn) for turn in range(1, inner)]
        for m in range(2, outer, 2):
            first[m + 1] = permute(first[m], lambda r, c: ((r // inner ^ 1) * inner + r % inner, c))
        pieces = [first[m] for m in range(outer)]
        for turn in range(1, inner):
            pieces += [beside[turn - 1]] + [to_inner(first[m], turn) for m in range(1, outer)]
        return pieces, (first[1], first[2])

    def gather_all(x):
        for groups in (
            [[o * inner + q for o in range(outer)] for q in range(inner)],
            [[o * inner + q for q in range(inner)] for o in range(outer)],
        ):
            x = lax.all_gather(x, "row", axis=0, tiled=True, axis_index_groups=groups)
        return x

    def exchange(away, cross):
        def flip(c):
            return (c // CORES) * CORES + (c + 1) % CORES

        def shift(c, d):
            return ((c // CORES + d) % n_chip) * CORES + c % CORES

        core = permute(cross, lambda r, c: (r, flip(c)))
        sent = (away + core[1:].astype(f32)).astype(bf16)
        chips = [
            permute(sent[d - 1], lambda r, c, d=d: (r, shift(c, d))) for d in range(1, n_chip)
        ]
        return core, chips

    def total_of(own, core, chips):
        value = own + core[0].astype(f32)
        for part in chips:
            value = value + part.astype(f32)
        return value.astype(bf16)

    def mirror_send(x, landing):
        return [
            permute(
                x,
                lambda r, c, m=m: (
                    inner * group_of(c) + (r % inner + m) % inner,
                    landing(r // inner),
                ),
            )
            for m in range(inner)
        ]

    def sum_over_devices(x):
        for axis in ("col", "row"):
            x = lax.all_gather(x, axis, axis=0, tiled=False).sum(0)
        return x

    smem = pl.BlockSpec(memory_space=pltpu.SMEM)
    vmem = pl.BlockSpec(memory_space=pltpu.VMEM)
    anywhere = pl.BlockSpec(memory_space=pl.ANY)
    partial_shapes = (
        jax.ShapeDtypeStruct((blocks, side, side), f32),
        jax.ShapeDtypeStruct((n_chip - 1, blocks, side, side), f32),
        jax.ShapeDtypeStruct((n_chip, blocks, side, side), bf16),
    )
    params = pltpu.CompilerParams(vmem_limit_bytes=16 * 2**20)

    def block_scratch(count, pieces):
        return [
            pltpu.VMEM((count + 1, side, side), bf16),
            pltpu.SemaphoreType.DMA((pieces,)),
        ]

    cost = pl.CostEstimate(
        flops=2 * CORES * n_chip * blocks * slots * side**3,
        bytes_accessed=4 * 2**20,
        transcendentals=0,
    )

    flat = lambda x: x.reshape(blocks, side, side)
    inter = flat(intersection)
    moved = relayout(
        jnp.stack([flat(step_dir), inter, flat(density), flat(kohn_sham)])
    )
    pieces, early = gather_pieces(inter, moved[1])
    dens_in, kohn_in, _ = lax.optimization_barrier((moved[2], moved[3], early))
    dens_rows = gather_all(dens_in)
    kohn_rows = gather_all(kohn_in)

    own, away, cross = pl.pallas_call(
        functools.partial(first_kernel, rows, slots, n_row),
        out_shape=partial_shapes,
        in_specs=[smem, vmem] + [anywhere] * n_row,
        out_specs=(vmem,) * 3,
        scratch_shapes=block_scratch(n_row * blocks, n_row),
        compiler_params=params,
        cost_estimate=cost,
        name="scaled_step_product",
    )(piece_index, moved[0], *pieces)
    core, chips = exchange(away, cross)

    own, away, cross = pl.pallas_call(
        functools.partial(second_kernel, rows, slots),
        out_shape=partial_shapes,
        in_specs=[smem, anywhere] + [vmem] * (2 + len(chips)),
        out_specs=(vmem,) * 3,
        scratch_shapes=block_scratch(n_row * blocks, 1),
        compiler_params=params,
        cost_estimate=cost,
        name="change_product",
    )(index, dens_rows, own, core, *chips)
    core, chips = exchange(away, cross)
    mirrored = mirror_send(total_of(own, core, chips), place_of)

    own, away, cross, trace = pl.pallas_call(
        functools.partial(third_kernel, rows, slots, inner),
        out_shape=partial_shapes + (jax.ShapeDtypeStruct((8, side), f32),),
        in_specs=[smem, smem, vmem, anywhere, vmem, vmem]
        + [anywhere] * inner
        + [vmem] * len(chips),
        out_specs=(vmem,) * 4,
        scratch_shapes=block_scratch(n_row * blocks, 1)
        + block_scratch(inner * blocks, inner)
        + [pltpu.VMEM((blocks, side, side), bf16)],
        compiler_params=params,
        cost_estimate=cost,
        name="commutator_product",
    )(index, mirror, kohn_in, kohn_rows, own, core, *mirrored, *chips)
    trace = sum_over_devices(trace)
    core, chips = exchange(away, cross)
    total = total_of(own, core, chips)
    mirrored = mirror_send(total, lambda o: o)
    own = permute(total, lambda r, c: (r, group_of(c)))

    commutator = pl.pallas_call(
        functools.partial(last_kernel, inner),
        out_shape=jax.ShapeDtypeStruct((blocks, side, side), bf16),
        in_specs=[smem, vmem] + [anywhere] * inner,
        out_specs=vmem,
        scratch_shapes=block_scratch(inner * blocks, inner),
        compiler_params=params,
        name="commutator_difference",
    )(out_mirror, own, *mirrored)
    trace_value = trace.sum() / (blocks_total * side * side)
    return commutator.reshape(step_dir.shape), trace_value


def solution(mesh):
    in_specs = (P(),) + (P("row", "col", None, None),) * 4
    out_specs = (P("row", "col", None, None), P())
    return jax.shard_map(
        functools.partial(per_device, mesh.shape["row"], mesh.shape["col"]),
        mesh=mesh,
        in_specs=in_specs,
        out_specs=out_specs,
        check_vma=False,
    )
```

```python
import functools

import jax
import jax.numpy as jnp
from jax import lax
from jax.experimental import pallas as pl
from jax.experimental.pallas import tpu as pltpu
from jax.sharding import PartitionSpec as P

CORES = 2


def row_major_perm(n_row, n_col, target):
    pairs = []
    for r in range(n_row):
        for c in range(n_col):
            to_r, to_c = target(r, c)
            pairs.append((r * n_col + c, to_r * n_col + to_c))
    return pairs


def load_blocks(pieces, scratch, sems):
    copies = []
    start = 0
    for index, piece in enumerate(pieces):
        count = piece.shape[0]
        copy = pltpu.make_async_copy(piece, scratch.at[pl.ds(start, count)], sems.at[index])
        copy.start()
        copies.append(copy)
        start += count
    scratch[start] = jnp.zeros(scratch.shape[1:], scratch.dtype)
    return copies


def multiply(index_ref, left_of, scratch, outs, rows, slots, contract):
    for i in range(rows):
        left = left_of(i)
        for d, out in enumerate(outs):
            for s in range(slots):
                base = ((d * rows + i) * slots + s) * slots
                right = jnp.concatenate(
                    [scratch[index_ref[base + a]] for a in range(slots)], axis=1
                )
                out[i * slots + s] = lax.dot_general(
                    right,
                    left,
                    (((1,), (contract,)), ((), ())),
                    preferred_element_type=jnp.float32,
                ).astype(out.dtype)


def summed(parts, block):
    value = parts[0][block]
    for part in parts[1:]:
        value = value + part[block].astype(jnp.float32)
    return value


def first_kernel(rows, slots, n_pieces, n_out, index_ref, left_ref, *refs):
    pieces, outs, (scratch, sems) = refs[:n_pieces], refs[-2 - n_out : -2], refs[-2:]
    copies = load_blocks(pieces, scratch, sems)
    for copy in copies:
        copy.wait()

    def left_of(i):
        return jnp.concatenate([left_ref[i * slots + a] for a in range(slots)], axis=1)

    multiply(index_ref, left_of, scratch, outs, rows, slots, 1)


def second_kernel(rows, slots, n_pieces, n_out, index_ref, *refs):
    pieces, parts = refs[:n_pieces], refs[n_pieces : n_pieces + n_out]
    outs, (scratch, sems) = refs[-2 - n_out : -2], refs[-2:]
    copies = load_blocks(pieces, scratch, sems)

    def left_of(i):
        blocks = [summed(parts, i * slots + a).astype(jnp.bfloat16) for a in range(slots)]
        return jnp.concatenate(blocks, axis=0)

    for copy in copies:
        copy.wait()
    multiply(index_ref, left_of, scratch, outs, rows, slots, 0)


def third_kernel(rows, slots, n_pieces, n_mirror, n_out, index_ref, mirror_ref, kohn_ref, *refs):
    pieces, refs = refs[:n_pieces], refs[n_pieces:]
    mirrored, refs = refs[:n_mirror], refs[n_mirror:]
    parts, outs = refs[:n_out], refs[n_out : 2 * n_out]
    trace, scratch, sems, mirror_scratch, mirror_sems, change = refs[2 * n_out :]
    mirror_copies = load_blocks(mirrored, mirror_scratch, mirror_sems)
    copies = load_blocks(pieces, scratch, sems)
    for copy in mirror_copies:
        copy.wait()
    total_trace = jnp.zeros(trace.shape, jnp.float32)
    for b in range(rows * slots):
        other = mirror_scratch[mirror_ref[b]].astype(jnp.float32).T
        value = (-(summed(parts, b) + other)).astype(jnp.bfloat16)
        change[b] = value
        product = value.astype(jnp.float32) * kohn_ref[b].astype(jnp.float32).T
        total_trace = total_trace + product.reshape((-1,) + trace.shape).sum(0)
    trace[...] = total_trace

    def left_of(i):
        return jnp.concatenate([change[i * slots + a] for a in range(slots)], axis=0)

    for copy in copies:
        copy.wait()
    multiply(index_ref, left_of, scratch, outs, rows, slots, 0)


def last_kernel(n_mirror, mirror_ref, own_ref, *refs):
    mirrored, (out, mirror_scratch, mirror_sems) = refs[:n_mirror], refs[n_mirror:]
    copies = load_blocks(mirrored, mirror_scratch, mirror_sems)
    for copy in copies:
        copy.wait()
    for b in range(out.shape[0]):
        other = mirror_scratch[mirror_ref[b]].astype(jnp.float32)
        out[b] = (other - own_ref[b].astype(jnp.float32).T).astype(out.dtype)


def per_device(n_row, n_col, block_cols, step_dir, intersection, density, kohn_sham):
    rows, slots, side = step_dir.shape[:3]
    blocks = rows * slots
    blocks_total = block_cols.shape[0]
    inner = n_row // n_col
    outer = n_row // inner
    assert inner == CORES and outer == n_col and outer & (outer - 1) == 0
    row_index = lax.axis_index("row")
    col_index = lax.axis_index("col")
    outer_index, inner_index = row_index // inner, row_index % inner
    bf16, f32 = jnp.bfloat16, jnp.float32

    def place(o, g):
        return g ^ ((o % 2) * (n_col // 2))

    def at(o, h, g):
        p = place(o, g)
        return o * inner + p % inner, (p // inner) * CORES + h

    def inside(r, c):
        o = r // inner
        return o, c % CORES, place(o, (c // CORES) * inner + r % inner)

    o_in, h_in, g_in = inside(row_index, col_index)

    by_group = block_cols.reshape(blocks_total, n_col, slots)
    mirror_cols = lax.dynamic_slice_in_dim(by_group, o_in, 1, 1)[:, 0]

    def rows_of(o, h):
        return lax.dynamic_slice_in_dim(by_group, (o * inner + h) * rows, rows, 0)

    def group_cols_of(cols, g):
        return lax.dynamic_slice_in_dim(cols, g, 1, 1)[:, 0]

    own_rows = rows_of(o_in, h_in)
    own_cols = group_cols_of(own_rows, g_in)
    group_cols = group_cols_of(by_group, g_in)
    wanted = own_rows[:, g_in ^ jnp.arange(n_col)].transpose(1, 0, 2)
    safe = jnp.clip(wanted, 0, blocks_total - 1)
    matched = (
        (group_cols[safe][..., None, :] == own_cols[None, :, None, :, None])
        & (wanted >= 0)[..., None, None]
        & (own_cols >= 0)[None, :, None, :, None]
    )
    piece = ((safe // rows % inner) ^ h_in) * outer + (safe // rows // inner ^ o_in)
    first_slot = (piece * rows + safe % rows) * slots
    index = jnp.where(
        matched.any(-1), first_slot[..., None] + jnp.argmax(matched, axis=-1), n_row * blocks
    ).astype(jnp.int32).reshape(-1)

    def mirror_table(h, cols):
        own_ids = (o_in * inner + h) * rows + jnp.arange(rows)
        safe_own = jnp.clip(cols, 0, blocks_total - 1)
        found = mirror_cols[safe_own] == own_ids[:, None, None]
        source = (safe_own // rows % inner) ^ h
        return jnp.where(
            cols >= 0,
            (source * rows + safe_own % rows) * slots + jnp.argmax(found, axis=-1),
            inner * blocks,
        ).astype(jnp.int32).reshape(-1)

    mirror = mirror_table(h_in, own_cols)
    out_mirror = mirror_table(
        inner_index, group_cols_of(rows_of(outer_index, inner_index), col_index)
    )

    def permute(x, target):
        return lax.ppermute(x, ("row", "col"), row_major_perm(n_row, n_col, target))

    def relayout(x, m=0):
        return permute(x, lambda r, c: at((r // inner) ^ m, r % inner, c))

    def inside_permute(x, move):
        return permute(x, lambda r, c: at(*move(*inside(r, c))))

    def share(x):
        return inside_permute(x, lambda o, h, g: (o, h ^ 1, g))

    def gather_direct(x):
        return {m: relayout(x, m) for m in range(outer - 1, 0, -1)}

    def gather_forwarded(x):
        pieces = {m: relayout(x, m) for m in range(2, outer, 2)}
        pieces[1] = relayout(x, 1)
        early = [pieces[1], pieces[2]]
        for m in range(2, outer, 2):
            pieces[m + 1] = inside_permute(pieces[m], lambda o, h, g: (o ^ 1, h, g))
        return pieces, early

    def exchange(outs):
        return [outs[0]] + [
            inside_permute(out, lambda o, h, g, d=d: (o, h, g ^ d))
            for d, out in enumerate(outs)
            if d
        ]

    def total_of(parts):
        value = parts[0]
        for part in parts[1:]:
            value = value + part.astype(f32)
        return value.astype(bf16)

    def sum_over_devices(x):
        for axis, size in (("col", n_col), ("row", n_row)):
            step = 1
            while step < size:
                x = x + lax.ppermute(x, axis, [(d, d ^ step) for d in range(size)])
                step *= 2
        return x

    smem = pl.BlockSpec(memory_space=pltpu.SMEM)
    vmem = pl.BlockSpec(memory_space=pltpu.VMEM)
    anywhere = pl.BlockSpec(memory_space=pl.ANY)
    out_shapes = tuple(
        jax.ShapeDtypeStruct((blocks, side, side), bf16 if d else f32) for d in range(n_col)
    )
    params = pltpu.CompilerParams(vmem_limit_bytes=16 * 2**20)

    def block_scratch(count, pieces):
        return [
            pltpu.VMEM((count + 1, side, side), bf16),
            pltpu.SemaphoreType.DMA((pieces,)),
        ]

    cost = pl.CostEstimate(
        flops=2 * n_col * blocks * slots * side**3,
        bytes_accessed=4 * 2**20,
        transcendentals=0,
    )

    flat = lambda x: x.reshape(blocks, side, side)
    inter, dens, kohn = flat(intersection), flat(density), flat(kohn_sham)
    inter_pieces, inter_early = gather_forwarded(inter)
    moved = relayout(jnp.concatenate([flat(step_dir), inter, dens, kohn]))
    step, inter_own, dens_own, kohn_own = (
        moved[i * blocks : (i + 1) * blocks] for i in range(4)
    )
    beside = share(moved[blocks:])
    inter_beside, dens_beside, kohn_beside = (
        beside[i * blocks : (i + 1) * blocks] for i in range(3)
    )
    dens_in, _ = lax.optimization_barrier((dens, inter_early))
    dens_pieces = gather_direct(dens_in)
    kohn_in, _ = lax.optimization_barrier((kohn, [dens_pieces[m] for m in dens_pieces]))
    kohn_pieces = gather_direct(kohn_in)

    def all_pieces(own, own_beside, pieces, joined):
        order = range(1, outer)
        if joined:
            shared = [share(jnp.concatenate([pieces[m] for m in order]))]
        else:
            shared = [share(pieces[m]) for m in order]
        return [own] + [pieces[m] for m in order] + [own_beside] + shared

    inter_all = all_pieces(inter_own, inter_beside, inter_pieces, False)
    dens_all = all_pieces(dens_own, dens_beside, dens_pieces, True)
    kohn_all = all_pieces(kohn_own, kohn_beside, kohn_pieces, True)

    outs = pl.pallas_call(
        functools.partial(first_kernel, rows, slots, len(inter_all), n_col),
        out_shape=out_shapes,
        in_specs=[smem, vmem] + [anywhere] * len(inter_all),
        out_specs=(vmem,) * n_col,
        scratch_shapes=block_scratch(n_row * blocks, len(inter_all)),
        compiler_params=params,
        cost_estimate=cost,
        name="scaled_step_product",
    )(index, step, *inter_all)
    parts = exchange(outs)

    outs = pl.pallas_call(
        functools.partial(second_kernel, rows, slots, len(dens_all), n_col),
        out_shape=out_shapes,
        in_specs=[smem] + [anywhere] * len(dens_all) + [vmem] * n_col,
        out_specs=(vmem,) * n_col,
        scratch_shapes=block_scratch(n_row * blocks, len(dens_all)),
        compiler_params=params,
        cost_estimate=cost,
        name="change_product",
    )(index, *dens_all, *parts)
    parts = exchange(outs)
    mirrored = [inside_permute(total_of(parts), lambda o, h, g: (g, h, o))]
    mirrored.append(share(mirrored[0]))

    *outs, trace = pl.pallas_call(
        functools.partial(third_kernel, rows, slots, len(kohn_all), inner, n_col),
        out_shape=out_shapes + (jax.ShapeDtypeStruct((8, side), f32),),
        in_specs=[smem, smem, vmem] + [anywhere] * (len(kohn_all) + inner) + [vmem] * n_col,
        out_specs=(vmem,) * (n_col + 1),
        scratch_shapes=block_scratch(n_row * blocks, len(kohn_all))
        + block_scratch(inner * blocks, inner)
        + [pltpu.VMEM((blocks, side, side), bf16)],
        compiler_params=params,
        cost_estimate=cost,
        name="commutator_product",
    )(index, mirror, kohn_own, *kohn_all, *mirrored, *parts)
    total = total_of(exchange(outs))
    trace = sum_over_devices(trace)

    def outside(move):
        return permute(total, lambda r, c: move(*inside(r, c)))

    mirrored = [outside(lambda o, h, g, t=t: (g * inner + (h ^ t), o)) for t in range(inner)]
    own = outside(lambda o, h, g: (o * inner + h, g))

    commutator = pl.pallas_call(
        functools.partial(last_kernel, inner),
        out_shape=jax.ShapeDtypeStruct((blocks, side, side), bf16),
        in_specs=[smem, vmem] + [anywhere] * inner,
        out_specs=vmem,
        scratch_shapes=block_scratch(inner * blocks, inner),
        compiler_params=params,
        name="commutator_difference",
    )(out_mirror, own, *mirrored)
    trace_value = trace.sum() / (blocks_total * side * side)
    return commutator.reshape(step_dir.shape), trace_value


def solution(mesh):
    in_specs = (P(),) + (P("row", "col", None, None),) * 4
    out_specs = (P("row", "col", None, None), P())
    return jax.shard_map(
        functools.partial(per_device, mesh.shape["row"], mesh.shape["col"]),
        mesh=mesh,
        in_specs=in_specs,
        out_specs=out_specs,
        check_vma=False,
    )
```

```python
import functools

import jax
import jax.numpy as jnp
from jax import lax
from jax.experimental import pallas as pl
from jax.experimental.pallas import tpu as pltpu
from jax.sharding import PartitionSpec as P

CORES = 2


def row_major_perm(n_row, n_col, target):
    pairs = []
    for r in range(n_row):
        for c in range(n_col):
            to_r, to_c = target(r, c)
            pairs.append((r * n_col + c, to_r * n_col + to_c))
    return pairs


def load_blocks(pieces, scratch, sems):
    copies = []
    start = 0
    for index, piece in enumerate(pieces):
        count = piece.shape[0]
        copy = pltpu.make_async_copy(piece, scratch.at[pl.ds(start, count)], sems.at[index])
        copy.start()
        copies.append(copy)
        start += count
    scratch[start] = jnp.zeros(scratch.shape[1:], scratch.dtype)
    return copies


def multiply(index_ref, left_of, scratch, outs, rows, slots, contract):
    for i in range(rows):
        left = left_of(i)
        for d, out in enumerate(outs):
            for s in range(slots):
                base = ((d * rows + i) * slots + s) * slots
                right = jnp.concatenate(
                    [scratch[index_ref[base + a]] for a in range(slots)], axis=1
                )
                out[i * slots + s] = lax.dot_general(
                    right,
                    left,
                    (((1,), (contract,)), ((), ())),
                    preferred_element_type=jnp.float32,
                ).astype(out.dtype)


def summed(parts, block):
    value = parts[0][block]
    for part in parts[1:]:
        value = value + part[block].astype(jnp.float32)
    return value


def first_kernel(rows, slots, n_pieces, n_out, index_ref, left_ref, *refs):
    pieces, outs, (scratch, sems) = refs[:n_pieces], refs[-2 - n_out : -2], refs[-2:]
    copies = load_blocks(pieces, scratch, sems)
    for copy in copies:
        copy.wait()

    def left_of(i):
        return jnp.concatenate([left_ref[i * slots + a] for a in range(slots)], axis=1)

    multiply(index_ref, left_of, scratch, outs, rows, slots, 1)


def second_kernel(rows, slots, n_pieces, n_out, index_ref, *refs):
    pieces, parts = refs[:n_pieces], refs[n_pieces : n_pieces + n_out]
    outs, (scratch, sems) = refs[-2 - n_out : -2], refs[-2:]
    copies = load_blocks(pieces, scratch, sems)

    def left_of(i):
        blocks = [summed(parts, i * slots + a).astype(jnp.bfloat16) for a in range(slots)]
        return jnp.concatenate(blocks, axis=0)

    for copy in copies:
        copy.wait()
    multiply(index_ref, left_of, scratch, outs, rows, slots, 0)


def third_kernel(rows, slots, n_pieces, n_mirror, index_ref, mirror_ref, kohn_ref, own_ref, *refs):
    pieces, refs = refs[:n_pieces], refs[n_pieces:]
    mirrored, refs = refs[:n_mirror], refs[n_mirror:]
    outs, (trace, scratch, sems, mirror_scratch, mirror_sems, change) = refs[:-6], refs[-6:]
    mirror_copies = load_blocks(mirrored, mirror_scratch, mirror_sems)
    copies = load_blocks(pieces, scratch, sems)
    for copy in mirror_copies:
        copy.wait()
    total_trace = jnp.zeros(trace.shape, jnp.float32)
    for b in range(rows * slots):
        other = mirror_scratch[mirror_ref[b]].astype(jnp.float32).T
        value = (-(own_ref[b].astype(jnp.float32) + other)).astype(jnp.bfloat16)
        change[b] = value
        product = value.astype(jnp.float32) * kohn_ref[b].astype(jnp.float32).T
        total_trace = total_trace + product.reshape((-1,) + trace.shape).sum(0)
    trace[...] = total_trace

    def left_of(i):
        return jnp.concatenate([change[i * slots + a] for a in range(slots)], axis=0)

    for copy in copies:
        copy.wait()
    multiply(index_ref, left_of, scratch, outs, rows, slots, 0)


def last_kernel(n_mirror, mirror_ref, own_ref, *refs):
    mirrored, (out, mirror_scratch, mirror_sems) = refs[:n_mirror], refs[n_mirror:]
    copies = load_blocks(mirrored, mirror_scratch, mirror_sems)
    for copy in copies:
        copy.wait()
    for b in range(out.shape[0]):
        other = mirror_scratch[mirror_ref[b]].astype(jnp.float32)
        out[b] = (other - own_ref[b].astype(jnp.float32).T).astype(out.dtype)


def per_device(n_row, n_col, block_cols, step_dir, intersection, density, kohn_sham):
    rows, slots, side = step_dir.shape[:3]
    blocks = rows * slots
    blocks_total = block_cols.shape[0]
    inner = n_row // n_col
    outer = n_row // inner
    assert inner == CORES and outer == n_col and outer & (outer - 1) == 0
    row_index = lax.axis_index("row")
    col_index = lax.axis_index("col")
    outer_index, inner_index = row_index // inner, row_index % inner
    bf16, f32 = jnp.bfloat16, jnp.float32

    def at(o, h, g):
        return o * inner + g % inner, (g // inner) * CORES + h

    def inside(r, c):
        return r // inner, c % CORES, (c // CORES) * inner + r % inner

    def spread(o, g):
        return g ^ ((o % 2) * (n_col // 2))

    o_in, h_in, g_in = inside(row_index, col_index)

    by_group = block_cols.reshape(blocks_total, n_col, slots)
    mirror_cols = lax.dynamic_slice_in_dim(by_group, o_in, 1, 1)[:, 0]

    def rows_of(o, h):
        return lax.dynamic_slice_in_dim(by_group, (o * inner + h) * rows, rows, 0)

    def group_cols_of(cols, g):
        return lax.dynamic_slice_in_dim(cols, g, 1, 1)[:, 0]

    own_rows = rows_of(o_in, h_in)
    own_cols = group_cols_of(own_rows, g_in)
    group_cols = group_cols_of(by_group, g_in)

    def index_table(first):
        wanted = own_rows[:, first ^ jnp.arange(n_col)].transpose(1, 0, 2)
        safe = jnp.clip(wanted, 0, blocks_total - 1)
        matched = (
            (group_cols[safe][..., None, :] == own_cols[None, :, None, :, None])
            & (wanted >= 0)[..., None, None]
            & (own_cols >= 0)[None, :, None, :, None]
        )
        piece = ((safe // rows % inner) ^ h_in) * outer + (safe // rows // inner ^ o_in)
        slot = ((piece * rows + safe % rows) * slots)[..., None] + jnp.argmax(matched, axis=-1)
        return jnp.where(matched.any(-1), slot, n_row * blocks).astype(jnp.int32).reshape(-1)

    index, spread_index = index_table(g_in), index_table(spread(o_in, g_in))

    def mirror_table(h, cols):
        own_ids = (o_in * inner + h) * rows + jnp.arange(rows)
        safe_own = jnp.clip(cols, 0, blocks_total - 1)
        found = mirror_cols[safe_own] == own_ids[:, None, None]
        source = (safe_own // rows % inner) ^ h
        return jnp.where(
            cols >= 0,
            (source * rows + safe_own % rows) * slots + jnp.argmax(found, axis=-1),
            inner * blocks,
        ).astype(jnp.int32).reshape(-1)

    mirror = mirror_table(h_in, own_cols)
    out_mirror = mirror_table(
        inner_index, group_cols_of(rows_of(outer_index, inner_index), col_index)
    )

    smem = pl.BlockSpec(memory_space=pltpu.SMEM)
    vmem = pl.BlockSpec(memory_space=pltpu.VMEM)
    anywhere = pl.BlockSpec(memory_space=pl.ANY)

    def permute(x, target):
        return lax.ppermute(x, ("row", "col"), row_major_perm(n_row, n_col, target))

    def relayout(x, m=0):
        return permute(x, lambda r, c: at((r // inner) ^ m, r % inner, c))

    def inside_permute(x, move):
        return permute(x, lambda r, c: at(*move(*inside(r, c))))

    def share(x):
        return inside_permute(x, lambda o, h, g: (o, h ^ 1, g))

    def join(pieces):
        def body(*refs):
            pieces, (out, sems) = refs[:-2], refs[-2:]
            copies = []
            start = 0
            for i, piece in enumerate(pieces):
                count = piece.shape[0]
                copies.append(
                    pltpu.make_async_copy(piece, out.at[pl.ds(start, count)], sems.at[i])
                )
                copies[-1].start()
                start += count
            for copy in copies:
                copy.wait()

        return pl.pallas_call(
            body,
            out_shape=jax.ShapeDtypeStruct((len(pieces) * blocks, side, side), bf16),
            in_specs=[anywhere] * len(pieces),
            out_specs=anywhere,
            scratch_shapes=[pltpu.SemaphoreType.DMA((len(pieces),))],
            name="join_pieces",
        )(*pieces)

    def gather_direct(x):
        return [relayout(x, m) for m in range(outer - 1, -1, -1)][::-1]

    def gather_forwarded(x):
        pieces = {m: relayout(x, m) for m in range(2, outer, 2)}
        pieces[1] = relayout(x, 1)
        pieces[0] = relayout(x)
        for m in range(2, outer, 2):
            pieces[m + 1] = inside_permute(pieces[m], lambda o, h, g: (o ^ 1, h, g))
        pieces = [pieces[m] for m in range(outer)]
        return pieces, [share(piece) for piece in pieces]

    def exchange(outs):
        return [outs[0]] + [
            inside_permute(out, lambda o, h, g, d=d: (o, h, g ^ d))
            for d, out in enumerate(outs)
            if d
        ]

    def total_of(parts):
        value = parts[0]
        for part in parts[1:]:
            value = value + part.astype(f32)
        return value.astype(bf16)

    def sum_over(x, axis, size):
        step = 1
        while step < size:
            x = x + lax.ppermute(x, axis, [(d, d ^ step) for d in range(size)])
            step *= 2
        return x

    out_shapes = tuple(
        jax.ShapeDtypeStruct((blocks, side, side), bf16 if d else f32) for d in range(n_col)
    )
    params = pltpu.CompilerParams(vmem_limit_bytes=16 * 2**20)

    def block_scratch(count, pieces):
        return [
            pltpu.VMEM((count + 1, side, side), bf16),
            pltpu.SemaphoreType.DMA((pieces,)),
        ]

    cost = pl.CostEstimate(
        flops=2 * n_col * blocks * slots * side**3,
        bytes_accessed=4 * 2**20,
        transcendentals=0,
    )

    flat = lambda x: x.reshape(blocks, side, side)
    inter, dens, kohn = flat(intersection), flat(density), flat(kohn_sham)
    inter_pieces, inter_beside = gather_forwarded(inter)
    step = relayout(flat(step_dir))
    dens_in, _ = lax.optimization_barrier((dens, inter_pieces[1:]))
    dens_pieces = gather_direct(dens_in)
    kohn_in, _ = lax.optimization_barrier((kohn, dens_pieces[1:]))
    kohn_pieces = gather_direct(kohn_in)
    inter_all = inter_pieces + inter_beside
    dens_all = dens_pieces + [share(join(dens_pieces))]

    outs = pl.pallas_call(
        functools.partial(first_kernel, rows, slots, len(inter_all), n_col),
        out_shape=out_shapes,
        in_specs=[smem, vmem] + [anywhere] * len(inter_all),
        out_specs=(vmem,) * n_col,
        scratch_shapes=block_scratch(n_row * blocks, len(inter_all)),
        compiler_params=params,
        cost_estimate=cost,
        name="scaled_step_product",
    )(index, step, *inter_all)
    parts = exchange(outs)

    outs = pl.pallas_call(
        functools.partial(second_kernel, rows, slots, len(dens_all), n_col),
        out_shape=out_shapes,
        in_specs=[smem] + [anywhere] * len(dens_all) + [vmem] * n_col,
        out_specs=(vmem,) * n_col,
        scratch_shapes=block_scratch(n_row * blocks, len(dens_all)),
        compiler_params=params,
        cost_estimate=cost,
        name="change_product",
    )(spread_index, *dens_all, *parts)
    total = total_of(exchange(outs))
    mirrored = [inside_permute(total, lambda o, h, g: (spread(o, g), h, o))]
    own = inside_permute(total, lambda o, h, g: (o, h, spread(o, g)))
    mirrored.append(share(mirrored[0]))
    kohn_pieces, _ = lax.optimization_barrier((kohn_pieces, total))
    kohn_all = kohn_pieces + [share(join(kohn_pieces))]

    *outs, trace = pl.pallas_call(
        functools.partial(third_kernel, rows, slots, len(kohn_all), inner),
        out_shape=out_shapes + (jax.ShapeDtypeStruct((8, side), f32),),
        in_specs=[smem, smem, vmem, vmem] + [anywhere] * (len(kohn_all) + inner),
        out_specs=(vmem,) * (n_col + 1),
        scratch_shapes=block_scratch(n_row * blocks, len(kohn_all))
        + block_scratch(inner * blocks, inner)
        + [pltpu.VMEM((blocks, side, side), bf16)],
        compiler_params=params,
        cost_estimate=cost,
        name="commutator_product",
    )(spread_index, mirror, kohn_all[0], own, *kohn_all, *mirrored)
    parts = exchange(outs)
    total = total_of(parts)

    def outside(move):
        def target(r, c):
            o, h, g = inside(r, c)
            return move(o, h, spread(o, g))

        return permute(total, target)

    mirrored = [outside(lambda o, h, g, t=t: (g * inner + (h ^ t), o)) for t in range(inner)]
    own = outside(lambda o, h, g: (o * inner + h, g))

    trace, _ = lax.optimization_barrier((trace, parts[1]))
    trace = sum_over(trace, "col", n_col)
    trace, _ = lax.optimization_barrier((trace, own))
    trace = sum_over(trace, "row", n_row)

    commutator = pl.pallas_call(
        functools.partial(last_kernel, inner),
        out_shape=jax.ShapeDtypeStruct((blocks, side, side), bf16),
        in_specs=[smem, vmem] + [anywhere] * inner,
        out_specs=vmem,
        scratch_shapes=block_scratch(inner * blocks, inner),
        compiler_params=params,
        name="commutator_difference",
    )(out_mirror, own, *mirrored)
    trace_value = trace.sum() / (blocks_total * side * side)
    return commutator.reshape(step_dir.shape), trace_value


def solution(mesh):
    in_specs = (P(),) + (P("row", "col", None, None),) * 4
    out_specs = (P("row", "col", None, None), P())
    return jax.shard_map(
        functools.partial(per_device, mesh.shape["row"], mesh.shape["col"]),
        mesh=mesh,
        in_specs=in_specs,
        out_specs=out_specs,
        check_vma=False,
    )
```

```python
import functools

import jax
import jax.numpy as jnp
from jax import lax
from jax.experimental import pallas as pl
from jax.experimental.pallas import tpu as pltpu
from jax.sharding import PartitionSpec as P

CORES = 2


def row_major_perm(n_row, n_col, target):
    pairs = []
    for r in range(n_row):
        for c in range(n_col):
            to_r, to_c = target(r, c)
            pairs.append((r * n_col + c, to_r * n_col + to_c))
    return pairs


def load_blocks(pieces, scratch, sems):
    copies = []
    start = 0
    for index, piece in enumerate(pieces):
        count = piece.shape[0]
        copy = pltpu.make_async_copy(piece, scratch.at[pl.ds(start, count)], sems.at[index])
        copy.start()
        copies.append(copy)
        start += count
    scratch[start] = jnp.zeros(scratch.shape[1:], scratch.dtype)
    return copies


def multiply(index_ref, left_of, scratch, outs, rows, slots, contract):
    for i in range(rows):
        left = left_of(i)
        for d, out in enumerate(outs):
            for s in range(slots):
                base = ((d * rows + i) * slots + s) * slots
                right = jnp.concatenate(
                    [scratch[index_ref[base + a]] for a in range(slots)], axis=1
                )
                out[i * slots + s] = lax.dot_general(
                    right,
                    left,
                    (((1,), (contract,)), ((), ())),
                    preferred_element_type=jnp.float32,
                ).astype(out.dtype)


def split_outs(own, away, cross):
    return (
        [own]
        + [away.at[x] for x in range(away.shape[0])]
        + [cross.at[x] for x in range(cross.shape[0])]
    )


def first_kernel(rows, slots, n_pieces, index_ref, left_ref, *refs):
    pieces, outs, (scratch, sems) = refs[:n_pieces], refs[n_pieces:-2], refs[-2:]
    copies = load_blocks(pieces, scratch, sems)
    for copy in copies:
        copy.wait()

    def left_of(i):
        return jnp.concatenate([left_ref[i * slots + a] for a in range(slots)], axis=1)

    multiply(index_ref, left_of, scratch, outs, rows, slots, 1)


def second_kernel(rows, slots, n_pieces, index_ref, *refs):
    pieces, parts, (own, away, cross, scratch, sems) = (
        refs[:n_pieces],
        refs[n_pieces:-5],
        refs[-5:],
    )
    copies = load_blocks(pieces, scratch, sems)

    def summed(block):
        return sum(part[block].astype(jnp.float32) for part in parts).astype(jnp.bfloat16)

    def left_of(i):
        return jnp.concatenate([summed(i * slots + a) for a in range(slots)], axis=0)

    for copy in copies:
        copy.wait()
    multiply(index_ref, left_of, scratch, split_outs(own, away, cross), rows, slots, 0)


def third_kernel(rows, slots, n_pieces, n_mirror, index_ref, mirror_ref, kohn_ref, *refs):
    pieces, refs = refs[:n_pieces], refs[n_pieces:]
    mirrored, refs = refs[:n_mirror], refs[n_mirror:]
    (own_in, core_in, *chips_in), refs = refs[:-9], refs[-9:]
    own, away, cross, trace, scratch, sems, mirror_scratch, mirror_sems, change = refs
    mirror_copies = load_blocks(mirrored, mirror_scratch, mirror_sems)
    copies = load_blocks(pieces, scratch, sems)
    for copy in mirror_copies:
        copy.wait()
    total_trace = jnp.zeros(trace.shape, jnp.float32)
    for b in range(rows * slots):
        value = own_in[b] + core_in[0, b].astype(jnp.float32)
        for part in chips_in:
            value = value + part[b].astype(jnp.float32)
        value = value + mirror_scratch[mirror_ref[b]].astype(jnp.float32).T
        value = (-value).astype(jnp.bfloat16)
        change[b] = value
        product = value.astype(jnp.float32) * kohn_ref[b].astype(jnp.float32).T
        total_trace = total_trace + product.reshape((-1,) + trace.shape).sum(0)
    trace[...] = total_trace

    def left_of(i):
        return jnp.concatenate([change[i * slots + a] for a in range(slots)], axis=0)

    for copy in copies:
        copy.wait()
    multiply(index_ref, left_of, scratch, split_outs(own, away, cross), rows, slots, 0)


def last_kernel(n_mirror, mirror_ref, own_ref, *refs):
    mirrored, (out, mirror_scratch, mirror_sems) = refs[:n_mirror], refs[n_mirror:]
    copies = load_blocks(mirrored, mirror_scratch, mirror_sems)
    for copy in copies:
        copy.wait()
    for b in range(out.shape[0]):
        other = mirror_scratch[mirror_ref[b]].astype(jnp.float32)
        out[b] = (other - own_ref[b].astype(jnp.float32).T).astype(out.dtype)


def per_device(n_row, n_col, block_cols, step_dir, intersection, density, kohn_sham):
    rows, slots, side = step_dir.shape[:3]
    blocks = rows * slots
    blocks_total = block_cols.shape[0]
    n_chip = n_col // CORES
    inner = n_row // n_col
    outer = n_row // inner
    assert inner == CORES and outer == n_col and outer & (outer - 1) == 0
    row_index = lax.axis_index("row")
    col_index = lax.axis_index("col")
    bf16, f32 = jnp.bfloat16, jnp.float32

    def from_args(r, c):
        return r // inner, r % inner, c

    def to_args(o, q, g):
        return o * inner + q, g

    def from_first(r, c):
        return r // inner, c % CORES, (c // CORES) * inner + r % inner

    def to_first(o, q, g):
        return o * inner + g % inner, (g // inner) * CORES + q

    def from_later(r, c):
        return r // inner, r % inner, (c % CORES) * n_chip + c // CORES

    def to_later(o, q, g):
        return o * inner + q, (g % n_chip) * CORES + g // n_chip

    by_group = block_cols.reshape(blocks_total, n_col, slots)

    def cols_of(cols, g):
        return lax.dynamic_slice_in_dim(cols, g, 1, 1)[:, 0]

    def rows_of(o, q):
        return lax.dynamic_slice_in_dim(by_group, (o * inner + q) * rows, rows, 0)

    def index_table(o, q, g, out_groups):
        own_rows = rows_of(o, q)
        own_cols, group_cols = cols_of(own_rows, g), cols_of(by_group, g)
        wanted = own_rows[:, out_groups].transpose(1, 0, 2)
        safe = jnp.clip(wanted, 0, blocks_total - 1)
        matched = (
            (group_cols[safe][..., None, :] == own_cols[None, :, None, :, None])
            & (wanted >= 0)[..., None, None]
            & (own_cols >= 0)[None, :, None, :, None]
        )
        piece = ((safe // rows % inner) ^ q) * outer + (safe // rows // inner ^ o)
        slot = ((piece * rows + safe % rows) * slots)[..., None] + jnp.argmax(matched, axis=-1)
        return jnp.where(matched.any(-1), slot, n_row * blocks).astype(jnp.int32).reshape(-1)

    def mirror_table(o, q, g):
        own_cols = cols_of(rows_of(o, q), g)
        own_ids = (o * inner + q) * rows + jnp.arange(rows)
        safe_own = jnp.clip(own_cols, 0, blocks_total - 1)
        found = cols_of(by_group, o)[safe_own] == own_ids[:, None, None]
        source = (safe_own // rows % inner) ^ q
        return jnp.where(
            own_cols >= 0,
            (source * rows + safe_own % rows) * slots + jnp.argmax(found, axis=-1),
            inner * blocks,
        ).astype(jnp.int32).reshape(-1)

    first_at, later_at = from_first(row_index, col_index), from_later(row_index, col_index)
    first_index = index_table(*first_at, first_at[2] ^ jnp.arange(n_col))
    rel_core, rel_chip = jnp.meshgrid(jnp.arange(CORES), jnp.arange(n_chip), indexing="ij")
    rel_group = (col_index % CORES ^ rel_core) * n_chip + (col_index // CORES + rel_chip) % n_chip
    later_index = index_table(*later_at, rel_group.reshape(-1))
    mirror = mirror_table(*later_at)
    out_mirror = mirror_table(*from_args(row_index, col_index))

    smem = pl.BlockSpec(memory_space=pltpu.SMEM)
    vmem = pl.BlockSpec(memory_space=pltpu.VMEM)
    anywhere = pl.BlockSpec(memory_space=pl.ANY)

    def send(x, source, move, target):
        return lax.ppermute(
            x,
            ("row", "col"),
            row_major_perm(n_row, n_col, lambda r, c: target(*move(*source(r, c)))),
        )

    def stay(o, q, g):
        return o, q, g

    def plane(m):
        return lambda o, q, g: (o ^ m, q, g)

    def beside(o, q, g):
        return o, q ^ 1, g

    def gather_planes(x, target):
        pieces = {m: send(x, from_args, plane(m), target) for m in range(2, outer, 2)}
        pieces[1] = send(x, from_args, plane(1), target)
        pieces[0] = send(x, from_args, stay, target)
        source = from_first if target is to_first else from_later
        for m in range(2, outer, 2):
            pieces[m + 1] = send(pieces[m], source, plane(1), target)
        pieces = [pieces[m] for m in range(outer)]
        return pieces, [send(piece, source, beside, target) for piece in pieces]

    def exchange(away, cross):
        def flip(r, c):
            return r, c ^ 1

        def shift(d):
            return lambda r, c: (r, ((c // CORES + d) % n_chip) * CORES + c % CORES)

        def permute(x, target):
            return lax.ppermute(x, ("row", "col"), row_major_perm(n_row, n_col, target))

        core = permute(cross, flip)
        sent = (away + core[1:].astype(f32)).astype(bf16)
        return [core] + [permute(sent[d - 1], shift(d)) for d in range(1, n_chip)]

    def total_of(own, core, *chips):
        value = own + core[0].astype(f32)
        for part in chips:
            value = value + part.astype(f32)
        return value.astype(bf16)

    def mirror_send(x, target):
        return [
            send(x, from_later, lambda o, q, g, t=t: (g, q ^ t, o), target) for t in range(inner)
        ]

    def sum_over_devices(x):
        for axis, size in (("col", n_col), ("row", n_row)):
            step = 1
            while step < size:
                x = x + lax.ppermute(x, axis, [(d, d ^ step) for d in range(size)])
                step *= 2
        return x

    block_shape = (blocks, side, side)
    first_shapes = (jax.ShapeDtypeStruct(block_shape, bf16),) * n_col
    later_shapes = (
        jax.ShapeDtypeStruct(block_shape, f32),
        jax.ShapeDtypeStruct((n_chip - 1,) + block_shape, f32),
        jax.ShapeDtypeStruct((n_chip,) + block_shape, bf16),
    )
    params = pltpu.CompilerParams(vmem_limit_bytes=16 * 2**20)

    def block_scratch(count, pieces):
        return [
            pltpu.VMEM((count + 1, side, side), bf16),
            pltpu.SemaphoreType.DMA((pieces,)),
        ]

    cost = pl.CostEstimate(
        flops=2 * n_col * blocks * slots * side**3,
        bytes_accessed=4 * 2**20,
        transcendentals=0,
    )

    flat = lambda x: x.reshape(block_shape)
    inter_pieces, inter_beside = gather_planes(flat(intersection), to_first)
    step = send(flat(step_dir), from_args, stay, to_first)
    dens, _ = lax.optimization_barrier((flat(density), inter_beside[1:3]))
    dens_pieces, dens_beside = gather_planes(dens, to_later)
    kohn, _ = lax.optimization_barrier((flat(kohn_sham), dens_beside[1:3]))
    kohn_pieces, kohn_beside = gather_planes(kohn, to_later)

    outs = pl.pallas_call(
        functools.partial(first_kernel, rows, slots, n_row),
        out_shape=first_shapes,
        in_specs=[smem, vmem] + [anywhere] * n_row,
        out_specs=(vmem,) * n_col,
        scratch_shapes=block_scratch(n_row * blocks, n_row),
        compiler_params=params,
        cost_estimate=cost,
        name="scaled_step_product",
    )(first_index, step, *inter_pieces, *inter_beside)
    parts = [
        send(out, from_first, lambda o, q, g, d=d: (o, q, g ^ d), to_later)
        for d, out in enumerate(outs)
    ]

    own, away, cross = pl.pallas_call(
        functools.partial(second_kernel, rows, slots, n_row),
        out_shape=later_shapes,
        in_specs=[smem] + [anywhere] * n_row + [vmem] * n_col,
        out_specs=(vmem,) * 3,
        scratch_shapes=block_scratch(n_row * blocks, n_row),
        compiler_params=params,
        cost_estimate=cost,
        name="change_product",
    )(later_index, *dens_pieces, *dens_beside, *parts)
    parts = [own] + exchange(away, cross)
    mirrored = mirror_send(total_of(*parts), to_later)

    own, away, cross, trace = pl.pallas_call(
        functools.partial(third_kernel, rows, slots, n_row, inner),
        out_shape=later_shapes + (jax.ShapeDtypeStruct((8, side), f32),),
        in_specs=[smem, smem, vmem] + [anywhere] * (n_row + inner) + [vmem] * len(parts),
        out_specs=(vmem,) * 4,
        scratch_shapes=block_scratch(n_row * blocks, n_row)
        + block_scratch(inner * blocks, inner)
        + [pltpu.VMEM(block_shape, bf16)],
        compiler_params=params,
        cost_estimate=cost,
        name="commutator_product",
    )(later_index, mirror, kohn_pieces[0], *kohn_pieces, *kohn_beside, *mirrored, *parts)
    total = total_of(own, *exchange(away, cross))
    trace = sum_over_devices(trace)
    mirrored = mirror_send(total, to_args)
    own = send(total, from_later, stay, to_args)

    commutator = pl.pallas_call(
        functools.partial(last_kernel, inner),
        out_shape=jax.ShapeDtypeStruct(block_shape, bf16),
        in_specs=[smem, vmem] + [anywhere] * inner,
        out_specs=vmem,
        scratch_shapes=block_scratch(inner * blocks, inner),
        compiler_params=params,
        name="commutator_difference",
    )(out_mirror, own, *mirrored)
    trace_value = trace.sum() / (blocks_total * side * side)
    return commutator.reshape(step_dir.shape), trace_value


def solution(mesh):
    in_specs = (P(),) + (P("row", "col", None, None),) * 4
    out_specs = (P("row", "col", None, None), P())
    return jax.shard_map(
        functools.partial(per_device, mesh.shape["row"], mesh.shape["col"]),
        mesh=mesh,
        in_specs=in_specs,
        out_specs=out_specs,
        check_vma=False,
    )
```

```python
import functools

import jax
import jax.numpy as jnp
from jax import lax
from jax.experimental import pallas as pl
from jax.experimental.pallas import tpu as pltpu
from jax.sharding import PartitionSpec as P

CORES = 2


def row_major_perm(n_row, n_col, target):
    pairs = []
    for r in range(n_row):
        for c in range(n_col):
            to_r, to_c = target(r, c)
            pairs.append((r * n_col + c, to_r * n_col + to_c))
    return pairs


def load_blocks(pieces, scratch, sems, first=0):
    count = (scratch.shape[0] - 1) // len(pieces)
    copies = []
    for index, piece in enumerate(pieces):
        copy = pltpu.make_async_copy(
            piece.at[pl.ds(first, count)], scratch.at[pl.ds(index * count, count)], sems.at[index]
        )
        copy.start()
        copies.append(copy)
    scratch[len(pieces) * count] = jnp.zeros(scratch.shape[1:], scratch.dtype)
    return copies


def multiply(index_ref, left_of, scratch, outs, rows, slots, contract):
    for i in range(rows):
        left = left_of(i)
        for d, out in enumerate(outs):
            for s in range(slots):
                base = ((d * rows + i) * slots + s) * slots
                right = jnp.concatenate(
                    [scratch[index_ref[base + a]] for a in range(slots)], axis=1
                )
                out[i * slots + s] = lax.dot_general(
                    right,
                    left,
                    (((1,), (contract,)), ((), ())),
                    preferred_element_type=jnp.float32,
                ).astype(out.dtype)


def summed(parts, block):
    value = parts[0][block]
    for part in parts[1:]:
        value = value + part[block].astype(jnp.float32)
    return value


def first_kernel(rows, slots, n_pieces, n_out, index_ref, left_ref, *refs):
    pieces, outs, (scratch, sems) = refs[:n_pieces], refs[-2 - n_out : -2], refs[-2:]
    copies = load_blocks(pieces, scratch, sems)
    for copy in copies:
        copy.wait()

    def left_of(i):
        return jnp.concatenate([left_ref[i * slots + a] for a in range(slots)], axis=1)

    multiply(index_ref, left_of, scratch, outs, rows, slots, 1)


def second_kernel(rows, slots, n_pieces, n_out, index_ref, *refs):
    pieces, parts = refs[:n_pieces], refs[n_pieces : n_pieces + n_out]
    outs, (scratch, sems) = refs[-2 - n_out : -2], refs[-2:]
    copies = load_blocks(pieces, scratch, sems)

    def left_of(i):
        blocks = [summed(parts, i * slots + a).astype(jnp.bfloat16) for a in range(slots)]
        return jnp.concatenate(blocks, axis=0)

    for copy in copies:
        copy.wait()
    multiply(index_ref, left_of, scratch, outs, rows, slots, 0)


def third_kernel(rows, slots, n_pieces, n_mirror, index_ref, mirror_ref, own_ref, *refs):
    pieces, refs = refs[:n_pieces], refs[n_pieces:]
    mirrored, refs = refs[:n_mirror], refs[n_mirror:]
    outs, (trace, scratch, sems, mirror_scratch, mirror_sems, change) = refs[:-6], refs[-6:]
    mirror_copies = load_blocks(mirrored, mirror_scratch, mirror_sems)
    copies = load_blocks(pieces, scratch, sems, rows * slots)
    for copy in mirror_copies + copies:
        copy.wait()
    total_trace = jnp.zeros(trace.shape, jnp.float32)
    for b in range(rows * slots):
        other = mirror_scratch[mirror_ref[b]].astype(jnp.float32).T
        value = (-(own_ref[b].astype(jnp.float32) + other)).astype(jnp.bfloat16)
        change[b] = value
        product = value.astype(jnp.float32) * scratch[b].astype(jnp.float32).T
        total_trace = total_trace + product.reshape((-1,) + trace.shape).sum(0)
    trace[...] = total_trace

    def left_of(i):
        return jnp.concatenate([change[i * slots + a] for a in range(slots)], axis=0)

    multiply(index_ref, left_of, scratch, outs, rows, slots, 0)


def last_kernel(n_mirror, mirror_ref, own_ref, *refs):
    mirrored, (out, mirror_scratch, mirror_sems) = refs[:n_mirror], refs[n_mirror:]
    copies = load_blocks(mirrored, mirror_scratch, mirror_sems)
    for copy in copies:
        copy.wait()
    for b in range(out.shape[0]):
        other = mirror_scratch[mirror_ref[b]].astype(jnp.float32)
        out[b] = (other - own_ref[b].astype(jnp.float32).T).astype(out.dtype)


def per_device(n_row, n_col, block_cols, step_dir, intersection, density, kohn_sham):
    rows, slots, side = step_dir.shape[:3]
    blocks = rows * slots
    blocks_total = block_cols.shape[0]
    inner = n_row // n_col
    outer = n_row // inner
    assert inner == CORES and outer == n_col and outer & (outer - 1) == 0
    row_index = lax.axis_index("row")
    col_index = lax.axis_index("col")
    outer_index, inner_index = row_index // inner, row_index % inner
    bf16, f32 = jnp.bfloat16, jnp.float32

    def at(o, h, g):
        return o * inner + g % inner, (g // inner) * CORES + h

    def inside(r, c):
        return r // inner, c % CORES, (c // CORES) * inner + r % inner

    def spread(o, g):
        return g ^ ((o % 2) * (n_col // 2))

    o_in, h_in, g_in = inside(row_index, col_index)

    by_group = block_cols.reshape(blocks_total, n_col, slots)
    mirror_cols = lax.dynamic_slice_in_dim(by_group, o_in, 1, 1)[:, 0]

    def rows_of(o, h):
        return lax.dynamic_slice_in_dim(by_group, (o * inner + h) * rows, rows, 0)

    def group_cols_of(cols, g):
        return lax.dynamic_slice_in_dim(cols, g, 1, 1)[:, 0]

    own_rows = rows_of(o_in, h_in)
    own_cols = group_cols_of(own_rows, g_in)
    group_cols = group_cols_of(by_group, g_in)

    def index_table(first):
        wanted = own_rows[:, first ^ jnp.arange(n_col)].transpose(1, 0, 2)
        safe = jnp.clip(wanted, 0, blocks_total - 1)
        matched = (
            (group_cols[safe][..., None, :] == own_cols[None, :, None, :, None])
            & (wanted >= 0)[..., None, None]
            & (own_cols >= 0)[None, :, None, :, None]
        )
        piece = ((safe // rows % inner) ^ h_in) * outer + (safe // rows // inner ^ o_in)
        slot = ((piece * rows + safe % rows) * slots)[..., None] + jnp.argmax(matched, axis=-1)
        return jnp.where(matched.any(-1), slot, n_row * blocks).astype(jnp.int32).reshape(-1)

    index, spread_index = index_table(g_in), index_table(spread(o_in, g_in))

    def mirror_table(h, cols):
        own_ids = (o_in * inner + h) * rows + jnp.arange(rows)
        safe_own = jnp.clip(cols, 0, blocks_total - 1)
        found = mirror_cols[safe_own] == own_ids[:, None, None]
        source = (safe_own // rows % inner) ^ h
        return jnp.where(
            cols >= 0,
            (source * rows + safe_own % rows) * slots + jnp.argmax(found, axis=-1),
            inner * blocks,
        ).astype(jnp.int32).reshape(-1)

    mirror = mirror_table(h_in, own_cols)
    out_mirror = mirror_table(
        inner_index, group_cols_of(rows_of(outer_index, inner_index), col_index)
    )

    smem = pl.BlockSpec(memory_space=pltpu.SMEM)
    vmem = pl.BlockSpec(memory_space=pltpu.VMEM)
    anywhere = pl.BlockSpec(memory_space=pl.ANY)

    def permute(x, target):
        return lax.ppermute(x, ("row", "col"), row_major_perm(n_row, n_col, target))

    def relayout(x, m=0):
        return permute(x, lambda r, c: at((r // inner) ^ m, r % inner, c))

    def inside_permute(x, move):
        return permute(x, lambda r, c: at(*move(*inside(r, c))))

    def share(x):
        return inside_permute(x, lambda o, h, g: (o, h ^ 1, g))

    def gather_planes(x, behind=None):
        own = relayout(x)
        if behind is not None:
            x, _ = lax.optimization_barrier((x, behind))
        pieces = {m: relayout(x, m) for m in range(2, outer, 2)}
        pieces[1] = relayout(x, 1)
        pieces[0] = own
        for m in range(2, outer, 2):
            pieces[m + 1] = inside_permute(pieces[m], lambda o, h, g: (o ^ 1, h, g))
        pieces = [pieces[m] for m in range(outer)]
        return pieces + [share(piece) for piece in pieces]

    def exchange(outs):
        return [outs[0]] + [
            inside_permute(out, lambda o, h, g, d=d: (o, h, g ^ d))
            for d, out in enumerate(outs)
            if d
        ]

    def total_of(parts):
        value = parts[0]
        for part in parts[1:]:
            value = value + part.astype(f32)
        return value.astype(bf16)

    def sum_over(x, axis, size):
        step = 1
        while step < size:
            x = x + lax.ppermute(x, axis, [(d, d ^ step) for d in range(size)])
            step *= 2
        return x

    out_shapes = tuple(
        jax.ShapeDtypeStruct((blocks, side, side), bf16 if d else f32) for d in range(n_col)
    )
    params = pltpu.CompilerParams(vmem_limit_bytes=16 * 2**20)

    def block_scratch(count, pieces):
        return [
            pltpu.VMEM((count + 1, side, side), bf16),
            pltpu.SemaphoreType.DMA((pieces,)),
        ]

    cost = pl.CostEstimate(
        flops=2 * n_col * blocks * slots * side**3,
        bytes_accessed=4 * 2**20,
        transcendentals=0,
    )

    flat = lambda x: x.reshape(blocks, side, side)
    inter, dens, kohn = flat(intersection), flat(density), flat(kohn_sham)
    inter_all = gather_planes(inter)
    step = relayout(flat(step_dir))
    both_all = gather_planes(jnp.concatenate([dens, kohn]), inter_all[1:3])

    outs = pl.pallas_call(
        functools.partial(first_kernel, rows, slots, n_row, n_col),
        out_shape=out_shapes,
        in_specs=[smem, vmem] + [anywhere] * n_row,
        out_specs=(vmem,) * n_col,
        scratch_shapes=block_scratch(n_row * blocks, n_row),
        compiler_params=params,
        cost_estimate=cost,
        name="scaled_step_product",
    )(index, step, *inter_all)
    parts = exchange(outs)

    outs = pl.pallas_call(
        functools.partial(second_kernel, rows, slots, n_row, n_col),
        out_shape=out_shapes,
        in_specs=[smem] + [anywhere] * n_row + [vmem] * n_col,
        out_specs=(vmem,) * n_col,
        scratch_shapes=block_scratch(n_row * blocks, n_row),
        compiler_params=params,
        cost_estimate=cost,
        name="change_product",
    )(spread_index, *both_all, *parts)
    total = total_of(exchange(outs))
    mirrored = [inside_permute(total, lambda o, h, g: (spread(o, g), h, o))]
    own = inside_permute(total, lambda o, h, g: (o, h, spread(o, g)))
    mirrored.append(share(mirrored[0]))

    *outs, trace = pl.pallas_call(
        functools.partial(third_kernel, rows, slots, n_row, inner),
        out_shape=out_shapes + (jax.ShapeDtypeStruct((8, side), f32),),
        in_specs=[smem, smem, vmem] + [anywhere] * (n_row + inner),
        out_specs=(vmem,) * (n_col + 1),
        scratch_shapes=block_scratch(n_row * blocks, n_row)
        + block_scratch(inner * blocks, inner)
        + [pltpu.VMEM((blocks, side, side), bf16)],
        compiler_params=params,
        cost_estimate=cost,
        name="commutator_product",
    )(spread_index, mirror, own, *both_all, *mirrored)
    parts = exchange(outs)
    total = total_of(parts)

    def outside(move):
        def target(r, c):
            o, h, g = inside(r, c)
            return move(o, h, spread(o, g))

        return permute(total, target)

    mirrored = [outside(lambda o, h, g, t=t: (g * inner + (h ^ t), o)) for t in range(inner)]
    own = outside(lambda o, h, g: (o * inner + h, g))

    trace = sum_over(sum_over(trace, "col", n_col), "row", n_row)

    commutator = pl.pallas_call(
        functools.partial(last_kernel, inner),
        out_shape=jax.ShapeDtypeStruct((blocks, side, side), bf16),
        in_specs=[smem, vmem] + [anywhere] * inner,
        out_specs=vmem,
        scratch_shapes=block_scratch(inner * blocks, inner),
        compiler_params=params,
        name="commutator_difference",
    )(out_mirror, own, *mirrored)
    trace_value = trace.sum() / (blocks_total * side * side)
    return commutator.reshape(step_dir.shape), trace_value


def solution(mesh):
    in_specs = (P(),) + (P("row", "col", None, None),) * 4
    out_specs = (P("row", "col", None, None), P())
    return jax.shard_map(
        functools.partial(per_device, mesh.shape["row"], mesh.shape["col"]),
        mesh=mesh,
        in_specs=in_specs,
        out_specs=out_specs,
        check_vma=False,
    )
```

```python
import functools

import jax
import jax.numpy as jnp
from jax import lax
from jax.experimental import pallas as pl
from jax.experimental.pallas import tpu as pltpu
from jax.sharding import PartitionSpec as P

CORES = 2


def row_major_perm(n_row, n_col, target):
    pairs = []
    for r in range(n_row):
        for c in range(n_col):
            to_r, to_c = target(r, c)
            pairs.append((r * n_col + c, to_r * n_col + to_c))
    return pairs


def start_copies(pairs, sems):
    copies = [pltpu.make_async_copy(*pair, sems.at[i]) for i, pair in enumerate(pairs)]
    for copy in copies:
        copy.start()
    return copies


def wait_for(copies):
    for copy in copies:
        copy.wait()


def into(pieces, scratch):
    count = pieces[0].shape[0]
    scratch[len(pieces) * count] = jnp.zeros(scratch.shape[1:], scratch.dtype)
    return [
        (piece, scratch.at[pl.ds(index * count, count)]) for index, piece in enumerate(pieces)
    ]


def multiply(index_ref, left_of, right, results, outs, sems, rows, slots, contract):
    copies = []
    for d in range(len(outs) - 1, -1, -1):
        for i in range(rows):
            left = left_of(i)
            for s in range(slots):
                base = ((d * rows + i) * slots + s) * slots
                blocks = jnp.concatenate(
                    [right[index_ref[base + a]] for a in range(slots)], axis=1
                )
                results[d][i * slots + s] = lax.dot_general(
                    blocks,
                    left,
                    (((1,), (contract,)), ((), ())),
                    preferred_element_type=jnp.float32,
                ).astype(results[d].dtype)
        copy = pltpu.make_async_copy(results[d], outs[d], sems.at[d])
        copy.start()
        copies.append(copy)
    wait_for(copies)


def split_results(first, others):
    return [first] + [others.at[d] for d in range(others.shape[0])]


def first_kernel(rows, slots, n_pieces, index_ref, left_ref, *refs):
    pieces, outs = refs[:n_pieces], refs[n_pieces:-6]
    right, left, first, others, sems, out_sems = refs[-6:]
    wait_for(start_copies(into(pieces, right) + [(left_ref, left)], sems))

    def left_of(i):
        return jnp.concatenate([left[i * slots + a] for a in range(slots)], axis=1)

    results = split_results(first, others)
    multiply(index_ref, left_of, right, results, outs, out_sems, rows, slots, 1)


def second_kernel(rows, slots, n_pieces, n_out, index_ref, *refs):
    pieces, parts = refs[:n_pieces], refs[n_pieces : n_pieces + n_out]
    right, left, part_first, part_others, first, others, sems, out_sems = refs[-8:]
    outs = refs[n_pieces + n_out : -8]
    held = split_results(part_first, part_others)
    wait_for(start_copies(list(zip(parts, held)) + into(pieces, right), sems))
    for b in range(rows * slots):
        value = held[0][b]
        for part in held[1:]:
            value = value + part[b].astype(jnp.float32)
        left[b] = value.astype(jnp.bfloat16)

    def left_of(i):
        return jnp.concatenate([left[i * slots + a] for a in range(slots)], axis=0)

    results = split_results(first, others)
    multiply(index_ref, left_of, right, results, outs, out_sems, rows, slots, 0)


def third_kernel(rows, slots, n_pieces, n_mirror, index_ref, mirror_ref, own_ref, *refs):
    pieces, mirrored = refs[:n_pieces], refs[n_pieces : n_pieces + n_mirror]
    *outs, trace = refs[n_pieces + n_mirror : -8]
    right, mirror, own, left, first, others, sems, out_sems = refs[-8:]
    pairs = into(pieces, right) + into(mirrored, mirror) + [(own_ref, own)]
    wait_for(start_copies(pairs, sems))
    total_trace = jnp.zeros(trace.shape, jnp.float32)
    for b in range(rows * slots):
        other = mirror[mirror_ref[b]].astype(jnp.float32).T
        value = (-(own[b].astype(jnp.float32) + other)).astype(jnp.bfloat16)
        left[b] = value
        product = value.astype(jnp.float32) * right[b].astype(jnp.float32).T
        total_trace = total_trace + product.reshape((-1,) + trace.shape).sum(0)
    trace[...] = total_trace

    def left_of(i):
        return jnp.concatenate([left[i * slots + a] for a in range(slots)], axis=0)

    results = split_results(first, others)
    multiply(index_ref, left_of, right, results, outs, out_sems, rows, slots, 0)


def last_kernel(n_mirror, mirror_ref, own_ref, *refs):
    mirrored, (out, mirror, own, result, sems, out_sems) = refs[:n_mirror], refs[n_mirror:]
    wait_for(start_copies(into(mirrored, mirror) + [(own_ref, own)], sems))
    for b in range(own.shape[0]):
        other = mirror[mirror_ref[b]].astype(jnp.float32)
        result[b] = (other - own[b].astype(jnp.float32).T).astype(result.dtype)
    wait_for(start_copies([(result, out)], out_sems))


def per_device(n_row, n_col, block_cols, step_dir, intersection, density, kohn_sham):
    rows, slots, side = step_dir.shape[:3]
    blocks = rows * slots
    blocks_total = block_cols.shape[0]
    inner = n_row // n_col
    outer = n_row // inner
    assert inner == CORES and outer == n_col and outer & (outer - 1) == 0
    row_index = lax.axis_index("row")
    col_index = lax.axis_index("col")
    outer_index, inner_index = row_index // inner, row_index % inner
    bf16, f32 = jnp.bfloat16, jnp.float32

    def at(o, h, g):
        return o * inner + g % inner, (g // inner) * CORES + h

    def inside(r, c):
        return r // inner, c % CORES, (c // CORES) * inner + r % inner

    def spread(o, g):
        return g ^ ((o % 2) * (n_col // 2))

    o_in, h_in, g_in = inside(row_index, col_index)

    by_group = block_cols.reshape(blocks_total, n_col, slots)
    mirror_cols = lax.dynamic_slice_in_dim(by_group, o_in, 1, 1)[:, 0]

    def rows_of(o, h):
        return lax.dynamic_slice_in_dim(by_group, (o * inner + h) * rows, rows, 0)

    def group_cols_of(cols, g):
        return lax.dynamic_slice_in_dim(cols, g, 1, 1)[:, 0]

    own_rows = rows_of(o_in, h_in)
    own_cols = group_cols_of(own_rows, g_in)
    group_cols = group_cols_of(by_group, g_in)

    def index_table(first):
        wanted = own_rows[:, first ^ jnp.arange(n_col)].transpose(1, 0, 2)
        safe = jnp.clip(wanted, 0, blocks_total - 1)
        matched = (
            (group_cols[safe][..., None, :] == own_cols[None, :, None, :, None])
            & (wanted >= 0)[..., None, None]
            & (own_cols >= 0)[None, :, None, :, None]
        )
        piece = ((safe // rows % inner) ^ h_in) * outer + (safe // rows // inner ^ o_in)
        slot = ((piece * rows + safe % rows) * slots)[..., None] + jnp.argmax(matched, axis=-1)
        return jnp.where(matched.any(-1), slot, n_row * blocks).astype(jnp.int32).reshape(-1)

    index, spread_index = index_table(g_in), index_table(spread(o_in, g_in))

    def mirror_table(h, cols):
        own_ids = (o_in * inner + h) * rows + jnp.arange(rows)
        safe_own = jnp.clip(cols, 0, blocks_total - 1)
        found = mirror_cols[safe_own] == own_ids[:, None, None]
        source = (safe_own // rows % inner) ^ h
        return jnp.where(
            cols >= 0,
            (source * rows + safe_own % rows) * slots + jnp.argmax(found, axis=-1),
            inner * blocks,
        ).astype(jnp.int32).reshape(-1)

    mirror = mirror_table(h_in, own_cols)
    out_mirror = mirror_table(
        inner_index, group_cols_of(rows_of(outer_index, inner_index), col_index)
    )

    smem = pl.BlockSpec(memory_space=pltpu.SMEM)
    vmem = pl.BlockSpec(memory_space=pltpu.VMEM)
    anywhere = pl.BlockSpec(memory_space=pl.ANY)

    def permute(x, target):
        return lax.ppermute(x, ("row", "col"), row_major_perm(n_row, n_col, target))

    def relayout(x, m=0):
        return permute(x, lambda r, c: at((r // inner) ^ m, r % inner, c))

    def inside_permute(x, move):
        return permute(x, lambda r, c: at(*move(*inside(r, c))))

    def share(x):
        return inside_permute(x, lambda o, h, g: (o, h ^ 1, g))

    def after(x, done):
        return lax.optimization_barrier((x, done))[0]

    def forward(x):
        return inside_permute(x, lambda o, h, g: (o ^ 1, h, g))

    def near(x):
        return {m: relayout(x, m) for m in [*range(2, outer, 2), 1]}

    def far(pieces):
        return {m + 1: forward(pieces[m]) for m in range(2, outer, 2)}

    def all_pieces(*groups):
        pieces, shared = {}, {}
        for group, other in groups:
            pieces |= group
            shared |= other
        return [pieces[m] for m in range(outer)] + [shared[m] for m in range(outer)]

    def share_all(pieces):
        return {m: share(piece) for m, piece in pieces.items()}

    def exchange(outs):
        return [outs[0]] + [
            inside_permute(out, lambda o, h, g, d=d: (o, h, g ^ d))
            for d, out in enumerate(outs)
            if d
        ]

    def total_of(parts):
        value = parts[0]
        for part in parts[1:]:
            value = value + part.astype(f32)
        return value.astype(bf16)

    def sum_over(x, axis, size):
        step = 1
        while step < size:
            x = x + lax.ppermute(x, axis, [(d, d ^ step) for d in range(size)])
            step *= 2
        return x

    block_shape = (blocks, side, side)
    out_shapes = tuple(
        jax.ShapeDtypeStruct(block_shape, bf16 if d else f32) for d in range(n_col)
    )
    params = pltpu.CompilerParams(vmem_limit_bytes=14 * 2**20)

    def held(count):
        return pltpu.VMEM((count, side, side), bf16)

    def dma(count):
        return pltpu.SemaphoreType.DMA((count,))

    sums = [pltpu.VMEM(block_shape, f32), pltpu.VMEM((n_col - 1,) + block_shape, bf16)]
    cost = pl.CostEstimate(
        flops=2 * n_col * blocks * slots * side**3,
        bytes_accessed=4 * 2**20,
        transcendentals=0,
    )

    flat = lambda x: x.reshape(block_shape)
    inter, dens, kohn = flat(intersection), flat(density), flat(kohn_sham)

    inter_near = near(inter)
    inter_own = {0: relayout(inter)}
    step = relayout(flat(step_dir))
    inter_far = far(inter_near)
    inter_early = inter_own | inter_near
    dens_near = near(after(dens, inter_near))
    outs = pl.pallas_call(
        functools.partial(first_kernel, rows, slots, n_row),
        out_shape=out_shapes,
        in_specs=[smem] + [anywhere] * (1 + n_row),
        out_specs=(anywhere,) * n_col,
        scratch_shapes=[held(n_row * blocks + 1), held(blocks), *sums, dma(n_row + 1), dma(n_col)],
        compiler_params=params,
        cost_estimate=cost,
        name="scaled_step_product",
    )(
        index,
        step,
        *all_pieces((inter_early, share_all(inter_early)), (inter_far, share_all(inter_far))),
    )
    parts = exchange(outs)

    dens_near, dens, kohn = after((dens_near, dens, kohn), outs)
    dens_early = {0: relayout(dens)} | dens_near
    dens_far = far(dens_near)
    kohn_near = near(after(kohn, dens_near))
    outs = pl.pallas_call(
        functools.partial(second_kernel, rows, slots, n_row, n_col),
        out_shape=out_shapes,
        in_specs=[smem] + [anywhere] * (n_row + n_col),
        out_specs=(anywhere,) * n_col,
        scratch_shapes=[
            held(n_row * blocks + 1),
            held(blocks),
            *sums,
            *sums,
            dma(n_row + n_col),
            dma(n_col),
        ],
        compiler_params=params,
        cost_estimate=cost,
        name="change_product",
    )(
        spread_index,
        *all_pieces((dens_early, share_all(dens_early)), (dens_far, share_all(dens_far))),
        *parts,
    )
    total = total_of(exchange(outs))
    mirrored = [inside_permute(total, lambda o, h, g: (spread(o, g), h, o))]
    own = inside_permute(total, lambda o, h, g: (o, h, spread(o, g)))
    mirrored.append(share(mirrored[0]))

    kohn_near, kohn = after((kohn_near, kohn), outs)
    kohn_early = {0: relayout(kohn)} | kohn_near
    kohn_far = far(kohn_near)
    kohn_pieces = all_pieces(
        (kohn_early, share_all(kohn_early)), (kohn_far, share_all(after(kohn_far, total)))
    )
    *outs, trace = pl.pallas_call(
        functools.partial(third_kernel, rows, slots, n_row, inner),
        out_shape=out_shapes + (jax.ShapeDtypeStruct((8, side), f32),),
        in_specs=[smem, smem] + [anywhere] * (1 + n_row + inner),
        out_specs=(anywhere,) * n_col + (vmem,),
        scratch_shapes=[
            held(n_row * blocks + 1),
            held(inner * blocks + 1),
            held(blocks),
            held(blocks),
            *sums,
            dma(n_row + inner + 1),
            dma(n_col),
        ],
        compiler_params=params,
        cost_estimate=cost,
        name="commutator_product",
    )(spread_index, mirror, own, *kohn_pieces, *mirrored)
    total = total_of(exchange(outs))

    def outside(move):
        def target(r, c):
            o, h, g = inside(r, c)
            return move(o, h, spread(o, g))

        return permute(total, target)

    mirrored = [outside(lambda o, h, g, t=t: (g * inner + (h ^ t), o)) for t in range(inner)]
    own = outside(lambda o, h, g: (o * inner + h, g))
    trace = sum_over(sum_over(trace, "col", n_col), "row", n_row)

    commutator = pl.pallas_call(
        functools.partial(last_kernel, inner),
        out_shape=jax.ShapeDtypeStruct(block_shape, bf16),
        in_specs=[smem] + [anywhere] * (1 + inner),
        out_specs=anywhere,
        scratch_shapes=[
            held(inner * blocks + 1),
            held(blocks),
            held(blocks),
            dma(inner + 1),
            dma(1),
        ],
        compiler_params=params,
        name="commutator_difference",
    )(out_mirror, own, *mirrored)
    trace_value = trace.sum() / (blocks_total * side * side)
    return commutator.reshape(step_dir.shape), trace_value


def solution(mesh):
    in_specs = (P(),) + (P("row", "col", None, None),) * 4
    out_specs = (P("row", "col", None, None), P())
    return jax.shard_map(
        functools.partial(per_device, mesh.shape["row"], mesh.shape["col"]),
        mesh=mesh,
        in_specs=in_specs,
        out_specs=out_specs,
        check_vma=False,
    )
```

```python
import functools

import jax
import jax.numpy as jnp
from jax import lax
from jax.experimental import pallas as pl
from jax.experimental.pallas import tpu as pltpu
from jax.sharding import PartitionSpec as P

CORES = 2


def row_major_perm(n_row, n_col, target):
    pairs = []
    for r in range(n_row):
        for c in range(n_col):
            to_r, to_c = target(r, c)
            pairs.append((r * n_col + c, to_r * n_col + to_c))
    return pairs


def start_copies(pairs, sems):
    copies = [pltpu.make_async_copy(*pair, sems.at[i]) for i, pair in enumerate(pairs)]
    for copy in copies:
        copy.start()
    return copies


def wait_for(copies):
    for copy in copies:
        copy.wait()


def into(pieces, scratch):
    count = pieces[0].shape[0]
    scratch[len(pieces) * count] = jnp.zeros(scratch.shape[1:], scratch.dtype)
    return [
        (piece, scratch.at[pl.ds(index * count, count)]) for index, piece in enumerate(pieces)
    ]


def multiply(index_ref, left_of, right, results, outs, sems, rows, slots, contract):
    copies = []
    for d in range(len(outs) - 1, -1, -1):
        for i in range(rows):
            left = left_of(i)
            for s in range(slots):
                base = ((d * rows + i) * slots + s) * slots
                blocks = jnp.concatenate(
                    [right[index_ref[base + a]] for a in range(slots)], axis=1
                )
                value = lax.dot_general(
                    blocks,
                    left,
                    (((1,), (contract,)), ((), ())),
                    preferred_element_type=jnp.float32,
                ).astype(results[d].dtype)
                if len(results[d].shape) == 3:
                    results[d][i * slots + s] = value
                else:
                    side = value.shape[0]
                    results[d][pl.ds((i * slots + s) * side, side)] = value
        copy = pltpu.make_async_copy(results[d], outs[d], sems.at[d])
        copy.start()
        copies.append(copy)
    wait_for(copies)


def split_results(first, others):
    return [first] + [others.at[d] for d in range(others.shape[0])]


def first_kernel(rows, slots, n_pieces, index_ref, left_ref, *refs):
    pieces, outs = refs[:n_pieces], refs[n_pieces:-6]
    right, left, first, others, sems, out_sems = refs[-6:]
    wait_for(start_copies(into(pieces, right) + [(left_ref, left)], sems))

    def left_of(i):
        return jnp.concatenate([left[i * slots + a] for a in range(slots)], axis=1)

    results = split_results(first, others)
    multiply(index_ref, left_of, right, results, outs, out_sems, rows, slots, 1)


def second_kernel(rows, slots, n_pieces, n_out, index_ref, *refs):
    pieces, parts = refs[:n_pieces], refs[n_pieces : n_pieces + n_out]
    right, left, part_first, part_others, first, others, sems, out_sems = refs[-8:]
    outs = refs[n_pieces + n_out : -8]
    held = split_results(part_first, part_others)
    wait_for(start_copies(list(zip(parts, held)) + into(pieces, right), sems))
    for b in range(rows * slots):
        value = held[0][b]
        for part in held[1:]:
            value = value + part[b].astype(jnp.float32)
        left[b] = value.astype(jnp.bfloat16)

    def left_of(i):
        return jnp.concatenate([left[i * slots + a] for a in range(slots)], axis=0)

    results = split_results(first, others)
    multiply(index_ref, left_of, right, results, outs, out_sems, rows, slots, 0)


def two_parts(x):
    high = x.astype(jnp.bfloat16)
    low = (x - high.astype(jnp.float32)).astype(jnp.bfloat16)
    return jnp.concatenate([high, low], axis=0)


def one_part(x):
    x = x.astype(jnp.float32)
    half = x.shape[0] // 2
    return x[:half] + x[half:]


def tree_sum(values):
    while len(values) > 1:
        values = [values[i] + values[i + 1] for i in range(0, len(values), 2)]
    return values[0]


def third_kernel(rows, slots, n_pieces, n_mirror, index_ref, mirror_ref, own_ref, *refs):
    pieces, mirrored = refs[:n_pieces], refs[n_pieces : n_pieces + n_mirror]
    *outs, trace = refs[n_pieces + n_mirror : -8]
    right, mirror, own, left, first, others, sems, out_sems = refs[-8:]
    pairs = into(pieces, right) + into(mirrored, mirror) + [(own_ref, own)]
    wait_for(start_copies(pairs, sems))
    blocks, side = rows * slots, right.shape[1]
    part_rows = trace.shape[0] // 2
    total_trace = jnp.zeros((part_rows, side), jnp.float32)
    for b in range(blocks):
        other = mirror[mirror_ref[b]].astype(jnp.float32).T
        value = (-(own[b].astype(jnp.float32) + other)).astype(jnp.bfloat16)
        left[b] = value
        product = value.astype(jnp.float32) * right[b].astype(jnp.float32).T
        total_trace = total_trace + product.reshape(-1, part_rows, side).sum(0)
    total_trace = two_parts(total_trace)
    trace[...] = total_trace
    results = split_results(first, others)
    for result in results[1:]:
        result[pl.ds(blocks * side, 2 * part_rows)] = total_trace

    def left_of(i):
        return jnp.concatenate([left[i * slots + a] for a in range(slots)], axis=0)

    multiply(index_ref, left_of, right, results, outs, out_sems, rows, slots, 0)


def sum_kernel(n_out, trace_ref, own_ref, *refs):
    parts, (out, own, others, result, sems, out_sems) = refs[: n_out - 1], refs[n_out - 1 :]
    pairs = [(part, others.at[d]) for d, part in enumerate(parts)]
    wait_for(start_copies([(own_ref, own)] + pairs, sems))
    blocks, side = own.shape[:2]
    for b in range(blocks):
        value = own[b]
        for d in range(n_out - 1):
            value = value + others[d, pl.ds(b * side, side)].astype(jnp.float32)
        result[pl.ds(b * side, side)] = value.astype(result.dtype)
    tail = pl.ds(blocks * side, trace_ref.shape[0])
    tiles = [trace_ref[...]] + [others[d, tail] for d in range(n_out - 1)]
    result[tail] = two_parts(tree_sum([one_part(tile) for tile in tiles]))
    wait_for(start_copies([(result, out)], out_sems))


def last_kernel(n_mirror, blocks, mirror_ref, own_ref, *refs):
    mirrored, (out, mirror, own, result, sems, out_sems) = refs[:n_mirror], refs[n_mirror:]
    side = own.shape[1]
    count = blocks * side
    body = pl.ds(0, count)
    pairs = [(own_ref.at[body], own)] + [
        (piece.at[body], mirror.at[pl.ds(t * count, count)]) for t, piece in enumerate(mirrored)
    ]
    copies = start_copies(pairs, sems)
    mirror[pl.ds(n_mirror * count, side)] = jnp.zeros((side, side), mirror.dtype)
    wait_for(copies)
    for b in range(blocks):
        start = pl.multiple_of(mirror_ref[b] * side, side)
        other = mirror[pl.ds(start, side)].astype(jnp.float32)
        value = other - own[pl.ds(b * side, side)].astype(jnp.float32).T
        result[b] = value.astype(result.dtype)
    wait_for(start_copies([(result, out)], out_sems))


def per_device(n_row, n_col, block_cols, step_dir, intersection, density, kohn_sham):
    rows, slots, side = step_dir.shape[:3]
    blocks = rows * slots
    blocks_total = block_cols.shape[0]
    inner = n_row // n_col
    outer = n_row // inner
    assert inner == CORES and outer == n_col and outer & (outer - 1) == 0
    row_index = lax.axis_index("row")
    col_index = lax.axis_index("col")
    bf16, f32 = jnp.bfloat16, jnp.float32

    def at(o, h, g):
        return o * inner + g % inner, (g // inner) * CORES + h

    def inside(r, c):
        return r // inner, c % CORES, (c // CORES) * inner + r % inner

    def spread(o, g):
        return g ^ ((o % 2) * (n_col // 2))

    o_in, h_in, g_in = inside(row_index, col_index)

    by_group = block_cols.reshape(blocks_total, n_col, slots)
    mirror_cols = lax.dynamic_slice_in_dim(by_group, o_in, 1, 1)[:, 0]

    def rows_of(o, h):
        return lax.dynamic_slice_in_dim(by_group, (o * inner + h) * rows, rows, 0)

    def group_cols_of(cols, g):
        return lax.dynamic_slice_in_dim(cols, g, 1, 1)[:, 0]

    own_rows = rows_of(o_in, h_in)
    own_cols = group_cols_of(own_rows, g_in)
    group_cols = group_cols_of(by_group, g_in)

    def index_table(first):
        wanted = own_rows[:, first ^ jnp.arange(n_col)].transpose(1, 0, 2)
        safe = jnp.clip(wanted, 0, blocks_total - 1)
        matched = (
            (group_cols[safe][..., None, :] == own_cols[None, :, None, :, None])
            & (wanted >= 0)[..., None, None]
            & (own_cols >= 0)[None, :, None, :, None]
        )
        piece = ((safe // rows % inner) ^ h_in) * outer + (safe // rows // inner ^ o_in)
        slot = ((piece * rows + safe % rows) * slots)[..., None] + jnp.argmax(matched, axis=-1)
        return jnp.where(matched.any(-1), slot, n_row * blocks).astype(jnp.int32).reshape(-1)

    index, spread_index = index_table(g_in), index_table(spread(o_in, g_in))

    def mirror_table(h, cols):
        own_ids = (o_in * inner + h) * rows + jnp.arange(rows)
        safe_own = jnp.clip(cols, 0, blocks_total - 1)
        found = mirror_cols[safe_own] == own_ids[:, None, None]
        source = (safe_own // rows % inner) ^ h
        return jnp.where(
            cols >= 0,
            (source * rows + safe_own % rows) * slots + jnp.argmax(found, axis=-1),
            inner * blocks,
        ).astype(jnp.int32).reshape(-1)

    mirror = mirror_table(h_in, own_cols)

    smem = pl.BlockSpec(memory_space=pltpu.SMEM)
    vmem = pl.BlockSpec(memory_space=pltpu.VMEM)
    anywhere = pl.BlockSpec(memory_space=pl.ANY)

    def permute(x, target):
        return lax.ppermute(x, ("row", "col"), row_major_perm(n_row, n_col, target))

    def relayout(x, m=0):
        return permute(x, lambda r, c: at((r // inner) ^ m, r % inner, c))

    def inside_permute(x, move):
        return permute(x, lambda r, c: at(*move(*inside(r, c))))

    def share(x):
        return inside_permute(x, lambda o, h, g: (o, h ^ 1, g))

    def after(x, done):
        return lax.optimization_barrier((x, done))[0]

    def forward(x):
        return inside_permute(x, lambda o, h, g: (o ^ 1, h, g))

    def near(x):
        return {m: relayout(x, m) for m in [*range(2, outer, 2), 1]}

    def far(pieces):
        return {m + 1: forward(pieces[m]) for m in range(2, outer, 2)}

    def all_pieces(*groups):
        pieces, shared = {}, {}
        for group, other in groups:
            pieces |= group
            shared |= other
        return [pieces[m] for m in range(outer)] + [shared[m] for m in range(outer)]

    def share_all(pieces):
        return {m: share(piece) for m, piece in pieces.items()}

    def exchange(outs):
        return [outs[0]] + [
            inside_permute(out, lambda o, h, g, d=d: (o, h, g ^ d))
            for d, out in enumerate(outs)
            if d
        ]

    def total_of(parts):
        value = parts[0]
        for part in parts[1:]:
            value = value + part.astype(f32)
        return value.astype(bf16)

    block_shape = (blocks, side, side)
    out_shapes = tuple(
        jax.ShapeDtypeStruct(block_shape, bf16 if d else f32) for d in range(n_col)
    )
    params = pltpu.CompilerParams(vmem_limit_bytes=14 * 2**20)

    def held(count):
        return pltpu.VMEM((count, side, side), bf16)

    def dma(count):
        return pltpu.SemaphoreType.DMA((count,))

    tail_shape = jax.ShapeDtypeStruct((16, side), bf16)
    long_shape = jax.ShapeDtypeStruct((blocks * side + tail_shape.shape[0], side), bf16)
    long_sums = [
        pltpu.VMEM(block_shape, f32),
        pltpu.VMEM((n_col - 1,) + long_shape.shape, bf16),
    ]
    sums = [pltpu.VMEM(block_shape, f32), pltpu.VMEM((n_col - 1,) + block_shape, bf16)]
    cost = pl.CostEstimate(
        flops=2 * n_col * blocks * slots * side**3,
        bytes_accessed=4 * 2**20,
        transcendentals=0,
    )

    flat = lambda x: x.reshape(block_shape)
    inter, dens, kohn = flat(intersection), flat(density), flat(kohn_sham)

    inter_near = near(inter)
    inter_own = {0: relayout(inter)}
    step = relayout(flat(step_dir))
    inter_far = far(inter_near)
    inter_early = inter_own | inter_near
    dens_near = near(after(dens, (inter_near, inter_far)))
    outs = pl.pallas_call(
        functools.partial(first_kernel, rows, slots, n_row),
        out_shape=out_shapes,
        in_specs=[smem] + [anywhere] * (1 + n_row),
        out_specs=(anywhere,) * n_col,
        scratch_shapes=[held(n_row * blocks + 1), held(blocks), *sums, dma(n_row + 1), dma(n_col)],
        compiler_params=params,
        cost_estimate=cost,
        name="scaled_step_product",
    )(
        index,
        step,
        *all_pieces((inter_early, share_all(inter_early)), (inter_far, share_all(inter_far))),
    )
    parts = exchange(outs)

    dens_near, dens, kohn = after((dens_near, dens, kohn), parts[1])
    dens_early = {0: relayout(dens)} | dens_near
    dens_far = far(dens_near)
    kohn_near = near(after(kohn, dens_near))
    outs = pl.pallas_call(
        functools.partial(second_kernel, rows, slots, n_row, n_col),
        out_shape=out_shapes,
        in_specs=[smem] + [anywhere] * (n_row + n_col),
        out_specs=(anywhere,) * n_col,
        scratch_shapes=[
            held(n_row * blocks + 1),
            held(blocks),
            *sums,
            *sums,
            dma(n_row + n_col),
            dma(n_col),
        ],
        compiler_params=params,
        cost_estimate=cost,
        name="change_product",
    )(
        spread_index,
        *all_pieces((dens_early, share_all(dens_early)), (dens_far, share_all(dens_far))),
        *parts,
    )
    total = total_of(exchange(outs))
    mirrored = [inside_permute(total, lambda o, h, g: (spread(o, g), h, o))]
    own = inside_permute(total, lambda o, h, g: (o, h, spread(o, g)))
    mirrored.append(share(mirrored[0]))

    kohn_near, kohn = after((kohn_near, kohn), outs)
    kohn_early = {0: relayout(kohn)} | kohn_near
    kohn_far = far(kohn_near)
    kohn_pieces = all_pieces(
        (kohn_early, share_all(kohn_early)), (kohn_far, share_all(after(kohn_far, total)))
    )
    *outs, trace = pl.pallas_call(
        functools.partial(third_kernel, rows, slots, n_row, inner),
        out_shape=out_shapes[:1] + (long_shape,) * (n_col - 1) + (tail_shape,),
        in_specs=[smem, smem] + [anywhere] * (1 + n_row + inner),
        out_specs=(anywhere,) * n_col + (vmem,),
        scratch_shapes=[
            held(n_row * blocks + 1),
            held(inner * blocks + 1),
            held(blocks),
            held(blocks),
            *long_sums,
            dma(n_row + inner + 1),
            dma(n_col),
        ],
        compiler_params=params,
        cost_estimate=cost,
        name="commutator_product",
    )(spread_index, mirror, own, *kohn_pieces, *mirrored)
    own, *parts = exchange(outs)
    total = pl.pallas_call(
        functools.partial(sum_kernel, n_col),
        out_shape=long_shape,
        in_specs=[vmem] + [anywhere] * n_col,
        out_specs=anywhere,
        scratch_shapes=[*long_sums, pltpu.VMEM(long_shape.shape, bf16), dma(n_col), dma(1)],
        compiler_params=params,
        name="plane_sum",
    )(trace, own, *parts)
    mirrored = [inside_permute(total, lambda o, h, g: (spread(o, g), h, o))]
    own = inside_permute(total, lambda o, h, g: (o, h, spread(o, g)))
    mirrored.append(share(mirrored[0]))

    commutator = pl.pallas_call(
        functools.partial(last_kernel, inner, blocks),
        out_shape=jax.ShapeDtypeStruct(block_shape, bf16),
        in_specs=[smem] + [anywhere] * (1 + inner),
        out_specs=anywhere,
        scratch_shapes=[
            pltpu.VMEM(((inner * blocks + 1) * side, side), bf16),
            pltpu.VMEM((blocks * side, side), bf16),
            held(blocks),
            dma(inner + 1),
            dma(1),
        ],
        compiler_params=params,
        name="commutator_difference",
    )(mirror, own, *mirrored)
    commutator = permute(
        commutator, lambda r, c: (lambda o, h, g: (o * inner + h, g))(*inside(r, c))
    )

    plane_trace = tree_sum([one_part(piece[blocks * side :]) for piece in mirrored])
    trace = tree_sum(
        [plane_trace]
        + [
            inside_permute(plane_trace, lambda o, h, g, d=d: (o, h, g ^ d))
            for d in range(1, n_col)
        ]
    )
    trace_value = trace.sum() / (blocks_total * side * side)
    return commutator.reshape(step_dir.shape), trace_value


def solution(mesh):
    in_specs = (P(),) + (P("row", "col", None, None),) * 4
    out_specs = (P("row", "col", None, None), P())
    return jax.shard_map(
        functools.partial(per_device, mesh.shape["row"], mesh.shape["col"]),
        mesh=mesh,
        in_specs=in_specs,
        out_specs=out_specs,
        check_vma=False,
    )
```

```python
import functools

import jax
import jax.numpy as jnp
from jax import lax
from jax.experimental import pallas as pl
from jax.experimental.pallas import tpu as pltpu
from jax.sharding import PartitionSpec as P

CORES = 2


def row_major_perm(n_row, n_col, target):
    pairs = []
    for r in range(n_row):
        for c in range(n_col):
            to_r, to_c = target(r, c)
            pairs.append((r * n_col + c, to_r * n_col + to_c))
    return pairs


def start_copies(pairs, sems):
    copies = [pltpu.make_async_copy(*pair, sems.at[i]) for i, pair in enumerate(pairs)]
    for copy in copies:
        copy.start()
    return copies


def wait_for(copies):
    for copy in copies:
        copy.wait()


def into(pieces, scratch, count):
    scratch[len(pieces) * count] = jnp.zeros(scratch.shape[1:], scratch.dtype)
    return [
        (piece, scratch.at[pl.ds(index * count, count)]) for index, piece in enumerate(pieces)
    ]


def multiply(index_ref, left_of, right, results, outs, sems, rows, slots, contract):
    copies = []
    for d in range(len(outs) - 1, -1, -1):
        for i in range(rows):
            left = left_of(i)
            for s in range(slots):
                base = ((d * rows + i) * slots + s) * slots
                blocks = jnp.concatenate(
                    [right[index_ref[base + a]] for a in range(slots)], axis=1
                )
                value = lax.dot_general(
                    blocks,
                    left,
                    (((1,), (contract,)), ((), ())),
                    preferred_element_type=jnp.float32,
                ).astype(results[d].dtype)
                if len(results[d].shape) == 3:
                    results[d][i * slots + s] = value
                else:
                    side = value.shape[0]
                    results[d][pl.ds((i * slots + s) * side, side)] = value
        copy = pltpu.make_async_copy(results[d], outs[d], sems.at[d])
        copy.start()
        copies.append(copy)
    wait_for(copies)


def split_results(first, others):
    return [first] + [others.at[d] for d in range(others.shape[0])]


def part_of(ref, index, count):
    return ref.at[pl.ds(index * count, count)]


def with_own(pieces, moved, moved_beside, index, count):
    half = len(pieces) // 2
    own, beside = part_of(moved, index, count), part_of(moved_beside, index, count)
    return [own, *pieces[:half], beside, *pieces[half:]]


def first_kernel(rows, slots, n_pieces, index_ref, moved, moved_beside, *refs):
    pieces, outs = refs[:n_pieces], refs[n_pieces:-6]
    right, left, first, others, sems, out_sems = refs[-6:]
    count = rows * slots
    pieces = with_own(pieces, moved, moved_beside, 1, count)
    pairs = into(pieces, right, count) + [(part_of(moved, 0, count), left)]
    wait_for(start_copies(pairs, sems))

    def left_of(i):
        return jnp.concatenate([left[i * slots + a] for a in range(slots)], axis=1)

    results = split_results(first, others)
    multiply(index_ref, left_of, right, results, outs, out_sems, rows, slots, 1)


def second_kernel(rows, slots, n_pieces, n_out, n_early, index_ref, moved, moved_beside, *refs):
    pieces, parts = refs[:n_pieces], refs[n_pieces : n_pieces + n_out]
    right, left, part_first, part_others, first, others, sems, out_sems = refs[-8:]
    outs = refs[n_pieces + n_out + n_early : -8]
    pieces = with_own(pieces, moved, moved_beside, 2, rows * slots)
    held = split_results(part_first, part_others)
    wait_for(start_copies(list(zip(parts, held)) + into(pieces, right, rows * slots), sems))
    for b in range(rows * slots):
        value = held[0][b]
        for part in held[1:]:
            value = value + part[b].astype(jnp.float32)
        left[b] = value.astype(jnp.bfloat16)

    def left_of(i):
        return jnp.concatenate([left[i * slots + a] for a in range(slots)], axis=0)

    results = split_results(first, others)
    multiply(index_ref, left_of, right, results, outs, out_sems, rows, slots, 0)


def two_parts(x):
    high = x.astype(jnp.bfloat16)
    low = (x - high.astype(jnp.float32)).astype(jnp.bfloat16)
    return jnp.concatenate([high, low], axis=0)


def one_part(x):
    x = x.astype(jnp.float32)
    half = x.shape[0] // 2
    return x[:half] + x[half:]


def tree_sum(values):
    while len(values) > 1:
        values = [values[i] + values[i + 1] for i in range(0, len(values), 2)]
    return values[0]


def third_kernel(rows, slots, n_pieces, n_mirror, index_ref, mirror_ref, own_ref, *refs):
    pieces, mirrored = refs[:n_pieces], refs[n_pieces : n_pieces + n_mirror]
    *outs, trace = refs[n_pieces + n_mirror : -8]
    right, mirror, own, left, first, others, sems, out_sems = refs[-8:]
    pairs = into(pieces, right, rows * slots) + into(mirrored, mirror, rows * slots) + [(own_ref, own)]
    wait_for(start_copies(pairs, sems))
    blocks, side = rows * slots, right.shape[1]
    part_rows = trace.shape[0] // 2
    total_trace = jnp.zeros((part_rows, side), jnp.float32)
    for b in range(blocks):
        other = mirror[mirror_ref[b]].astype(jnp.float32).T
        value = (-(own[b].astype(jnp.float32) + other)).astype(jnp.bfloat16)
        left[b] = value
        product = value.astype(jnp.float32) * right[b].astype(jnp.float32).T
        total_trace = total_trace + product.reshape(-1, part_rows, side).sum(0)
    total_trace = two_parts(total_trace)
    trace[...] = total_trace
    results = split_results(first, others)
    for result in results[1:]:
        result[pl.ds(blocks * side, 2 * part_rows)] = total_trace

    def left_of(i):
        return jnp.concatenate([left[i * slots + a] for a in range(slots)], axis=0)

    multiply(index_ref, left_of, right, results, outs, out_sems, rows, slots, 0)


def sum_kernel(n_out, trace_ref, own_ref, *refs):
    parts, (out, own, others, result, sems, out_sems) = refs[: n_out - 1], refs[n_out - 1 :]
    pairs = [(part, others.at[d]) for d, part in enumerate(parts)]
    wait_for(start_copies([(own_ref, own)] + pairs, sems))
    blocks, side = own.shape[:2]
    for b in range(blocks):
        value = own[b]
        for d in range(n_out - 1):
            value = value + others[d, pl.ds(b * side, side)].astype(jnp.float32)
        result[pl.ds(b * side, side)] = value.astype(result.dtype)
    tail = pl.ds(blocks * side, trace_ref.shape[0])
    tiles = [trace_ref[...]] + [others[d, tail] for d in range(n_out - 1)]
    result[tail] = two_parts(tree_sum([one_part(tile) for tile in tiles]))
    wait_for(start_copies([(result, out)], out_sems))


def last_kernel(n_mirror, blocks, mirror_ref, own_ref, *refs):
    mirrored, (out, mirror, own, result, sems, out_sems) = refs[:n_mirror], refs[n_mirror:]
    side = own.shape[1]
    count = blocks * side
    body = pl.ds(0, count)
    pairs = [(own_ref.at[body], own)] + [
        (piece.at[body], mirror.at[pl.ds(t * count, count)]) for t, piece in enumerate(mirrored)
    ]
    copies = start_copies(pairs, sems)
    mirror[pl.ds(n_mirror * count, side)] = jnp.zeros((side, side), mirror.dtype)
    wait_for(copies)
    for b in range(blocks):
        start = pl.multiple_of(mirror_ref[b] * side, side)
        other = mirror[pl.ds(start, side)].astype(jnp.float32)
        value = other - own[pl.ds(b * side, side)].astype(jnp.float32).T
        result[b] = value.astype(result.dtype)
    wait_for(start_copies([(result, out)], out_sems))


def per_device(n_row, n_col, block_cols, step_dir, intersection, density, kohn_sham):
    rows, slots, side = step_dir.shape[:3]
    blocks = rows * slots
    blocks_total = block_cols.shape[0]
    inner = n_row // n_col
    outer = n_row // inner
    assert inner == CORES and outer == n_col and outer & (outer - 1) == 0
    row_index = lax.axis_index("row")
    col_index = lax.axis_index("col")
    bf16, f32 = jnp.bfloat16, jnp.float32

    def at(o, h, g):
        return o * inner + g % inner, (g // inner) * CORES + h

    def inside(r, c):
        return r // inner, c % CORES, (c // CORES) * inner + r % inner

    def spread(o, g):
        bits = (n_col - 1).bit_length()
        return g ^ sum(((o >> b) & 1) << (bits - 1 - b) for b in range(bits))

    def at_spread(o, h, g):
        return at(o, h, spread(o, g))

    def inside_spread(r, c):
        o, h, p = inside(r, c)
        return o, h, spread(o, p)

    o_in, h_in, g_in = inside(row_index, col_index)

    by_group = block_cols.reshape(blocks_total, n_col, slots)
    mirror_cols = lax.dynamic_slice_in_dim(by_group, o_in, 1, 1)[:, 0]

    def rows_of(o, h):
        return lax.dynamic_slice_in_dim(by_group, (o * inner + h) * rows, rows, 0)

    def group_cols_of(cols, g):
        return lax.dynamic_slice_in_dim(cols, g, 1, 1)[:, 0]

    own_rows = rows_of(o_in, h_in)

    def index_table(group, first_out):
        own_cols, group_cols = group_cols_of(own_rows, group), group_cols_of(by_group, group)
        wanted = own_rows[:, first_out ^ jnp.arange(n_col)].transpose(1, 0, 2)
        safe = jnp.clip(wanted, 0, blocks_total - 1)
        matched = (
            (group_cols[safe][..., None, :] == own_cols[None, :, None, :, None])
            & (wanted >= 0)[..., None, None]
            & (own_cols >= 0)[None, :, None, :, None]
        )
        piece = ((safe // rows % inner) ^ h_in) * outer + (safe // rows // inner ^ o_in)
        slot = ((piece * rows + safe % rows) * slots)[..., None] + jnp.argmax(matched, axis=-1)
        return jnp.where(matched.any(-1), slot, n_row * blocks).astype(jnp.int32).reshape(-1)

    spread_in = spread(o_in, g_in)
    first_index = index_table(g_in, g_in)
    second_index = index_table(g_in, spread_in)
    third_index = index_table(spread_in, spread_in)

    def mirror_table(h, cols):
        own_ids = (o_in * inner + h) * rows + jnp.arange(rows)
        safe_own = jnp.clip(cols, 0, blocks_total - 1)
        found = mirror_cols[safe_own] == own_ids[:, None, None]
        source = (safe_own // rows % inner) ^ h
        return jnp.where(
            cols >= 0,
            (source * rows + safe_own % rows) * slots + jnp.argmax(found, axis=-1),
            inner * blocks,
        ).astype(jnp.int32).reshape(-1)

    mirror_index = mirror_table(h_in, group_cols_of(own_rows, spread_in))

    smem = pl.BlockSpec(memory_space=pltpu.SMEM)
    vmem = pl.BlockSpec(memory_space=pltpu.VMEM)
    anywhere = pl.BlockSpec(memory_space=pl.ANY)

    def permute(x, target):
        return lax.ppermute(x, ("row", "col"), row_major_perm(n_row, n_col, target))

    def relayout(x, m=0, target=at):
        return permute(x, lambda r, c: target((r // inner) ^ m, r % inner, c))

    def inside_permute(x, move, source=inside, target=at):
        return permute(x, lambda r, c: target(*move(*source(r, c))))

    def share(x):
        return inside_permute(x, lambda o, h, g: (o, h ^ 1, g))

    def after(x, done):
        return lax.optimization_barrier((x, done))[0]

    def forward(x):
        return inside_permute(x, lambda o, h, g: (o ^ 1, h, g))

    def listed(pieces):
        order = sorted(pieces)
        return [pieces[m] for m in order] + [share(pieces[m]) for m in order]

    def mirror(x):
        moved = inside_permute(x, lambda o, h, g: (g, h, o), inside_spread, at_spread)
        return [moved, share(moved)]

    def exchange(outs):
        return [outs[0]] + [
            inside_permute(out, lambda o, h, g, d=d: (o, h, g ^ d))
            for d, out in enumerate(outs)
            if d
        ]

    def total_of(parts):
        value = parts[0]
        for part in parts[1:]:
            value = value + part.astype(f32)
        return value.astype(bf16)

    block_shape = (blocks, side, side)
    out_shapes = tuple(
        jax.ShapeDtypeStruct(block_shape, bf16 if d else f32) for d in range(n_col)
    )
    params = pltpu.CompilerParams(vmem_limit_bytes=14 * 2**20)

    def held(count):
        return pltpu.VMEM((count, side, side), bf16)

    def dma(count):
        return pltpu.SemaphoreType.DMA((count,))

    tail_shape = jax.ShapeDtypeStruct((16, side), bf16)
    long_shape = jax.ShapeDtypeStruct((blocks * side + tail_shape.shape[0], side), bf16)
    long_sums = [
        pltpu.VMEM(block_shape, f32),
        pltpu.VMEM((n_col - 1,) + long_shape.shape, bf16),
    ]
    sums = [pltpu.VMEM(block_shape, f32), pltpu.VMEM((n_col - 1,) + block_shape, bf16)]
    cost = pl.CostEstimate(
        flops=2 * n_col * blocks * slots * side**3,
        bytes_accessed=4 * 2**20,
        transcendentals=0,
    )

    flat = lambda x: x.reshape(block_shape)
    inter, dens, kohn = flat(intersection), flat(density), flat(kohn_sham)

    inter_pieces = {m: relayout(inter, m) for m in [*range(2, outer, 2), 1]}
    moved = relayout(jnp.concatenate([flat(step_dir), inter, dens]))
    dens_pieces = {1: relayout(dens, 1)}
    inter_pieces |= {m + 1: forward(inter_pieces[m]) for m in range(2, outer, 2)}
    dens_behind = after(dens, inter_pieces)
    dens_pieces |= {m: relayout(dens_behind, m) for m in range(2, outer)}
    beside = share(moved)
    outs = pl.pallas_call(
        functools.partial(first_kernel, rows, slots, n_row - inner),
        out_shape=out_shapes,
        in_specs=[smem] + [anywhere] * n_row,
        out_specs=(anywhere,) * n_col,
        scratch_shapes=[held(n_row * blocks + 1), held(blocks), *sums, dma(n_row + 1), dma(n_col)],
        compiler_params=params,
        cost_estimate=cost,
        name="scaled_step_product",
    )(first_index, moved, beside, *listed(inter_pieces))
    parts = exchange(outs)

    dens_pieces, kohn = after((dens_pieces, kohn), parts[1:])
    kohn_pieces = {m: relayout(kohn, m, at_spread) for m in range(2)}
    kohn_behind = after(kohn, dens_pieces)
    outs = pl.pallas_call(
        functools.partial(second_kernel, rows, slots, n_row - inner, n_col, 2),
        out_shape=out_shapes,
        in_specs=[smem] + [anywhere] * (n_row + n_col + 2),
        out_specs=(anywhere,) * n_col,
        scratch_shapes=[
            held(n_row * blocks + 1),
            held(blocks),
            *sums,
            *sums,
            dma(n_row + n_col),
            dma(n_col),
        ],
        compiler_params=params,
        cost_estimate=cost,
        name="change_product",
    )(second_index, moved, beside, *listed(dens_pieces), *parts, *kohn_pieces.values())
    kohn_far = {m: relayout(kohn_behind, m, at_spread) for m in range(2, outer, 2)}
    total = total_of(exchange(outs))

    kohn_far |= {
        m + 1: inside_permute(kohn_far[m], lambda o, h, g: (o ^ 1, h, g), inside_spread, at_spread)
        for m in range(2, outer, 2)
    }
    kohn_pieces |= after(kohn_far, total)
    *outs, trace = pl.pallas_call(
        functools.partial(third_kernel, rows, slots, n_row, inner),
        out_shape=out_shapes[:1] + (long_shape,) * (n_col - 1) + (tail_shape,),
        in_specs=[smem, smem] + [anywhere] * (1 + n_row + inner),
        out_specs=(anywhere,) * n_col + (vmem,),
        scratch_shapes=[
            held(n_row * blocks + 1),
            held(inner * blocks + 1),
            held(blocks),
            held(blocks),
            *long_sums,
            dma(n_row + inner + 1),
            dma(n_col),
        ],
        compiler_params=params,
        cost_estimate=cost,
        name="commutator_product",
    )(third_index, mirror_index, total, *listed(kohn_pieces), *mirror(total))
    own, *parts = exchange(outs)
    total = pl.pallas_call(
        functools.partial(sum_kernel, n_col),
        out_shape=long_shape,
        in_specs=[vmem] + [anywhere] * n_col,
        out_specs=anywhere,
        scratch_shapes=[*long_sums, pltpu.VMEM(long_shape.shape, bf16), dma(n_col), dma(1)],
        compiler_params=params,
        name="plane_sum",
    )(trace, own, *parts)
    mirrored = mirror(total)

    commutator = pl.pallas_call(
        functools.partial(last_kernel, inner, blocks),
        out_shape=jax.ShapeDtypeStruct(block_shape, bf16),
        in_specs=[smem] + [anywhere] * (1 + inner),
        out_specs=anywhere,
        scratch_shapes=[
            pltpu.VMEM(((inner * blocks + 1) * side, side), bf16),
            pltpu.VMEM((blocks * side, side), bf16),
            held(blocks),
            dma(inner + 1),
            dma(1),
        ],
        compiler_params=params,
        name="commutator_difference",
    )(mirror_index, total, *mirrored)
    commutator = inside_permute(
        commutator, lambda o, h, g: (o, h, g), inside_spread, lambda o, h, g: (o * inner + h, g)
    )

    plane_trace = tree_sum([one_part(piece[blocks * side :]) for piece in mirrored])
    trace = tree_sum(
        [plane_trace]
        + [
            inside_permute(plane_trace, lambda o, h, g, d=d: (o, h, g ^ d))
            for d in range(1, n_col)
        ]
    )
    trace_value = trace.sum() / (blocks_total * side * side)
    return commutator.reshape(step_dir.shape), trace_value


def solution(mesh):
    in_specs = (P(),) + (P("row", "col", None, None),) * 4
    out_specs = (P("row", "col", None, None), P())
    return jax.shard_map(
        functools.partial(per_device, mesh.shape["row"], mesh.shape["col"]),
        mesh=mesh,
        in_specs=in_specs,
        out_specs=out_specs,
        check_vma=False,
    )
```

```python
import functools

import jax
import jax.numpy as jnp
from jax import lax
from jax.experimental import pallas as pl
from jax.experimental.pallas import tpu as pltpu
from jax.sharding import PartitionSpec as P

CORES = 2


def row_major_perm(n_row, n_col, target):
    pairs = []
    for r in range(n_row):
        for c in range(n_col):
            to_r, to_c = target(r, c)
            pairs.append((r * n_col + c, to_r * n_col + to_c))
    return pairs


def start_copies(pairs, sems):
    copies = [pltpu.make_async_copy(*pair, sems.at[i]) for i, pair in enumerate(pairs)]
    for copy in copies:
        copy.start()
    return copies


def wait_for(copies):
    for copy in copies:
        copy.wait()


def into(pieces, scratch, count):
    scratch[len(pieces) * count] = jnp.zeros(scratch.shape[1:], scratch.dtype)
    return [
        (piece, scratch.at[pl.ds(index * count, count)]) for index, piece in enumerate(pieces)
    ]


def multiply(index_ref, left_of, right, results, outs, sems, rows, slots, contract):
    copies = []
    for d in range(len(outs) - 1, -1, -1):
        for i in range(rows):
            left = left_of(i)
            for s in range(slots):
                base = ((d * rows + i) * slots + s) * slots
                blocks = jnp.concatenate(
                    [right[index_ref[base + a]] for a in range(slots)], axis=1
                )
                value = lax.dot_general(
                    blocks,
                    left,
                    (((1,), (contract,)), ((), ())),
                    preferred_element_type=jnp.float32,
                ).astype(results[d].dtype)
                if len(results[d].shape) == 3:
                    results[d][i * slots + s] = value
                else:
                    side = value.shape[0]
                    results[d][pl.ds((i * slots + s) * side, side)] = value
        copy = pltpu.make_async_copy(results[d], outs[d], sems.at[d])
        copy.start()
        copies.append(copy)
    wait_for(copies)


def split_results(first, others):
    return [first] + [others.at[d] for d in range(others.shape[0])]


def first_kernel(rows, slots, n_pieces, index_ref, left_ref, *refs):
    pieces, outs = refs[:n_pieces], refs[n_pieces:-6]
    right, left, first, others, sems, out_sems = refs[-6:]
    wait_for(start_copies(into(pieces, right, rows * slots) + [(left_ref, left)], sems))

    def left_of(i):
        return jnp.concatenate([left[i * slots + a] for a in range(slots)], axis=1)

    results = split_results(first, others)
    multiply(index_ref, left_of, right, results, outs, out_sems, rows, slots, 1)


def second_kernel(rows, slots, n_pieces, n_out, index_ref, *refs):
    pieces, parts = refs[:n_pieces], refs[n_pieces : n_pieces + n_out]
    right, left, part_first, part_others, first, others, sems, out_sems = refs[-8:]
    outs = refs[n_pieces + n_out : -8]
    held = split_results(part_first, part_others)
    wait_for(start_copies(list(zip(parts, held)) + into(pieces, right, rows * slots), sems))
    for b in range(rows * slots):
        value = held[0][b]
        for part in held[1:]:
            value = value + part[b].astype(jnp.float32)
        left[b] = value.astype(jnp.bfloat16)

    def left_of(i):
        return jnp.concatenate([left[i * slots + a] for a in range(slots)], axis=0)

    results = split_results(first, others)
    multiply(index_ref, left_of, right, results, outs, out_sems, rows, slots, 0)


def two_parts(x):
    high = x.astype(jnp.bfloat16)
    low = (x - high.astype(jnp.float32)).astype(jnp.bfloat16)
    return jnp.concatenate([high, low], axis=0)


def one_part(x):
    x = x.astype(jnp.float32)
    half = x.shape[0] // 2
    return x[:half] + x[half:]


def tree_sum(values):
    while len(values) > 1:
        values = [values[i] + values[i + 1] for i in range(0, len(values), 2)]
    return values[0]


def third_kernel(rows, slots, n_pieces, n_mirror, index_ref, mirror_ref, own_ref, *refs):
    pieces, mirrored = refs[:n_pieces], refs[n_pieces : n_pieces + n_mirror]
    *outs, trace = refs[n_pieces + n_mirror : -8]
    right, mirror, own, left, first, others, sems, out_sems = refs[-8:]
    pairs = into(pieces, right, rows * slots) + into(mirrored, mirror, rows * slots) + [(own_ref, own)]
    wait_for(start_copies(pairs, sems))
    blocks, side = rows * slots, right.shape[1]
    part_rows = trace.shape[0] // 2
    total_trace = jnp.zeros((part_rows, side), jnp.float32)
    for b in range(blocks):
        other = mirror[mirror_ref[b]].astype(jnp.float32).T
        value = (-(own[b].astype(jnp.float32) + other)).astype(jnp.bfloat16)
        left[b] = value
        product = value.astype(jnp.float32) * right[b].astype(jnp.float32).T
        total_trace = total_trace + product.reshape(-1, part_rows, side).sum(0)
    total_trace = two_parts(total_trace)
    trace[...] = total_trace
    results = split_results(first, others)
    for result in results[1:]:
        result[pl.ds(blocks * side, 2 * part_rows)] = total_trace

    def left_of(i):
        return jnp.concatenate([left[i * slots + a] for a in range(slots)], axis=0)

    multiply(index_ref, left_of, right, results, outs, out_sems, rows, slots, 0)


def sum_kernel(n_out, trace_ref, own_ref, *refs):
    parts, (out, own, others, result, sems, out_sems) = refs[: n_out - 1], refs[n_out - 1 :]
    pairs = [(part, others.at[d]) for d, part in enumerate(parts)]
    wait_for(start_copies([(own_ref, own)] + pairs, sems))
    blocks, side = own.shape[:2]
    for b in range(blocks):
        value = own[b]
        for d in range(n_out - 1):
            value = value + others[d, pl.ds(b * side, side)].astype(jnp.float32)
        result[pl.ds(b * side, side)] = value.astype(result.dtype)
    tail = pl.ds(blocks * side, trace_ref.shape[0])
    tiles = [trace_ref[...]] + [others[d, tail] for d in range(n_out - 1)]
    result[tail] = two_parts(tree_sum([one_part(tile) for tile in tiles]))
    wait_for(start_copies([(result, out)], out_sems))


def last_kernel(n_mirror, blocks, mirror_ref, own_ref, *refs):
    mirrored, (out, mirror, own, result, sems, out_sems) = refs[:n_mirror], refs[n_mirror:]
    side = own.shape[1]
    count = blocks * side
    body = pl.ds(0, count)
    pairs = [(own_ref.at[body], own)] + [
        (piece.at[body], mirror.at[pl.ds(t * count, count)]) for t, piece in enumerate(mirrored)
    ]
    copies = start_copies(pairs, sems)
    mirror[pl.ds(n_mirror * count, side)] = jnp.zeros((side, side), mirror.dtype)
    wait_for(copies)
    for b in range(blocks):
        start = pl.multiple_of(mirror_ref[b] * side, side)
        other = mirror[pl.ds(start, side)].astype(jnp.float32)
        value = other - own[pl.ds(b * side, side)].astype(jnp.float32).T
        result[b] = value.astype(result.dtype)
    wait_for(start_copies([(result, out)], out_sems))


def per_device(n_row, n_col, block_cols, step_dir, intersection, density, kohn_sham):
    rows, slots, side = step_dir.shape[:3]
    blocks = rows * slots
    blocks_total = block_cols.shape[0]
    inner = n_row // n_col
    outer = n_row // inner
    assert inner == CORES and outer == n_col and outer & (outer - 1) == 0
    row_index = lax.axis_index("row")
    col_index = lax.axis_index("col")
    bf16, f32 = jnp.bfloat16, jnp.float32

    def at(o, h, g):
        return o * inner + g % inner, (g // inner) * CORES + h

    def inside(r, c):
        return r // inner, c % CORES, (c // CORES) * inner + r % inner

    def spread(o, g):
        bits = (n_col - 1).bit_length()
        return g ^ sum(((o >> b) & 1) << (bits - 1 - b) for b in range(bits))

    def at_spread(o, h, g):
        return at(o, h, spread(o, g))

    def inside_spread(r, c):
        o, h, p = inside(r, c)
        return o, h, spread(o, p)

    o_in, h_in, g_in = inside(row_index, col_index)

    by_group = block_cols.reshape(blocks_total, n_col, slots)
    mirror_cols = lax.dynamic_slice_in_dim(by_group, o_in, 1, 1)[:, 0]

    def rows_of(o, h):
        return lax.dynamic_slice_in_dim(by_group, (o * inner + h) * rows, rows, 0)

    def group_cols_of(cols, g):
        return lax.dynamic_slice_in_dim(cols, g, 1, 1)[:, 0]

    own_rows = rows_of(o_in, h_in)

    def index_table(group, first_out):
        own_cols, group_cols = group_cols_of(own_rows, group), group_cols_of(by_group, group)
        wanted = own_rows[:, first_out ^ jnp.arange(n_col)].transpose(1, 0, 2)
        safe = jnp.clip(wanted, 0, blocks_total - 1)
        matched = (
            (group_cols[safe][..., None, :] == own_cols[None, :, None, :, None])
            & (wanted >= 0)[..., None, None]
            & (own_cols >= 0)[None, :, None, :, None]
        )
        piece = ((safe // rows % inner) ^ h_in) * outer + (safe // rows // inner ^ o_in)
        slot = ((piece * rows + safe % rows) * slots)[..., None] + jnp.argmax(matched, axis=-1)
        return jnp.where(matched.any(-1), slot, n_row * blocks).astype(jnp.int32).reshape(-1)

    spread_in = spread(o_in, g_in)
    first_index = index_table(g_in, g_in)
    second_index = index_table(g_in, spread_in)
    third_index = index_table(spread_in, spread_in)

    def mirror_table(h, cols):
        own_ids = (o_in * inner + h) * rows + jnp.arange(rows)
        safe_own = jnp.clip(cols, 0, blocks_total - 1)
        found = mirror_cols[safe_own] == own_ids[:, None, None]
        source = (safe_own // rows % inner) ^ h
        return jnp.where(
            cols >= 0,
            (source * rows + safe_own % rows) * slots + jnp.argmax(found, axis=-1),
            inner * blocks,
        ).astype(jnp.int32).reshape(-1)

    mirror_index = mirror_table(h_in, group_cols_of(own_rows, spread_in))

    smem = pl.BlockSpec(memory_space=pltpu.SMEM)
    vmem = pl.BlockSpec(memory_space=pltpu.VMEM)
    anywhere = pl.BlockSpec(memory_space=pl.ANY)

    def permute(x, target):
        return lax.ppermute(x, ("row", "col"), row_major_perm(n_row, n_col, target))

    def relayout(x, m=0, target=at):
        return permute(x, lambda r, c: target((r // inner) ^ m, r % inner, c))

    def inside_permute(x, move, source=inside, target=at):
        return permute(x, lambda r, c: target(*move(*source(r, c))))

    def share(x):
        return inside_permute(x, lambda o, h, g: (o, h ^ 1, g))

    def after(x, done):
        return lax.optimization_barrier((x, done))[0]

    def to_plane(x, m, source=inside, target=at):
        return inside_permute(x, lambda o, h, g: (o ^ m, h, g), source, target)

    def share_all(pieces):
        return {m: share(piece) for m, piece in pieces.items()}

    def listed(pieces, shared):
        return [pieces[m] for m in range(outer)] + [shared[m] for m in range(outer)]

    def mirror(x):
        moved = inside_permute(x, lambda o, h, g: (g, h, o), inside_spread, at_spread)
        return [moved, share(moved)]

    def exchange(outs):
        return [outs[0]] + [
            inside_permute(out, lambda o, h, g, d=d: (o, h, g ^ d))
            for d, out in enumerate(outs)
            if d
        ]

    def total_of(parts):
        value = parts[0]
        for part in parts[1:]:
            value = value + part.astype(f32)
        return value.astype(bf16)

    block_shape = (blocks, side, side)
    out_shapes = tuple(
        jax.ShapeDtypeStruct(block_shape, bf16 if d else f32) for d in range(n_col)
    )
    params = pltpu.CompilerParams(vmem_limit_bytes=14 * 2**20)

    def held(count):
        return pltpu.VMEM((count, side, side), bf16)

    def dma(count):
        return pltpu.SemaphoreType.DMA((count,))

    tail_shape = jax.ShapeDtypeStruct((16, side), bf16)
    long_shape = jax.ShapeDtypeStruct((blocks * side + tail_shape.shape[0], side), bf16)
    long_sums = [
        pltpu.VMEM(block_shape, f32),
        pltpu.VMEM((n_col - 1,) + long_shape.shape, bf16),
    ]
    sums = [pltpu.VMEM(block_shape, f32), pltpu.VMEM((n_col - 1,) + block_shape, bf16)]
    cost = pl.CostEstimate(
        flops=2 * n_col * blocks * slots * side**3,
        bytes_accessed=4 * 2**20,
        transcendentals=0,
    )

    flat = lambda x: x.reshape(block_shape)
    inter, dens, kohn = flat(intersection), flat(density), flat(kohn_sham)

    far_from = range(2, outer, 2)
    near = [*far_from, 1]

    inter_near = {m: relayout(inter, m) for m in near}
    inter_early = {0: relayout(inter)} | inter_near
    step = relayout(flat(step_dir))
    dens_own = relayout(dens)
    inter_far = {m + 1: to_plane(inter_near[m], 1) for m in far_from}
    dens_behind = after(dens_own, (inter_near, inter_far))
    dens_near = {m: to_plane(dens_behind, m) for m in near}
    inter_all = listed(inter_early | inter_far, share_all(inter_early) | share_all(inter_far))
    outs = pl.pallas_call(
        functools.partial(first_kernel, rows, slots, n_row),
        out_shape=out_shapes,
        in_specs=[smem] + [anywhere] * (1 + n_row),
        out_specs=(anywhere,) * n_col,
        scratch_shapes=[held(n_row * blocks + 1), held(blocks), *sums, dma(n_row + 1), dma(n_col)],
        compiler_params=params,
        cost_estimate=cost,
        name="scaled_step_product",
    )(first_index, step, *inter_all)
    parts = exchange(outs)

    dens_beside = {0: share(dens_own)}
    dens_near, kohn = after((dens_near, kohn), parts[1:])
    dens_far = {m + 1: to_plane(dens_near[m], 1) for m in far_from}
    dens_beside |= share_all(dens_near) | share_all(dens_far)
    dens_all = listed({0: dens_own} | dens_near | dens_far, dens_beside)
    kohn_own = relayout(kohn, 0, at_spread)
    kohn_behind = after(kohn, dens_near)
    kohn_near = {m: relayout(kohn_behind, m, at_spread) for m in near}
    outs = pl.pallas_call(
        functools.partial(second_kernel, rows, slots, n_row, n_col),
        out_shape=out_shapes,
        in_specs=[smem] + [anywhere] * (n_row + n_col),
        out_specs=(anywhere,) * n_col,
        scratch_shapes=[
            held(n_row * blocks + 1),
            held(blocks),
            *sums,
            *sums,
            dma(n_row + n_col),
            dma(n_col),
        ],
        compiler_params=params,
        cost_estimate=cost,
        name="change_product",
    )(second_index, *dens_all, *parts)
    total = total_of(exchange(outs))

    kohn_beside = {0: share(kohn_own)}
    kohn_near = after(kohn_near, total)
    kohn_far = {m + 1: to_plane(kohn_near[m], 1, inside_spread, at_spread) for m in far_from}
    kohn_beside |= share_all(kohn_near) | share_all(kohn_far)
    kohn_all = listed({0: kohn_own} | kohn_near | kohn_far, kohn_beside)
    *outs, trace = pl.pallas_call(
        functools.partial(third_kernel, rows, slots, n_row, inner),
        out_shape=out_shapes[:1] + (long_shape,) * (n_col - 1) + (tail_shape,),
        in_specs=[smem, smem] + [anywhere] * (1 + n_row + inner),
        out_specs=(anywhere,) * n_col + (vmem,),
        scratch_shapes=[
            held(n_row * blocks + 1),
            held(inner * blocks + 1),
            held(blocks),
            held(blocks),
            *long_sums,
            dma(n_row + inner + 1),
            dma(n_col),
        ],
        compiler_params=params,
        cost_estimate=cost,
        name="commutator_product",
    )(third_index, mirror_index, total, *kohn_all, *mirror(total))
    own, *parts = exchange(outs)
    total = pl.pallas_call(
        functools.partial(sum_kernel, n_col),
        out_shape=long_shape,
        in_specs=[vmem] + [anywhere] * n_col,
        out_specs=anywhere,
        scratch_shapes=[*long_sums, pltpu.VMEM(long_shape.shape, bf16), dma(n_col), dma(1)],
        compiler_params=params,
        name="plane_sum",
    )(trace, own, *parts)
    mirrored = mirror(total)

    commutator = pl.pallas_call(
        functools.partial(last_kernel, inner, blocks),
        out_shape=jax.ShapeDtypeStruct(block_shape, bf16),
        in_specs=[smem] + [anywhere] * (1 + inner),
        out_specs=anywhere,
        scratch_shapes=[
            pltpu.VMEM(((inner * blocks + 1) * side, side), bf16),
            pltpu.VMEM((blocks * side, side), bf16),
            held(blocks),
            dma(inner + 1),
            dma(1),
        ],
        compiler_params=params,
        name="commutator_difference",
    )(mirror_index, total, *mirrored)
    commutator = inside_permute(
        commutator, lambda o, h, g: (o, h, g), inside_spread, lambda o, h, g: (o * inner + h, g)
    )

    plane_trace = tree_sum([one_part(piece[blocks * side :]) for piece in mirrored])
    trace = tree_sum(
        [plane_trace]
        + [
            inside_permute(plane_trace, lambda o, h, g, d=d: (o, h, g ^ d))
            for d in range(1, n_col)
        ]
    )
    trace_value = trace.sum() / (blocks_total * side * side)
    return commutator.reshape(step_dir.shape), trace_value


def solution(mesh):
    in_specs = (P(),) + (P("row", "col", None, None),) * 4
    out_specs = (P("row", "col", None, None), P())
    return jax.shard_map(
        functools.partial(per_device, mesh.shape["row"], mesh.shape["col"]),
        mesh=mesh,
        in_specs=in_specs,
        out_specs=out_specs,
        check_vma=False,
    )
```

```python
import functools

import jax
import jax.numpy as jnp
from jax import lax
from jax.experimental import pallas as pl
from jax.experimental.pallas import tpu as pltpu
from jax.sharding import PartitionSpec as P

CORES = 2


def row_major_perm(n_row, n_col, target):
    pairs = []
    for r in range(n_row):
        for c in range(n_col):
            to_r, to_c = target(r, c)
            pairs.append((r * n_col + c, to_r * n_col + to_c))
    return pairs


def start_copies(pairs, sems):
    copies = [pltpu.make_async_copy(*pair, sems.at[i]) for i, pair in enumerate(pairs)]
    for copy in copies:
        copy.start()
    return copies


def wait_for(copies):
    for copy in copies:
        copy.wait()


def into(pieces, scratch, count):
    scratch[len(pieces) * count] = jnp.zeros(scratch.shape[1:], scratch.dtype)
    return [
        (piece, scratch.at[pl.ds(index * count, count)]) for index, piece in enumerate(pieces)
    ]


def multiply(index_ref, left_of, right, results, outs, sems, rows, slots, contract):
    copies = []
    for d in range(len(outs) - 1, -1, -1):
        for i in range(rows):
            left = left_of(i)
            for s in range(slots):
                base = ((d * rows + i) * slots + s) * slots
                blocks = jnp.concatenate(
                    [right[index_ref[base + a]] for a in range(slots)], axis=1
                )
                value = lax.dot_general(
                    blocks,
                    left,
                    (((1,), (contract,)), ((), ())),
                    preferred_element_type=jnp.float32,
                ).astype(results[d].dtype)
                if len(results[d].shape) == 3:
                    results[d][i * slots + s] = value
                else:
                    side = value.shape[0]
                    results[d][pl.ds((i * slots + s) * side, side)] = value
        copy = pltpu.make_async_copy(results[d], outs[d], sems.at[d])
        copy.start()
        copies.append(copy)
    wait_for(copies)


def split_results(first, others):
    return [first] + [others.at[d] for d in range(others.shape[0])]


def first_kernel(rows, slots, n_pieces, index_ref, left_ref, *refs):
    pieces, outs = refs[:n_pieces], refs[n_pieces:-6]
    right, left, first, others, sems, out_sems = refs[-6:]
    wait_for(start_copies(into(pieces, right, rows * slots) + [(left_ref, left)], sems))

    def left_of(i):
        return jnp.concatenate([left[i * slots + a] for a in range(slots)], axis=1)

    results = split_results(first, others)
    multiply(index_ref, left_of, right, results, outs, out_sems, rows, slots, 1)


def second_kernel(rows, slots, n_pieces, n_out, n_early, index_ref, *refs):
    pieces, parts = refs[:n_pieces], refs[n_pieces : n_pieces + n_out]
    right, left, part_first, part_others, first, others, sems, out_sems = refs[-8:]
    outs = refs[n_pieces + n_out + n_early : -8]
    held = split_results(part_first, part_others)
    wait_for(start_copies(list(zip(parts, held)) + into(pieces, right, rows * slots), sems))
    for b in range(rows * slots):
        value = held[0][b]
        for part in held[1:]:
            value = value + part[b].astype(jnp.float32)
        left[b] = value.astype(jnp.bfloat16)

    def left_of(i):
        return jnp.concatenate([left[i * slots + a] for a in range(slots)], axis=0)

    results = split_results(first, others)
    multiply(index_ref, left_of, right, results, outs, out_sems, rows, slots, 0)


def two_parts(x):
    high = x.astype(jnp.bfloat16)
    low = (x - high.astype(jnp.float32)).astype(jnp.bfloat16)
    return jnp.concatenate([high, low], axis=0)


def one_part(x):
    x = x.astype(jnp.float32)
    half = x.shape[0] // 2
    return x[:half] + x[half:]


def tree_sum(values):
    while len(values) > 1:
        values = [values[i] + values[i + 1] for i in range(0, len(values), 2)]
    return values[0]


def third_kernel(rows, slots, n_pieces, n_mirror, index_ref, mirror_ref, own_ref, *refs):
    pieces, mirrored = refs[:n_pieces], refs[n_pieces : n_pieces + n_mirror]
    *outs, trace = refs[n_pieces + n_mirror : -8]
    right, mirror, own, left, first, others, sems, out_sems = refs[-8:]
    pairs = into(pieces, right, rows * slots) + into(mirrored, mirror, rows * slots) + [(own_ref, own)]
    wait_for(start_copies(pairs, sems))
    blocks, side = rows * slots, right.shape[1]
    part_rows = trace.shape[0] // 2
    total_trace = jnp.zeros((part_rows, side), jnp.float32)
    for b in range(blocks):
        other = mirror[mirror_ref[b]].astype(jnp.float32).T
        value = (-(own[b].astype(jnp.float32) + other)).astype(jnp.bfloat16)
        left[b] = value
        product = value.astype(jnp.float32) * right[b].astype(jnp.float32).T
        total_trace = total_trace + product.reshape(-1, part_rows, side).sum(0)
    total_trace = two_parts(total_trace)
    trace[...] = total_trace
    results = split_results(first, others)
    for result in results[1:]:
        result[pl.ds(blocks * side, 2 * part_rows)] = total_trace

    def left_of(i):
        return jnp.concatenate([left[i * slots + a] for a in range(slots)], axis=0)

    multiply(index_ref, left_of, right, results, outs, out_sems, rows, slots, 0)


def sum_kernel(n_out, trace_ref, own_ref, *refs):
    parts, (out, own, others, result, sems, out_sems) = refs[: n_out - 1], refs[n_out - 1 :]
    pairs = [(part, others.at[d]) for d, part in enumerate(parts)]
    wait_for(start_copies([(own_ref, own)] + pairs, sems))
    blocks, side = own.shape[:2]
    for b in range(blocks):
        value = own[b]
        for d in range(n_out - 1):
            value = value + others[d, pl.ds(b * side, side)].astype(jnp.float32)
        result[pl.ds(b * side, side)] = value.astype(result.dtype)
    tail = pl.ds(blocks * side, trace_ref.shape[0])
    tiles = [trace_ref[...]] + [others[d, tail] for d in range(n_out - 1)]
    result[tail] = two_parts(tree_sum([one_part(tile) for tile in tiles]))
    wait_for(start_copies([(result, out)], out_sems))


def last_kernel(n_mirror, blocks, mirror_ref, own_ref, *refs):
    mirrored, (out, mirror, own, result, sems, out_sems) = refs[:n_mirror], refs[n_mirror:]
    side = own.shape[1]
    count = blocks * side
    body = pl.ds(0, count)
    pairs = [(own_ref.at[body], own)] + [
        (piece.at[body], mirror.at[pl.ds(t * count, count)]) for t, piece in enumerate(mirrored)
    ]
    copies = start_copies(pairs, sems)
    mirror[pl.ds(n_mirror * count, side)] = jnp.zeros((side, side), mirror.dtype)
    wait_for(copies)
    for b in range(blocks):
        start = pl.multiple_of(mirror_ref[b] * side, side)
        other = mirror[pl.ds(start, side)].astype(jnp.float32)
        value = other - own[pl.ds(b * side, side)].astype(jnp.float32).T
        result[b] = value.astype(result.dtype)
    wait_for(start_copies([(result, out)], out_sems))


def per_device(n_row, n_col, block_cols, step_dir, intersection, density, kohn_sham):
    rows, slots, side = step_dir.shape[:3]
    blocks = rows * slots
    blocks_total = block_cols.shape[0]
    inner = n_row // n_col
    outer = n_row // inner
    assert inner == CORES and outer == n_col and outer & (outer - 1) == 0
    row_index = lax.axis_index("row")
    col_index = lax.axis_index("col")
    bf16, f32 = jnp.bfloat16, jnp.float32

    def at(o, h, g):
        return o * inner + g % inner, (g // inner) * CORES + h

    def inside(r, c):
        return r // inner, c % CORES, (c // CORES) * inner + r % inner

    def spread(o, g):
        bits = (n_col - 1).bit_length()
        return g ^ sum(((o >> b) & 1) << (bits - 1 - b) for b in range(bits))

    def at_spread(o, h, g):
        return at(o, h, spread(o, g))

    def inside_spread(r, c):
        o, h, p = inside(r, c)
        return o, h, spread(o, p)

    o_in, h_in, g_in = inside(row_index, col_index)

    by_group = block_cols.reshape(blocks_total, n_col, slots)
    mirror_cols = lax.dynamic_slice_in_dim(by_group, o_in, 1, 1)[:, 0]

    def rows_of(o, h):
        return lax.dynamic_slice_in_dim(by_group, (o * inner + h) * rows, rows, 0)

    def group_cols_of(cols, g):
        return lax.dynamic_slice_in_dim(cols, g, 1, 1)[:, 0]

    own_rows = rows_of(o_in, h_in)

    def index_table(group, first_out):
        own_cols, group_cols = group_cols_of(own_rows, group), group_cols_of(by_group, group)
        wanted = own_rows[:, first_out ^ jnp.arange(n_col)].transpose(1, 0, 2)
        safe = jnp.clip(wanted, 0, blocks_total - 1)
        matched = (
            (group_cols[safe][..., None, :] == own_cols[None, :, None, :, None])
            & (wanted >= 0)[..., None, None]
            & (own_cols >= 0)[None, :, None, :, None]
        )
        piece = ((safe // rows % inner) ^ h_in) * outer + (safe // rows // inner ^ o_in)
        slot = ((piece * rows + safe % rows) * slots)[..., None] + jnp.argmax(matched, axis=-1)
        return jnp.where(matched.any(-1), slot, n_row * blocks).astype(jnp.int32).reshape(-1)

    spread_in = spread(o_in, g_in)
    first_index = index_table(g_in, g_in)
    second_index = index_table(g_in, spread_in)
    third_index = index_table(spread_in, spread_in)

    def mirror_table(h, cols):
        own_ids = (o_in * inner + h) * rows + jnp.arange(rows)
        safe_own = jnp.clip(cols, 0, blocks_total - 1)
        found = mirror_cols[safe_own] == own_ids[:, None, None]
        source = (safe_own // rows % inner) ^ h
        return jnp.where(
            cols >= 0,
            (source * rows + safe_own % rows) * slots + jnp.argmax(found, axis=-1),
            inner * blocks,
        ).astype(jnp.int32).reshape(-1)

    mirror_index = mirror_table(h_in, group_cols_of(own_rows, spread_in))

    smem = pl.BlockSpec(memory_space=pltpu.SMEM)
    vmem = pl.BlockSpec(memory_space=pltpu.VMEM)
    anywhere = pl.BlockSpec(memory_space=pl.ANY)

    def permute(x, target):
        return lax.ppermute(x, ("row", "col"), row_major_perm(n_row, n_col, target))

    def relayout(x, m=0, target=at):
        return permute(x, lambda r, c: target((r // inner) ^ m, r % inner, c))

    def inside_permute(x, move, source=inside, target=at):
        return permute(x, lambda r, c: target(*move(*source(r, c))))

    def share(x):
        return inside_permute(x, lambda o, h, g: (o, h ^ 1, g))

    def after(x, done):
        return lax.optimization_barrier((x, done))[0]

    def to_plane(x, m, source=inside, target=at):
        return inside_permute(x, lambda o, h, g: (o ^ m, h, g), source, target)

    def share_all(pieces):
        return {m: share(piece) for m, piece in pieces.items()}

    def listed(pieces, shared):
        return [pieces[m] for m in range(outer)] + [shared[m] for m in range(outer)]

    def mirror(x):
        moved = inside_permute(x, lambda o, h, g: (g, h, o), inside_spread, at_spread)
        return [moved, share(moved)]

    def exchange(outs):
        return [outs[0]] + [
            inside_permute(out, lambda o, h, g, d=d: (o, h, g ^ d))
            for d, out in enumerate(outs)
            if d
        ]

    def total_of(parts):
        value = parts[0]
        for part in parts[1:]:
            value = value + part.astype(f32)
        return value.astype(bf16)

    block_shape = (blocks, side, side)
    out_shapes = tuple(
        jax.ShapeDtypeStruct(block_shape, bf16 if d else f32) for d in range(n_col)
    )
    params = pltpu.CompilerParams(vmem_limit_bytes=14 * 2**20)

    def held(count):
        return pltpu.VMEM((count, side, side), bf16)

    def dma(count):
        return pltpu.SemaphoreType.DMA((count,))

    tail_shape = jax.ShapeDtypeStruct((16, side), bf16)
    long_shape = jax.ShapeDtypeStruct((blocks * side + tail_shape.shape[0], side), bf16)
    long_sums = [
        pltpu.VMEM(block_shape, f32),
        pltpu.VMEM((n_col - 1,) + long_shape.shape, bf16),
    ]
    sums = [pltpu.VMEM(block_shape, f32), pltpu.VMEM((n_col - 1,) + block_shape, bf16)]
    cost = pl.CostEstimate(
        flops=2 * n_col * blocks * slots * side**3,
        bytes_accessed=4 * 2**20,
        transcendentals=0,
    )

    flat = lambda x: x.reshape(block_shape)
    inter, dens, kohn = flat(intersection), flat(density), flat(kohn_sham)

    far_from = range(2, outer, 2)
    near = [*far_from, 1]

    inter_near = {m: relayout(inter, m) for m in near}
    inter_early = {0: relayout(inter)} | inter_near
    step, dens = after((flat(step_dir), dens), inter_near)
    step = relayout(step)
    dens_own = relayout(dens)
    inter_far = {m + 1: to_plane(inter_near[m], 1) for m in far_from}
    dens_behind = after(dens_own, (inter_near, inter_far))
    dens_near = {m: to_plane(dens_behind, m) for m in near}
    inter_all = listed(inter_early | inter_far, share_all(inter_early) | share_all(inter_far))
    outs = pl.pallas_call(
        functools.partial(first_kernel, rows, slots, n_row),
        out_shape=out_shapes,
        in_specs=[smem] + [anywhere] * (1 + n_row),
        out_specs=(anywhere,) * n_col,
        scratch_shapes=[held(n_row * blocks + 1), held(blocks), *sums, dma(n_row + 1), dma(n_col)],
        compiler_params=params,
        cost_estimate=cost,
        name="scaled_step_product",
    )(first_index, step, *inter_all)
    parts = exchange(outs)

    dens_beside = {0: share(dens_own)}
    kohn_near = {m: relayout(after(kohn, dens_near), m, at_spread) for m in far_from}
    dens_near, kohn = after((dens_near, kohn), parts[1:])
    kohn_own = relayout(kohn, 0, at_spread)
    dens_far = {m + 1: to_plane(dens_near[m], 1) for m in far_from}
    dens_beside |= share_all(dens_near) | share_all(dens_far)
    dens_all = listed({0: dens_own} | dens_near | dens_far, dens_beside)
    kohn_early = [kohn_own, *kohn_near.values()]
    outs = pl.pallas_call(
        functools.partial(second_kernel, rows, slots, n_row, n_col, len(kohn_early)),
        out_shape=out_shapes,
        in_specs=[smem] + [anywhere] * (n_row + n_col + len(kohn_early)),
        out_specs=(anywhere,) * n_col,
        scratch_shapes=[
            held(n_row * blocks + 1),
            held(blocks),
            *sums,
            *sums,
            dma(n_row + n_col),
            dma(n_col),
        ],
        compiler_params=params,
        cost_estimate=cost,
        name="change_product",
    )(second_index, *dens_all, *parts, *kohn_early)
    parts = exchange(outs)
    total = total_of(parts)

    kohn, kohn_near, kohn_own = after((kohn, kohn_near, kohn_own), outs)
    kohn_beside = {0: share(kohn_own)} | share_all(kohn_near)
    kohn_next = relayout(kohn, 1, at_spread)
    kohn_far = {
        m + 1: to_plane(after(kohn_near[m], parts[1]), 1, inside_spread, at_spread) for m in far_from
    }
    kohn_last = after({1: kohn_next} | kohn_far, total)
    kohn_all = listed({0: kohn_own} | kohn_near | kohn_last, kohn_beside | share_all(kohn_last))
    *outs, trace = pl.pallas_call(
        functools.partial(third_kernel, rows, slots, n_row, inner),
        out_shape=out_shapes[:1] + (long_shape,) * (n_col - 1) + (tail_shape,),
        in_specs=[smem, smem] + [anywhere] * (1 + n_row + inner),
        out_specs=(anywhere,) * n_col + (vmem,),
        scratch_shapes=[
            held(n_row * blocks + 1),
            held(inner * blocks + 1),
            held(blocks),
            held(blocks),
            *long_sums,
            dma(n_row + inner + 1),
            dma(n_col),
        ],
        compiler_params=params,
        cost_estimate=cost,
        name="commutator_product",
    )(third_index, mirror_index, total, *kohn_all, *mirror(total))
    own, *parts = exchange(outs)
    total = pl.pallas_call(
        functools.partial(sum_kernel, n_col),
        out_shape=long_shape,
        in_specs=[vmem] + [anywhere] * n_col,
        out_specs=anywhere,
        scratch_shapes=[*long_sums, pltpu.VMEM(long_shape.shape, bf16), dma(n_col), dma(1)],
        compiler_params=params,
        name="plane_sum",
    )(trace, own, *parts)
    mirrored = mirror(total)

    commutator = pl.pallas_call(
        functools.partial(last_kernel, inner, blocks),
        out_shape=jax.ShapeDtypeStruct(block_shape, bf16),
        in_specs=[smem] + [anywhere] * (1 + inner),
        out_specs=anywhere,
        scratch_shapes=[
            pltpu.VMEM(((inner * blocks + 1) * side, side), bf16),
            pltpu.VMEM((blocks * side, side), bf16),
            held(blocks),
            dma(inner + 1),
            dma(1),
        ],
        compiler_params=params,
        name="commutator_difference",
    )(mirror_index, total, *mirrored)
    commutator = inside_permute(
        commutator, lambda o, h, g: (o, h, g), inside_spread, lambda o, h, g: (o * inner + h, g)
    )

    plane_trace = tree_sum([one_part(piece[blocks * side :]) for piece in mirrored])
    trace = tree_sum(
        [plane_trace]
        + [
            inside_permute(plane_trace, lambda o, h, g, d=d: (o, h, g ^ d))
            for d in range(1, n_col)
        ]
    )
    trace_value = trace.sum() / (blocks_total * side * side)
    return commutator.reshape(step_dir.shape), trace_value


def solution(mesh):
    in_specs = (P(),) + (P("row", "col", None, None),) * 4
    out_specs = (P("row", "col", None, None), P())
    return jax.shard_map(
        functools.partial(per_device, mesh.shape["row"], mesh.shape["col"]),
        mesh=mesh,
        in_specs=in_specs,
        out_specs=out_specs,
        check_vma=False,
    )
```

```python
import functools

import jax
import jax.numpy as jnp
from jax import lax
from jax.experimental import pallas as pl
from jax.experimental.pallas import tpu as pltpu
from jax.sharding import PartitionSpec as P

CORES = 2


def row_major_perm(n_row, n_col, target):
    pairs = []
    for r in range(n_row):
        for c in range(n_col):
            to_r, to_c = target(r, c)
            pairs.append((r * n_col + c, to_r * n_col + to_c))
    return pairs


def start_copies(pairs, sems):
    copies = [pltpu.make_async_copy(*pair, sems.at[i]) for i, pair in enumerate(pairs)]
    for copy in copies:
        copy.start()
    return copies


def wait_for(copies):
    for copy in copies:
        copy.wait()


def into(pieces, scratch, count):
    scratch[len(pieces) * count] = jnp.zeros(scratch.shape[1:], scratch.dtype)
    return [
        (piece, scratch.at[pl.ds(index * count, count)]) for index, piece in enumerate(pieces)
    ]


def multiply(index_ref, left_of, right, results, outs, sems, rows, slots, contract):
    copies = []
    for d in range(len(outs) - 1, -1, -1):
        for i in range(rows):
            left = left_of(i)
            for s in range(slots):
                base = ((d * rows + i) * slots + s) * slots
                blocks = jnp.concatenate(
                    [right[index_ref[base + a]] for a in range(slots)], axis=1
                )
                value = lax.dot_general(
                    blocks,
                    left,
                    (((1,), (contract,)), ((), ())),
                    preferred_element_type=jnp.float32,
                ).astype(results[d].dtype)
                if len(results[d].shape) == 3:
                    results[d][i * slots + s] = value
                else:
                    side = value.shape[0]
                    results[d][pl.ds((i * slots + s) * side, side)] = value
        copy = pltpu.make_async_copy(results[d], outs[d], sems.at[d])
        copy.start()
        copies.append(copy)
    wait_for(copies)


def split_results(first, others):
    return [first] + [others.at[d] for d in range(others.shape[0])]


def first_kernel(rows, slots, n_pieces, index_ref, left_ref, *refs):
    pieces, outs = refs[:n_pieces], refs[n_pieces:-6]
    right, left, first, others, sems, out_sems = refs[-6:]
    wait_for(start_copies(into(pieces, right, rows * slots) + [(left_ref, left)], sems))

    def left_of(i):
        return jnp.concatenate([left[i * slots + a] for a in range(slots)], axis=1)

    results = split_results(first, others)
    multiply(index_ref, left_of, right, results, outs, out_sems, rows, slots, 1)


def second_kernel(rows, slots, n_pieces, n_out, index_ref, *refs):
    pieces, parts = refs[:n_pieces], refs[n_pieces : n_pieces + n_out]
    right, left, part_first, part_others, first, others, sems, out_sems = refs[-8:]
    outs = refs[n_pieces + n_out : -8]
    held = split_results(part_first, part_others)
    wait_for(start_copies(list(zip(parts, held)) + into(pieces, right, rows * slots), sems))
    for b in range(rows * slots):
        value = held[0][b]
        for part in held[1:]:
            value = value + part[b].astype(jnp.float32)
        left[b] = value.astype(jnp.bfloat16)

    def left_of(i):
        return jnp.concatenate([left[i * slots + a] for a in range(slots)], axis=0)

    results = split_results(first, others)
    multiply(index_ref, left_of, right, results, outs, out_sems, rows, slots, 0)


def two_parts(x):
    high = x.astype(jnp.bfloat16)
    low = (x - high.astype(jnp.float32)).astype(jnp.bfloat16)
    return jnp.concatenate([high, low], axis=0)


def one_part(x):
    x = x.astype(jnp.float32)
    half = x.shape[0] // 2
    return x[:half] + x[half:]


def tree_sum(values):
    while len(values) > 1:
        values = [values[i] + values[i + 1] for i in range(0, len(values), 2)]
    return values[0]


def third_kernel(rows, slots, n_pieces, n_mirror, index_ref, mirror_ref, own_ref, *refs):
    pieces, mirrored = refs[:n_pieces], refs[n_pieces : n_pieces + n_mirror]
    *outs, trace = refs[n_pieces + n_mirror : -8]
    right, mirror, own, left, first, others, sems, out_sems = refs[-8:]
    pairs = into(pieces, right, rows * slots) + into(mirrored, mirror, rows * slots) + [(own_ref, own)]
    wait_for(start_copies(pairs, sems))
    blocks, side = rows * slots, right.shape[1]
    part_rows = trace.shape[0] // 2
    total_trace = jnp.zeros((part_rows, side), jnp.float32)
    for b in range(blocks):
        other = mirror[mirror_ref[b]].astype(jnp.float32).T
        value = (-(own[b].astype(jnp.float32) + other)).astype(jnp.bfloat16)
        left[b] = value
        product = value.astype(jnp.float32) * right[b].astype(jnp.float32).T
        total_trace = total_trace + product.reshape(-1, part_rows, side).sum(0)
    total_trace = two_parts(total_trace)
    trace[...] = total_trace
    results = split_results(first, others)
    for result in results[1:]:
        result[pl.ds(blocks * side, 2 * part_rows)] = total_trace

    def left_of(i):
        return jnp.concatenate([left[i * slots + a] for a in range(slots)], axis=0)

    multiply(index_ref, left_of, right, results, outs, out_sems, rows, slots, 0)


def sum_kernel(n_out, trace_ref, own_ref, *refs):
    parts, (out, own, others, result, sems, out_sems) = refs[: n_out - 1], refs[n_out - 1 :]
    pairs = [(part, others.at[d]) for d, part in enumerate(parts)]
    wait_for(start_copies([(own_ref, own)] + pairs, sems))
    blocks, side = own.shape[:2]
    for b in range(blocks):
        value = own[b]
        for d in range(n_out - 1):
            value = value + others[d, pl.ds(b * side, side)].astype(jnp.float32)
        result[pl.ds(b * side, side)] = value.astype(result.dtype)
    tail = pl.ds(blocks * side, trace_ref.shape[0])
    tiles = [trace_ref[...]] + [others[d, tail] for d in range(n_out - 1)]
    result[tail] = two_parts(tree_sum([one_part(tile) for tile in tiles]))
    wait_for(start_copies([(result, out)], out_sems))


def last_kernel(n_mirror, blocks, mirror_ref, own_ref, *refs):
    mirrored, (out, mirror, own, result, sems, out_sems) = refs[:n_mirror], refs[n_mirror:]
    side = own.shape[1]
    count = blocks * side
    body = pl.ds(0, count)
    pairs = [(own_ref.at[body], own)] + [
        (piece.at[body], mirror.at[pl.ds(t * count, count)]) for t, piece in enumerate(mirrored)
    ]
    copies = start_copies(pairs, sems)
    mirror[pl.ds(n_mirror * count, side)] = jnp.zeros((side, side), mirror.dtype)
    wait_for(copies)
    for b in range(blocks):
        start = pl.multiple_of(mirror_ref[b] * side, side)
        other = mirror[pl.ds(start, side)].astype(jnp.float32)
        value = other - own[pl.ds(b * side, side)].astype(jnp.float32).T
        result[b] = value.astype(result.dtype)
    wait_for(start_copies([(result, out)], out_sems))


def per_device(n_row, n_col, block_cols, step_dir, intersection, density, kohn_sham):
    rows, slots, side = step_dir.shape[:3]
    blocks = rows * slots
    blocks_total = block_cols.shape[0]
    inner = n_row // n_col
    outer = n_row // inner
    assert inner == CORES and outer == n_col and outer & (outer - 1) == 0
    row_index = lax.axis_index("row")
    col_index = lax.axis_index("col")
    bf16, f32 = jnp.bfloat16, jnp.float32

    def at(o, h, g):
        return o * inner + g % inner, (g // inner) * CORES + h

    def inside(r, c):
        return r // inner, c % CORES, (c // CORES) * inner + r % inner

    def spread(o, g):
        bits = (n_col - 1).bit_length()
        return g ^ sum(((o >> b) & 1) << (bits - 1 - b) for b in range(bits))

    def at_spread(o, h, g):
        return at(o, h, spread(o, g))

    def inside_spread(r, c):
        o, h, p = inside(r, c)
        return o, h, spread(o, p)

    o_in, h_in, g_in = inside(row_index, col_index)

    by_group = block_cols.reshape(blocks_total, n_col, slots)
    mirror_cols = lax.dynamic_slice_in_dim(by_group, o_in, 1, 1)[:, 0]

    def rows_of(o, h):
        return lax.dynamic_slice_in_dim(by_group, (o * inner + h) * rows, rows, 0)

    def group_cols_of(cols, g):
        return lax.dynamic_slice_in_dim(cols, g, 1, 1)[:, 0]

    own_rows = rows_of(o_in, h_in)

    def index_table(group, first_out):
        own_cols, group_cols = group_cols_of(own_rows, group), group_cols_of(by_group, group)
        wanted = own_rows[:, first_out ^ jnp.arange(n_col)].transpose(1, 0, 2)
        safe = jnp.clip(wanted, 0, blocks_total - 1)
        matched = (
            (group_cols[safe][..., None, :] == own_cols[None, :, None, :, None])
            & (wanted >= 0)[..., None, None]
            & (own_cols >= 0)[None, :, None, :, None]
        )
        piece = ((safe // rows % inner) ^ h_in) * outer + (safe // rows // inner ^ o_in)
        slot = ((piece * rows + safe % rows) * slots)[..., None] + jnp.argmax(matched, axis=-1)
        return jnp.where(matched.any(-1), slot, n_row * blocks).astype(jnp.int32).reshape(-1)

    spread_in = spread(o_in, g_in)
    first_index, later_index = index_table(g_in, g_in), index_table(g_in, spread_in)

    def mirror_table(h, cols):
        own_ids = (o_in * inner + h) * rows + jnp.arange(rows)
        safe_own = jnp.clip(cols, 0, blocks_total - 1)
        found = mirror_cols[safe_own] == own_ids[:, None, None]
        source = (safe_own // rows % inner) ^ h
        return jnp.where(
            cols >= 0,
            (source * rows + safe_own % rows) * slots + jnp.argmax(found, axis=-1),
            inner * blocks,
        ).astype(jnp.int32).reshape(-1)

    mirror_index = mirror_table(h_in, group_cols_of(own_rows, g_in))
    last_mirror_index = mirror_table(h_in, group_cols_of(own_rows, spread_in))

    smem = pl.BlockSpec(memory_space=pltpu.SMEM)
    vmem = pl.BlockSpec(memory_space=pltpu.VMEM)
    anywhere = pl.BlockSpec(memory_space=pl.ANY)

    def permute(x, target):
        return lax.ppermute(x, ("row", "col"), row_major_perm(n_row, n_col, target))

    def relayout(x, m=0, target=at):
        return permute(x, lambda r, c: target((r // inner) ^ m, r % inner, c))

    def inside_permute(x, move, source=inside, target=at):
        return permute(x, lambda r, c: target(*move(*source(r, c))))

    def share(x):
        return inside_permute(x, lambda o, h, g: (o, h ^ 1, g))

    def after(x, done):
        return lax.optimization_barrier((x, done))[0]

    def to_plane(x, m):
        return inside_permute(x, lambda o, h, g: (o ^ m, h, g))

    def share_all(pieces):
        return {m: share(piece) for m, piece in pieces.items()}

    def listed(pieces, shared):
        return [pieces[m] for m in range(outer)] + [shared[m] for m in range(outer)]

    def mirror(x, target):
        moved = inside_permute(x, lambda o, h, g: (g, h, o), inside_spread, target)
        return [moved, share(moved)]

    def exchange(outs):
        return [outs[0]] + [
            inside_permute(out, lambda o, h, g, d=d: (o, h, g ^ d))
            for d, out in enumerate(outs)
            if d
        ]

    def total_of(parts):
        value = parts[0]
        for part in parts[1:]:
            value = value + part.astype(f32)
        return value.astype(bf16)

    block_shape = (blocks, side, side)
    out_shapes = tuple(
        jax.ShapeDtypeStruct(block_shape, bf16 if d else f32) for d in range(n_col)
    )
    params = pltpu.CompilerParams(vmem_limit_bytes=14 * 2**20)

    def held(count):
        return pltpu.VMEM((count, side, side), bf16)

    def dma(count):
        return pltpu.SemaphoreType.DMA((count,))

    tail_shape = jax.ShapeDtypeStruct((16, side), bf16)
    long_shape = jax.ShapeDtypeStruct((blocks * side + tail_shape.shape[0], side), bf16)
    long_sums = [
        pltpu.VMEM(block_shape, f32),
        pltpu.VMEM((n_col - 1,) + long_shape.shape, bf16),
    ]
    sums = [pltpu.VMEM(block_shape, f32), pltpu.VMEM((n_col - 1,) + block_shape, bf16)]
    cost = pl.CostEstimate(
        flops=2 * n_col * blocks * slots * side**3,
        bytes_accessed=4 * 2**20,
        transcendentals=0,
    )

    flat = lambda x: x.reshape(block_shape)
    inter, dens, kohn = flat(intersection), flat(density), flat(kohn_sham)

    far_from = range(2, outer, 2)
    near = [*far_from, 1]

    inter_near = {m: relayout(inter, m) for m in near}
    inter_early = {0: relayout(inter)} | inter_near
    step = relayout(flat(step_dir))
    dens_own = relayout(dens)
    inter_far = {m + 1: to_plane(inter_near[m], 1) for m in far_from}
    dens_behind = after(dens_own, (inter_near, inter_far))
    dens_near = {m: to_plane(dens_behind, m) for m in near}
    inter_all = listed(inter_early | inter_far, share_all(inter_early) | share_all(inter_far))
    outs = pl.pallas_call(
        functools.partial(first_kernel, rows, slots, n_row),
        out_shape=out_shapes,
        in_specs=[smem] + [anywhere] * (1 + n_row),
        out_specs=(anywhere,) * n_col,
        scratch_shapes=[held(n_row * blocks + 1), held(blocks), *sums, dma(n_row + 1), dma(n_col)],
        compiler_params=params,
        cost_estimate=cost,
        name="scaled_step_product",
    )(first_index, step, *inter_all)
    parts = exchange(outs)

    dens_beside = {0: share(dens_own)}
    dens_near, kohn = after((dens_near, kohn), parts[1:])
    dens_far = {m + 1: to_plane(dens_near[m], 1) for m in far_from}
    dens_beside |= share_all(dens_near) | share_all(dens_far)
    dens_all = listed({0: dens_own} | dens_near | dens_far, dens_beside)
    kohn_own = relayout(kohn)
    kohn_behind = after(kohn_own, dens_near)
    kohn_near = {m: to_plane(kohn_behind, m) for m in near}
    outs = pl.pallas_call(
        functools.partial(second_kernel, rows, slots, n_row, n_col),
        out_shape=out_shapes,
        in_specs=[smem] + [anywhere] * (n_row + n_col),
        out_specs=(anywhere,) * n_col,
        scratch_shapes=[
            held(n_row * blocks + 1),
            held(blocks),
            *sums,
            *sums,
            dma(n_row + n_col),
            dma(n_col),
        ],
        compiler_params=params,
        cost_estimate=cost,
        name="change_product",
    )(later_index, *dens_all, *parts)
    total = total_of(exchange(outs))

    mirrored = mirror(total, at)
    own = inside_permute(total, lambda o, h, g: (o, h, g), inside_spread)
    kohn_beside = {0: share(kohn_own)}
    kohn_near = after(kohn_near, total)
    kohn_far = {m + 1: to_plane(kohn_near[m], 1) for m in far_from}
    kohn_beside |= share_all(kohn_near) | share_all(kohn_far)
    kohn_all = listed({0: kohn_own} | kohn_near | kohn_far, kohn_beside)
    *outs, trace = pl.pallas_call(
        functools.partial(third_kernel, rows, slots, n_row, inner),
        out_shape=out_shapes[:1] + (long_shape,) * (n_col - 1) + (tail_shape,),
        in_specs=[smem, smem] + [anywhere] * (1 + n_row + inner),
        out_specs=(anywhere,) * n_col + (vmem,),
        scratch_shapes=[
            held(n_row * blocks + 1),
            held(inner * blocks + 1),
            held(blocks),
            held(blocks),
            *long_sums,
            dma(n_row + inner + 1),
            dma(n_col),
        ],
        compiler_params=params,
        cost_estimate=cost,
        name="commutator_product",
    )(later_index, mirror_index, own, *kohn_all, *mirrored)
    own, *parts = exchange(outs)
    total = pl.pallas_call(
        functools.partial(sum_kernel, n_col),
        out_shape=long_shape,
        in_specs=[vmem] + [anywhere] * n_col,
        out_specs=anywhere,
        scratch_shapes=[*long_sums, pltpu.VMEM(long_shape.shape, bf16), dma(n_col), dma(1)],
        compiler_params=params,
        name="plane_sum",
    )(trace, own, *parts)
    mirrored = mirror(total, at_spread)

    commutator = pl.pallas_call(
        functools.partial(last_kernel, inner, blocks),
        out_shape=jax.ShapeDtypeStruct(block_shape, bf16),
        in_specs=[smem] + [anywhere] * (1 + inner),
        out_specs=anywhere,
        scratch_shapes=[
            pltpu.VMEM(((inner * blocks + 1) * side, side), bf16),
            pltpu.VMEM((blocks * side, side), bf16),
            held(blocks),
            dma(inner + 1),
            dma(1),
        ],
        compiler_params=params,
        name="commutator_difference",
    )(last_mirror_index, total, *mirrored)
    commutator = inside_permute(
        commutator, lambda o, h, g: (o, h, g), inside_spread, lambda o, h, g: (o * inner + h, g)
    )

    plane_trace = tree_sum([one_part(piece[blocks * side :]) for piece in mirrored])
    trace = tree_sum(
        [plane_trace]
        + [
            inside_permute(plane_trace, lambda o, h, g, d=d: (o, h, g ^ d))
            for d in range(1, n_col)
        ]
    )
    trace_value = trace.sum() / (blocks_total * side * side)
    return commutator.reshape(step_dir.shape), trace_value


def solution(mesh):
    in_specs = (P(),) + (P("row", "col", None, None),) * 4
    out_specs = (P("row", "col", None, None), P())
    return jax.shard_map(
        functools.partial(per_device, mesh.shape["row"], mesh.shape["col"]),
        mesh=mesh,
        in_specs=in_specs,
        out_specs=out_specs,
        check_vma=False,
    )
```

```python
import functools

import jax
import jax.numpy as jnp
from jax import lax
from jax.experimental import pallas as pl
from jax.experimental.pallas import tpu as pltpu
from jax.sharding import PartitionSpec as P

CORES = 2


def row_major_perm(n_row, n_col, target):
    pairs = []
    for r in range(n_row):
        for c in range(n_col):
            to_r, to_c = target(r, c)
            pairs.append((r * n_col + c, to_r * n_col + to_c))
    return pairs


def start_copies(pairs, sems):
    copies = [pltpu.make_async_copy(*pair, sems.at[i]) for i, pair in enumerate(pairs)]
    for copy in copies:
        copy.start()
    return copies


def wait_for(copies):
    for copy in copies:
        copy.wait()


def into(pieces, scratch, count):
    scratch[len(pieces) * count] = jnp.zeros(scratch.shape[1:], scratch.dtype)
    return [
        (piece, scratch.at[pl.ds(index * count, count)]) for index, piece in enumerate(pieces)
    ]


def multiply(index_ref, index_at, left_of, right, results, outs, sems, rows, slots, contract):
    copies = []
    for d in range(len(outs) - 1, -1, -1):
        for i in range(rows):
            left = left_of(i)
            for s in range(slots):
                base = index_at + ((d * rows + i) * slots + s) * slots
                blocks = jnp.concatenate(
                    [right[index_ref[base + a]] for a in range(slots)], axis=1
                )
                value = lax.dot_general(
                    blocks,
                    left,
                    (((1,), (contract,)), ((), ())),
                    preferred_element_type=jnp.float32,
                ).astype(results[d].dtype)
                if len(results[d].shape) == 3:
                    results[d][i * slots + s] = value
                else:
                    side = value.shape[0]
                    results[d][pl.ds((i * slots + s) * side, side)] = value
        copy = pltpu.make_async_copy(results[d], outs[d], sems.at[d])
        copy.start()
        copies.append(copy)
    wait_for(copies)


def split_results(first, others):
    return [first] + [others.at[d] for d in range(others.shape[0])]


def first_kernel(rows, slots, n_pieces, n_early, index_at, index_ref, left_ref, *refs):
    pieces, outs = refs[:n_pieces], refs[n_pieces + n_early : -6]
    right, left, first, others, sems, out_sems = refs[-6:]
    wait_for(start_copies(into(pieces, right, rows * slots) + [(left_ref, left)], sems))

    def left_of(i):
        return jnp.concatenate([left[i * slots + a] for a in range(slots)], axis=1)

    results = split_results(first, others)
    multiply(index_ref, index_at, left_of, right, results, outs, out_sems, rows, slots, 1)


def second_kernel(rows, slots, n_pieces, n_out, n_early, index_at, index_ref, *refs):
    pieces, parts = refs[:n_pieces], refs[n_pieces : n_pieces + n_out]
    right, left, part_first, part_others, first, others, sems, out_sems = refs[-8:]
    outs = refs[n_pieces + n_out + n_early : -8]
    held = split_results(part_first, part_others)
    wait_for(start_copies(list(zip(parts, held)) + into(pieces, right, rows * slots), sems))
    for b in range(rows * slots):
        value = held[0][b]
        for part in held[1:]:
            value = value + part[b].astype(jnp.float32)
        left[b] = value.astype(jnp.bfloat16)

    def left_of(i):
        return jnp.concatenate([left[i * slots + a] for a in range(slots)], axis=0)

    results = split_results(first, others)
    multiply(index_ref, index_at, left_of, right, results, outs, out_sems, rows, slots, 0)


def two_parts(x):
    high = x.astype(jnp.bfloat16)
    low = (x - high.astype(jnp.float32)).astype(jnp.bfloat16)
    return jnp.concatenate([high, low], axis=0)


def one_part(x):
    x = x.astype(jnp.float32)
    half = x.shape[0] // 2
    return x[:half] + x[half:]


def tree_sum(values):
    while len(values) > 1:
        values = [values[i] + values[i + 1] for i in range(0, len(values), 2)]
    return values[0]


def third_kernel(rows, slots, n_pieces, n_mirror, index_at, mirror_at, index_ref, own_ref, *refs):
    pieces, mirrored = refs[:n_pieces], refs[n_pieces : n_pieces + n_mirror]
    *outs, trace = refs[n_pieces + n_mirror : -8]
    right, mirror, own, left, first, others, sems, out_sems = refs[-8:]
    pairs = into(pieces, right, rows * slots) + into(mirrored, mirror, rows * slots) + [(own_ref, own)]
    wait_for(start_copies(pairs, sems))
    blocks, side = rows * slots, right.shape[1]
    part_rows = trace.shape[0] // 2
    total_trace = jnp.zeros((part_rows, side), jnp.float32)
    for b in range(blocks):
        other = mirror[index_ref[mirror_at + b]].astype(jnp.float32).T
        value = (-(own[b].astype(jnp.float32) + other)).astype(jnp.bfloat16)
        left[b] = value
        product = value.astype(jnp.float32) * right[b].astype(jnp.float32).T
        total_trace = total_trace + product.reshape(-1, part_rows, side).sum(0)
    total_trace = two_parts(total_trace)
    trace[...] = total_trace
    results = split_results(first, others)
    for result in results[1:]:
        result[pl.ds(blocks * side, 2 * part_rows)] = total_trace

    def left_of(i):
        return jnp.concatenate([left[i * slots + a] for a in range(slots)], axis=0)

    multiply(index_ref, index_at, left_of, right, results, outs, out_sems, rows, slots, 0)


def sum_kernel(n_out, trace_ref, own_ref, *refs):
    parts, (out, own, others, result, sems, out_sems) = refs[: n_out - 1], refs[n_out - 1 :]
    pairs = [(part, others.at[d]) for d, part in enumerate(parts)]
    wait_for(start_copies([(own_ref, own)] + pairs, sems))
    blocks, side = own.shape[:2]
    for b in range(blocks):
        value = own[b]
        for d in range(n_out - 1):
            value = value + others[d, pl.ds(b * side, side)].astype(jnp.float32)
        result[pl.ds(b * side, side)] = value.astype(result.dtype)
    tail = pl.ds(blocks * side, trace_ref.shape[0])
    tiles = [trace_ref[...]] + [others[d, tail] for d in range(n_out - 1)]
    result[tail] = two_parts(tree_sum([one_part(tile) for tile in tiles]))
    wait_for(start_copies([(result, out)], out_sems))


def last_kernel(n_mirror, blocks, mirror_at, index_ref, own_ref, *refs):
    mirrored, (out, mirror, own, result, sems, out_sems) = refs[:n_mirror], refs[n_mirror:]
    side = own.shape[1]
    count = blocks * side
    body = pl.ds(0, count)
    pairs = [(own_ref.at[body], own)] + [
        (piece.at[body], mirror.at[pl.ds(t * count, count)]) for t, piece in enumerate(mirrored)
    ]
    copies = start_copies(pairs, sems)
    mirror[pl.ds(n_mirror * count, side)] = jnp.zeros((side, side), mirror.dtype)
    wait_for(copies)
    for b in range(blocks):
        start = pl.multiple_of(index_ref[mirror_at + b] * side, side)
        other = mirror[pl.ds(start, side)].astype(jnp.float32)
        value = other - own[pl.ds(b * side, side)].astype(jnp.float32).T
        result[b] = value.astype(result.dtype)
    wait_for(start_copies([(result, out)], out_sems))


def per_device(n_row, n_col, block_cols, step_dir, intersection, density, kohn_sham):
    rows, slots, side = step_dir.shape[:3]
    blocks = rows * slots
    blocks_total = block_cols.shape[0]
    inner = n_row // n_col
    outer = n_row // inner
    assert inner == CORES and outer == n_col and outer & (outer - 1) == 0
    row_index = lax.axis_index("row")
    col_index = lax.axis_index("col")
    bf16, f32 = jnp.bfloat16, jnp.float32

    def at(o, h, g):
        return o * inner + g % inner, (g // inner) * CORES + h

    def inside(r, c):
        return r // inner, c % CORES, (c // CORES) * inner + r % inner

    def spread(o, g):
        bits = (n_col - 1).bit_length()
        return g ^ sum(((o >> b) & 1) << (bits - 1 - b) for b in range(bits))

    def at_spread(o, h, g):
        return at(o, h, spread(o, g))

    def inside_spread(r, c):
        o, h, p = inside(r, c)
        return o, h, spread(o, p)

    o_in, h_in, g_in = inside(row_index, col_index)

    by_group = block_cols.reshape(blocks_total, n_col, slots)
    mirror_cols = lax.dynamic_slice_in_dim(by_group, o_in, 1, 1)[:, 0]

    def rows_of(o, h):
        return lax.dynamic_slice_in_dim(by_group, (o * inner + h) * rows, rows, 0)

    def group_cols_of(cols, g):
        return lax.dynamic_slice_in_dim(cols, g, 1, 1)[:, 0]

    own_rows = rows_of(o_in, h_in)

    def index_table(group, first_out):
        own_cols, group_cols = group_cols_of(own_rows, group), group_cols_of(by_group, group)
        wanted = own_rows[:, first_out ^ jnp.arange(n_col)].transpose(1, 0, 2)
        safe = jnp.clip(wanted, 0, blocks_total - 1)
        matched = (
            (group_cols[safe][..., None, :] == own_cols[None, :, None, :, None])
            & (wanted >= 0)[..., None, None]
            & (own_cols >= 0)[None, :, None, :, None]
        )
        piece = ((safe // rows % inner) ^ h_in) * outer + (safe // rows // inner ^ o_in)
        slot = ((piece * rows + safe % rows) * slots)[..., None] + jnp.argmax(matched, axis=-1)
        return jnp.where(matched.any(-1), slot, n_row * blocks).astype(jnp.int32).reshape(-1)

    spread_in = spread(o_in, g_in)
    all_tables = [index_table(g_in, g_in), index_table(g_in, spread_in)]

    def mirror_table(h, cols):
        own_ids = (o_in * inner + h) * rows + jnp.arange(rows)
        safe_own = jnp.clip(cols, 0, blocks_total - 1)
        found = mirror_cols[safe_own] == own_ids[:, None, None]
        source = (safe_own // rows % inner) ^ h
        return jnp.where(
            cols >= 0,
            (source * rows + safe_own % rows) * slots + jnp.argmax(found, axis=-1),
            inner * blocks,
        ).astype(jnp.int32).reshape(-1)

    all_tables += [mirror_table(h_in, group_cols_of(own_rows, g)) for g in (g_in, spread_in)]
    starts = [sum(table.size for table in all_tables[:t]) for t in range(len(all_tables))]
    first_at, later_at, mirror_at, last_mirror_at = starts
    tables = jnp.concatenate(all_tables)

    smem = pl.BlockSpec(memory_space=pltpu.SMEM)
    vmem = pl.BlockSpec(memory_space=pltpu.VMEM)
    anywhere = pl.BlockSpec(memory_space=pl.ANY)

    def permute(x, target):
        return lax.ppermute(x, ("row", "col"), row_major_perm(n_row, n_col, target))

    def relayout(x, m=0, target=at):
        return permute(x, lambda r, c: target((r // inner) ^ m, r % inner, c))

    def inside_permute(x, move, source=inside, target=at):
        return permute(x, lambda r, c: target(*move(*source(r, c))))

    def share(x):
        return inside_permute(x, lambda o, h, g: (o, h ^ 1, g))

    def after(x, done):
        return lax.optimization_barrier((x, done))[0]

    def to_plane(x, m):
        return inside_permute(x, lambda o, h, g: (o ^ m, h, g))

    def share_all(pieces):
        return {m: share(piece) for m, piece in pieces.items()}

    def listed(pieces, shared):
        return [pieces[m] for m in range(outer)] + [shared[m] for m in range(outer)]

    def mirror(x, target):
        moved = inside_permute(x, lambda o, h, g: (g, h, o), inside_spread, target)
        return [moved, share(moved)]

    def exchange(outs):
        return [outs[0]] + [
            inside_permute(out, lambda o, h, g, d=d: (o, h, g ^ d))
            for d, out in enumerate(outs)
            if d
        ]

    def total_of(parts):
        value = parts[0]
        for part in parts[1:]:
            value = value + part.astype(f32)
        return value.astype(bf16)

    block_shape = (blocks, side, side)
    out_shapes = tuple(
        jax.ShapeDtypeStruct(block_shape, bf16 if d else f32) for d in range(n_col)
    )
    params = pltpu.CompilerParams(vmem_limit_bytes=14 * 2**20)

    def held(count):
        return pltpu.VMEM((count, side, side), bf16)

    def dma(count):
        return pltpu.SemaphoreType.DMA((count,))

    tail_shape = jax.ShapeDtypeStruct((16, side), bf16)
    long_shape = jax.ShapeDtypeStruct((blocks * side + tail_shape.shape[0], side), bf16)
    long_sums = [
        pltpu.VMEM(block_shape, f32),
        pltpu.VMEM((n_col - 1,) + long_shape.shape, bf16),
    ]
    sums = [pltpu.VMEM(block_shape, f32), pltpu.VMEM((n_col - 1,) + block_shape, bf16)]
    cost = pl.CostEstimate(
        flops=2 * n_col * blocks * slots * side**3,
        bytes_accessed=4 * 2**20,
        transcendentals=0,
    )

    flat = lambda x: x.reshape(block_shape)
    inter, dens, kohn = flat(intersection), flat(density), flat(kohn_sham)

    far_from = range(2, outer, 2)
    near = [*far_from, 1]

    inter_near = {m: relayout(inter, m) for m in near}
    inter_early = {0: relayout(inter)} | inter_near
    step = relayout(flat(step_dir))
    dens_own = relayout(dens)
    kohn_own = relayout(after(kohn, inter_near))
    inter_far = {m + 1: to_plane(inter_near[m], 1) for m in far_from}
    dens_behind = after(dens_own, (inter_near, inter_far))
    dens_near = {m: to_plane(dens_behind, m) for m in near}
    inter_all = listed(inter_early | inter_far, share_all(inter_early) | share_all(inter_far))
    outs = pl.pallas_call(
        functools.partial(first_kernel, rows, slots, n_row, 1, first_at),
        out_shape=out_shapes,
        in_specs=[smem] + [anywhere] * (1 + n_row + 1),
        out_specs=(anywhere,) * n_col,
        scratch_shapes=[held(n_row * blocks + 1), held(blocks), *sums, dma(n_row + 1), dma(n_col)],
        compiler_params=params,
        cost_estimate=cost,
        name="scaled_step_product",
    )(tables, step, *inter_all, kohn_own)
    parts = exchange(outs)

    dens_beside = {0: share(dens_own)}
    kohn_behind = after(kohn_own, dens_near)
    kohn_pieces = {m: to_plane(kohn_behind, m) for m in far_from}
    kohn_early = list(kohn_pieces.values())
    dens_near = after(dens_near, parts[1:])
    dens_far = {m + 1: to_plane(dens_near[m], 1) for m in far_from}
    dens_beside |= share_all(dens_near) | share_all(dens_far)
    dens_all = listed({0: dens_own} | dens_near | dens_far, dens_beside)
    outs = pl.pallas_call(
        functools.partial(second_kernel, rows, slots, n_row, n_col, len(kohn_early), later_at),
        out_shape=out_shapes,
        in_specs=[smem] + [anywhere] * (n_row + n_col + len(kohn_early)),
        out_specs=(anywhere,) * n_col,
        scratch_shapes=[
            held(n_row * blocks + 1),
            held(blocks),
            *sums,
            *sums,
            dma(n_row + n_col),
            dma(n_col),
        ],
        compiler_params=params,
        cost_estimate=cost,
        name="change_product",
    )(tables, *dens_all, *parts, *kohn_early)
    second_outs = outs
    total = total_of(exchange(outs))

    mirrored = mirror(total, at)
    own = inside_permute(total, lambda o, h, g: (o, h, g), inside_spread)
    kohn_pieces = {0: kohn_own} | after(kohn_pieces, second_outs)
    kohn_beside = share_all(kohn_pieces)
    kohn_last = {m + 1: to_plane(kohn_pieces[m], 1) for m in range(0, outer, 2)}
    kohn_last = after(kohn_last, total)
    kohn_all = listed(kohn_pieces | kohn_last, kohn_beside | share_all(kohn_last))
    *outs, trace = pl.pallas_call(
        functools.partial(third_kernel, rows, slots, n_row, inner, later_at, mirror_at),
        out_shape=out_shapes[:1] + (long_shape,) * (n_col - 1) + (tail_shape,),
        in_specs=[smem] + [anywhere] * (1 + n_row + inner),
        out_specs=(anywhere,) * n_col + (vmem,),
        scratch_shapes=[
            held(n_row * blocks + 1),
            held(inner * blocks + 1),
            held(blocks),
            held(blocks),
            *long_sums,
            dma(n_row + inner + 1),
            dma(n_col),
        ],
        compiler_params=params,
        cost_estimate=cost,
        name="commutator_product",
    )(tables, own, *kohn_all, *mirrored)
    own, *parts = exchange(outs)
    total = pl.pallas_call(
        functools.partial(sum_kernel, n_col),
        out_shape=long_shape,
        in_specs=[vmem] + [anywhere] * n_col,
        out_specs=anywhere,
        scratch_shapes=[*long_sums, pltpu.VMEM(long_shape.shape, bf16), dma(n_col), dma(1)],
        compiler_params=params,
        name="plane_sum",
    )(trace, own, *parts)
    mirrored = mirror(total, at_spread)

    commutator = pl.pallas_call(
        functools.partial(last_kernel, inner, blocks, last_mirror_at),
        out_shape=jax.ShapeDtypeStruct(block_shape, bf16),
        in_specs=[smem] + [anywhere] * (1 + inner),
        out_specs=anywhere,
        scratch_shapes=[
            pltpu.VMEM(((inner * blocks + 1) * side, side), bf16),
            pltpu.VMEM((blocks * side, side), bf16),
            held(blocks),
            dma(inner + 1),
            dma(1),
        ],
        compiler_params=params,
        name="commutator_difference",
    )(tables, total, *mirrored)
    commutator = inside_permute(
        commutator, lambda o, h, g: (o, h, g), inside_spread, lambda o, h, g: (o * inner + h, g)
    )

    plane_trace = tree_sum([one_part(piece[blocks * side :]) for piece in mirrored])
    trace = tree_sum(
        [plane_trace]
        + [
            inside_permute(plane_trace, lambda o, h, g, d=d: (o, h, g ^ d))
            for d in range(1, n_col)
        ]
    )
    trace_value = trace.sum() / (blocks_total * side * side)
    return commutator.reshape(step_dir.shape), trace_value


def solution(mesh):
    in_specs = (P(),) + (P("row", "col", None, None),) * 4
    out_specs = (P("row", "col", None, None), P())
    return jax.shard_map(
        functools.partial(per_device, mesh.shape["row"], mesh.shape["col"]),
        mesh=mesh,
        in_specs=in_specs,
        out_specs=out_specs,
        check_vma=False,
    )
```

```python
import functools

import jax
import jax.numpy as jnp
from jax import lax
from jax.experimental import pallas as pl
from jax.experimental.pallas import tpu as pltpu
from jax.sharding import PartitionSpec as P

CORES = 2


def row_major_perm(n_row, n_col, target):
    pairs = []
    for r in range(n_row):
        for c in range(n_col):
            to_r, to_c = target(r, c)
            pairs.append((r * n_col + c, to_r * n_col + to_c))
    return pairs


def start_copies(pairs, sems):
    copies = [pltpu.make_async_copy(*pair, sems.at[i]) for i, pair in enumerate(pairs)]
    for copy in copies:
        copy.start()
    return copies


def wait_for(copies):
    for copy in copies:
        copy.wait()


def into(pieces, scratch, count, index=0):
    pieces = [
        piece if piece.shape[0] == count else piece.at[pl.ds(index * count, count)]
        for piece in pieces
    ]
    scratch[len(pieces) * count] = jnp.zeros(scratch.shape[1:], scratch.dtype)
    return [
        (piece, scratch.at[pl.ds(index * count, count)]) for index, piece in enumerate(pieces)
    ]


def multiply(index_ref, index_at, left_of, right, results, outs, sems, rows, slots, contract):
    copies = []
    for d in range(len(outs) - 1, -1, -1):
        for i in range(rows):
            left = left_of(i)
            for s in range(slots):
                base = index_at + ((d * rows + i) * slots + s) * slots
                blocks = jnp.concatenate(
                    [right[index_ref[base + a]] for a in range(slots)], axis=1
                )
                value = lax.dot_general(
                    blocks,
                    left,
                    (((1,), (contract,)), ((), ())),
                    preferred_element_type=jnp.float32,
                ).astype(results[d].dtype)
                if len(results[d].shape) == 3:
                    results[d][i * slots + s] = value
                else:
                    side = value.shape[0]
                    results[d][pl.ds((i * slots + s) * side, side)] = value
        copy = pltpu.make_async_copy(results[d], outs[d], sems.at[d])
        copy.start()
        copies.append(copy)
    wait_for(copies)


def split_results(first, others):
    return [first] + [others.at[d] for d in range(others.shape[0])]


def first_kernel(rows, slots, n_pieces, index_at, index_ref, left_ref, *refs):
    pieces, outs = refs[:n_pieces], refs[n_pieces:-6]
    right, left, first, others, sems, out_sems = refs[-6:]
    wait_for(start_copies(into(pieces, right, rows * slots) + [(left_ref, left)], sems))

    def left_of(i):
        return jnp.concatenate([left[i * slots + a] for a in range(slots)], axis=1)

    results = split_results(first, others)
    multiply(index_ref, index_at, left_of, right, results, outs, out_sems, rows, slots, 1)


def second_kernel(rows, slots, n_pieces, n_out, index_at, index_ref, *refs):
    pieces, parts = refs[:n_pieces], refs[n_pieces : n_pieces + n_out]
    right, left, part_first, part_others, first, others, sems, out_sems = refs[-8:]
    outs = refs[n_pieces + n_out : -8]
    held = split_results(part_first, part_others)
    wait_for(start_copies(list(zip(parts, held)) + into(pieces, right, rows * slots), sems))
    for b in range(rows * slots):
        value = held[0][b]
        for part in held[1:]:
            value = value + part[b].astype(jnp.float32)
        left[b] = value.astype(jnp.bfloat16)

    def left_of(i):
        return jnp.concatenate([left[i * slots + a] for a in range(slots)], axis=0)

    results = split_results(first, others)
    multiply(index_ref, index_at, left_of, right, results, outs, out_sems, rows, slots, 0)


def two_parts(x):
    high = x.astype(jnp.bfloat16)
    low = (x - high.astype(jnp.float32)).astype(jnp.bfloat16)
    return jnp.concatenate([high, low], axis=0)


def one_part(x):
    x = x.astype(jnp.float32)
    half = x.shape[0] // 2
    return x[:half] + x[half:]


def tree_sum(values):
    while len(values) > 1:
        values = [values[i] + values[i + 1] for i in range(0, len(values), 2)]
    return values[0]


def third_kernel(rows, slots, n_pieces, n_mirror, index_at, mirror_at, index_ref, own_ref, *refs):
    pieces, mirrored = refs[:n_pieces], refs[n_pieces : n_pieces + n_mirror]
    *outs, trace = refs[n_pieces + n_mirror : -8]
    right, mirror, own, left, first, others, sems, out_sems = refs[-8:]
    pairs = into(pieces, right, rows * slots, 1) + into(mirrored, mirror, rows * slots)
    pairs.append((own_ref, own))
    wait_for(start_copies(pairs, sems))
    blocks, side = rows * slots, right.shape[1]
    part_rows = trace.shape[0] // 2
    total_trace = jnp.zeros((part_rows, side), jnp.float32)
    for b in range(blocks):
        other = mirror[index_ref[mirror_at + b]].astype(jnp.float32).T
        value = (-(own[b].astype(jnp.float32) + other)).astype(jnp.bfloat16)
        left[b] = value
        product = value.astype(jnp.float32) * right[b].astype(jnp.float32).T
        total_trace = total_trace + product.reshape(-1, part_rows, side).sum(0)
    total_trace = two_parts(total_trace)
    trace[...] = total_trace
    results = split_results(first, others)
    for result in results[1:]:
        result[pl.ds(blocks * side, 2 * part_rows)] = total_trace

    def left_of(i):
        return jnp.concatenate([left[i * slots + a] for a in range(slots)], axis=0)

    multiply(index_ref, index_at, left_of, right, results, outs, out_sems, rows, slots, 0)


def sum_kernel(n_out, trace_ref, own_ref, *refs):
    parts, (out, own, others, result, sems, out_sems) = refs[: n_out - 1], refs[n_out - 1 :]
    pairs = [(part, others.at[d]) for d, part in enumerate(parts)]
    wait_for(start_copies([(own_ref, own)] + pairs, sems))
    blocks, side = own.shape[:2]
    for b in range(blocks):
        value = own[b]
        for d in range(n_out - 1):
            value = value + others[d, pl.ds(b * side, side)].astype(jnp.float32)
        result[pl.ds(b * side, side)] = value.astype(result.dtype)
    tail = pl.ds(blocks * side, trace_ref.shape[0])
    tiles = [trace_ref[...]] + [others[d, tail] for d in range(n_out - 1)]
    result[tail] = two_parts(tree_sum([one_part(tile) for tile in tiles]))
    wait_for(start_copies([(result, out)], out_sems))


def last_kernel(n_mirror, blocks, mirror_at, index_ref, own_ref, *refs):
    mirrored, (out, mirror, own, result, sems, out_sems) = refs[:n_mirror], refs[n_mirror:]
    side = own.shape[1]
    count = blocks * side
    body = pl.ds(0, count)
    pairs = [(own_ref.at[body], own)] + [
        (piece.at[body], mirror.at[pl.ds(t * count, count)]) for t, piece in enumerate(mirrored)
    ]
    copies = start_copies(pairs, sems)
    mirror[pl.ds(n_mirror * count, side)] = jnp.zeros((side, side), mirror.dtype)
    wait_for(copies)
    for b in range(blocks):
        start = pl.multiple_of(index_ref[mirror_at + b] * side, side)
        other = mirror[pl.ds(start, side)].astype(jnp.float32)
        value = other - own[pl.ds(b * side, side)].astype(jnp.float32).T
        result[b] = value.astype(result.dtype)
    wait_for(start_copies([(result, out)], out_sems))


def per_device(n_row, n_col, block_cols, step_dir, intersection, density, kohn_sham):
    rows, slots, side = step_dir.shape[:3]
    blocks = rows * slots
    blocks_total = block_cols.shape[0]
    inner = n_row // n_col
    outer = n_row // inner
    assert inner == CORES and outer == n_col and outer & (outer - 1) == 0
    row_index = lax.axis_index("row")
    col_index = lax.axis_index("col")
    bf16, f32 = jnp.bfloat16, jnp.float32

    def at(o, h, g):
        return o * inner + g % inner, (g // inner) * CORES + h

    def inside(r, c):
        return r // inner, c % CORES, (c // CORES) * inner + r % inner

    def spread(o, g):
        bits = (n_col - 1).bit_length()
        return g ^ sum(((o >> b) & 1) << (bits - 1 - b) for b in range(bits))

    def at_spread(o, h, g):
        return at(o, h, spread(o, g))

    def inside_spread(r, c):
        o, h, p = inside(r, c)
        return o, h, spread(o, p)

    o_in, h_in, g_in = inside(row_index, col_index)

    by_group = block_cols.reshape(blocks_total, n_col, slots)
    mirror_cols = lax.dynamic_slice_in_dim(by_group, o_in, 1, 1)[:, 0]

    def rows_of(o, h):
        return lax.dynamic_slice_in_dim(by_group, (o * inner + h) * rows, rows, 0)

    def group_cols_of(cols, g):
        return lax.dynamic_slice_in_dim(cols, g, 1, 1)[:, 0]

    own_rows = rows_of(o_in, h_in)

    def index_table(group, first_out):
        own_cols, group_cols = group_cols_of(own_rows, group), group_cols_of(by_group, group)
        wanted = own_rows[:, first_out ^ jnp.arange(n_col)].transpose(1, 0, 2)
        safe = jnp.clip(wanted, 0, blocks_total - 1)
        matched = (
            (group_cols[safe][..., None, :] == own_cols[None, :, None, :, None])
            & (wanted >= 0)[..., None, None]
            & (own_cols >= 0)[None, :, None, :, None]
        )
        piece = ((safe // rows % inner) ^ h_in) * outer + (safe // rows // inner ^ o_in)
        slot = ((piece * rows + safe % rows) * slots)[..., None] + jnp.argmax(matched, axis=-1)
        return jnp.where(matched.any(-1), slot, n_row * blocks).astype(jnp.int32).reshape(-1)

    spread_in = spread(o_in, g_in)
    all_tables = [index_table(g_in, g_in), index_table(g_in, spread_in)]

    def mirror_table(h, cols):
        own_ids = (o_in * inner + h) * rows + jnp.arange(rows)
        safe_own = jnp.clip(cols, 0, blocks_total - 1)
        found = mirror_cols[safe_own] == own_ids[:, None, None]
        source = (safe_own // rows % inner) ^ h
        return jnp.where(
            cols >= 0,
            (source * rows + safe_own % rows) * slots + jnp.argmax(found, axis=-1),
            inner * blocks,
        ).astype(jnp.int32).reshape(-1)

    all_tables += [mirror_table(h_in, group_cols_of(own_rows, g)) for g in (g_in, spread_in)]
    starts = [sum(table.size for table in all_tables[:t]) for t in range(len(all_tables))]
    first_at, later_at, mirror_at, last_mirror_at = starts
    tables = jnp.concatenate(all_tables)

    smem = pl.BlockSpec(memory_space=pltpu.SMEM)
    vmem = pl.BlockSpec(memory_space=pltpu.VMEM)
    anywhere = pl.BlockSpec(memory_space=pl.ANY)

    def permute(x, target):
        return lax.ppermute(x, ("row", "col"), row_major_perm(n_row, n_col, target))

    def relayout(x, m=0, target=at):
        return permute(x, lambda r, c: target((r // inner) ^ m, r % inner, c))

    def inside_permute(x, move, source=inside, target=at):
        return permute(x, lambda r, c: target(*move(*source(r, c))))

    def share(x):
        return inside_permute(x, lambda o, h, g: (o, h ^ 1, g))

    def after(x, done):
        return lax.optimization_barrier((x, done))[0]

    def to_plane(x, m):
        return inside_permute(x, lambda o, h, g: (o ^ m, h, g))

    def share_all(pieces):
        return {m: share(piece) for m, piece in pieces.items()}

    def listed(pieces, shared):
        return [pieces[m] for m in range(outer)] + [shared[m] for m in range(outer)]

    def mirror(x, target):
        moved = inside_permute(x, lambda o, h, g: (g, h, o), inside_spread, target)
        return [moved, share(moved)]

    def exchange(outs):
        return [outs[0]] + [
            inside_permute(out, lambda o, h, g, d=d: (o, h, g ^ d))
            for d, out in enumerate(outs)
            if d
        ]

    def total_of(parts):
        value = parts[0]
        for part in parts[1:]:
            value = value + part.astype(f32)
        return value.astype(bf16)

    block_shape = (blocks, side, side)
    out_shapes = tuple(
        jax.ShapeDtypeStruct(block_shape, bf16 if d else f32) for d in range(n_col)
    )
    params = pltpu.CompilerParams(vmem_limit_bytes=14 * 2**20)

    def held(count):
        return pltpu.VMEM((count, side, side), bf16)

    def dma(count):
        return pltpu.SemaphoreType.DMA((count,))

    tail_shape = jax.ShapeDtypeStruct((16, side), bf16)
    long_shape = jax.ShapeDtypeStruct((blocks * side + tail_shape.shape[0], side), bf16)
    long_sums = [
        pltpu.VMEM(block_shape, f32),
        pltpu.VMEM((n_col - 1,) + long_shape.shape, bf16),
    ]
    sums = [pltpu.VMEM(block_shape, f32), pltpu.VMEM((n_col - 1,) + block_shape, bf16)]
    cost = pl.CostEstimate(
        flops=2 * n_col * blocks * slots * side**3,
        bytes_accessed=4 * 2**20,
        transcendentals=0,
    )

    flat = lambda x: x.reshape(block_shape)
    inter, dens, kohn = flat(intersection), flat(density), flat(kohn_sham)

    far_from = range(2, outer, 2)
    near = [*far_from, 1]

    inter_near = {m: relayout(inter, m) for m in near}
    inter_early = {0: relayout(inter)} | inter_near
    step = relayout(flat(step_dir))
    both_own = relayout(jnp.concatenate([dens, kohn]))
    inter_far = {m + 1: to_plane(inter_near[m], 1) for m in far_from}
    both_behind = after(both_own, (inter_near, inter_far))
    both_pieces = {m: to_plane(both_behind, m) for m in near}
    inter_all = listed(inter_early | inter_far, share_all(inter_early) | share_all(inter_far))
    outs = pl.pallas_call(
        functools.partial(first_kernel, rows, slots, n_row, first_at),
        out_shape=out_shapes,
        in_specs=[smem] + [anywhere] * (1 + n_row),
        out_specs=(anywhere,) * n_col,
        scratch_shapes=[held(n_row * blocks + 1), held(blocks), *sums, dma(n_row + 1), dma(n_col)],
        compiler_params=params,
        cost_estimate=cost,
        name="scaled_step_product",
    )(tables, step, *inter_all)
    parts = exchange(outs)

    both_beside = {0: share(both_own)}
    both_pieces = after(both_pieces, parts[1:])
    both_beside |= share_all(both_pieces)
    both_pieces |= {0: both_own}
    dens_far = {m + 1: to_plane(both_pieces[m][:blocks], 1) for m in far_from}
    dens_all = listed(both_pieces | dens_far, both_beside | share_all(dens_far))
    outs = pl.pallas_call(
        functools.partial(second_kernel, rows, slots, n_row, n_col, later_at),
        out_shape=out_shapes,
        in_specs=[smem] + [anywhere] * (n_row + n_col),
        out_specs=(anywhere,) * n_col,
        scratch_shapes=[
            held(n_row * blocks + 1),
            held(blocks),
            *sums,
            *sums,
            dma(n_row + n_col),
            dma(n_col),
        ],
        compiler_params=params,
        cost_estimate=cost,
        name="change_product",
    )(tables, *dens_all, *parts)
    second_outs = outs
    total = total_of(exchange(outs))

    mirrored = mirror(total, at)
    own = inside_permute(total, lambda o, h, g: (o, h, g), inside_spread)
    kohn_far = {
        m + 1: to_plane(after(both_pieces[m][blocks:], second_outs), 1) for m in far_from
    }
    kohn_all = listed(both_pieces | kohn_far, both_beside | share_all(kohn_far))
    *outs, trace = pl.pallas_call(
        functools.partial(third_kernel, rows, slots, n_row, inner, later_at, mirror_at),
        out_shape=out_shapes[:1] + (long_shape,) * (n_col - 1) + (tail_shape,),
        in_specs=[smem] + [anywhere] * (1 + n_row + inner),
        out_specs=(anywhere,) * n_col + (vmem,),
        scratch_shapes=[
            held(n_row * blocks + 1),
            held(inner * blocks + 1),
            held(blocks),
            held(blocks),
            *long_sums,
            dma(n_row + inner + 1),
            dma(n_col),
        ],
        compiler_params=params,
        cost_estimate=cost,
        name="commutator_product",
    )(tables, own, *kohn_all, *mirrored)
    own, *parts = exchange(outs)
    total = pl.pallas_call(
        functools.partial(sum_kernel, n_col),
        out_shape=long_shape,
        in_specs=[vmem] + [anywhere] * n_col,
        out_specs=anywhere,
        scratch_shapes=[*long_sums, pltpu.VMEM(long_shape.shape, bf16), dma(n_col), dma(1)],
        compiler_params=params,
        name="plane_sum",
    )(trace, own, *parts)
    mirrored = mirror(total, at_spread)

    commutator = pl.pallas_call(
        functools.partial(last_kernel, inner, blocks, last_mirror_at),
        out_shape=jax.ShapeDtypeStruct(block_shape, bf16),
        in_specs=[smem] + [anywhere] * (1 + inner),
        out_specs=anywhere,
        scratch_shapes=[
            pltpu.VMEM(((inner * blocks + 1) * side, side), bf16),
            pltpu.VMEM((blocks * side, side), bf16),
            held(blocks),
            dma(inner + 1),
            dma(1),
        ],
        compiler_params=params,
        name="commutator_difference",
    )(tables, total, *mirrored)
    commutator = inside_permute(
        commutator, lambda o, h, g: (o, h, g), inside_spread, lambda o, h, g: (o * inner + h, g)
    )

    plane_trace = tree_sum([one_part(piece[blocks * side :]) for piece in mirrored])
    trace = tree_sum(
        [plane_trace]
        + [
            inside_permute(plane_trace, lambda o, h, g, d=d: (o, h, g ^ d))
            for d in range(1, n_col)
        ]
    )
    trace_value = trace.sum() / (blocks_total * side * side)
    return commutator.reshape(step_dir.shape), trace_value


def solution(mesh):
    in_specs = (P(),) + (P("row", "col", None, None),) * 4
    out_specs = (P("row", "col", None, None), P())
    return jax.shard_map(
        functools.partial(per_device, mesh.shape["row"], mesh.shape["col"]),
        mesh=mesh,
        in_specs=in_specs,
        out_specs=out_specs,
        check_vma=False,
    )
```

```python
import functools

import jax
import jax.numpy as jnp
from jax import lax
from jax.experimental import pallas as pl
from jax.experimental.pallas import tpu as pltpu
from jax.sharding import PartitionSpec as P

CORES = 2


def row_major_perm(n_row, n_col, target):
    pairs = []
    for r in range(n_row):
        for c in range(n_col):
            to_r, to_c = target(r, c)
            pairs.append((r * n_col + c, to_r * n_col + to_c))
    return pairs


def start_copies(pairs, sems):
    copies = [pltpu.make_async_copy(*pair, sems.at[i]) for i, pair in enumerate(pairs)]
    for copy in copies:
        copy.start()
    return copies


def wait_for(copies):
    for copy in copies:
        copy.wait()


def into(pieces, scratch, count):
    scratch[len(pieces) * count] = jnp.zeros(scratch.shape[1:], scratch.dtype)
    return [
        (piece, scratch.at[pl.ds(index * count, count)]) for index, piece in enumerate(pieces)
    ]


def multiply(index_ref, index_at, left_of, right, results, outs, sems, rows, slots, contract):
    copies = []
    for d in range(len(outs) - 1, -1, -1):
        for i in range(rows):
            left = left_of(i)
            for s in range(slots):
                base = index_at + ((d * rows + i) * slots + s) * slots
                blocks = jnp.concatenate(
                    [right[index_ref[base + a]] for a in range(slots)], axis=1
                )
                value = lax.dot_general(
                    blocks,
                    left,
                    (((1,), (contract,)), ((), ())),
                    preferred_element_type=jnp.float32,
                ).astype(results[d].dtype)
                if len(results[d].shape) == 3:
                    results[d][i * slots + s] = value
                else:
                    side = value.shape[0]
                    results[d][pl.ds((i * slots + s) * side, side)] = value
        copy = pltpu.make_async_copy(results[d], outs[d], sems.at[d])
        copy.start()
        copies.append(copy)
    wait_for(copies)


def split_results(first, others):
    return [first] + [others.at[d] for d in range(others.shape[0])]


def first_kernel(rows, slots, n_pieces, n_early, index_at, index_ref, left_ref, *refs):
    pieces, outs = refs[:n_pieces], refs[n_pieces + n_early : -6]
    right, left, first, others, sems, out_sems = refs[-6:]
    wait_for(start_copies(into(pieces, right, rows * slots) + [(left_ref, left)], sems))

    def left_of(i):
        return jnp.concatenate([left[i * slots + a] for a in range(slots)], axis=1)

    results = split_results(first, others)
    multiply(index_ref, index_at, left_of, right, results, outs, out_sems, rows, slots, 1)


def second_kernel(rows, slots, n_pieces, n_out, n_early, index_at, index_ref, *refs):
    pieces, parts = refs[:n_pieces], refs[n_pieces : n_pieces + n_out]
    right, left, part_first, part_others, first, others, sems, out_sems = refs[-8:]
    outs = refs[n_pieces + n_out + n_early : -8]
    held = split_results(part_first, part_others)
    wait_for(start_copies(list(zip(parts, held)) + into(pieces, right, rows * slots), sems))
    for b in range(rows * slots):
        value = held[0][b]
        for part in held[1:]:
            value = value + part[b].astype(jnp.float32)
        left[b] = value.astype(jnp.bfloat16)

    def left_of(i):
        return jnp.concatenate([left[i * slots + a] for a in range(slots)], axis=0)

    results = split_results(first, others)
    multiply(index_ref, index_at, left_of, right, results, outs, out_sems, rows, slots, 0)


def two_parts(x):
    high = x.astype(jnp.bfloat16)
    low = (x - high.astype(jnp.float32)).astype(jnp.bfloat16)
    return jnp.concatenate([high, low], axis=0)


def one_part(x):
    x = x.astype(jnp.float32)
    half = x.shape[0] // 2
    return x[:half] + x[half:]


def tree_sum(values):
    while len(values) > 1:
        values = [values[i] + values[i + 1] for i in range(0, len(values), 2)]
    return values[0]


def third_kernel(rows, slots, n_pieces, n_mirror, index_at, mirror_at, index_ref, own_ref, *refs):
    pieces, mirrored = refs[:n_pieces], refs[n_pieces : n_pieces + n_mirror]
    *outs, trace = refs[n_pieces + n_mirror : -8]
    right, mirror, own, left, first, others, sems, out_sems = refs[-8:]
    pairs = into(pieces, right, rows * slots) + into(mirrored, mirror, rows * slots) + [(own_ref, own)]
    wait_for(start_copies(pairs, sems))
    blocks, side = rows * slots, right.shape[1]
    part_rows = trace.shape[0] // 2
    total_trace = jnp.zeros((part_rows, side), jnp.float32)
    for b in range(blocks):
        other = mirror[index_ref[mirror_at + b]].astype(jnp.float32).T
        value = (-(own[b].astype(jnp.float32) + other)).astype(jnp.bfloat16)
        left[b] = value
        product = value.astype(jnp.float32) * right[b].astype(jnp.float32).T
        total_trace = total_trace + product.reshape(-1, part_rows, side).sum(0)
    total_trace = two_parts(total_trace)
    trace[...] = total_trace
    results = split_results(first, others)
    for result in results[1:]:
        result[pl.ds(blocks * side, 2 * part_rows)] = total_trace

    def left_of(i):
        return jnp.concatenate([left[i * slots + a] for a in range(slots)], axis=0)

    multiply(index_ref, index_at, left_of, right, results, outs, out_sems, rows, slots, 0)


def sum_kernel(n_out, trace_ref, own_ref, *refs):
    parts, (out, own, others, result, sems, out_sems) = refs[: n_out - 1], refs[n_out - 1 :]
    pairs = [(part, others.at[d]) for d, part in enumerate(parts)]
    wait_for(start_copies([(own_ref, own)] + pairs, sems))
    blocks, side = own.shape[:2]
    for b in range(blocks):
        value = own[b]
        for d in range(n_out - 1):
            value = value + others[d, pl.ds(b * side, side)].astype(jnp.float32)
        result[pl.ds(b * side, side)] = value.astype(result.dtype)
    tail = pl.ds(blocks * side, trace_ref.shape[0])
    tiles = [trace_ref[...]] + [others[d, tail] for d in range(n_out - 1)]
    result[tail] = two_parts(tree_sum([one_part(tile) for tile in tiles]))
    wait_for(start_copies([(result, out)], out_sems))


def last_kernel(n_mirror, blocks, mirror_at, index_ref, own_ref, *refs):
    mirrored, (out, mirror, own, result, sems, out_sems) = refs[:n_mirror], refs[n_mirror:]
    side = own.shape[1]
    count = blocks * side
    body = pl.ds(0, count)
    pairs = [(own_ref.at[body], own)] + [
        (piece.at[body], mirror.at[pl.ds(t * count, count)]) for t, piece in enumerate(mirrored)
    ]
    copies = start_copies(pairs, sems)
    mirror[pl.ds(n_mirror * count, side)] = jnp.zeros((side, side), mirror.dtype)
    wait_for(copies)
    for b in range(blocks):
        start = pl.multiple_of(index_ref[mirror_at + b] * side, side)
        other = mirror[pl.ds(start, side)].astype(jnp.float32)
        value = other - own[pl.ds(b * side, side)].astype(jnp.float32).T
        result[b] = value.astype(result.dtype)
    wait_for(start_copies([(result, out)], out_sems))


def per_device(n_row, n_col, block_cols, step_dir, intersection, density, kohn_sham):
    rows, slots, side = step_dir.shape[:3]
    blocks = rows * slots
    blocks_total = block_cols.shape[0]
    inner = n_row // n_col
    outer = n_row // inner
    assert inner == CORES and outer == n_col and outer & (outer - 1) == 0
    row_index = lax.axis_index("row")
    col_index = lax.axis_index("col")
    bf16, f32 = jnp.bfloat16, jnp.float32

    def at(o, h, g):
        return o * inner + g % inner, (g // inner) * CORES + h

    def inside(r, c):
        return r // inner, c % CORES, (c // CORES) * inner + r % inner

    def spread(o, g):
        bits = (n_col - 1).bit_length()
        return g ^ sum(((o >> b) & 1) << (bits - 1 - b) for b in range(bits))

    def at_spread(o, h, g):
        return at(o, h, spread(o, g))

    def inside_spread(r, c):
        o, h, p = inside(r, c)
        return o, h, spread(o, p)

    o_in, h_in, g_in = inside(row_index, col_index)

    by_group = block_cols.reshape(blocks_total, n_col, slots)
    mirror_cols = lax.dynamic_slice_in_dim(by_group, o_in, 1, 1)[:, 0]

    def rows_of(o, h):
        return lax.dynamic_slice_in_dim(by_group, (o * inner + h) * rows, rows, 0)

    def group_cols_of(cols, g):
        return lax.dynamic_slice_in_dim(cols, g, 1, 1)[:, 0]

    own_rows = rows_of(o_in, h_in)

    def index_table(group, first_out):
        own_cols, group_cols = group_cols_of(own_rows, group), group_cols_of(by_group, group)
        wanted = own_rows[:, first_out ^ jnp.arange(n_col)].transpose(1, 0, 2)
        safe = jnp.clip(wanted, 0, blocks_total - 1)
        matched = (
            (group_cols[safe][..., None, :] == own_cols[None, :, None, :, None])
            & (wanted >= 0)[..., None, None]
            & (own_cols >= 0)[None, :, None, :, None]
        )
        piece = ((safe // rows % inner) ^ h_in) * outer + (safe // rows // inner ^ o_in)
        slot = ((piece * rows + safe % rows) * slots)[..., None] + jnp.argmax(matched, axis=-1)
        return jnp.where(matched.any(-1), slot, n_row * blocks).astype(jnp.int32).reshape(-1)

    spread_in = spread(o_in, g_in)
    all_tables = [index_table(g_in, g_in), index_table(g_in, spread_in)]

    def mirror_table(h, cols):
        own_ids = (o_in * inner + h) * rows + jnp.arange(rows)
        safe_own = jnp.clip(cols, 0, blocks_total - 1)
        found = mirror_cols[safe_own] == own_ids[:, None, None]
        source = (safe_own // rows % inner) ^ h
        return jnp.where(
            cols >= 0,
            (source * rows + safe_own % rows) * slots + jnp.argmax(found, axis=-1),
            inner * blocks,
        ).astype(jnp.int32).reshape(-1)

    all_tables += [mirror_table(h_in, group_cols_of(own_rows, g)) for g in (g_in, spread_in)]
    starts = [sum(table.size for table in all_tables[:t]) for t in range(len(all_tables))]
    first_at, later_at, mirror_at, last_mirror_at = starts
    tables = jnp.concatenate(all_tables)

    smem = pl.BlockSpec(memory_space=pltpu.SMEM)
    vmem = pl.BlockSpec(memory_space=pltpu.VMEM)
    anywhere = pl.BlockSpec(memory_space=pl.ANY)

    def permute(x, target):
        return lax.ppermute(x, ("row", "col"), row_major_perm(n_row, n_col, target))

    def relayout(x, m=0, target=at):
        return permute(x, lambda r, c: target((r // inner) ^ m, r % inner, c))

    def inside_permute(x, move, source=inside, target=at):
        return permute(x, lambda r, c: target(*move(*source(r, c))))

    def share(x):
        return inside_permute(x, lambda o, h, g: (o, h ^ 1, g))

    def after(x, done):
        return lax.optimization_barrier((x, done))[0]

    def to_plane(x, m):
        return inside_permute(x, lambda o, h, g: (o ^ m, h, g))

    def share_all(pieces):
        return {m: share(piece) for m, piece in pieces.items()}

    def listed(pieces, shared):
        return [pieces[m] for m in range(outer)] + [shared[m] for m in range(outer)]

    def mirror(x, target):
        moved = inside_permute(x, lambda o, h, g: (g, h, o), inside_spread, target)
        return [moved, share(moved)]

    def exchange(outs):
        return [outs[0]] + [
            inside_permute(out, lambda o, h, g, d=d: (o, h, g ^ d))
            for d, out in enumerate(outs)
            if d
        ]

    def total_of(parts):
        value = parts[0]
        for part in parts[1:]:
            value = value + part.astype(f32)
        return value.astype(bf16)

    block_shape = (blocks, side, side)
    out_shapes = tuple(
        jax.ShapeDtypeStruct(block_shape, bf16 if d else f32) for d in range(n_col)
    )
    params = pltpu.CompilerParams(vmem_limit_bytes=14 * 2**20)

    def held(count):
        return pltpu.VMEM((count, side, side), bf16)

    def dma(count):
        return pltpu.SemaphoreType.DMA((count,))

    tail_shape = jax.ShapeDtypeStruct((16, side), bf16)
    long_shape = jax.ShapeDtypeStruct((blocks * side + tail_shape.shape[0], side), bf16)
    long_sums = [
        pltpu.VMEM(block_shape, f32),
        pltpu.VMEM((n_col - 1,) + long_shape.shape, bf16),
    ]
    sums = [pltpu.VMEM(block_shape, f32), pltpu.VMEM((n_col - 1,) + block_shape, bf16)]
    cost = pl.CostEstimate(
        flops=2 * n_col * blocks * slots * side**3,
        bytes_accessed=4 * 2**20,
        transcendentals=0,
    )

    flat = lambda x: x.reshape(block_shape)
    inter, dens, kohn = flat(intersection), flat(density), flat(kohn_sham)

    far_from = range(2, outer, 2)
    near = [*far_from, 1]

    inter_near = {m: relayout(inter, m) for m in near}
    inter_early = {0: relayout(inter)} | inter_near
    step = relayout(flat(step_dir))
    dens_own = relayout(dens)
    kohn_own = relayout(after(kohn, inter_near))
    inter_far = {m + 1: to_plane(inter_near[m], 1) for m in far_from}
    dens_behind = after(dens_own, inter_near)
    dens_near = {m: to_plane(dens_behind, m) for m in near}
    inter_all = listed(inter_early | inter_far, share_all(inter_early) | share_all(inter_far))
    outs = pl.pallas_call(
        functools.partial(first_kernel, rows, slots, n_row, 1, first_at),
        out_shape=out_shapes,
        in_specs=[smem] + [anywhere] * (1 + n_row + 1),
        out_specs=(anywhere,) * n_col,
        scratch_shapes=[held(n_row * blocks + 1), held(blocks), *sums, dma(n_row + 1), dma(n_col)],
        compiler_params=params,
        cost_estimate=cost,
        name="scaled_step_product",
    )(tables, step, *inter_all, kohn_own)
    parts = exchange(outs)

    dens_beside = {0: share(dens_own)}
    dens_near = after(dens_near, outs)
    dens_far = {m + 1: to_plane(dens_near[m], 1) for m in far_from}
    kohn_behind = after(kohn_own, (dens_near, outs))
    kohn_pieces = {m: to_plane(kohn_behind, m) for m in far_from}
    kohn_early = list(kohn_pieces.values())
    dens_near, dens_far = after((dens_near, dens_far), parts[1:])
    dens_beside |= share_all(dens_near) | share_all(dens_far)
    dens_all = listed({0: dens_own} | dens_near | dens_far, dens_beside)
    outs = pl.pallas_call(
        functools.partial(second_kernel, rows, slots, n_row, n_col, len(kohn_early), later_at),
        out_shape=out_shapes,
        in_specs=[smem] + [anywhere] * (n_row + n_col + len(kohn_early)),
        out_specs=(anywhere,) * n_col,
        scratch_shapes=[
            held(n_row * blocks + 1),
            held(blocks),
            *sums,
            *sums,
            dma(n_row + n_col),
            dma(n_col),
        ],
        compiler_params=params,
        cost_estimate=cost,
        name="change_product",
    )(tables, *dens_all, *parts, *kohn_early)
    second_outs = outs
    total = total_of(exchange(outs))

    mirrored = mirror(total, at)
    own = inside_permute(total, lambda o, h, g: (o, h, g), inside_spread)
    kohn_pieces = {0: kohn_own} | after(kohn_pieces, second_outs)
    kohn_beside = share_all(kohn_pieces)
    kohn_last = {m + 1: to_plane(kohn_pieces[m], 1) for m in range(0, outer, 2)}
    kohn_last = after(kohn_last, total)
    kohn_all = listed(kohn_pieces | kohn_last, kohn_beside | share_all(kohn_last))
    *outs, trace = pl.pallas_call(
        functools.partial(third_kernel, rows, slots, n_row, inner, later_at, mirror_at),
        out_shape=out_shapes[:1] + (long_shape,) * (n_col - 1) + (tail_shape,),
        in_specs=[smem] + [anywhere] * (1 + n_row + inner),
        out_specs=(anywhere,) * n_col + (vmem,),
        scratch_shapes=[
            held(n_row * blocks + 1),
            held(inner * blocks + 1),
            held(blocks),
            held(blocks),
            *long_sums,
            dma(n_row + inner + 1),
            dma(n_col),
        ],
        compiler_params=params,
        cost_estimate=cost,
        name="commutator_product",
    )(tables, own, *kohn_all, *mirrored)
    own, *parts = exchange(outs)
    total = pl.pallas_call(
        functools.partial(sum_kernel, n_col),
        out_shape=long_shape,
        in_specs=[vmem] + [anywhere] * n_col,
        out_specs=anywhere,
        scratch_shapes=[*long_sums, pltpu.VMEM(long_shape.shape, bf16), dma(n_col), dma(1)],
        compiler_params=params,
        name="plane_sum",
    )(trace, own, *parts)
    mirrored = mirror(total, at_spread)

    commutator = pl.pallas_call(
        functools.partial(last_kernel, inner, blocks, last_mirror_at),
        out_shape=jax.ShapeDtypeStruct(block_shape, bf16),
        in_specs=[smem] + [anywhere] * (1 + inner),
        out_specs=anywhere,
        scratch_shapes=[
            pltpu.VMEM(((inner * blocks + 1) * side, side), bf16),
            pltpu.VMEM((blocks * side, side), bf16),
            held(blocks),
            dma(inner + 1),
            dma(1),
        ],
        compiler_params=params,
        name="commutator_difference",
    )(tables, total, *mirrored)
    commutator = inside_permute(
        commutator, lambda o, h, g: (o, h, g), inside_spread, lambda o, h, g: (o * inner + h, g)
    )

    plane_trace = tree_sum([one_part(piece[blocks * side :]) for piece in mirrored])
    trace = tree_sum(
        [plane_trace]
        + [
            inside_permute(plane_trace, lambda o, h, g, d=d: (o, h, g ^ d))
            for d in range(1, n_col)
        ]
    )
    trace_value = trace.sum() / (blocks_total * side * side)
    return commutator.reshape(step_dir.shape), trace_value


def solution(mesh):
    in_specs = (P(),) + (P("row", "col", None, None),) * 4
    out_specs = (P("row", "col", None, None), P())
    return jax.shard_map(
        functools.partial(per_device, mesh.shape["row"], mesh.shape["col"]),
        mesh=mesh,
        in_specs=in_specs,
        out_specs=out_specs,
        check_vma=False,
    )
```

```python
import functools

import jax
import jax.numpy as jnp
from jax import lax
from jax.experimental import pallas as pl
from jax.experimental.pallas import tpu as pltpu
from jax.sharding import PartitionSpec as P

CORES = 2


def row_major_perm(n_row, n_col, target):
    pairs = []
    for r in range(n_row):
        for c in range(n_col):
            to_r, to_c = target(r, c)
            pairs.append((r * n_col + c, to_r * n_col + to_c))
    return pairs


def start_copies(pairs, sems):
    copies = [pltpu.make_async_copy(*pair, sems.at[i]) for i, pair in enumerate(pairs)]
    for copy in copies:
        copy.start()
    return copies


def wait_for(copies):
    for copy in copies:
        copy.wait()


def into(pieces, scratch, count):
    scratch[len(pieces) * count] = jnp.zeros(scratch.shape[1:], scratch.dtype)
    return [
        (piece, scratch.at[pl.ds(index * count, count)]) for index, piece in enumerate(pieces)
    ]


def multiply(index_ref, index_at, left_of, right, results, outs, sems, rows, slots, contract):
    copies = []
    for d in range(len(outs) - 1, -1, -1):
        for i in range(rows):
            left = left_of(i)
            for s in range(slots):
                base = index_at + ((d * rows + i) * slots + s) * slots
                blocks = jnp.concatenate(
                    [right[index_ref[base + a]] for a in range(slots)], axis=1
                )
                value = lax.dot_general(
                    blocks,
                    left,
                    (((1,), (contract,)), ((), ())),
                    preferred_element_type=jnp.float32,
                ).astype(results[d].dtype)
                if len(results[d].shape) == 3:
                    results[d][i * slots + s] = value
                else:
                    side = value.shape[0]
                    results[d][pl.ds((i * slots + s) * side, side)] = value
        copy = pltpu.make_async_copy(results[d], outs[d], sems.at[d])
        copy.start()
        copies.append(copy)
    wait_for(copies)


def split_results(first, others):
    return [first] + [others.at[d] for d in range(others.shape[0])]


def first_kernel(rows, slots, n_pieces, n_early, index_at, index_ref, left_ref, *refs):
    pieces, outs = refs[:n_pieces], refs[n_pieces + n_early : -6]
    right, left, first, others, sems, out_sems = refs[-6:]
    wait_for(start_copies(into(pieces, right, rows * slots) + [(left_ref, left)], sems))

    def left_of(i):
        return jnp.concatenate([left[i * slots + a] for a in range(slots)], axis=1)

    results = split_results(first, others)
    multiply(index_ref, index_at, left_of, right, results, outs, out_sems, rows, slots, 1)


def second_kernel(rows, slots, n_pieces, n_out, n_early, index_at, index_ref, *refs):
    pieces, parts = refs[:n_pieces], refs[n_pieces : n_pieces + n_out]
    right, left, part_first, part_others, first, others, sems, out_sems = refs[-8:]
    outs = refs[n_pieces + n_out + n_early : -8]
    held = split_results(part_first, part_others)
    wait_for(start_copies(list(zip(parts, held)) + into(pieces, right, rows * slots), sems))
    for b in range(rows * slots):
        value = held[0][b]
        for part in held[1:]:
            value = value + part[b].astype(jnp.float32)
        left[b] = value.astype(jnp.bfloat16)

    def left_of(i):
        return jnp.concatenate([left[i * slots + a] for a in range(slots)], axis=0)

    results = split_results(first, others)
    multiply(index_ref, index_at, left_of, right, results, outs, out_sems, rows, slots, 0)


def two_parts(x):
    high = x.astype(jnp.bfloat16)
    low = (x - high.astype(jnp.float32)).astype(jnp.bfloat16)
    return jnp.concatenate([high, low], axis=0)


def one_part(x):
    x = x.astype(jnp.float32)
    half = x.shape[0] // 2
    return x[:half] + x[half:]


def tree_sum(values):
    while len(values) > 1:
        values = [values[i] + values[i + 1] for i in range(0, len(values), 2)]
    return values[0]


def third_kernel(rows, slots, n_pieces, n_mirror, index_at, mirror_at, index_ref, own_ref, *refs):
    pieces, mirrored = refs[:n_pieces], refs[n_pieces : n_pieces + n_mirror]
    *outs, trace = refs[n_pieces + n_mirror : -8]
    right, mirror, own, left, first, others, sems, out_sems = refs[-8:]
    pairs = into(pieces, right, rows * slots) + into(mirrored, mirror, rows * slots) + [(own_ref, own)]
    wait_for(start_copies(pairs, sems))
    blocks, side = rows * slots, right.shape[1]
    part_rows = trace.shape[0] // 2
    total_trace = jnp.zeros((part_rows, side), jnp.float32)
    for b in range(blocks):
        other = mirror[index_ref[mirror_at + b]].astype(jnp.float32).T
        value = (-(own[b].astype(jnp.float32) + other)).astype(jnp.bfloat16)
        left[b] = value
        product = value.astype(jnp.float32) * right[b].astype(jnp.float32).T
        total_trace = total_trace + product.reshape(-1, part_rows, side).sum(0)
    total_trace = two_parts(total_trace)
    trace[...] = total_trace
    results = split_results(first, others)
    for result in results[1:]:
        result[pl.ds(blocks * side, 2 * part_rows)] = total_trace

    def left_of(i):
        return jnp.concatenate([left[i * slots + a] for a in range(slots)], axis=0)

    multiply(index_ref, index_at, left_of, right, results, outs, out_sems, rows, slots, 0)


def sum_kernel(n_out, trace_ref, own_ref, *refs):
    parts, (out, own, others, result, sems, out_sems) = refs[: n_out - 1], refs[n_out - 1 :]
    pairs = [(part, others.at[d]) for d, part in enumerate(parts)]
    wait_for(start_copies([(own_ref, own)] + pairs, sems))
    blocks, side = own.shape[:2]
    for b in range(blocks):
        value = own[b]
        for d in range(n_out - 1):
            value = value + others[d, pl.ds(b * side, side)].astype(jnp.float32)
        result[pl.ds(b * side, side)] = value.astype(result.dtype)
    tail = pl.ds(blocks * side, trace_ref.shape[0])
    tiles = [trace_ref[...]] + [others[d, tail] for d in range(n_out - 1)]
    result[tail] = two_parts(tree_sum([one_part(tile) for tile in tiles]))
    wait_for(start_copies([(result, out)], out_sems))


def last_kernel(n_mirror, blocks, mirror_at, index_ref, own_ref, *refs):
    mirrored, (out, mirror, own, result, sems, out_sems) = refs[:n_mirror], refs[n_mirror:]
    side = own.shape[1]
    count = blocks * side
    body = pl.ds(0, count)
    pairs = [(own_ref.at[body], own)] + [
        (piece.at[body], mirror.at[pl.ds(t * count, count)]) for t, piece in enumerate(mirrored)
    ]
    copies = start_copies(pairs, sems)
    mirror[pl.ds(n_mirror * count, side)] = jnp.zeros((side, side), mirror.dtype)
    wait_for(copies)
    for b in range(blocks):
        start = pl.multiple_of(index_ref[mirror_at + b] * side, side)
        other = mirror[pl.ds(start, side)].astype(jnp.float32)
        value = other - own[pl.ds(b * side, side)].astype(jnp.float32).T
        result[b] = value.astype(result.dtype)
    wait_for(start_copies([(result, out)], out_sems))


def per_device(n_row, n_col, block_cols, step_dir, intersection, density, kohn_sham):
    rows, slots, side = step_dir.shape[:3]
    blocks = rows * slots
    blocks_total = block_cols.shape[0]
    inner = n_row // n_col
    outer = n_row // inner
    assert inner == CORES and outer == n_col and outer & (outer - 1) == 0
    row_index = lax.axis_index("row")
    col_index = lax.axis_index("col")
    bf16, f32 = jnp.bfloat16, jnp.float32

    def at(o, h, g):
        return o * inner + g % inner, (g // inner) * CORES + h

    def inside(r, c):
        return r // inner, c % CORES, (c // CORES) * inner + r % inner

    def spread(o, g):
        bits = (n_col - 1).bit_length()
        return g ^ sum(((o >> b) & 1) << (bits - 1 - b) for b in range(bits))

    def at_spread(o, h, g):
        return at(o, h, spread(o, g))

    def inside_spread(r, c):
        o, h, p = inside(r, c)
        return o, h, spread(o, p)

    o_in, h_in, g_in = inside(row_index, col_index)

    by_group = block_cols.reshape(blocks_total, n_col, slots)
    mirror_cols = lax.dynamic_slice_in_dim(by_group, o_in, 1, 1)[:, 0]

    def rows_of(o, h):
        return lax.dynamic_slice_in_dim(by_group, (o * inner + h) * rows, rows, 0)

    def group_cols_of(cols, g):
        return lax.dynamic_slice_in_dim(cols, g, 1, 1)[:, 0]

    own_rows = rows_of(o_in, h_in)

    def index_table(group, first_out):
        own_cols, group_cols = group_cols_of(own_rows, group), group_cols_of(by_group, group)
        wanted = own_rows[:, first_out ^ jnp.arange(n_col)].transpose(1, 0, 2)
        safe = jnp.clip(wanted, 0, blocks_total - 1)
        matched = (
            (group_cols[safe][..., None, :] == own_cols[None, :, None, :, None])
            & (wanted >= 0)[..., None, None]
            & (own_cols >= 0)[None, :, None, :, None]
        )
        piece = ((safe // rows % inner) ^ h_in) * outer + (safe // rows // inner ^ o_in)
        slot = ((piece * rows + safe % rows) * slots)[..., None] + jnp.argmax(matched, axis=-1)
        return jnp.where(matched.any(-1), slot, n_row * blocks).astype(jnp.int32).reshape(-1)

    spread_in = spread(o_in, g_in)
    all_tables = [index_table(g_in, g_in), index_table(g_in, spread_in)]

    def mirror_table(h, cols):
        own_ids = (o_in * inner + h) * rows + jnp.arange(rows)
        safe_own = jnp.clip(cols, 0, blocks_total - 1)
        found = mirror_cols[safe_own] == own_ids[:, None, None]
        source = (safe_own // rows % inner) ^ h
        return jnp.where(
            cols >= 0,
            (source * rows + safe_own % rows) * slots + jnp.argmax(found, axis=-1),
            inner * blocks,
        ).astype(jnp.int32).reshape(-1)

    all_tables += [mirror_table(h_in, group_cols_of(own_rows, g)) for g in (g_in, spread_in)]
    starts = [sum(table.size for table in all_tables[:t]) for t in range(len(all_tables))]
    first_at, later_at, mirror_at, last_mirror_at = starts
    tables = jnp.concatenate(all_tables)

    smem = pl.BlockSpec(memory_space=pltpu.SMEM)
    vmem = pl.BlockSpec(memory_space=pltpu.VMEM)
    anywhere = pl.BlockSpec(memory_space=pl.ANY)

    def permute(x, target):
        return lax.ppermute(x, ("row", "col"), row_major_perm(n_row, n_col, target))

    def relayout(x, m=0, target=at):
        return permute(x, lambda r, c: target((r // inner) ^ m, r % inner, c))

    def inside_permute(x, move, source=inside, target=at):
        return permute(x, lambda r, c: target(*move(*source(r, c))))

    def share(x):
        return inside_permute(x, lambda o, h, g: (o, h ^ 1, g))

    def after(x, done):
        return lax.optimization_barrier((x, done))[0]

    def to_plane(x, m):
        return inside_permute(x, lambda o, h, g: (o ^ m, h, g))

    def share_all(pieces):
        return {m: share(piece) for m, piece in pieces.items()}

    def listed(pieces, shared):
        return [pieces[m] for m in range(outer)] + [shared[m] for m in range(outer)]

    def mirror(x, target):
        moved = inside_permute(x, lambda o, h, g: (g, h, o), inside_spread, target)
        return [moved, share(moved)]

    def exchange(outs):
        return [outs[0]] + [
            inside_permute(out, lambda o, h, g, d=d: (o, h, g ^ d))
            for d, out in enumerate(outs)
            if d
        ]

    def total_of(parts):
        value = parts[0]
        for part in parts[1:]:
            value = value + part.astype(f32)
        return value.astype(bf16)

    block_shape = (blocks, side, side)
    out_shapes = tuple(
        jax.ShapeDtypeStruct(block_shape, bf16 if d else f32) for d in range(n_col)
    )
    params = pltpu.CompilerParams(vmem_limit_bytes=14 * 2**20)

    def held(count):
        return pltpu.VMEM((count, side, side), bf16)

    def dma(count):
        return pltpu.SemaphoreType.DMA((count,))

    tail_shape = jax.ShapeDtypeStruct((16, side), bf16)
    long_shape = jax.ShapeDtypeStruct((blocks * side + tail_shape.shape[0], side), bf16)
    long_sums = [
        pltpu.VMEM(block_shape, f32),
        pltpu.VMEM((n_col - 1,) + long_shape.shape, bf16),
    ]
    sums = [pltpu.VMEM(block_shape, f32), pltpu.VMEM((n_col - 1,) + block_shape, bf16)]
    cost = pl.CostEstimate(
        flops=2 * n_col * blocks * slots * side**3,
        bytes_accessed=4 * 2**20,
        transcendentals=0,
    )

    flat = lambda x: x.reshape(block_shape)
    inter, dens, kohn = flat(intersection), flat(density), flat(kohn_sham)

    far_from = range(2, outer, 2)
    near = [*far_from, 1]

    inter_near = {m: relayout(inter, m) for m in near}
    inter_early = {0: relayout(inter)} | inter_near
    step = relayout(flat(step_dir))
    dens_own = relayout(dens)
    inter_far = {m + 1: to_plane(inter_near[m], 1) for m in far_from}
    dens_behind = after(dens_own, inter_near)
    dens_near = {m: to_plane(dens_behind, m) for m in far_from}
    dens_behind, kohn = after((dens_own, kohn), (inter_near, inter_far))
    dens_near[1] = to_plane(dens_behind, 1)
    kohn_own = relayout(kohn)
    inter_all = listed(inter_early | inter_far, share_all(inter_early) | share_all(inter_far))
    outs = pl.pallas_call(
        functools.partial(first_kernel, rows, slots, n_row, 1, first_at),
        out_shape=out_shapes,
        in_specs=[smem] + [anywhere] * (1 + n_row + 1),
        out_specs=(anywhere,) * n_col,
        scratch_shapes=[held(n_row * blocks + 1), held(blocks), *sums, dma(n_row + 1), dma(n_col)],
        compiler_params=params,
        cost_estimate=cost,
        name="scaled_step_product",
    )(tables, step, *inter_all, kohn_own)
    parts = exchange(outs)

    dens_beside = {0: share(dens_own)}
    dens_far = {m + 1: to_plane(after(dens_near[m], outs), 1) for m in far_from}
    kohn_behind = after(kohn_own, (dens_near, outs))
    kohn_pieces = {m: to_plane(kohn_behind, m) for m in far_from}
    kohn_early = list(kohn_pieces.values())
    dens_near, dens_far = after((dens_near, dens_far), parts[1:])
    dens_beside |= share_all(dens_near) | share_all(dens_far)
    dens_all = listed({0: dens_own} | dens_near | dens_far, dens_beside)
    outs = pl.pallas_call(
        functools.partial(second_kernel, rows, slots, n_row, n_col, len(kohn_early), later_at),
        out_shape=out_shapes,
        in_specs=[smem] + [anywhere] * (n_row + n_col + len(kohn_early)),
        out_specs=(anywhere,) * n_col,
        scratch_shapes=[
            held(n_row * blocks + 1),
            held(blocks),
            *sums,
            *sums,
            dma(n_row + n_col),
            dma(n_col),
        ],
        compiler_params=params,
        cost_estimate=cost,
        name="change_product",
    )(tables, *dens_all, *parts, *kohn_early)
    second_outs = outs
    total = total_of(exchange(outs))

    mirrored = mirror(total, at)
    own = inside_permute(total, lambda o, h, g: (o, h, g), inside_spread)
    kohn_pieces = {0: kohn_own} | after(kohn_pieces, second_outs)
    kohn_beside = share_all(kohn_pieces)
    kohn_last = {m + 1: to_plane(kohn_pieces[m], 1) for m in range(0, outer, 2)}
    kohn_last = after(kohn_last, total)
    kohn_all = listed(kohn_pieces | kohn_last, kohn_beside | share_all(kohn_last))
    *outs, trace = pl.pallas_call(
        functools.partial(third_kernel, rows, slots, n_row, inner, later_at, mirror_at),
        out_shape=out_shapes[:1] + (long_shape,) * (n_col - 1) + (tail_shape,),
        in_specs=[smem] + [anywhere] * (1 + n_row + inner),
        out_specs=(anywhere,) * n_col + (vmem,),
        scratch_shapes=[
            held(n_row * blocks + 1),
            held(inner * blocks + 1),
            held(blocks),
            held(blocks),
            *long_sums,
            dma(n_row + inner + 1),
            dma(n_col),
        ],
        compiler_params=params,
        cost_estimate=cost,
        name="commutator_product",
    )(tables, own, *kohn_all, *mirrored)
    own, *parts = exchange(outs)
    total = pl.pallas_call(
        functools.partial(sum_kernel, n_col),
        out_shape=long_shape,
        in_specs=[vmem] + [anywhere] * n_col,
        out_specs=anywhere,
        scratch_shapes=[*long_sums, pltpu.VMEM(long_shape.shape, bf16), dma(n_col), dma(1)],
        compiler_params=params,
        name="plane_sum",
    )(trace, own, *parts)
    mirrored = mirror(total, at_spread)

    commutator = pl.pallas_call(
        functools.partial(last_kernel, inner, blocks, last_mirror_at),
        out_shape=jax.ShapeDtypeStruct(block_shape, bf16),
        in_specs=[smem] + [anywhere] * (1 + inner),
        out_specs=anywhere,
        scratch_shapes=[
            pltpu.VMEM(((inner * blocks + 1) * side, side), bf16),
            pltpu.VMEM((blocks * side, side), bf16),
            held(blocks),
            dma(inner + 1),
            dma(1),
        ],
        compiler_params=params,
        name="commutator_difference",
    )(tables, total, *mirrored)
    commutator = inside_permute(
        commutator, lambda o, h, g: (o, h, g), inside_spread, lambda o, h, g: (o * inner + h, g)
    )

    plane_trace = tree_sum([one_part(piece[blocks * side :]) for piece in mirrored])
    trace = tree_sum(
        [plane_trace]
        + [
            inside_permute(plane_trace, lambda o, h, g, d=d: (o, h, g ^ d))
            for d in range(1, n_col)
        ]
    )
    trace_value = trace.sum() / (blocks_total * side * side)
    return commutator.reshape(step_dir.shape), trace_value


def solution(mesh):
    in_specs = (P(),) + (P("row", "col", None, None),) * 4
    out_specs = (P("row", "col", None, None), P())
    return jax.shard_map(
        functools.partial(per_device, mesh.shape["row"], mesh.shape["col"]),
        mesh=mesh,
        in_specs=in_specs,
        out_specs=out_specs,
        check_vma=False,
    )
```

```python
import functools

import jax
import jax.numpy as jnp
from jax import lax
from jax.experimental import pallas as pl
from jax.experimental.pallas import tpu as pltpu
from jax.sharding import PartitionSpec as P

CORES = 2


def row_major_perm(n_row, n_col, target):
    pairs = []
    for r in range(n_row):
        for c in range(n_col):
            to_r, to_c = target(r, c)
            pairs.append((r * n_col + c, to_r * n_col + to_c))
    return pairs


def start_copies(pairs, sems):
    copies = [pltpu.make_async_copy(*pair, sems.at[i]) for i, pair in enumerate(pairs)]
    for copy in copies:
        copy.start()
    return copies


def wait_for(copies):
    for copy in copies:
        copy.wait()


def into(pieces, scratch, count):
    scratch[len(pieces) * count] = jnp.zeros(scratch.shape[1:], scratch.dtype)
    return [
        (piece, scratch.at[pl.ds(index * count, count)]) for index, piece in enumerate(pieces)
    ]


def multiply(index_ref, index_at, left_of, right, results, outs, sems, rows, slots, contract):
    copies = []
    for d in range(len(outs) - 1, -1, -1):
        for i in range(rows):
            left = left_of(i)
            for s in range(slots):
                base = index_at + ((d * rows + i) * slots + s) * slots
                blocks = jnp.concatenate(
                    [right[index_ref[base + a]] for a in range(slots)], axis=1
                )
                value = lax.dot_general(
                    blocks,
                    left,
                    (((1,), (contract,)), ((), ())),
                    preferred_element_type=jnp.float32,
                ).astype(results[d].dtype)
                if len(results[d].shape) == 3:
                    results[d][i * slots + s] = value
                else:
                    side = value.shape[0]
                    results[d][pl.ds((i * slots + s) * side, side)] = value
        copy = pltpu.make_async_copy(results[d], outs[d], sems.at[d])
        copy.start()
        copies.append(copy)
    wait_for(copies)


def split_results(first, others):
    return [first] + [others.at[d] for d in range(others.shape[0])]


def first_kernel(rows, slots, n_pieces, n_early, index_at, index_ref, left_ref, *refs):
    pieces, outs = refs[:n_pieces], refs[n_pieces + n_early : -6]
    right, left, first, others, sems, out_sems = refs[-6:]
    wait_for(start_copies(into(pieces, right, rows * slots) + [(left_ref, left)], sems))

    def left_of(i):
        return jnp.concatenate([left[i * slots + a] for a in range(slots)], axis=1)

    results = split_results(first, others)
    multiply(index_ref, index_at, left_of, right, results, outs, out_sems, rows, slots, 1)


def second_kernel(rows, slots, n_pieces, n_out, index_at, index_ref, *refs):
    pieces, parts = refs[:n_pieces], refs[n_pieces : n_pieces + n_out]
    right, left, part_first, part_others, first, others, sems, out_sems = refs[-8:]
    outs = refs[n_pieces + n_out : -8]
    held = split_results(part_first, part_others)
    wait_for(start_copies(list(zip(parts, held)) + into(pieces, right, rows * slots), sems))
    for b in range(rows * slots):
        value = held[0][b]
        for part in held[1:]:
            value = value + part[b].astype(jnp.float32)
        left[b] = value.astype(jnp.bfloat16)

    def left_of(i):
        return jnp.concatenate([left[i * slots + a] for a in range(slots)], axis=0)

    results = split_results(first, others)
    multiply(index_ref, index_at, left_of, right, results, outs, out_sems, rows, slots, 0)


def two_parts(x):
    high = x.astype(jnp.bfloat16)
    low = (x - high.astype(jnp.float32)).astype(jnp.bfloat16)
    return jnp.concatenate([high, low], axis=0)


def one_part(x):
    x = x.astype(jnp.float32)
    half = x.shape[0] // 2
    return x[:half] + x[half:]


def tree_sum(values):
    while len(values) > 1:
        values = [values[i] + values[i + 1] for i in range(0, len(values), 2)]
    return values[0]


def third_kernel(rows, slots, n_pieces, n_mirror, index_at, mirror_at, index_ref, own_ref, *refs):
    pieces, mirrored = refs[:n_pieces], refs[n_pieces : n_pieces + n_mirror]
    *outs, trace = refs[n_pieces + n_mirror : -8]
    right, mirror, own, left, first, others, sems, out_sems = refs[-8:]
    pairs = into(pieces, right, rows * slots) + into(mirrored, mirror, rows * slots) + [(own_ref, own)]
    wait_for(start_copies(pairs, sems))
    blocks, side = rows * slots, right.shape[1]
    part_rows = trace.shape[0] // 2
    total_trace = jnp.zeros((part_rows, side), jnp.float32)
    for b in range(blocks):
        other = mirror[index_ref[mirror_at + b]].astype(jnp.float32).T
        value = (-(own[b].astype(jnp.float32) + other)).astype(jnp.bfloat16)
        left[b] = value
        product = value.astype(jnp.float32) * right[b].astype(jnp.float32).T
        total_trace = total_trace + product.reshape(-1, part_rows, side).sum(0)
    total_trace = two_parts(total_trace)
    trace[...] = total_trace
    results = split_results(first, others)
    for result in results[1:]:
        result[pl.ds(blocks * side, 2 * part_rows)] = total_trace

    def left_of(i):
        return jnp.concatenate([left[i * slots + a] for a in range(slots)], axis=0)

    multiply(index_ref, index_at, left_of, right, results, outs, out_sems, rows, slots, 0)


def sum_kernel(n_out, trace_ref, own_ref, *refs):
    parts, (out, own, others, result, sems, out_sems) = refs[: n_out - 1], refs[n_out - 1 :]
    pairs = [(part, others.at[d]) for d, part in enumerate(parts)]
    wait_for(start_copies([(own_ref, own)] + pairs, sems))
    blocks, side = own.shape[:2]
    for b in range(blocks):
        value = own[b]
        for d in range(n_out - 1):
            value = value + others[d, pl.ds(b * side, side)].astype(jnp.float32)
        result[pl.ds(b * side, side)] = value.astype(result.dtype)
    tail = pl.ds(blocks * side, trace_ref.shape[0])
    tiles = [trace_ref[...]] + [others[d, tail] for d in range(n_out - 1)]
    result[tail] = two_parts(tree_sum([one_part(tile) for tile in tiles]))
    wait_for(start_copies([(result, out)], out_sems))


def last_kernel(n_mirror, blocks, mirror_at, index_ref, own_ref, *refs):
    mirrored, (out, mirror, own, result, sems, out_sems) = refs[:n_mirror], refs[n_mirror:]
    side = own.shape[1]
    count = blocks * side
    body = pl.ds(0, count)
    pairs = [(own_ref.at[body], own)] + [
        (piece.at[body], mirror.at[pl.ds(t * count, count)]) for t, piece in enumerate(mirrored)
    ]
    copies = start_copies(pairs, sems)
    mirror[pl.ds(n_mirror * count, side)] = jnp.zeros((side, side), mirror.dtype)
    wait_for(copies)
    for b in range(blocks):
        start = pl.multiple_of(index_ref[mirror_at + b] * side, side)
        other = mirror[pl.ds(start, side)].astype(jnp.float32)
        value = other - own[pl.ds(b * side, side)].astype(jnp.float32).T
        result[b] = value.astype(result.dtype)
    wait_for(start_copies([(result, out)], out_sems))


def per_device(n_row, n_col, block_cols, step_dir, intersection, density, kohn_sham):
    rows, slots, side = step_dir.shape[:3]
    blocks = rows * slots
    blocks_total = block_cols.shape[0]
    inner = n_row // n_col
    outer = n_row // inner
    assert inner == CORES and outer == n_col and outer & (outer - 1) == 0
    row_index = lax.axis_index("row")
    col_index = lax.axis_index("col")
    bf16, f32 = jnp.bfloat16, jnp.float32

    def at(o, h, g):
        return o * inner + g % inner, (g // inner) * CORES + h

    def inside(r, c):
        return r // inner, c % CORES, (c // CORES) * inner + r % inner

    def spread(o, g):
        bits = (n_col - 1).bit_length()
        return g ^ sum(((o >> b) & 1) << (bits - 1 - b) for b in range(bits))

    def at_spread(o, h, g):
        return at(o, h, spread(o, g))

    def inside_spread(r, c):
        o, h, p = inside(r, c)
        return o, h, spread(o, p)

    o_in, h_in, g_in = inside(row_index, col_index)

    by_group = block_cols.reshape(blocks_total, n_col, slots)
    mirror_cols = lax.dynamic_slice_in_dim(by_group, o_in, 1, 1)[:, 0]

    def rows_of(o, h):
        return lax.dynamic_slice_in_dim(by_group, (o * inner + h) * rows, rows, 0)

    def group_cols_of(cols, g):
        return lax.dynamic_slice_in_dim(cols, g, 1, 1)[:, 0]

    own_rows = rows_of(o_in, h_in)

    def index_table(group, first_out):
        own_cols, group_cols = group_cols_of(own_rows, group), group_cols_of(by_group, group)
        wanted = own_rows[:, first_out ^ jnp.arange(n_col)].transpose(1, 0, 2)
        safe = jnp.clip(wanted, 0, blocks_total - 1)
        matched = (
            (group_cols[safe][..., None, :] == own_cols[None, :, None, :, None])
            & (wanted >= 0)[..., None, None]
            & (own_cols >= 0)[None, :, None, :, None]
        )
        piece = ((safe // rows % inner) ^ h_in) * outer + (safe // rows // inner ^ o_in)
        slot = ((piece * rows + safe % rows) * slots)[..., None] + jnp.argmax(matched, axis=-1)
        return jnp.where(matched.any(-1), slot, n_row * blocks).astype(jnp.int32).reshape(-1)

    spread_in = spread(o_in, g_in)
    all_tables = [index_table(g_in, g_in), index_table(g_in, spread_in)]

    def mirror_table(h, cols):
        own_ids = (o_in * inner + h) * rows + jnp.arange(rows)
        safe_own = jnp.clip(cols, 0, blocks_total - 1)
        found = mirror_cols[safe_own] == own_ids[:, None, None]
        source = (safe_own // rows % inner) ^ h
        return jnp.where(
            cols >= 0,
            (source * rows + safe_own % rows) * slots + jnp.argmax(found, axis=-1),
            inner * blocks,
        ).astype(jnp.int32).reshape(-1)

    all_tables += [mirror_table(h_in, group_cols_of(own_rows, g)) for g in (g_in, spread_in)]
    starts = [sum(table.size for table in all_tables[:t]) for t in range(len(all_tables))]
    first_at, later_at, mirror_at, last_mirror_at = starts
    tables = jnp.concatenate(all_tables)

    smem = pl.BlockSpec(memory_space=pltpu.SMEM)
    vmem = pl.BlockSpec(memory_space=pltpu.VMEM)
    anywhere = pl.BlockSpec(memory_space=pl.ANY)

    def permute(x, target):
        return lax.ppermute(x, ("row", "col"), row_major_perm(n_row, n_col, target))

    def relayout(x, m=0, target=at):
        return permute(x, lambda r, c: target((r // inner) ^ m, r % inner, c))

    def inside_permute(x, move, source=inside, target=at):
        return permute(x, lambda r, c: target(*move(*source(r, c))))

    def share(x):
        return inside_permute(x, lambda o, h, g: (o, h ^ 1, g))

    def after(x, done):
        return lax.optimization_barrier((x, done))[0]

    def to_plane(x, m):
        return inside_permute(x, lambda o, h, g: (o ^ m, h, g))

    def share_all(pieces):
        return {m: share(piece) for m, piece in pieces.items()}

    def listed(pieces, shared):
        return [pieces[m] for m in range(outer)] + [shared[m] for m in range(outer)]

    def mirror(x, target):
        moved = inside_permute(x, lambda o, h, g: (g, h, o), inside_spread, target)
        return [moved, share(moved)]

    def exchange(outs):
        return [outs[0]] + [
            inside_permute(out, lambda o, h, g, d=d: (o, h, g ^ d))
            for d, out in enumerate(outs)
            if d
        ]

    def total_of(parts):
        value = parts[0]
        for part in parts[1:]:
            value = value + part.astype(f32)
        return value.astype(bf16)

    block_shape = (blocks, side, side)
    out_shapes = tuple(
        jax.ShapeDtypeStruct(block_shape, bf16 if d else f32) for d in range(n_col)
    )
    params = pltpu.CompilerParams(vmem_limit_bytes=14 * 2**20)

    def held(count):
        return pltpu.VMEM((count, side, side), bf16)

    def dma(count):
        return pltpu.SemaphoreType.DMA((count,))

    tail_shape = jax.ShapeDtypeStruct((16, side), bf16)
    long_shape = jax.ShapeDtypeStruct((blocks * side + tail_shape.shape[0], side), bf16)
    long_sums = [
        pltpu.VMEM(block_shape, f32),
        pltpu.VMEM((n_col - 1,) + long_shape.shape, bf16),
    ]
    sums = [pltpu.VMEM(block_shape, f32), pltpu.VMEM((n_col - 1,) + block_shape, bf16)]
    cost = pl.CostEstimate(
        flops=2 * n_col * blocks * slots * side**3,
        bytes_accessed=4 * 2**20,
        transcendentals=0,
    )

    flat = lambda x: x.reshape(block_shape)
    inter, dens, kohn = flat(intersection), flat(density), flat(kohn_sham)

    far_from = range(2, outer, 2)
    near = [*far_from, 1]

    inter_near = {m: relayout(inter, m) for m in near}
    inter_early = {0: relayout(inter)} | inter_near
    step = relayout(flat(step_dir))
    dens_own = relayout(dens)
    inter_far = {m + 1: to_plane(inter_near[m], 1) for m in far_from}
    dens_behind = after(dens_own, inter_near)
    dens_near = {m: to_plane(dens_behind, m) for m in far_from}
    dens_behind, kohn = after((dens_own, kohn), (inter_near, inter_far))
    dens_near[1] = to_plane(dens_behind, 1)
    kohn_own = relayout(kohn)
    inter_all = listed(inter_early | inter_far, share_all(inter_early) | share_all(inter_far))
    outs = pl.pallas_call(
        functools.partial(first_kernel, rows, slots, n_row, 1, first_at),
        out_shape=out_shapes,
        in_specs=[smem] + [anywhere] * (1 + n_row + 1),
        out_specs=(anywhere,) * n_col,
        scratch_shapes=[held(n_row * blocks + 1), held(blocks), *sums, dma(n_row + 1), dma(n_col)],
        compiler_params=params,
        cost_estimate=cost,
        name="scaled_step_product",
    )(tables, step, *inter_all, kohn_own)
    parts = exchange(outs)

    dens_beside = {0: share(dens_own)}
    dens_far = {m + 1: to_plane(after(dens_near[m], outs), 1) for m in far_from}
    kohn_behind = after(kohn_own, (dens_near, outs))
    kohn_pieces = {m: to_plane(kohn_behind, m) for m in far_from}
    dens_near, dens_far = after((dens_near, dens_far), parts[1:])
    dens_beside |= share_all(dens_near) | share_all(dens_far)
    dens_all = listed({0: dens_own} | dens_near | dens_far, dens_beside)
    outs = pl.pallas_call(
        functools.partial(second_kernel, rows, slots, n_row, n_col, later_at),
        out_shape=out_shapes,
        in_specs=[smem] + [anywhere] * (n_row + n_col),
        out_specs=(anywhere,) * n_col,
        scratch_shapes=[
            held(n_row * blocks + 1),
            held(blocks),
            *sums,
            *sums,
            dma(n_row + n_col),
            dma(n_col),
        ],
        compiler_params=params,
        cost_estimate=cost,
        name="change_product",
    )(tables, *dens_all, *parts)
    second_outs = outs
    total = total_of(exchange(outs))

    mirrored = mirror(total, at)
    own = inside_permute(total, lambda o, h, g: (o, h, g), inside_spread)
    kohn_pieces = {0: kohn_own} | after(kohn_pieces, second_outs)
    kohn_beside = share_all(kohn_pieces)
    kohn_last = {m + 1: to_plane(kohn_pieces[m], 1) for m in range(0, outer, 2)}
    kohn_last = after(kohn_last, total)
    kohn_all = listed(kohn_pieces | kohn_last, kohn_beside | share_all(kohn_last))
    *outs, trace = pl.pallas_call(
        functools.partial(third_kernel, rows, slots, n_row, inner, later_at, mirror_at),
        out_shape=out_shapes[:1] + (long_shape,) * (n_col - 1) + (tail_shape,),
        in_specs=[smem] + [anywhere] * (1 + n_row + inner),
        out_specs=(anywhere,) * n_col + (vmem,),
        scratch_shapes=[
            held(n_row * blocks + 1),
            held(inner * blocks + 1),
            held(blocks),
            held(blocks),
            *long_sums,
            dma(n_row + inner + 1),
            dma(n_col),
        ],
        compiler_params=params,
        cost_estimate=cost,
        name="commutator_product",
    )(tables, own, *kohn_all, *mirrored)
    own, *parts = exchange(outs)
    total = pl.pallas_call(
        functools.partial(sum_kernel, n_col),
        out_shape=long_shape,
        in_specs=[vmem] + [anywhere] * n_col,
        out_specs=anywhere,
        scratch_shapes=[*long_sums, pltpu.VMEM(long_shape.shape, bf16), dma(n_col), dma(1)],
        compiler_params=params,
        name="plane_sum",
    )(trace, own, *parts)
    mirrored = mirror(total, at_spread)

    commutator = pl.pallas_call(
        functools.partial(last_kernel, inner, blocks, last_mirror_at),
        out_shape=jax.ShapeDtypeStruct(block_shape, bf16),
        in_specs=[smem] + [anywhere] * (1 + inner),
        out_specs=anywhere,
        scratch_shapes=[
            pltpu.VMEM(((inner * blocks + 1) * side, side), bf16),
            pltpu.VMEM((blocks * side, side), bf16),
            held(blocks),
            dma(inner + 1),
            dma(1),
        ],
        compiler_params=params,
        name="commutator_difference",
    )(tables, total, *mirrored)
    commutator = inside_permute(
        commutator, lambda o, h, g: (o, h, g), inside_spread, lambda o, h, g: (o * inner + h, g)
    )

    plane_trace = tree_sum([one_part(piece[blocks * side :]) for piece in mirrored])
    trace = tree_sum(
        [plane_trace]
        + [
            inside_permute(plane_trace, lambda o, h, g, d=d: (o, h, g ^ d))
            for d in range(1, n_col)
        ]
    )
    trace_value = trace.sum() / (blocks_total * side * side)
    return commutator.reshape(step_dir.shape), trace_value


def solution(mesh):
    in_specs = (P(),) + (P("row", "col", None, None),) * 4
    out_specs = (P("row", "col", None, None), P())
    return jax.shard_map(
        functools.partial(per_device, mesh.shape["row"], mesh.shape["col"]),
        mesh=mesh,
        in_specs=in_specs,
        out_specs=out_specs,
        check_vma=False,
    )
```

```python
import functools

import jax
import jax.numpy as jnp
from jax import lax
from jax.experimental import pallas as pl
from jax.experimental.pallas import tpu as pltpu
from jax.sharding import PartitionSpec as P

CORES = 2


def row_major_perm(n_row, n_col, target):
    pairs = []
    for r in range(n_row):
        for c in range(n_col):
            to_r, to_c = target(r, c)
            pairs.append((r * n_col + c, to_r * n_col + to_c))
    return pairs


def start_copies(pairs, sems):
    copies = [pltpu.make_async_copy(*pair, sems.at[i]) for i, pair in enumerate(pairs)]
    for copy in copies:
        copy.start()
    return copies


def wait_for(copies):
    for copy in copies:
        copy.wait()


def into(pieces, scratch, count):
    scratch[len(pieces) * count] = jnp.zeros(scratch.shape[1:], scratch.dtype)
    return [
        (piece, scratch.at[pl.ds(index * count, count)]) for index, piece in enumerate(pieces)
    ]


def multiply(index_ref, index_at, left_of, right, results, outs, sems, rows, slots, contract):
    copies = []
    for d in range(len(outs) - 1, -1, -1):
        for i in range(rows):
            left = left_of(i)
            for s in range(slots):
                base = index_at + ((d * rows + i) * slots + s) * slots
                blocks = jnp.concatenate(
                    [right[index_ref[base + a]] for a in range(slots)], axis=1
                )
                value = lax.dot_general(
                    blocks,
                    left,
                    (((1,), (contract,)), ((), ())),
                    preferred_element_type=jnp.float32,
                ).astype(results[d].dtype)
                if len(results[d].shape) == 3:
                    results[d][i * slots + s] = value
                else:
                    side = value.shape[0]
                    results[d][pl.ds((i * slots + s) * side, side)] = value
        copy = pltpu.make_async_copy(results[d], outs[d], sems.at[d])
        copy.start()
        copies.append(copy)
    wait_for(copies)


def split_results(first, others):
    return [first] + [others.at[d] for d in range(others.shape[0])]


def first_kernel(rows, slots, n_pieces, n_early, index_at, index_ref, left_ref, *refs):
    pieces, outs = refs[:n_pieces], refs[n_pieces + n_early : -6]
    right, left, first, others, sems, out_sems = refs[-6:]
    wait_for(start_copies(into(pieces, right, rows * slots) + [(left_ref, left)], sems))

    def left_of(i):
        return jnp.concatenate([left[i * slots + a] for a in range(slots)], axis=1)

    results = split_results(first, others)
    multiply(index_ref, index_at, left_of, right, results, outs, out_sems, rows, slots, 1)


def second_kernel(rows, slots, n_pieces, n_out, index_at, index_ref, *refs):
    pieces, parts = refs[:n_pieces], refs[n_pieces : n_pieces + n_out]
    right, left, part_first, part_others, first, others, sems, out_sems = refs[-8:]
    outs = refs[n_pieces + n_out : -8]
    held = split_results(part_first, part_others)
    wait_for(start_copies(list(zip(parts, held)) + into(pieces, right, rows * slots), sems))
    for b in range(rows * slots):
        value = held[0][b]
        for part in held[1:]:
            value = value + part[b].astype(jnp.float32)
        left[b] = value.astype(jnp.bfloat16)

    def left_of(i):
        return jnp.concatenate([left[i * slots + a] for a in range(slots)], axis=0)

    results = split_results(first, others)
    multiply(index_ref, index_at, left_of, right, results, outs, out_sems, rows, slots, 0)


def two_parts(x):
    high = x.astype(jnp.bfloat16)
    low = (x - high.astype(jnp.float32)).astype(jnp.bfloat16)
    return jnp.concatenate([high, low], axis=0)


def one_part(x):
    x = x.astype(jnp.float32)
    half = x.shape[0] // 2
    return x[:half] + x[half:]


def tree_sum(values):
    while len(values) > 1:
        values = [values[i] + values[i + 1] for i in range(0, len(values), 2)]
    return values[0]


def third_kernel(rows, slots, n_pieces, n_mirror, index_at, mirror_at, index_ref, own_ref, *refs):
    pieces, mirrored = refs[:n_pieces], refs[n_pieces : n_pieces + n_mirror]
    *outs, trace = refs[n_pieces + n_mirror : -8]
    right, mirror, own, left, first, others, sems, out_sems = refs[-8:]
    pairs = into(pieces, right, rows * slots) + into(mirrored, mirror, rows * slots) + [(own_ref, own)]
    wait_for(start_copies(pairs, sems))
    blocks, side = rows * slots, right.shape[1]
    part_rows = trace.shape[0] // 2
    total_trace = jnp.zeros((part_rows, side), jnp.float32)
    for b in range(blocks):
        other = mirror[index_ref[mirror_at + b]].astype(jnp.float32).T
        value = (-(own[b].astype(jnp.float32) + other)).astype(jnp.bfloat16)
        left[b] = value
        product = value.astype(jnp.float32) * right[b].astype(jnp.float32).T
        total_trace = total_trace + product.reshape(-1, part_rows, side).sum(0)
    total_trace = two_parts(total_trace)
    trace[...] = total_trace
    results = split_results(first, others)
    for result in results[1:]:
        result[pl.ds(blocks * side, 2 * part_rows)] = total_trace

    def left_of(i):
        return jnp.concatenate([left[i * slots + a] for a in range(slots)], axis=0)

    multiply(index_ref, index_at, left_of, right, results, outs, out_sems, rows, slots, 0)


def sum_kernel(n_out, trace_ref, own_ref, *refs):
    parts, (out, own, others, result, sems, out_sems) = refs[: n_out - 1], refs[n_out - 1 :]
    pairs = [(part, others.at[d]) for d, part in enumerate(parts)]
    wait_for(start_copies([(own_ref, own)] + pairs, sems))
    blocks, side = own.shape[:2]
    for b in range(blocks):
        value = own[b]
        for d in range(n_out - 1):
            value = value + others[d, pl.ds(b * side, side)].astype(jnp.float32)
        result[pl.ds(b * side, side)] = value.astype(result.dtype)
    tail = pl.ds(blocks * side, trace_ref.shape[0])
    tiles = [trace_ref[...]] + [others[d, tail] for d in range(n_out - 1)]
    result[tail] = two_parts(tree_sum([one_part(tile) for tile in tiles]))
    wait_for(start_copies([(result, out)], out_sems))


def last_kernel(n_mirror, blocks, mirror_at, index_ref, own_ref, *refs):
    mirrored, (out, mirror, own, result, sems, out_sems) = refs[:n_mirror], refs[n_mirror:]
    side = own.shape[1]
    count = blocks * side
    body = pl.ds(0, count)
    pairs = [(own_ref.at[body], own)] + [
        (piece.at[body], mirror.at[pl.ds(t * count, count)]) for t, piece in enumerate(mirrored)
    ]
    copies = start_copies(pairs, sems)
    mirror[pl.ds(n_mirror * count, side)] = jnp.zeros((side, side), mirror.dtype)
    wait_for(copies)
    for b in range(blocks):
        start = pl.multiple_of(index_ref[mirror_at + b] * side, side)
        other = mirror[pl.ds(start, side)].astype(jnp.float32)
        value = other - own[pl.ds(b * side, side)].astype(jnp.float32).T
        result[b] = value.astype(result.dtype)
    wait_for(start_copies([(result, out)], out_sems))


def per_device(n_row, n_col, block_cols, step_dir, intersection, density, kohn_sham):
    rows, slots, side = step_dir.shape[:3]
    blocks = rows * slots
    blocks_total = block_cols.shape[0]
    inner = n_row // n_col
    outer = n_row // inner
    assert inner == CORES and outer == n_col and outer & (outer - 1) == 0
    row_index = lax.axis_index("row")
    col_index = lax.axis_index("col")
    bf16, f32 = jnp.bfloat16, jnp.float32

    def at(o, h, g):
        return o * inner + g % inner, (g // inner) * CORES + h

    def inside(r, c):
        return r // inner, c % CORES, (c // CORES) * inner + r % inner

    def spread(o, g):
        bits = (n_col - 1).bit_length()
        return g ^ sum(((o >> b) & 1) << (bits - 1 - b) for b in range(bits))

    def inside_spread(r, c):
        o, h, p = inside(r, c)
        return o, h, spread(o, p)

    o_in, h_in, g_in = inside(row_index, col_index)

    by_group = block_cols.reshape(blocks_total, n_col, slots)
    mirror_cols = lax.dynamic_slice_in_dim(by_group, o_in, 1, 1)[:, 0]

    def rows_of(o, h):
        return lax.dynamic_slice_in_dim(by_group, (o * inner + h) * rows, rows, 0)

    def group_cols_of(cols, g):
        return lax.dynamic_slice_in_dim(cols, g, 1, 1)[:, 0]

    own_rows = rows_of(o_in, h_in)

    def index_table(group, first_out):
        own_cols, group_cols = group_cols_of(own_rows, group), group_cols_of(by_group, group)
        wanted = own_rows[:, first_out ^ jnp.arange(n_col)].transpose(1, 0, 2)
        safe = jnp.clip(wanted, 0, blocks_total - 1)
        matched = (
            (group_cols[safe][..., None, :] == own_cols[None, :, None, :, None])
            & (wanted >= 0)[..., None, None]
            & (own_cols >= 0)[None, :, None, :, None]
        )
        piece = ((safe // rows % inner) ^ h_in) * outer + (safe // rows // inner ^ o_in)
        slot = ((piece * rows + safe % rows) * slots)[..., None] + jnp.argmax(matched, axis=-1)
        return jnp.where(matched.any(-1), slot, n_row * blocks).astype(jnp.int32).reshape(-1)

    spread_in = spread(o_in, g_in)
    all_tables = [index_table(g_in, g_in), index_table(g_in, spread_in)]

    def mirror_table(h, cols):
        own_ids = (o_in * inner + h) * rows + jnp.arange(rows)
        safe_own = jnp.clip(cols, 0, blocks_total - 1)
        found = mirror_cols[safe_own] == own_ids[:, None, None]
        source = (safe_own // rows % inner) ^ h
        return jnp.where(
            cols >= 0,
            (source * rows + safe_own % rows) * slots + jnp.argmax(found, axis=-1),
            inner * blocks,
        ).astype(jnp.int32).reshape(-1)

    all_tables.append(mirror_table(h_in, group_cols_of(own_rows, g_in)))
    q_out = row_index % inner
    all_tables.append(mirror_table(q_out, group_cols_of(rows_of(o_in, q_out), col_index)))
    starts = [sum(table.size for table in all_tables[:t]) for t in range(len(all_tables))]
    first_at, later_at, mirror_at, last_mirror_at = starts
    tables = jnp.concatenate(all_tables)

    smem = pl.BlockSpec(memory_space=pltpu.SMEM)
    vmem = pl.BlockSpec(memory_space=pltpu.VMEM)
    anywhere = pl.BlockSpec(memory_space=pl.ANY)

    def permute(x, target):
        return lax.ppermute(x, ("row", "col"), row_major_perm(n_row, n_col, target))

    def relayout(x, m=0, target=at):
        return permute(x, lambda r, c: target((r // inner) ^ m, r % inner, c))

    def inside_permute(x, move, source=inside, target=at):
        return permute(x, lambda r, c: target(*move(*source(r, c))))

    def share(x):
        return inside_permute(x, lambda o, h, g: (o, h ^ 1, g))

    def after(x, done):
        return lax.optimization_barrier((x, done))[0]

    def to_plane(x, m):
        return inside_permute(x, lambda o, h, g: (o ^ m, h, g))

    def share_all(pieces):
        return {m: share(piece) for m, piece in pieces.items()}

    def listed(pieces, shared):
        return [pieces[m] for m in range(outer)] + [shared[m] for m in range(outer)]

    def exchange(outs):
        return [outs[0]] + [
            inside_permute(out, lambda o, h, g, d=d: (o, h, g ^ d))
            for d, out in enumerate(outs)
            if d
        ]

    def total_of(parts):
        value = parts[0]
        for part in parts[1:]:
            value = value + part.astype(f32)
        return value.astype(bf16)

    block_shape = (blocks, side, side)
    out_shapes = tuple(
        jax.ShapeDtypeStruct(block_shape, bf16 if d else f32) for d in range(n_col)
    )
    params = pltpu.CompilerParams(vmem_limit_bytes=14 * 2**20)

    def held(count):
        return pltpu.VMEM((count, side, side), bf16)

    def dma(count):
        return pltpu.SemaphoreType.DMA((count,))

    tail_shape = jax.ShapeDtypeStruct((16, side), bf16)
    long_shape = jax.ShapeDtypeStruct((blocks * side + tail_shape.shape[0], side), bf16)
    long_sums = [
        pltpu.VMEM(block_shape, f32),
        pltpu.VMEM((n_col - 1,) + long_shape.shape, bf16),
    ]
    sums = [pltpu.VMEM(block_shape, f32), pltpu.VMEM((n_col - 1,) + block_shape, bf16)]
    cost = pl.CostEstimate(
        flops=2 * n_col * blocks * slots * side**3,
        bytes_accessed=4 * 2**20,
        transcendentals=0,
    )

    flat = lambda x: x.reshape(block_shape)
    inter, dens, kohn = flat(intersection), flat(density), flat(kohn_sham)

    far_from = range(2, outer, 2)
    near = [*far_from, 1]

    inter_near = {m: relayout(inter, m) for m in near}
    inter_early = {0: relayout(inter)} | inter_near
    step = relayout(flat(step_dir))
    dens_own = relayout(dens)
    inter_far = {m + 1: to_plane(inter_near[m], 1) for m in far_from}
    dens_behind = after(dens_own, inter_near)
    dens_near = {m: to_plane(dens_behind, m) for m in far_from}
    dens_behind, kohn = after((dens_own, kohn), (inter_near, inter_far))
    dens_near[1] = to_plane(dens_behind, 1)
    kohn_own = relayout(kohn)
    inter_early = after(inter_early, inter_far)
    inter_all = listed(inter_early | inter_far, share_all(inter_early) | share_all(inter_far))
    outs = pl.pallas_call(
        functools.partial(first_kernel, rows, slots, n_row, 1, first_at),
        out_shape=out_shapes,
        in_specs=[smem] + [anywhere] * (1 + n_row + 1),
        out_specs=(anywhere,) * n_col,
        scratch_shapes=[held(n_row * blocks + 1), held(blocks), *sums, dma(n_row + 1), dma(n_col)],
        compiler_params=params,
        cost_estimate=cost,
        name="scaled_step_product",
    )(tables, step, *inter_all, kohn_own)
    parts = exchange(outs)

    dens_beside = {0: share(dens_own)}
    dens_far = {m + 1: to_plane(after(dens_near[m], outs), 1) for m in far_from}
    kohn_behind = after(kohn_own, (dens_near, outs))
    kohn_pieces = {m: to_plane(kohn_behind, m) for m in far_from}
    dens_near, dens_far = after((dens_near, dens_far), parts[1:])
    dens_beside |= share_all(dens_near) | share_all(dens_far)
    dens_all = listed({0: dens_own} | dens_near | dens_far, dens_beside)
    outs = pl.pallas_call(
        functools.partial(second_kernel, rows, slots, n_row, n_col, later_at),
        out_shape=out_shapes,
        in_specs=[smem] + [anywhere] * (n_row + n_col),
        out_specs=(anywhere,) * n_col,
        scratch_shapes=[
            held(n_row * blocks + 1),
            held(blocks),
            *sums,
            *sums,
            dma(n_row + n_col),
            dma(n_col),
        ],
        compiler_params=params,
        cost_estimate=cost,
        name="change_product",
    )(tables, *dens_all, *parts)
    second_outs = outs
    total = total_of(exchange(outs))

    mirrored = [inside_permute(total, lambda o, h, g: (g, h, o), inside_spread)]
    mirrored.append(share(mirrored[0]))
    own = inside_permute(total, lambda o, h, g: (o, h, g), inside_spread)
    kohn_pieces = {0: kohn_own} | after(kohn_pieces, second_outs)
    kohn_beside = share_all(kohn_pieces)
    kohn_last = {m + 1: to_plane(kohn_pieces[m], 1) for m in range(0, outer, 2)}
    kohn_last = after(kohn_last, total)
    kohn_all = listed(kohn_pieces | kohn_last, kohn_beside | share_all(kohn_last))
    *outs, trace = pl.pallas_call(
        functools.partial(third_kernel, rows, slots, n_row, inner, later_at, mirror_at),
        out_shape=out_shapes[:1] + (long_shape,) * (n_col - 1) + (tail_shape,),
        in_specs=[smem] + [anywhere] * (1 + n_row + inner),
        out_specs=(anywhere,) * n_col + (vmem,),
        scratch_shapes=[
            held(n_row * blocks + 1),
            held(inner * blocks + 1),
            held(blocks),
            held(blocks),
            *long_sums,
            dma(n_row + inner + 1),
            dma(n_col),
        ],
        compiler_params=params,
        cost_estimate=cost,
        name="commutator_product",
    )(tables, own, *kohn_all, *mirrored)
    own, *parts = exchange(outs)
    total = pl.pallas_call(
        functools.partial(sum_kernel, n_col),
        out_shape=long_shape,
        in_specs=[vmem] + [anywhere] * n_col,
        out_specs=anywhere,
        scratch_shapes=[*long_sums, pltpu.VMEM(long_shape.shape, bf16), dma(n_col), dma(1)],
        compiler_params=params,
        name="plane_sum",
    )(trace, own, *parts)

    def outside(move):
        return inside_permute(total, move, inside_spread, lambda o, q, g: (o * inner + q, g))

    mirrored = [outside(lambda o, h, g, t=t: (g, h ^ t, o)) for t in range(inner)]
    own = outside(lambda o, h, g: (o, h, g))

    commutator = pl.pallas_call(
        functools.partial(last_kernel, inner, blocks, last_mirror_at),
        out_shape=jax.ShapeDtypeStruct(block_shape, bf16),
        in_specs=[smem] + [anywhere] * (1 + inner),
        out_specs=anywhere,
        scratch_shapes=[
            pltpu.VMEM(((inner * blocks + 1) * side, side), bf16),
            pltpu.VMEM((blocks * side, side), bf16),
            held(blocks),
            dma(inner + 1),
            dma(1),
        ],
        compiler_params=params,
        name="commutator_difference",
    )(tables, own, *mirrored)

    plane_trace = tree_sum([one_part(piece[blocks * side :]) for piece in mirrored])
    trace = tree_sum(
        [plane_trace]
        + [permute(plane_trace, lambda r, c, d=d: (r, c ^ d)) for d in range(1, n_col)]
    )
    trace_value = trace.sum() / (blocks_total * side * side)
    return commutator.reshape(step_dir.shape), trace_value


def solution(mesh):
    in_specs = (P(),) + (P("row", "col", None, None),) * 4
    out_specs = (P("row", "col", None, None), P())
    return jax.shard_map(
        functools.partial(per_device, mesh.shape["row"], mesh.shape["col"]),
        mesh=mesh,
        in_specs=in_specs,
        out_specs=out_specs,
        check_vma=False,
    )
```

```python
import functools

import jax
import jax.numpy as jnp
from jax import lax
from jax.experimental import pallas as pl
from jax.experimental.pallas import tpu as pltpu
from jax.sharding import PartitionSpec as P

CORES = 2


def row_major_perm(n_row, n_col, target):
    pairs = []
    for r in range(n_row):
        for c in range(n_col):
            to_r, to_c = target(r, c)
            pairs.append((r * n_col + c, to_r * n_col + to_c))
    return pairs


def start_copies(pairs, sems):
    copies = [pltpu.make_async_copy(*pair, sems.at[i]) for i, pair in enumerate(pairs)]
    for copy in copies:
        copy.start()
    return copies


def wait_for(copies):
    for copy in copies:
        copy.wait()


def into(pieces, scratch, count):
    scratch[len(pieces) * count] = jnp.zeros(scratch.shape[1:], scratch.dtype)
    return [
        (piece, scratch.at[pl.ds(index * count, count)]) for index, piece in enumerate(pieces)
    ]


def multiply(index_ref, index_at, left_of, right, results, outs, sems, rows, slots, contract):
    copies = []
    for d in range(len(outs) - 1, -1, -1):
        for i in range(rows):
            left = left_of(i)
            for s in range(slots):
                base = index_at + ((d * rows + i) * slots + s) * slots
                blocks = jnp.concatenate(
                    [right[index_ref[base + a]] for a in range(slots)], axis=1
                )
                value = lax.dot_general(
                    blocks,
                    left,
                    (((1,), (contract,)), ((), ())),
                    preferred_element_type=jnp.float32,
                ).astype(results[d].dtype)
                if len(results[d].shape) == 3:
                    results[d][i * slots + s] = value
                else:
                    side = value.shape[0]
                    results[d][pl.ds((i * slots + s) * side, side)] = value
        copy = pltpu.make_async_copy(results[d], outs[d], sems.at[d])
        copy.start()
        copies.append(copy)
    wait_for(copies)


def split_results(first, others):
    return [first] + [others.at[d] for d in range(others.shape[0])]


def first_kernel(rows, slots, n_pieces, n_early, index_at, index_ref, left_ref, *refs):
    pieces, outs = refs[:n_pieces], refs[n_pieces + n_early : -6]
    right, left, first, others, sems, out_sems = refs[-6:]
    wait_for(start_copies(into(pieces, right, rows * slots) + [(left_ref, left)], sems))

    def left_of(i):
        return jnp.concatenate([left[i * slots + a] for a in range(slots)], axis=1)

    results = split_results(first, others)
    multiply(index_ref, index_at, left_of, right, results, outs, out_sems, rows, slots, 1)


def second_kernel(rows, slots, n_pieces, n_out, index_at, index_ref, *refs):
    pieces, parts = refs[:n_pieces], refs[n_pieces : n_pieces + n_out]
    right, left, part_first, part_others, first, others, sems, out_sems = refs[-8:]
    outs = refs[n_pieces + n_out : -8]
    held = split_results(part_first, part_others)
    wait_for(start_copies(list(zip(parts, held)) + into(pieces, right, rows * slots), sems))
    for b in range(rows * slots):
        value = held[0][b]
        for part in held[1:]:
            value = value + part[b].astype(jnp.float32)
        left[b] = value.astype(jnp.bfloat16)

    def left_of(i):
        return jnp.concatenate([left[i * slots + a] for a in range(slots)], axis=0)

    results = split_results(first, others)
    multiply(index_ref, index_at, left_of, right, results, outs, out_sems, rows, slots, 0)


def two_parts(x):
    high = x.astype(jnp.bfloat16)
    low = (x - high.astype(jnp.float32)).astype(jnp.bfloat16)
    return jnp.concatenate([high, low], axis=0)


def one_part(x):
    x = x.astype(jnp.float32)
    half = x.shape[0] // 2
    return x[:half] + x[half:]


def tree_sum(values):
    while len(values) > 1:
        values = [values[i] + values[i + 1] for i in range(0, len(values), 2)]
    return values[0]


def third_kernel(rows, slots, n_pieces, n_mirror, index_at, mirror_at, index_ref, own_ref, *refs):
    pieces, mirrored = refs[:n_pieces], refs[n_pieces : n_pieces + n_mirror]
    *outs, trace = refs[n_pieces + n_mirror : -8]
    right, mirror, own, left, first, others, sems, out_sems = refs[-8:]
    pairs = into(pieces, right, rows * slots) + into(mirrored, mirror, rows * slots) + [(own_ref, own)]
    wait_for(start_copies(pairs, sems))
    blocks, side = rows * slots, right.shape[1]
    part_rows = trace.shape[0] // 2
    total_trace = jnp.zeros((part_rows, side), jnp.float32)
    for b in range(blocks):
        other = mirror[index_ref[mirror_at + b]].astype(jnp.float32).T
        value = (-(own[b].astype(jnp.float32) + other)).astype(jnp.bfloat16)
        left[b] = value
        product = value.astype(jnp.float32) * right[b].astype(jnp.float32).T
        total_trace = total_trace + product.reshape(-1, part_rows, side).sum(0)
    total_trace = two_parts(total_trace)
    trace[...] = total_trace
    results = split_results(first, others)
    for result in results[1:]:
        result[pl.ds(blocks * side, 2 * part_rows)] = total_trace

    def left_of(i):
        return jnp.concatenate([left[i * slots + a] for a in range(slots)], axis=0)

    multiply(index_ref, index_at, left_of, right, results, outs, out_sems, rows, slots, 0)


def sum_kernel(n_out, trace_ref, own_ref, *refs):
    parts, (out, own, others, result, sems, out_sems) = refs[: n_out - 1], refs[n_out - 1 :]
    pairs = [(part, others.at[d]) for d, part in enumerate(parts)]
    wait_for(start_copies([(own_ref, own)] + pairs, sems))
    blocks, side = own.shape[:2]
    for b in range(blocks):
        value = own[b]
        for d in range(n_out - 1):
            value = value + others[d, pl.ds(b * side, side)].astype(jnp.float32)
        result[pl.ds(b * side, side)] = value.astype(result.dtype)
    tail = pl.ds(blocks * side, trace_ref.shape[0])
    tiles = [trace_ref[...]] + [others[d, tail] for d in range(n_out - 1)]
    result[tail] = two_parts(tree_sum([one_part(tile) for tile in tiles]))
    wait_for(start_copies([(result, out)], out_sems))


def last_kernel(n_mirror, blocks, mirror_at, index_ref, own_ref, *refs):
    mirrored, (out, mirror, own, result, sems, out_sems) = refs[:n_mirror], refs[n_mirror:]
    side = own.shape[1]
    count = blocks * side
    body = pl.ds(0, count)
    pairs = [(own_ref.at[body], own)] + [
        (piece.at[body], mirror.at[pl.ds(t * count, count)]) for t, piece in enumerate(mirrored)
    ]
    copies = start_copies(pairs, sems)
    mirror[pl.ds(n_mirror * count, side)] = jnp.zeros((side, side), mirror.dtype)
    wait_for(copies)
    for b in range(blocks):
        start = pl.multiple_of(index_ref[mirror_at + b] * side, side)
        other = mirror[pl.ds(start, side)].astype(jnp.float32)
        value = other - own[pl.ds(b * side, side)].astype(jnp.float32).T
        result[b] = value.astype(result.dtype)
    wait_for(start_copies([(result, out)], out_sems))


def per_device(n_row, n_col, block_cols, step_dir, intersection, density, kohn_sham):
    rows, slots, side = step_dir.shape[:3]
    blocks = rows * slots
    blocks_total = block_cols.shape[0]
    inner = n_row // n_col
    outer = n_row // inner
    assert inner == CORES and outer == n_col and outer & (outer - 1) == 0
    row_index = lax.axis_index("row")
    col_index = lax.axis_index("col")
    bf16, f32 = jnp.bfloat16, jnp.float32

    def at(o, h, g):
        return o * inner + g % inner, (g // inner) * CORES + h

    def inside(r, c):
        return r // inner, c % CORES, (c // CORES) * inner + r % inner

    def spread(o, g):
        bits = (n_col - 1).bit_length()
        return g ^ sum(((o >> b) & 1) << (bits - 1 - b) for b in range(bits))

    def inside_spread(r, c):
        o, h, p = inside(r, c)
        return o, h, spread(o, p)

    o_in, h_in, g_in = inside(row_index, col_index)

    by_group = block_cols.reshape(blocks_total, n_col, slots)
    mirror_cols = lax.dynamic_slice_in_dim(by_group, o_in, 1, 1)[:, 0]

    def rows_of(o, h):
        return lax.dynamic_slice_in_dim(by_group, (o * inner + h) * rows, rows, 0)

    def group_cols_of(cols, g):
        return lax.dynamic_slice_in_dim(cols, g, 1, 1)[:, 0]

    own_rows = rows_of(o_in, h_in)

    def index_table(group, first_out):
        own_cols, group_cols = group_cols_of(own_rows, group), group_cols_of(by_group, group)
        wanted = own_rows[:, first_out ^ jnp.arange(n_col)].transpose(1, 0, 2)
        safe = jnp.clip(wanted, 0, blocks_total - 1)
        matched = (
            (group_cols[safe][..., None, :] == own_cols[None, :, None, :, None])
            & (wanted >= 0)[..., None, None]
            & (own_cols >= 0)[None, :, None, :, None]
        )
        piece = ((safe // rows % inner) ^ h_in) * outer + (safe // rows // inner ^ o_in)
        slot = ((piece * rows + safe % rows) * slots)[..., None] + jnp.argmax(matched, axis=-1)
        return jnp.where(matched.any(-1), slot, n_row * blocks).astype(jnp.int32).reshape(-1)

    spread_in = spread(o_in, g_in)
    all_tables = [index_table(g_in, g_in), index_table(g_in, spread_in)]

    def mirror_table(h, cols):
        own_ids = (o_in * inner + h) * rows + jnp.arange(rows)
        safe_own = jnp.clip(cols, 0, blocks_total - 1)
        found = mirror_cols[safe_own] == own_ids[:, None, None]
        source = (safe_own // rows % inner) ^ h
        return jnp.where(
            cols >= 0,
            (source * rows + safe_own % rows) * slots + jnp.argmax(found, axis=-1),
            inner * blocks,
        ).astype(jnp.int32).reshape(-1)

    all_tables.append(mirror_table(h_in, group_cols_of(own_rows, g_in)))
    starts = [sum(table.size for table in all_tables[:t]) for t in range(len(all_tables))]
    first_at, later_at, mirror_at = starts
    tables = jnp.concatenate(all_tables)

    smem = pl.BlockSpec(memory_space=pltpu.SMEM)
    vmem = pl.BlockSpec(memory_space=pltpu.VMEM)
    anywhere = pl.BlockSpec(memory_space=pl.ANY)

    def permute(x, target):
        return lax.ppermute(x, ("row", "col"), row_major_perm(n_row, n_col, target))

    def relayout(x, m=0, target=at):
        return permute(x, lambda r, c: target((r // inner) ^ m, r % inner, c))

    def inside_permute(x, move, source=inside, target=at):
        return permute(x, lambda r, c: target(*move(*source(r, c))))

    def share(x):
        return inside_permute(x, lambda o, h, g: (o, h ^ 1, g))

    def after(x, done):
        return lax.optimization_barrier((x, done))[0]

    def to_plane(x, m):
        return inside_permute(x, lambda o, h, g: (o ^ m, h, g))

    def share_all(pieces):
        return {m: share(piece) for m, piece in pieces.items()}

    def listed(pieces, shared):
        return [pieces[m] for m in range(outer)] + [shared[m] for m in range(outer)]

    def settle(x):
        mirrored = inside_permute(x, lambda o, h, g: (g, h, o), inside_spread)
        own = inside_permute(x, lambda o, h, g: (o, h, g), inside_spread)
        return own, [mirrored, share(mirrored)]

    def exchange(outs):
        return [outs[0]] + [
            inside_permute(out, lambda o, h, g, d=d: (o, h, g ^ d))
            for d, out in enumerate(outs)
            if d
        ]

    def total_of(parts):
        value = parts[0]
        for part in parts[1:]:
            value = value + part.astype(f32)
        return value.astype(bf16)

    block_shape = (blocks, side, side)
    out_shapes = tuple(
        jax.ShapeDtypeStruct(block_shape, bf16 if d else f32) for d in range(n_col)
    )
    params = pltpu.CompilerParams(vmem_limit_bytes=14 * 2**20)

    def held(count):
        return pltpu.VMEM((count, side, side), bf16)

    def dma(count):
        return pltpu.SemaphoreType.DMA((count,))

    tail_shape = jax.ShapeDtypeStruct((16, side), bf16)
    long_shape = jax.ShapeDtypeStruct((blocks * side + tail_shape.shape[0], side), bf16)
    long_sums = [
        pltpu.VMEM(block_shape, f32),
        pltpu.VMEM((n_col - 1,) + long_shape.shape, bf16),
    ]
    sums = [pltpu.VMEM(block_shape, f32), pltpu.VMEM((n_col - 1,) + block_shape, bf16)]
    cost = pl.CostEstimate(
        flops=2 * n_col * blocks * slots * side**3,
        bytes_accessed=4 * 2**20,
        transcendentals=0,
    )

    flat = lambda x: x.reshape(block_shape)
    inter, dens, kohn = flat(intersection), flat(density), flat(kohn_sham)

    far_from = range(2, outer, 2)
    near = [*far_from, 1]

    inter_near = {m: relayout(inter, m) for m in near}
    inter_early = {0: relayout(inter)} | inter_near
    step = relayout(flat(step_dir))
    dens_own = relayout(dens)
    inter_far = {m + 1: to_plane(inter_near[m], 1) for m in far_from}
    dens_behind = after(dens, inter_near)
    dens_near = {m: relayout(dens_behind, m) for m in far_from}
    dens_behind, kohn = after((dens_own, kohn), (inter_near, inter_far))
    dens_near[1] = to_plane(dens_behind, 1)
    kohn_own = relayout(kohn)
    inter_all = listed(inter_early | inter_far, share_all(inter_early) | share_all(inter_far))
    outs = pl.pallas_call(
        functools.partial(first_kernel, rows, slots, n_row, 1, first_at),
        out_shape=out_shapes,
        in_specs=[smem] + [anywhere] * (1 + n_row + 1),
        out_specs=(anywhere,) * n_col,
        scratch_shapes=[held(n_row * blocks + 1), held(blocks), *sums, dma(n_row + 1), dma(n_col)],
        compiler_params=params,
        cost_estimate=cost,
        name="scaled_step_product",
    )(tables, step, *inter_all, kohn_own)
    parts = exchange(outs)

    dens_beside = {0: share(dens_own)}
    dens_far = {m + 1: to_plane(after(dens_near[m], outs), 1) for m in far_from}
    kohn_behind = after(kohn_own, (dens_near, outs))
    kohn_pieces = {m: to_plane(kohn_behind, m) for m in far_from}
    dens_near, dens_far = after((dens_near, dens_far), parts[1:])
    dens_beside |= share_all(dens_near) | share_all(dens_far)
    dens_all = listed({0: dens_own} | dens_near | dens_far, dens_beside)
    outs = pl.pallas_call(
        functools.partial(second_kernel, rows, slots, n_row, n_col, later_at),
        out_shape=out_shapes,
        in_specs=[smem] + [anywhere] * (n_row + n_col),
        out_specs=(anywhere,) * n_col,
        scratch_shapes=[
            held(n_row * blocks + 1),
            held(blocks),
            *sums,
            *sums,
            dma(n_row + n_col),
            dma(n_col),
        ],
        compiler_params=params,
        cost_estimate=cost,
        name="change_product",
    )(tables, *dens_all, *parts)
    second_outs = outs
    total = total_of(exchange(outs))

    own, mirrored = settle(total)
    kohn_pieces = {0: kohn_own} | after(kohn_pieces, second_outs)
    kohn_beside = share_all(kohn_pieces)
    kohn_last = {m + 1: to_plane(kohn_pieces[m], 1) for m in range(0, outer, 2)}
    kohn_last = after(kohn_last, total)
    kohn_all = listed(kohn_pieces | kohn_last, kohn_beside | share_all(kohn_last))
    *outs, trace = pl.pallas_call(
        functools.partial(third_kernel, rows, slots, n_row, inner, later_at, mirror_at),
        out_shape=out_shapes[:1] + (long_shape,) * (n_col - 1) + (tail_shape,),
        in_specs=[smem] + [anywhere] * (1 + n_row + inner),
        out_specs=(anywhere,) * n_col + (vmem,),
        scratch_shapes=[
            held(n_row * blocks + 1),
            held(inner * blocks + 1),
            held(blocks),
            held(blocks),
            *long_sums,
            dma(n_row + inner + 1),
            dma(n_col),
        ],
        compiler_params=params,
        cost_estimate=cost,
        name="commutator_product",
    )(tables, own, *kohn_all, *mirrored)
    own, *parts = exchange(outs)
    total = pl.pallas_call(
        functools.partial(sum_kernel, n_col),
        out_shape=long_shape,
        in_specs=[vmem] + [anywhere] * n_col,
        out_specs=anywhere,
        scratch_shapes=[*long_sums, pltpu.VMEM(long_shape.shape, bf16), dma(n_col), dma(1)],
        compiler_params=params,
        name="plane_sum",
    )(trace, own, *parts)
    own, mirrored = settle(total)

    commutator = pl.pallas_call(
        functools.partial(last_kernel, inner, blocks, mirror_at),
        out_shape=jax.ShapeDtypeStruct(block_shape, bf16),
        in_specs=[smem] + [anywhere] * (1 + inner),
        out_specs=anywhere,
        scratch_shapes=[
            pltpu.VMEM(((inner * blocks + 1) * side, side), bf16),
            pltpu.VMEM((blocks * side, side), bf16),
            held(blocks),
            dma(inner + 1),
            dma(1),
        ],
        compiler_params=params,
        name="commutator_difference",
    )(tables, own, *mirrored)
    commutator = inside_permute(
        commutator, lambda o, h, g: (o, h, g), inside, lambda o, h, g: (o * inner + h, g)
    )

    plane_trace = tree_sum([one_part(piece[blocks * side :]) for piece in mirrored])
    trace = tree_sum(
        [plane_trace]
        + [
            inside_permute(plane_trace, lambda o, h, g, d=d: (o, h, g ^ d))
            for d in range(1, n_col)
        ]
    )
    trace_value = trace.sum() / (blocks_total * side * side)
    return commutator.reshape(step_dir.shape), trace_value


def solution(mesh):
    in_specs = (P(),) + (P("row", "col", None, None),) * 4
    out_specs = (P("row", "col", None, None), P())
    return jax.shard_map(
        functools.partial(per_device, mesh.shape["row"], mesh.shape["col"]),
        mesh=mesh,
        in_specs=in_specs,
        out_specs=out_specs,
        check_vma=False,
    )
```

```python
import functools

import jax
import jax.numpy as jnp
from jax import lax
from jax.experimental import pallas as pl
from jax.experimental.pallas import tpu as pltpu
from jax.sharding import PartitionSpec as P

CORES = 2


def row_major_perm(n_row, n_col, target):
    pairs = []
    for r in range(n_row):
        for c in range(n_col):
            to_r, to_c = target(r, c)
            pairs.append((r * n_col + c, to_r * n_col + to_c))
    return pairs


def start_copies(pairs, sems):
    copies = [pltpu.make_async_copy(*pair, sems.at[i]) for i, pair in enumerate(pairs)]
    for copy in copies:
        copy.start()
    return copies


def wait_for(copies):
    for copy in copies:
        copy.wait()


def into(pieces, scratch, count):
    scratch[len(pieces) * count] = jnp.zeros(scratch.shape[1:], scratch.dtype)
    return [
        (piece, scratch.at[pl.ds(index * count, count)]) for index, piece in enumerate(pieces)
    ]


def multiply(index_ref, index_at, left_of, right, results, outs, sems, rows, slots, contract):
    copies = []
    for d in range(len(outs) - 1, -1, -1):
        for i in range(rows):
            left = left_of(i)
            for s in range(slots):
                base = index_at + ((d * rows + i) * slots + s) * slots
                blocks = jnp.concatenate(
                    [right[index_ref[base + a]] for a in range(slots)], axis=1
                )
                value = lax.dot_general(
                    blocks,
                    left,
                    (((1,), (contract,)), ((), ())),
                    preferred_element_type=jnp.float32,
                ).astype(results[d].dtype)
                if len(results[d].shape) == 3:
                    results[d][i * slots + s] = value
                else:
                    side = value.shape[0]
                    results[d][pl.ds((i * slots + s) * side, side)] = value
        copy = pltpu.make_async_copy(results[d], outs[d], sems.at[d])
        copy.start()
        copies.append(copy)
    wait_for(copies)


def split_results(first, others):
    return [first] + [others.at[d] for d in range(others.shape[0])]


def first_kernel(rows, slots, n_pieces, n_early, index_at, index_ref, left_ref, *refs):
    pieces, outs = refs[:n_pieces], refs[n_pieces + n_early : -6]
    right, left, first, others, sems, out_sems = refs[-6:]
    wait_for(start_copies(into(pieces, right, rows * slots) + [(left_ref, left)], sems))

    def left_of(i):
        return jnp.concatenate([left[i * slots + a] for a in range(slots)], axis=1)

    results = split_results(first, others)
    multiply(index_ref, index_at, left_of, right, results, outs, out_sems, rows, slots, 1)


def second_kernel(rows, slots, n_pieces, n_out, index_at, index_ref, *refs):
    pieces, parts = refs[:n_pieces], refs[n_pieces : n_pieces + n_out]
    right, left, part_first, part_others, first, others, sems, out_sems = refs[-8:]
    outs = refs[n_pieces + n_out : -8]
    held = split_results(part_first, part_others)
    wait_for(start_copies(list(zip(parts, held)) + into(pieces, right, rows * slots), sems))
    for b in range(rows * slots):
        value = held[0][b]
        for part in held[1:]:
            value = value + part[b].astype(jnp.float32)
        left[b] = value.astype(jnp.bfloat16)

    def left_of(i):
        return jnp.concatenate([left[i * slots + a] for a in range(slots)], axis=0)

    results = split_results(first, others)
    multiply(index_ref, index_at, left_of, right, results, outs, out_sems, rows, slots, 0)


def two_parts(x):
    high = x.astype(jnp.bfloat16)
    low = (x - high.astype(jnp.float32)).astype(jnp.bfloat16)
    return jnp.concatenate([high, low], axis=0)


def one_part(x):
    x = x.astype(jnp.float32)
    half = x.shape[0] // 2
    return x[:half] + x[half:]


def tree_sum(values):
    while len(values) > 1:
        values = [values[i] + values[i + 1] for i in range(0, len(values), 2)]
    return values[0]


def third_kernel(rows, slots, n_pieces, n_mirror, index_at, mirror_at, index_ref, own_ref, *refs):
    pieces, mirrored = refs[:n_pieces], refs[n_pieces : n_pieces + n_mirror]
    *outs, trace = refs[n_pieces + n_mirror : -8]
    right, mirror, own, left, first, others, sems, out_sems = refs[-8:]
    pairs = into(pieces, right, rows * slots) + into(mirrored, mirror, rows * slots) + [(own_ref, own)]
    wait_for(start_copies(pairs, sems))
    blocks, side = rows * slots, right.shape[1]
    part_rows = trace.shape[0] // 2
    total_trace = jnp.zeros((part_rows, side), jnp.float32)
    for b in range(blocks):
        other = mirror[index_ref[mirror_at + b]].astype(jnp.float32).T
        value = (-(own[b].astype(jnp.float32) + other)).astype(jnp.bfloat16)
        left[b] = value
        product = value.astype(jnp.float32) * right[b].astype(jnp.float32).T
        total_trace = total_trace + product.reshape(-1, part_rows, side).sum(0)
    total_trace = two_parts(total_trace)
    trace[...] = total_trace
    results = split_results(first, others)
    for result in results[1:]:
        result[pl.ds(blocks * side, 2 * part_rows)] = total_trace

    def left_of(i):
        return jnp.concatenate([left[i * slots + a] for a in range(slots)], axis=0)

    multiply(index_ref, index_at, left_of, right, results, outs, out_sems, rows, slots, 0)


def sum_kernel(n_out, trace_ref, own_ref, *refs):
    parts, (out, own, others, result, sems, out_sems) = refs[: n_out - 1], refs[n_out - 1 :]
    pairs = [(part, others.at[d]) for d, part in enumerate(parts)]
    wait_for(start_copies([(own_ref, own)] + pairs, sems))
    blocks, side = own.shape[:2]
    for b in range(blocks):
        value = own[b]
        for d in range(n_out - 1):
            value = value + others[d, pl.ds(b * side, side)].astype(jnp.float32)
        result[pl.ds(b * side, side)] = value.astype(result.dtype)
    tail = pl.ds(blocks * side, trace_ref.shape[0])
    tiles = [trace_ref[...]] + [others[d, tail] for d in range(n_out - 1)]
    result[tail] = two_parts(tree_sum([one_part(tile) for tile in tiles]))
    wait_for(start_copies([(result, out)], out_sems))


def last_kernel(n_mirror, blocks, mirror_at, index_ref, own_ref, *refs):
    mirrored, (out, mirror, own, result, sems, out_sems) = refs[:n_mirror], refs[n_mirror:]
    side = own.shape[1]
    count = blocks * side
    body = pl.ds(0, count)
    pairs = [(own_ref.at[body], own)] + [
        (piece.at[body], mirror.at[pl.ds(t * count, count)]) for t, piece in enumerate(mirrored)
    ]
    copies = start_copies(pairs, sems)
    mirror[pl.ds(n_mirror * count, side)] = jnp.zeros((side, side), mirror.dtype)
    wait_for(copies)
    for b in range(blocks):
        start = pl.multiple_of(index_ref[mirror_at + b] * side, side)
        other = mirror[pl.ds(start, side)].astype(jnp.float32)
        value = other - own[pl.ds(b * side, side)].astype(jnp.float32).T
        result[b] = value.astype(result.dtype)
    wait_for(start_copies([(result, out)], out_sems))


def per_device(n_row, n_col, block_cols, step_dir, intersection, density, kohn_sham):
    rows, slots, side = step_dir.shape[:3]
    blocks = rows * slots
    blocks_total = block_cols.shape[0]
    inner = n_row // n_col
    outer = n_row // inner
    assert inner == CORES and outer == n_col and outer & (outer - 1) == 0
    row_index = lax.axis_index("row")
    col_index = lax.axis_index("col")
    bf16, f32 = jnp.bfloat16, jnp.float32

    def at(o, h, g):
        return o * inner + g % inner, (g // inner) * CORES + h

    def inside(r, c):
        return r // inner, c % CORES, (c // CORES) * inner + r % inner

    def spread(o, g):
        bits = (n_col - 1).bit_length()
        return g ^ sum(((o >> b) & 1) << (bits - 1 - b) for b in range(bits))

    def at_spread(o, h, g):
        return at(o, h, spread(o, g))

    def inside_spread(r, c):
        o, h, p = inside(r, c)
        return o, h, spread(o, p)

    o_in, h_in, g_in = inside(row_index, col_index)

    by_group = block_cols.reshape(blocks_total, n_col, slots)
    mirror_cols = lax.dynamic_slice_in_dim(by_group, o_in, 1, 1)[:, 0]

    def rows_of(o, h):
        return lax.dynamic_slice_in_dim(by_group, (o * inner + h) * rows, rows, 0)

    def group_cols_of(cols, g):
        return lax.dynamic_slice_in_dim(cols, g, 1, 1)[:, 0]

    own_rows = rows_of(o_in, h_in)

    def index_table(group, first_out):
        own_cols, group_cols = group_cols_of(own_rows, group), group_cols_of(by_group, group)
        wanted = own_rows[:, first_out ^ jnp.arange(n_col)].transpose(1, 0, 2)
        safe = jnp.clip(wanted, 0, blocks_total - 1)
        matched = (
            (group_cols[safe][..., None, :] == own_cols[None, :, None, :, None])
            & (wanted >= 0)[..., None, None]
            & (own_cols >= 0)[None, :, None, :, None]
        )
        piece = ((safe // rows % inner) ^ h_in) * outer + (safe // rows // inner ^ o_in)
        slot = ((piece * rows + safe % rows) * slots)[..., None] + jnp.argmax(matched, axis=-1)
        return jnp.where(matched.any(-1), slot, n_row * blocks).astype(jnp.int32).reshape(-1)

    spread_in = spread(o_in, g_in)
    all_tables = [index_table(g_in, g_in), index_table(g_in, spread_in)]

    def mirror_table(h, cols):
        own_ids = (o_in * inner + h) * rows + jnp.arange(rows)
        safe_own = jnp.clip(cols, 0, blocks_total - 1)
        found = mirror_cols[safe_own] == own_ids[:, None, None]
        source = (safe_own // rows % inner) ^ h
        return jnp.where(
            cols >= 0,
            (source * rows + safe_own % rows) * slots + jnp.argmax(found, axis=-1),
            inner * blocks,
        ).astype(jnp.int32).reshape(-1)

    all_tables += [mirror_table(h_in, group_cols_of(own_rows, g)) for g in (g_in, spread_in)]
    starts = [sum(table.size for table in all_tables[:t]) for t in range(len(all_tables))]
    first_at, later_at, mirror_at, last_mirror_at = starts
    tables = jnp.concatenate(all_tables)

    smem = pl.BlockSpec(memory_space=pltpu.SMEM)
    vmem = pl.BlockSpec(memory_space=pltpu.VMEM)
    anywhere = pl.BlockSpec(memory_space=pl.ANY)

    def permute(x, target):
        return lax.ppermute(x, ("row", "col"), row_major_perm(n_row, n_col, target))

    def relayout(x, m=0, target=at):
        return permute(x, lambda r, c: target((r // inner) ^ m, r % inner, c))

    def inside_permute(x, move, source=inside, target=at):
        return permute(x, lambda r, c: target(*move(*source(r, c))))

    def share(x):
        return inside_permute(x, lambda o, h, g: (o, h ^ 1, g))

    def after(x, done):
        return lax.optimization_barrier((x, done))[0]

    def to_plane(x, m):
        return inside_permute(x, lambda o, h, g: (o ^ m, h, g))

    def share_all(pieces):
        return {m: share(piece) for m, piece in pieces.items()}

    def listed(pieces, shared):
        return [pieces[m] for m in range(outer)] + [shared[m] for m in range(outer)]

    def mirror(x, target):
        moved = inside_permute(x, lambda o, h, g: (g, h, o), inside_spread, target)
        return [moved, share(moved)]

    def exchange(outs):
        return [outs[0]] + [
            inside_permute(out, lambda o, h, g, d=d: (o, h, g ^ d))
            for d, out in enumerate(outs)
            if d
        ]

    def total_of(parts):
        value = parts[0]
        for part in parts[1:]:
            value = value + part.astype(f32)
        return value.astype(bf16)

    block_shape = (blocks, side, side)
    out_shapes = tuple(
        jax.ShapeDtypeStruct(block_shape, bf16 if d else f32) for d in range(n_col)
    )
    params = pltpu.CompilerParams(vmem_limit_bytes=14 * 2**20)

    def held(count):
        return pltpu.VMEM((count, side, side), bf16)

    def dma(count):
        return pltpu.SemaphoreType.DMA((count,))

    tail_shape = jax.ShapeDtypeStruct((16, side), bf16)
    long_shape = jax.ShapeDtypeStruct((blocks * side + tail_shape.shape[0], side), bf16)
    long_sums = [
        pltpu.VMEM(block_shape, f32),
        pltpu.VMEM((n_col - 1,) + long_shape.shape, bf16),
    ]
    sums = [pltpu.VMEM(block_shape, f32), pltpu.VMEM((n_col - 1,) + block_shape, bf16)]
    cost = pl.CostEstimate(
        flops=2 * n_col * blocks * slots * side**3,
        bytes_accessed=4 * 2**20,
        transcendentals=0,
    )

    flat = lambda x: x.reshape(block_shape)
    inter, dens, kohn = flat(intersection), flat(density), flat(kohn_sham)

    far_from = range(2, outer, 2)
    near = [*far_from, 1]

    inter_near = {m: relayout(inter, m) for m in near}
    inter_early = {0: relayout(inter)} | inter_near
    step = relayout(flat(step_dir))
    dens_own = relayout(dens)
    inter_far = {m + 1: to_plane(inter_near[m], 1) for m in far_from}
    dens_behind = after(dens_own, inter_near)
    dens_near = {m: to_plane(dens_behind, m) for m in far_from}
    dens_behind, kohn = after((dens_own, kohn), (inter_near, inter_far))
    dens_near[1] = to_plane(dens_behind, 1)
    kohn_own = relayout(kohn)
    inter_all = listed(inter_early | inter_far, share_all(inter_early) | share_all(inter_far))
    outs = pl.pallas_call(
        functools.partial(first_kernel, rows, slots, n_row, 1, first_at),
        out_shape=out_shapes,
        in_specs=[smem] + [anywhere] * (1 + n_row + 1),
        out_specs=(anywhere,) * n_col,
        scratch_shapes=[held(n_row * blocks + 1), held(blocks), *sums, dma(n_row + 1), dma(n_col)],
        compiler_params=params,
        cost_estimate=cost,
        name="scaled_step_product",
    )(tables, step, *inter_all, kohn_own)
    parts = exchange(outs)

    dens_beside = {0: share(dens_own)}
    dens_far = {m + 1: to_plane(after(dens_near[m], outs), 1) for m in far_from}
    dens_near, dens_far = after((dens_near, dens_far), parts[1:])
    dens_beside |= share_all(dens_near) | share_all(dens_far)
    dens_all = listed({0: dens_own} | dens_near | dens_far, dens_beside)
    outs = pl.pallas_call(
        functools.partial(second_kernel, rows, slots, n_row, n_col, later_at),
        out_shape=out_shapes,
        in_specs=[smem] + [anywhere] * (n_row + n_col),
        out_specs=(anywhere,) * n_col,
        scratch_shapes=[
            held(n_row * blocks + 1),
            held(blocks),
            *sums,
            *sums,
            dma(n_row + n_col),
            dma(n_col),
        ],
        compiler_params=params,
        cost_estimate=cost,
        name="change_product",
    )(tables, *dens_all, *parts)
    second_outs = outs
    total = total_of(exchange(outs))

    mirrored = mirror(total, at)
    own = inside_permute(total, lambda o, h, g: (o, h, g), inside_spread)
    kohn_own = after(kohn_own, second_outs)
    kohn_pieces = {0: kohn_own} | {m: to_plane(kohn_own, m) for m in far_from}
    kohn_beside = share_all(kohn_pieces)
    kohn_last = {m + 1: to_plane(kohn_pieces[m], 1) for m in range(0, outer, 2)}
    kohn_last = after(kohn_last, total)
    kohn_all = listed(kohn_pieces | kohn_last, kohn_beside | share_all(kohn_last))
    *outs, trace = pl.pallas_call(
        functools.partial(third_kernel, rows, slots, n_row, inner, later_at, mirror_at),
        out_shape=out_shapes[:1] + (long_shape,) * (n_col - 1) + (tail_shape,),
        in_specs=[smem] + [anywhere] * (1 + n_row + inner),
        out_specs=(anywhere,) * n_col + (vmem,),
        scratch_shapes=[
            held(n_row * blocks + 1),
            held(inner * blocks + 1),
            held(blocks),
            held(blocks),
            *long_sums,
            dma(n_row + inner + 1),
            dma(n_col),
        ],
        compiler_params=params,
        cost_estimate=cost,
        name="commutator_product",
    )(tables, own, *kohn_all, *mirrored)
    own, *parts = exchange(outs)
    total = pl.pallas_call(
        functools.partial(sum_kernel, n_col),
        out_shape=long_shape,
        in_specs=[vmem] + [anywhere] * n_col,
        out_specs=anywhere,
        scratch_shapes=[*long_sums, pltpu.VMEM(long_shape.shape, bf16), dma(n_col), dma(1)],
        compiler_params=params,
        name="plane_sum",
    )(trace, own, *parts)
    mirrored = mirror(total, at_spread)

    commutator = pl.pallas_call(
        functools.partial(last_kernel, inner, blocks, last_mirror_at),
        out_shape=jax.ShapeDtypeStruct(block_shape, bf16),
        in_specs=[smem] + [anywhere] * (1 + inner),
        out_specs=anywhere,
        scratch_shapes=[
            pltpu.VMEM(((inner * blocks + 1) * side, side), bf16),
            pltpu.VMEM((blocks * side, side), bf16),
            held(blocks),
            dma(inner + 1),
            dma(1),
        ],
        compiler_params=params,
        name="commutator_difference",
    )(tables, total, *mirrored)
    commutator = inside_permute(
        commutator, lambda o, h, g: (o, h, g), inside_spread, lambda o, h, g: (o * inner + h, g)
    )

    trace = one_part(total[blocks * side :])
    trace = trace + share(trace)
    step = 1
    while step < outer:
        trace = trace + to_plane(trace, step)
        step *= 2
    trace_value = trace.sum() / (blocks_total * side * side)
    return commutator.reshape(step_dir.shape), trace_value


def solution(mesh):
    in_specs = (P(),) + (P("row", "col", None, None),) * 4
    out_specs = (P("row", "col", None, None), P())
    return jax.shard_map(
        functools.partial(per_device, mesh.shape["row"], mesh.shape["col"]),
        mesh=mesh,
        in_specs=in_specs,
        out_specs=out_specs,
        check_vma=False,
    )
```

```python
import functools

import jax
import jax.numpy as jnp
from jax import lax
from jax.experimental import pallas as pl
from jax.experimental.pallas import tpu as pltpu
from jax.sharding import PartitionSpec as P

CORES = 2


def row_major_perm(n_row, n_col, target):
    pairs = []
    for r in range(n_row):
        for c in range(n_col):
            to_r, to_c = target(r, c)
            pairs.append((r * n_col + c, to_r * n_col + to_c))
    return pairs


def start_copies(pairs, sems):
    copies = [pltpu.make_async_copy(*pair, sems.at[i]) for i, pair in enumerate(pairs)]
    for copy in copies:
        copy.start()
    return copies


def wait_for(copies):
    for copy in copies:
        copy.wait()


def into(pieces, scratch, count):
    scratch[len(pieces) * count] = jnp.zeros(scratch.shape[1:], scratch.dtype)
    return [
        (piece, scratch.at[pl.ds(index * count, count)]) for index, piece in enumerate(pieces)
    ]


def multiply(index_ref, index_at, left_of, right, results, outs, sems, rows, slots, contract):
    copies = []
    for d in range(len(outs) - 1, -1, -1):
        for i in range(rows):
            left = left_of(i)
            for s in range(slots):
                base = index_at + ((d * rows + i) * slots + s) * slots
                blocks = jnp.concatenate(
                    [right[index_ref[base + a]] for a in range(slots)], axis=1
                )
                value = lax.dot_general(
                    blocks,
                    left,
                    (((1,), (contract,)), ((), ())),
                    preferred_element_type=jnp.float32,
                ).astype(results[d].dtype)
                if len(results[d].shape) == 3:
                    results[d][i * slots + s] = value
                else:
                    side = value.shape[0]
                    results[d][pl.ds((i * slots + s) * side, side)] = value
        copy = pltpu.make_async_copy(results[d], outs[d], sems.at[d])
        copy.start()
        copies.append(copy)
    wait_for(copies)


def split_results(first, others):
    return [first] + [others.at[d] for d in range(others.shape[0])]


def first_kernel(rows, slots, n_pieces, n_early, index_at, index_ref, left_ref, *refs):
    pieces, outs = refs[:n_pieces], refs[n_pieces + n_early : -6]
    right, left, first, others, sems, out_sems = refs[-6:]
    wait_for(start_copies(into(pieces, right, rows * slots) + [(left_ref, left)], sems))

    def left_of(i):
        return jnp.concatenate([left[i * slots + a] for a in range(slots)], axis=1)

    results = split_results(first, others)
    multiply(index_ref, index_at, left_of, right, results, outs, out_sems, rows, slots, 1)


def second_kernel(rows, slots, n_pieces, n_out, index_at, index_ref, *refs):
    pieces, parts = refs[:n_pieces], refs[n_pieces : n_pieces + n_out]
    right, left, part_first, part_others, first, others, sems, out_sems = refs[-8:]
    outs = refs[n_pieces + n_out : -8]
    held = split_results(part_first, part_others)
    wait_for(start_copies(list(zip(parts, held)) + into(pieces, right, rows * slots), sems))
    for b in range(rows * slots):
        value = held[0][b]
        for part in held[1:]:
            value = value + part[b].astype(jnp.float32)
        left[b] = value.astype(jnp.bfloat16)

    def left_of(i):
        return jnp.concatenate([left[i * slots + a] for a in range(slots)], axis=0)

    results = split_results(first, others)
    multiply(index_ref, index_at, left_of, right, results, outs, out_sems, rows, slots, 0)


def two_parts(x):
    high = x.astype(jnp.bfloat16)
    low = (x - high.astype(jnp.float32)).astype(jnp.bfloat16)
    return jnp.concatenate([high, low], axis=0)


def one_part(x):
    x = x.astype(jnp.float32)
    half = x.shape[0] // 2
    return x[:half] + x[half:]


def tree_sum(values):
    while len(values) > 1:
        values = [values[i] + values[i + 1] for i in range(0, len(values), 2)]
    return values[0]


def third_kernel(rows, slots, n_pieces, n_mirror, index_at, mirror_at, index_ref, own_ref, *refs):
    pieces, mirrored = refs[:n_pieces], refs[n_pieces : n_pieces + n_mirror]
    *outs, trace = refs[n_pieces + n_mirror : -8]
    right, mirror, own, left, first, others, sems, out_sems = refs[-8:]
    pairs = into(pieces, right, rows * slots) + into(mirrored, mirror, rows * slots) + [(own_ref, own)]
    wait_for(start_copies(pairs, sems))
    blocks, side = rows * slots, right.shape[1]
    part_rows = trace.shape[0] // 2
    total_trace = jnp.zeros((part_rows, side), jnp.float32)
    for b in range(blocks):
        other = mirror[index_ref[mirror_at + b]].astype(jnp.float32).T
        value = (-(own[b].astype(jnp.float32) + other)).astype(jnp.bfloat16)
        left[b] = value
        product = value.astype(jnp.float32) * right[b].astype(jnp.float32).T
        total_trace = total_trace + product.reshape(-1, part_rows, side).sum(0)
    total_trace = two_parts(total_trace)
    trace[...] = total_trace
    results = split_results(first, others)
    for result in results[1:]:
        result[pl.ds(blocks * side, 2 * part_rows)] = total_trace

    def left_of(i):
        return jnp.concatenate([left[i * slots + a] for a in range(slots)], axis=0)

    multiply(index_ref, index_at, left_of, right, results, outs, out_sems, rows, slots, 0)


def sum_kernel(n_out, trace_ref, own_ref, *refs):
    parts, (out, own, others, result, sems, out_sems) = refs[: n_out - 1], refs[n_out - 1 :]
    pairs = [(part, others.at[d]) for d, part in enumerate(parts)]
    wait_for(start_copies([(own_ref, own)] + pairs, sems))
    blocks, side = own.shape[:2]
    for b in range(blocks):
        value = own[b]
        for d in range(n_out - 1):
            value = value + others[d, pl.ds(b * side, side)].astype(jnp.float32)
        result[pl.ds(b * side, side)] = value.astype(result.dtype)
    tail = pl.ds(blocks * side, trace_ref.shape[0])
    tiles = [trace_ref[...]] + [others[d, tail] for d in range(n_out - 1)]
    result[tail] = two_parts(tree_sum([one_part(tile) for tile in tiles]))
    wait_for(start_copies([(result, out)], out_sems))


def last_kernel(n_mirror, blocks, mirror_at, index_ref, own_ref, *refs):
    mirrored, (out, mirror, own, result, sems, out_sems) = refs[:n_mirror], refs[n_mirror:]
    side = own.shape[1]
    count = blocks * side
    body = pl.ds(0, count)
    pairs = [(own_ref.at[body], own)] + [
        (piece.at[body], mirror.at[pl.ds(t * count, count)]) for t, piece in enumerate(mirrored)
    ]
    copies = start_copies(pairs, sems)
    mirror[pl.ds(n_mirror * count, side)] = jnp.zeros((side, side), mirror.dtype)
    wait_for(copies)
    for b in range(blocks):
        start = pl.multiple_of(index_ref[mirror_at + b] * side, side)
        other = mirror[pl.ds(start, side)].astype(jnp.float32)
        value = other - own[pl.ds(b * side, side)].astype(jnp.float32).T
        result[b] = value.astype(result.dtype)
    wait_for(start_copies([(result, out)], out_sems))


def per_device(n_row, n_col, block_cols, step_dir, intersection, density, kohn_sham):
    rows, slots, side = step_dir.shape[:3]
    blocks = rows * slots
    blocks_total = block_cols.shape[0]
    inner = n_row // n_col
    outer = n_row // inner
    assert inner == CORES and outer == n_col and outer & (outer - 1) == 0
    row_index = lax.axis_index("row")
    col_index = lax.axis_index("col")
    bf16, f32 = jnp.bfloat16, jnp.float32

    def at(o, h, g):
        return o * inner + g % inner, (g // inner) * CORES + h

    def inside(r, c):
        return r // inner, c % CORES, (c // CORES) * inner + r % inner

    def spread(o, g):
        bits = (n_col - 1).bit_length()
        return g ^ sum(((o >> b) & 1) << (bits - 1 - b) for b in range(bits))

    def at_spread(o, h, g):
        return at(o, h, spread(o, g))

    def inside_spread(r, c):
        o, h, p = inside(r, c)
        return o, h, spread(o, p)

    o_in, h_in, g_in = inside(row_index, col_index)

    by_group = block_cols.reshape(blocks_total, n_col, slots)
    mirror_cols = lax.dynamic_slice_in_dim(by_group, o_in, 1, 1)[:, 0]

    def rows_of(o, h):
        return lax.dynamic_slice_in_dim(by_group, (o * inner + h) * rows, rows, 0)

    def group_cols_of(cols, g):
        return lax.dynamic_slice_in_dim(cols, g, 1, 1)[:, 0]

    own_rows = rows_of(o_in, h_in)

    def index_table(group, first_out):
        own_cols, group_cols = group_cols_of(own_rows, group), group_cols_of(by_group, group)
        wanted = own_rows[:, first_out ^ jnp.arange(n_col)].transpose(1, 0, 2)
        safe = jnp.clip(wanted, 0, blocks_total - 1)
        matched = (
            (group_cols[safe][..., None, :] == own_cols[None, :, None, :, None])
            & (wanted >= 0)[..., None, None]
            & (own_cols >= 0)[None, :, None, :, None]
        )
        piece = ((safe // rows % inner) ^ h_in) * outer + (safe // rows // inner ^ o_in)
        slot = ((piece * rows + safe % rows) * slots)[..., None] + jnp.argmax(matched, axis=-1)
        return jnp.where(matched.any(-1), slot, n_row * blocks).astype(jnp.int32).reshape(-1)

    spread_in = spread(o_in, g_in)
    all_tables = [index_table(g_in, g_in), index_table(g_in, spread_in)]

    def mirror_table(h, cols):
        own_ids = (o_in * inner + h) * rows + jnp.arange(rows)
        safe_own = jnp.clip(cols, 0, blocks_total - 1)
        found = mirror_cols[safe_own] == own_ids[:, None, None]
        source = (safe_own // rows % inner) ^ h
        return jnp.where(
            cols >= 0,
            (source * rows + safe_own % rows) * slots + jnp.argmax(found, axis=-1),
            inner * blocks,
        ).astype(jnp.int32).reshape(-1)

    all_tables += [mirror_table(h_in, group_cols_of(own_rows, g)) for g in (g_in, spread_in)]
    starts = [sum(table.size for table in all_tables[:t]) for t in range(len(all_tables))]
    first_at, later_at, mirror_at, last_mirror_at = starts
    tables = jnp.concatenate(all_tables)

    smem = pl.BlockSpec(memory_space=pltpu.SMEM)
    vmem = pl.BlockSpec(memory_space=pltpu.VMEM)
    anywhere = pl.BlockSpec(memory_space=pl.ANY)

    def permute(x, target):
        return lax.ppermute(x, ("row", "col"), row_major_perm(n_row, n_col, target))

    def relayout(x, m=0, target=at):
        return permute(x, lambda r, c: target((r // inner) ^ m, r % inner, c))

    def inside_permute(x, move, source=inside, target=at):
        return permute(x, lambda r, c: target(*move(*source(r, c))))

    def share(x):
        return inside_permute(x, lambda o, h, g: (o, h ^ 1, g))

    def after(x, done):
        return lax.optimization_barrier((x, done))[0]

    def to_plane(x, m):
        return inside_permute(x, lambda o, h, g: (o ^ m, h, g))

    def share_all(pieces):
        return {m: share(piece) for m, piece in pieces.items()}

    def listed(pieces, shared):
        return [pieces[m] for m in range(outer)] + [shared[m] for m in range(outer)]

    def mirror(x, target):
        return inside_permute(x, lambda o, h, g: (g, h, o), inside_spread, target)

    def exchange(outs):
        return [outs[0]] + [
            inside_permute(out, lambda o, h, g, d=d: (o, h, g ^ d))
            for d, out in enumerate(outs)
            if d
        ]

    def total_of(parts):
        value = parts[0]
        for part in parts[1:]:
            value = value + part.astype(f32)
        return value.astype(bf16)

    block_shape = (blocks, side, side)
    out_shapes = tuple(
        jax.ShapeDtypeStruct(block_shape, bf16 if d else f32) for d in range(n_col)
    )
    params = pltpu.CompilerParams(vmem_limit_bytes=14 * 2**20)

    def held(count):
        return pltpu.VMEM((count, side, side), bf16)

    def dma(count):
        return pltpu.SemaphoreType.DMA((count,))

    tail_shape = jax.ShapeDtypeStruct((16, side), bf16)
    long_shape = jax.ShapeDtypeStruct((blocks * side + tail_shape.shape[0], side), bf16)
    long_sums = [
        pltpu.VMEM(block_shape, f32),
        pltpu.VMEM((n_col - 1,) + long_shape.shape, bf16),
    ]
    sums = [pltpu.VMEM(block_shape, f32), pltpu.VMEM((n_col - 1,) + block_shape, bf16)]
    cost = pl.CostEstimate(
        flops=2 * n_col * blocks * slots * side**3,
        bytes_accessed=4 * 2**20,
        transcendentals=0,
    )

    flat = lambda x: x.reshape(block_shape)
    inter, dens, kohn = flat(intersection), flat(density), flat(kohn_sham)

    far_from = range(2, outer, 2)
    near = [*far_from, 1]

    inter_near = {m: relayout(inter, m) for m in near}
    inter_early = {0: relayout(inter)} | inter_near
    step = relayout(flat(step_dir))
    dens_own = relayout(dens)
    inter_far = {m + 1: to_plane(inter_near[m], 1) for m in far_from}
    dens_behind = after(dens_own, inter_near)
    dens_near = {m: to_plane(dens_behind, m) for m in far_from}
    dens_behind, kohn = after((dens_own, kohn), (inter_near, inter_far))
    dens_near[1] = to_plane(dens_behind, 1)
    kohn_own = relayout(kohn)
    inter_all = listed(inter_early | inter_far, share_all(inter_early) | share_all(inter_far))
    outs = pl.pallas_call(
        functools.partial(first_kernel, rows, slots, n_row, 1, first_at),
        out_shape=out_shapes,
        in_specs=[smem] + [anywhere] * (1 + n_row + 1),
        out_specs=(anywhere,) * n_col,
        scratch_shapes=[held(n_row * blocks + 1), held(blocks), *sums, dma(n_row + 1), dma(n_col)],
        compiler_params=params,
        cost_estimate=cost,
        name="scaled_step_product",
    )(tables, step, *inter_all, kohn_own)
    parts = exchange(outs)

    dens_beside = {0: share(dens_own)}
    dens_far = {m + 1: to_plane(after(dens_near[m], outs), 1) for m in far_from}
    kohn_behind = after(kohn_own, (dens_near, outs))
    kohn_pieces = {m: to_plane(kohn_behind, m) for m in far_from}
    dens_near, dens_far = after((dens_near, dens_far), parts[1:])
    dens_beside |= share_all(dens_near) | share_all(dens_far)
    dens_all = listed({0: dens_own} | dens_near | dens_far, dens_beside)
    outs = pl.pallas_call(
        functools.partial(second_kernel, rows, slots, n_row, n_col, later_at),
        out_shape=out_shapes,
        in_specs=[smem] + [anywhere] * (n_row + n_col),
        out_specs=(anywhere,) * n_col,
        scratch_shapes=[
            held(n_row * blocks + 1),
            held(blocks),
            *sums,
            *sums,
            dma(n_row + n_col),
            dma(n_col),
        ],
        compiler_params=params,
        cost_estimate=cost,
        name="change_product",
    )(tables, *dens_all, *parts)
    second_outs = outs
    total = total_of(exchange(outs))

    mirrored = [mirror(total, at)]
    mirrored.append(share(mirrored[0]))
    own = inside_permute(total, lambda o, h, g: (o, h, g), inside_spread)
    kohn_pieces = {0: kohn_own} | after(kohn_pieces, second_outs)
    kohn_beside = share_all(kohn_pieces)
    kohn_last = {m + 1: to_plane(kohn_pieces[m], 1) for m in range(0, outer, 2)}
    kohn_last = after(kohn_last, total)
    kohn_all = listed(kohn_pieces | kohn_last, kohn_beside | share_all(kohn_last))
    *outs, trace = pl.pallas_call(
        functools.partial(third_kernel, rows, slots, n_row, inner, later_at, mirror_at),
        out_shape=out_shapes[:1] + (long_shape,) * (n_col - 1) + (tail_shape,),
        in_specs=[smem] + [anywhere] * (1 + n_row + inner),
        out_specs=(anywhere,) * n_col + (vmem,),
        scratch_shapes=[
            held(n_row * blocks + 1),
            held(inner * blocks + 1),
            held(blocks),
            held(blocks),
            *long_sums,
            dma(n_row + inner + 1),
            dma(n_col),
        ],
        compiler_params=params,
        cost_estimate=cost,
        name="commutator_product",
    )(tables, own, *kohn_all, *mirrored)
    own, *parts = exchange(outs)
    total = pl.pallas_call(
        functools.partial(sum_kernel, n_col),
        out_shape=long_shape,
        in_specs=[vmem] + [anywhere] * n_col,
        out_specs=anywhere,
        scratch_shapes=[*long_sums, pltpu.VMEM(long_shape.shape, bf16), dma(n_col), dma(1)],
        compiler_params=params,
        name="plane_sum",
    )(trace, own, *parts)
    mirrored = [mirror(total, at_spread)]

    trace = one_part(total[blocks * side :])
    trace = trace + share(trace)
    step = 1
    while step < outer:
        trace = trace + to_plane(trace, step)
        step *= 2
    mirrored.append(share(after(mirrored[0], trace)))

    commutator = pl.pallas_call(
        functools.partial(last_kernel, inner, blocks, last_mirror_at),
        out_shape=jax.ShapeDtypeStruct(block_shape, bf16),
        in_specs=[smem] + [anywhere] * (1 + inner),
        out_specs=anywhere,
        scratch_shapes=[
            pltpu.VMEM(((inner * blocks + 1) * side, side), bf16),
            pltpu.VMEM((blocks * side, side), bf16),
            held(blocks),
            dma(inner + 1),
            dma(1),
        ],
        compiler_params=params,
        name="commutator_difference",
    )(tables, total, *mirrored)
    commutator = inside_permute(
        commutator, lambda o, h, g: (o, h, g), inside_spread, lambda o, h, g: (o * inner + h, g)
    )

    trace_value = trace.sum() / (blocks_total * side * side)
    return commutator.reshape(step_dir.shape), trace_value


def solution(mesh):
    in_specs = (P(),) + (P("row", "col", None, None),) * 4
    out_specs = (P("row", "col", None, None), P())
    return jax.shard_map(
        functools.partial(per_device, mesh.shape["row"], mesh.shape["col"]),
        mesh=mesh,
        in_specs=in_specs,
        out_specs=out_specs,
        check_vma=False,
    )
```

```python
import functools

import jax
import jax.numpy as jnp
from jax import lax
from jax.experimental import pallas as pl
from jax.experimental.pallas import tpu as pltpu
from jax.sharding import PartitionSpec as P

CORES = 2


def row_major_perm(n_row, n_col, target):
    pairs = []
    for r in range(n_row):
        for c in range(n_col):
            to_r, to_c = target(r, c)
            pairs.append((r * n_col + c, to_r * n_col + to_c))
    return pairs


def start_copies(pairs, sems):
    copies = [pltpu.make_async_copy(*pair, sems.at[i]) for i, pair in enumerate(pairs)]
    for copy in copies:
        copy.start()
    return copies


def wait_for(copies):
    for copy in copies:
        copy.wait()


def into(pieces, scratch, count):
    scratch[len(pieces) * count] = jnp.zeros(scratch.shape[1:], scratch.dtype)
    return [
        (piece, scratch.at[pl.ds(index * count, count)]) for index, piece in enumerate(pieces)
    ]


def multiply(index_ref, index_at, left_of, right, results, outs, sems, rows, slots, contract):
    copies = []
    for d in range(len(outs) - 1, -1, -1):
        for i in range(rows):
            left = left_of(i)
            for s in range(slots):
                base = index_at + ((d * rows + i) * slots + s) * slots
                blocks = jnp.concatenate(
                    [right[index_ref[base + a]] for a in range(slots)], axis=1
                )
                value = lax.dot_general(
                    blocks,
                    left,
                    (((1,), (contract,)), ((), ())),
                    preferred_element_type=jnp.float32,
                ).astype(results[d].dtype)
                if len(results[d].shape) == 3:
                    results[d][i * slots + s] = value
                else:
                    side = value.shape[0]
                    results[d][pl.ds((i * slots + s) * side, side)] = value
        copy = pltpu.make_async_copy(results[d], outs[d], sems.at[d])
        copy.start()
        copies.append(copy)
    wait_for(copies)


def split_results(first, others):
    return [first] + [others.at[d] for d in range(others.shape[0])]


def first_kernel(rows, slots, n_pieces, n_early, index_at, index_ref, left_ref, *refs):
    pieces, outs = refs[:n_pieces], refs[n_pieces + n_early : -6]
    right, left, first, others, sems, out_sems = refs[-6:]
    wait_for(start_copies(into(pieces, right, rows * slots) + [(left_ref, left)], sems))

    def left_of(i):
        return jnp.concatenate([left[i * slots + a] for a in range(slots)], axis=1)

    results = split_results(first, others)
    multiply(index_ref, index_at, left_of, right, results, outs, out_sems, rows, slots, 1)


def second_kernel(rows, slots, n_pieces, n_out, index_at, index_ref, *refs):
    pieces, parts = refs[:n_pieces], refs[n_pieces : n_pieces + n_out]
    right, left, part_first, part_others, first, others, sems, out_sems = refs[-8:]
    outs = refs[n_pieces + n_out : -8]
    held = split_results(part_first, part_others)
    wait_for(start_copies(list(zip(parts, held)) + into(pieces, right, rows * slots), sems))
    for b in range(rows * slots):
        value = held[0][b]
        for part in held[1:]:
            value = value + part[b].astype(jnp.float32)
        left[b] = value.astype(jnp.bfloat16)

    def left_of(i):
        return jnp.concatenate([left[i * slots + a] for a in range(slots)], axis=0)

    results = split_results(first, others)
    multiply(index_ref, index_at, left_of, right, results, outs, out_sems, rows, slots, 0)


def two_parts(x):
    high = x.astype(jnp.bfloat16)
    low = (x - high.astype(jnp.float32)).astype(jnp.bfloat16)
    return jnp.concatenate([high, low], axis=0)


def one_part(x):
    x = x.astype(jnp.float32)
    half = x.shape[0] // 2
    return x[:half] + x[half:]


def tree_sum(values):
    while len(values) > 1:
        values = [values[i] + values[i + 1] for i in range(0, len(values), 2)]
    return values[0]


def third_kernel(rows, slots, n_pieces, n_mirror, index_at, mirror_at, index_ref, own_ref, *refs):
    pieces, mirrored = refs[:n_pieces], refs[n_pieces : n_pieces + n_mirror]
    *outs, trace = refs[n_pieces + n_mirror : -8]
    right, mirror, own, left, first, others, sems, out_sems = refs[-8:]
    pairs = into(pieces, right, rows * slots) + into(mirrored, mirror, rows * slots) + [(own_ref, own)]
    wait_for(start_copies(pairs, sems))
    blocks, side = rows * slots, right.shape[1]
    part_rows = trace.shape[0] // 2
    total_trace = jnp.zeros((part_rows, side), jnp.float32)
    for b in range(blocks):
        other = mirror[index_ref[mirror_at + b]].astype(jnp.float32).T
        value = (-(own[b].astype(jnp.float32) + other)).astype(jnp.bfloat16)
        left[b] = value
        product = value.astype(jnp.float32) * right[b].astype(jnp.float32).T
        total_trace = total_trace + product.reshape(-1, part_rows, side).sum(0)
    total_trace = two_parts(total_trace)
    trace[...] = total_trace
    results = split_results(first, others)
    for result in results[1:]:
        result[pl.ds(blocks * side, 2 * part_rows)] = total_trace

    def left_of(i):
        return jnp.concatenate([left[i * slots + a] for a in range(slots)], axis=0)

    multiply(index_ref, index_at, left_of, right, results, outs, out_sems, rows, slots, 0)


def sum_kernel(n_out, trace_ref, own_ref, *refs):
    parts, (out, own, others, result, sems, out_sems) = refs[: n_out - 1], refs[n_out - 1 :]
    pairs = [(part, others.at[d]) for d, part in enumerate(parts)]
    wait_for(start_copies([(own_ref, own)] + pairs, sems))
    blocks, side = own.shape[:2]
    for b in range(blocks):
        value = own[b]
        for d in range(n_out - 1):
            value = value + others[d, pl.ds(b * side, side)].astype(jnp.float32)
        result[pl.ds(b * side, side)] = value.astype(result.dtype)
    tail = pl.ds(blocks * side, trace_ref.shape[0])
    tiles = [trace_ref[...]] + [others[d, tail] for d in range(n_out - 1)]
    result[tail] = two_parts(tree_sum([one_part(tile) for tile in tiles]))
    wait_for(start_copies([(result, out)], out_sems))


def last_kernel(n_mirror, blocks, mirror_at, index_ref, own_ref, *refs):
    mirrored, (out, mirror, own, result, sems, out_sems) = refs[:n_mirror], refs[n_mirror:]
    side = own.shape[1]
    count = blocks * side
    body = pl.ds(0, count)
    pairs = [(own_ref.at[body], own)] + [
        (piece.at[body], mirror.at[pl.ds(t * count, count)]) for t, piece in enumerate(mirrored)
    ]
    copies = start_copies(pairs, sems)
    mirror[pl.ds(n_mirror * count, side)] = jnp.zeros((side, side), mirror.dtype)
    wait_for(copies)
    for b in range(blocks):
        start = pl.multiple_of(index_ref[mirror_at + b] * side, side)
        other = mirror[pl.ds(start, side)].astype(jnp.float32)
        value = other - own[pl.ds(b * side, side)].astype(jnp.float32).T
        result[b] = value.astype(result.dtype)
    wait_for(start_copies([(result, out)], out_sems))


def per_device(n_row, n_col, block_cols, step_dir, intersection, density, kohn_sham):
    rows, slots, side = step_dir.shape[:3]
    blocks = rows * slots
    blocks_total = block_cols.shape[0]
    inner = n_row // n_col
    outer = n_row // inner
    assert inner == CORES and outer == n_col and outer & (outer - 1) == 0
    row_index = lax.axis_index("row")
    col_index = lax.axis_index("col")
    bf16, f32 = jnp.bfloat16, jnp.float32

    def at(o, h, g):
        return o * inner + g % inner, (g // inner) * CORES + h

    def inside(r, c):
        return r // inner, c % CORES, (c // CORES) * inner + r % inner

    def spread(o, g):
        bits = (n_col - 1).bit_length()
        return g ^ sum(((o >> b) & 1) << (bits - 1 - b) for b in range(bits))

    def at_spread(o, h, g):
        return at(o, h, spread(o, g))

    def inside_spread(r, c):
        o, h, p = inside(r, c)
        return o, h, spread(o, p)

    o_in, h_in, g_in = inside(row_index, col_index)

    by_group = block_cols.reshape(blocks_total, n_col, slots)
    mirror_cols = lax.dynamic_slice_in_dim(by_group, o_in, 1, 1)[:, 0]

    def rows_of(o, h):
        return lax.dynamic_slice_in_dim(by_group, (o * inner + h) * rows, rows, 0)

    def group_cols_of(cols, g):
        return lax.dynamic_slice_in_dim(cols, g, 1, 1)[:, 0]

    own_rows = rows_of(o_in, h_in)

    def index_table(group, first_out):
        own_cols, group_cols = group_cols_of(own_rows, group), group_cols_of(by_group, group)
        wanted = own_rows[:, first_out ^ jnp.arange(n_col)].transpose(1, 0, 2)
        safe = jnp.clip(wanted, 0, blocks_total - 1)
        matched = (
            (group_cols[safe][..., None, :] == own_cols[None, :, None, :, None])
            & (wanted >= 0)[..., None, None]
            & (own_cols >= 0)[None, :, None, :, None]
        )
        piece = ((safe // rows % inner) ^ h_in) * outer + (safe // rows // inner ^ o_in)
        slot = ((piece * rows + safe % rows) * slots)[..., None] + jnp.argmax(matched, axis=-1)
        return jnp.where(matched.any(-1), slot, n_row * blocks).astype(jnp.int32).reshape(-1)

    spread_in = spread(o_in, g_in)
    all_tables = [index_table(g_in, g_in), index_table(g_in, spread_in)]

    def mirror_table(h, cols):
        own_ids = (o_in * inner + h) * rows + jnp.arange(rows)
        safe_own = jnp.clip(cols, 0, blocks_total - 1)
        found = mirror_cols[safe_own] == own_ids[:, None, None]
        source = (safe_own // rows % inner) ^ h
        return jnp.where(
            cols >= 0,
            (source * rows + safe_own % rows) * slots + jnp.argmax(found, axis=-1),
            inner * blocks,
        ).astype(jnp.int32).reshape(-1)

    all_tables += [mirror_table(h_in, group_cols_of(own_rows, g)) for g in (g_in, spread_in)]
    starts = [sum(table.size for table in all_tables[:t]) for t in range(len(all_tables))]
    first_at, later_at, mirror_at, last_mirror_at = starts
    tables = jnp.concatenate(all_tables)

    smem = pl.BlockSpec(memory_space=pltpu.SMEM)
    vmem = pl.BlockSpec(memory_space=pltpu.VMEM)
    anywhere = pl.BlockSpec(memory_space=pl.ANY)

    def permute(x, target):
        return lax.ppermute(x, ("row", "col"), row_major_perm(n_row, n_col, target))

    def relayout(x, m=0, target=at):
        return permute(x, lambda r, c: target((r // inner) ^ m, r % inner, c))

    def inside_permute(x, move, source=inside, target=at):
        return permute(x, lambda r, c: target(*move(*source(r, c))))

    def share(x):
        return inside_permute(x, lambda o, h, g: (o, h ^ 1, g))

    def after(x, done):
        return lax.optimization_barrier((x, done))[0]

    def to_plane(x, m):
        return inside_permute(x, lambda o, h, g: (o ^ m, h, g))

    def share_all(pieces):
        return {m: share(piece) for m, piece in pieces.items()}

    def listed(pieces, shared):
        return [pieces[m] for m in range(outer)] + [shared[m] for m in range(outer)]

    def mirror(x, target):
        moved = inside_permute(x, lambda o, h, g: (g, h, o), inside_spread, target)
        return [moved, share(moved)]

    def exchange(outs):
        return [outs[0]] + [
            inside_permute(out, lambda o, h, g, d=d: (o, h, g ^ d))
            for d, out in enumerate(outs)
            if d
        ]

    def total_of(parts):
        value = parts[0]
        for part in parts[1:]:
            value = value + part.astype(f32)
        return value.astype(bf16)

    block_shape = (blocks, side, side)
    out_shapes = tuple(
        jax.ShapeDtypeStruct(block_shape, bf16 if d else f32) for d in range(n_col)
    )
    params = pltpu.CompilerParams(vmem_limit_bytes=14 * 2**20)

    def held(count):
        return pltpu.VMEM((count, side, side), bf16)

    def dma(count):
        return pltpu.SemaphoreType.DMA((count,))

    tail_shape = jax.ShapeDtypeStruct((16, side), bf16)
    long_shape = jax.ShapeDtypeStruct((blocks * side + tail_shape.shape[0], side), bf16)
    long_sums = [
        pltpu.VMEM(block_shape, f32),
        pltpu.VMEM((n_col - 1,) + long_shape.shape, bf16),
    ]
    sums = [pltpu.VMEM(block_shape, f32), pltpu.VMEM((n_col - 1,) + block_shape, bf16)]
    cost = pl.CostEstimate(
        flops=2 * n_col * blocks * slots * side**3,
        bytes_accessed=4 * 2**20,
        transcendentals=0,
    )

    flat = lambda x: x.reshape(block_shape)
    inter, dens, kohn = flat(intersection), flat(density), flat(kohn_sham)

    far_from = range(2, outer, 2)
    near = [*far_from, 1]

    inter_near = {m: relayout(inter, m) for m in near}
    inter_early = {0: relayout(inter)} | inter_near
    step = relayout(flat(step_dir))
    dens_own = relayout(dens)
    inter_far = {m + 1: to_plane(inter_near[m], 1) for m in far_from}
    dens_behind = after(dens_own, inter_near)
    dens_near = {m: to_plane(dens_behind, m) for m in far_from}
    dens_behind, kohn = after((dens_own, kohn), (inter_near, inter_far))
    dens_near[1] = to_plane(dens_behind, 1)
    kohn_own = relayout(kohn)
    inter_all = listed(inter_early | inter_far, share_all(inter_early) | share_all(inter_far))
    outs = pl.pallas_call(
        functools.partial(first_kernel, rows, slots, n_row, 1, first_at),
        out_shape=out_shapes,
        in_specs=[smem] + [anywhere] * (1 + n_row + 1),
        out_specs=(anywhere,) * n_col,
        scratch_shapes=[held(n_row * blocks + 1), held(blocks), *sums, dma(n_row + 1), dma(n_col)],
        compiler_params=params,
        cost_estimate=cost,
        name="scaled_step_product",
    )(tables, step, *inter_all, kohn_own)
    parts = exchange(outs)

    dens_beside = {0: share(dens_own)}
    dens_far = {m + 1: to_plane(after(dens_near[m], outs), 1) for m in far_from}
    kohn_behind = after(kohn_own, (dens_near, outs))
    kohn_pieces = {m: to_plane(kohn_behind, m) for m in far_from}
    dens_near = after(dens_near, parts[1:])
    dens_beside |= share_all(dens_near) | share_all(dens_far)
    dens_all = listed({0: dens_own} | dens_near | dens_far, dens_beside)
    outs = pl.pallas_call(
        functools.partial(second_kernel, rows, slots, n_row, n_col, later_at),
        out_shape=out_shapes,
        in_specs=[smem] + [anywhere] * (n_row + n_col),
        out_specs=(anywhere,) * n_col,
        scratch_shapes=[
            held(n_row * blocks + 1),
            held(blocks),
            *sums,
            *sums,
            dma(n_row + n_col),
            dma(n_col),
        ],
        compiler_params=params,
        cost_estimate=cost,
        name="change_product",
    )(tables, *dens_all, *parts)
    second_outs = outs
    total = total_of(exchange(outs))

    mirrored = mirror(total, at)
    own = inside_permute(total, lambda o, h, g: (o, h, g), inside_spread)
    kohn_pieces = {0: kohn_own} | after(kohn_pieces, second_outs)
    kohn_beside = share_all(kohn_pieces)
    kohn_last = {m + 1: to_plane(kohn_pieces[m], 1) for m in range(0, outer, 2)}
    kohn_last = after(kohn_last, total)
    kohn_all = listed(kohn_pieces | kohn_last, kohn_beside | share_all(kohn_last))
    *outs, trace = pl.pallas_call(
        functools.partial(third_kernel, rows, slots, n_row, inner, later_at, mirror_at),
        out_shape=out_shapes[:1] + (long_shape,) * (n_col - 1) + (tail_shape,),
        in_specs=[smem] + [anywhere] * (1 + n_row + inner),
        out_specs=(anywhere,) * n_col + (vmem,),
        scratch_shapes=[
            held(n_row * blocks + 1),
            held(inner * blocks + 1),
            held(blocks),
            held(blocks),
            *long_sums,
            dma(n_row + inner + 1),
            dma(n_col),
        ],
        compiler_params=params,
        cost_estimate=cost,
        name="commutator_product",
    )(tables, own, *kohn_all, *mirrored)
    own, *parts = exchange(outs)
    total = pl.pallas_call(
        functools.partial(sum_kernel, n_col),
        out_shape=long_shape,
        in_specs=[vmem] + [anywhere] * n_col,
        out_specs=anywhere,
        scratch_shapes=[*long_sums, pltpu.VMEM(long_shape.shape, bf16), dma(n_col), dma(1)],
        compiler_params=params,
        name="plane_sum",
    )(trace, own, *parts)
    mirrored = mirror(total, at_spread)

    commutator = pl.pallas_call(
        functools.partial(last_kernel, inner, blocks, last_mirror_at),
        out_shape=jax.ShapeDtypeStruct(block_shape, bf16),
        in_specs=[smem] + [anywhere] * (1 + inner),
        out_specs=anywhere,
        scratch_shapes=[
            pltpu.VMEM(((inner * blocks + 1) * side, side), bf16),
            pltpu.VMEM((blocks * side, side), bf16),
            held(blocks),
            dma(inner + 1),
            dma(1),
        ],
        compiler_params=params,
        name="commutator_difference",
    )(tables, total, *mirrored)
    commutator = inside_permute(
        commutator, lambda o, h, g: (o, h, g), inside_spread, lambda o, h, g: (o * inner + h, g)
    )

    plane_trace = tree_sum([one_part(piece[blocks * side :]) for piece in mirrored])
    trace = tree_sum(
        [plane_trace]
        + [
            inside_permute(plane_trace, lambda o, h, g, d=d: (o, h, g ^ d))
            for d in range(1, n_col)
        ]
    )
    trace_value = trace.sum() / (blocks_total * side * side)
    return commutator.reshape(step_dir.shape), trace_value


def solution(mesh):
    in_specs = (P(),) + (P("row", "col", None, None),) * 4
    out_specs = (P("row", "col", None, None), P())
    return jax.shard_map(
        functools.partial(per_device, mesh.shape["row"], mesh.shape["col"]),
        mesh=mesh,
        in_specs=in_specs,
        out_specs=out_specs,
        check_vma=False,
    )
```

```python
import functools

import jax
import jax.numpy as jnp
from jax import lax
from jax.experimental import pallas as pl
from jax.experimental.pallas import tpu as pltpu
from jax.sharding import PartitionSpec as P

CORES = 2


def row_major_perm(n_row, n_col, target):
    pairs = []
    for r in range(n_row):
        for c in range(n_col):
            to_r, to_c = target(r, c)
            pairs.append((r * n_col + c, to_r * n_col + to_c))
    return pairs


def start_copies(pairs, sems):
    copies = [pltpu.make_async_copy(*pair, sems.at[i]) for i, pair in enumerate(pairs)]
    for copy in copies:
        copy.start()
    return copies


def wait_for(copies):
    for copy in copies:
        copy.wait()


def into(pieces, scratch, count):
    scratch[len(pieces) * count] = jnp.zeros(scratch.shape[1:], scratch.dtype)
    return [
        (piece, scratch.at[pl.ds(index * count, count)]) for index, piece in enumerate(pieces)
    ]


def multiply(index_ref, index_at, left_of, right, results, outs, sems, rows, slots, contract):
    copies = []
    for d in range(len(outs) - 1, -1, -1):
        for i in range(rows):
            left = left_of(i)
            for s in range(slots):
                base = index_at + ((d * rows + i) * slots + s) * slots
                blocks = jnp.concatenate(
                    [right[index_ref[base + a]] for a in range(slots)], axis=1
                )
                value = lax.dot_general(
                    blocks,
                    left,
                    (((1,), (contract,)), ((), ())),
                    preferred_element_type=jnp.float32,
                ).astype(results[d].dtype)
                if len(results[d].shape) == 3:
                    results[d][i * slots + s] = value
                else:
                    side = value.shape[0]
                    results[d][pl.ds((i * slots + s) * side, side)] = value
        copy = pltpu.make_async_copy(results[d], outs[d], sems.at[d])
        copy.start()
        copies.append(copy)
    wait_for(copies)


def split_results(first, others):
    return [first] + [others.at[d] for d in range(others.shape[0])]


def first_kernel(rows, slots, n_pieces, n_early, index_at, index_ref, left_ref, *refs):
    pieces, outs = refs[:n_pieces], refs[n_pieces + n_early : -6]
    right, left, first, others, sems, out_sems = refs[-6:]
    wait_for(start_copies(into(pieces, right, rows * slots) + [(left_ref, left)], sems))

    def left_of(i):
        return jnp.concatenate([left[i * slots + a] for a in range(slots)], axis=1)

    results = split_results(first, others)
    multiply(index_ref, index_at, left_of, right, results, outs, out_sems, rows, slots, 1)


def second_kernel(rows, slots, n_pieces, n_out, index_at, index_ref, *refs):
    pieces, parts = refs[:n_pieces], refs[n_pieces : n_pieces + n_out]
    right, left, part_first, part_others, first, others, sems, out_sems = refs[-8:]
    outs = refs[n_pieces + n_out : -8]
    held = split_results(part_first, part_others)
    wait_for(start_copies(list(zip(parts, held)) + into(pieces, right, rows * slots), sems))
    for b in range(rows * slots):
        value = held[0][b]
        for part in held[1:]:
            value = value + part[b].astype(jnp.float32)
        left[b] = value.astype(jnp.bfloat16)

    def left_of(i):
        return jnp.concatenate([left[i * slots + a] for a in range(slots)], axis=0)

    results = split_results(first, others)
    multiply(index_ref, index_at, left_of, right, results, outs, out_sems, rows, slots, 0)


def two_parts(x):
    high = x.astype(jnp.bfloat16)
    low = (x - high.astype(jnp.float32)).astype(jnp.bfloat16)
    return jnp.concatenate([high, low], axis=0)


def one_part(x):
    x = x.astype(jnp.float32)
    half = x.shape[0] // 2
    return x[:half] + x[half:]


def tree_sum(values):
    while len(values) > 1:
        values = [values[i] + values[i + 1] for i in range(0, len(values), 2)]
    return values[0]


def third_kernel(rows, slots, n_pieces, n_mirror, index_at, mirror_at, index_ref, own_ref, *refs):
    pieces, mirrored = refs[:n_pieces], refs[n_pieces : n_pieces + n_mirror]
    *outs, trace = refs[n_pieces + n_mirror : -8]
    right, mirror, own, left, first, others, sems, out_sems = refs[-8:]
    pairs = into(pieces, right, rows * slots) + into(mirrored, mirror, rows * slots) + [(own_ref, own)]
    wait_for(start_copies(pairs, sems))
    blocks, side = rows * slots, right.shape[1]
    part_rows = trace.shape[0] // 2
    total_trace = jnp.zeros((part_rows, side), jnp.float32)
    for b in range(blocks):
        other = mirror[index_ref[mirror_at + b]].astype(jnp.float32).T
        value = (-(own[b].astype(jnp.float32) + other)).astype(jnp.bfloat16)
        left[b] = value
        product = value.astype(jnp.float32) * right[b].astype(jnp.float32).T
        total_trace = total_trace + product.reshape(-1, part_rows, side).sum(0)
    total_trace = two_parts(total_trace)
    trace[...] = total_trace
    results = split_results(first, others)
    for result in results[1:]:
        result[pl.ds(blocks * side, 2 * part_rows)] = total_trace

    def left_of(i):
        return jnp.concatenate([left[i * slots + a] for a in range(slots)], axis=0)

    multiply(index_ref, index_at, left_of, right, results, outs, out_sems, rows, slots, 0)


def sum_kernel(n_out, trace_ref, own_ref, *refs):
    parts, (out, own, others, result, sems, out_sems) = refs[: n_out - 1], refs[n_out - 1 :]
    pairs = [(part, others.at[n_out - 2 - i]) for i, part in enumerate(parts)]
    wait_for(start_copies([(own_ref, own)] + pairs, sems))
    blocks, side = own.shape[:2]
    for b in range(blocks):
        value = own[b]
        for d in range(n_out - 1):
            value = value + others[d, pl.ds(b * side, side)].astype(jnp.float32)
        result[pl.ds(b * side, side)] = value.astype(result.dtype)
    tail = pl.ds(blocks * side, trace_ref.shape[0])
    tiles = [trace_ref[...]] + [others[d, tail] for d in range(n_out - 1)]
    result[tail] = two_parts(tree_sum([one_part(tile) for tile in tiles]))
    wait_for(start_copies([(result, out)], out_sems))


def last_kernel(n_mirror, blocks, mirror_at, index_ref, own_ref, *refs):
    mirrored, (out, mirror, own, result, sems, out_sems) = refs[:n_mirror], refs[n_mirror:]
    side = own.shape[1]
    count = blocks * side
    body = pl.ds(0, count)
    pairs = [(own_ref.at[body], own)] + [
        (piece.at[body], mirror.at[pl.ds(t * count, count)]) for t, piece in enumerate(mirrored)
    ]
    copies = start_copies(pairs, sems)
    mirror[pl.ds(n_mirror * count, side)] = jnp.zeros((side, side), mirror.dtype)
    wait_for(copies)
    for b in range(blocks):
        start = pl.multiple_of(index_ref[mirror_at + b] * side, side)
        other = mirror[pl.ds(start, side)].astype(jnp.float32)
        value = other - own[pl.ds(b * side, side)].astype(jnp.float32).T
        result[b] = value.astype(result.dtype)
    wait_for(start_copies([(result, out)], out_sems))


def per_device(n_row, n_col, block_cols, step_dir, intersection, density, kohn_sham):
    rows, slots, side = step_dir.shape[:3]
    blocks = rows * slots
    blocks_total = block_cols.shape[0]
    inner = n_row // n_col
    outer = n_row // inner
    assert inner == CORES and outer == n_col and outer & (outer - 1) == 0
    row_index = lax.axis_index("row")
    col_index = lax.axis_index("col")
    bf16, f32 = jnp.bfloat16, jnp.float32

    def at(o, h, g):
        return o * inner + g % inner, (g // inner) * CORES + h

    def inside(r, c):
        return r // inner, c % CORES, (c // CORES) * inner + r % inner

    def spread(o, g):
        bits = (n_col - 1).bit_length()
        return g ^ sum(((o >> b) & 1) << (bits - 1 - b) for b in range(bits))

    def at_spread(o, h, g):
        return at(o, h, spread(o, g))

    def inside_spread(r, c):
        o, h, p = inside(r, c)
        return o, h, spread(o, p)

    o_in, h_in, g_in = inside(row_index, col_index)

    by_group = block_cols.reshape(blocks_total, n_col, slots)
    mirror_cols = lax.dynamic_slice_in_dim(by_group, o_in, 1, 1)[:, 0]

    def rows_of(o, h):
        return lax.dynamic_slice_in_dim(by_group, (o * inner + h) * rows, rows, 0)

    def group_cols_of(cols, g):
        return lax.dynamic_slice_in_dim(cols, g, 1, 1)[:, 0]

    own_rows = rows_of(o_in, h_in)

    def index_table(group, first_out):
        own_cols, group_cols = group_cols_of(own_rows, group), group_cols_of(by_group, group)
        wanted = own_rows[:, first_out ^ jnp.arange(n_col)].transpose(1, 0, 2)
        safe = jnp.clip(wanted, 0, blocks_total - 1)
        matched = (
            (group_cols[safe][..., None, :] == own_cols[None, :, None, :, None])
            & (wanted >= 0)[..., None, None]
            & (own_cols >= 0)[None, :, None, :, None]
        )
        piece = ((safe // rows % inner) ^ h_in) * outer + (safe // rows // inner ^ o_in)
        slot = ((piece * rows + safe % rows) * slots)[..., None] + jnp.argmax(matched, axis=-1)
        return jnp.where(matched.any(-1), slot, n_row * blocks).astype(jnp.int32).reshape(-1)

    spread_in = spread(o_in, g_in)
    all_tables = [index_table(g_in, g_in), index_table(g_in, spread_in)]

    def mirror_table(h, cols):
        own_ids = (o_in * inner + h) * rows + jnp.arange(rows)
        safe_own = jnp.clip(cols, 0, blocks_total - 1)
        found = mirror_cols[safe_own] == own_ids[:, None, None]
        source = (safe_own // rows % inner) ^ h
        return jnp.where(
            cols >= 0,
            (source * rows + safe_own % rows) * slots + jnp.argmax(found, axis=-1),
            inner * blocks,
        ).astype(jnp.int32).reshape(-1)

    all_tables += [mirror_table(h_in, group_cols_of(own_rows, g)) for g in (g_in, spread_in)]
    starts = [sum(table.size for table in all_tables[:t]) for t in range(len(all_tables))]
    first_at, later_at, mirror_at, last_mirror_at = starts
    tables = jnp.concatenate(all_tables)

    smem = pl.BlockSpec(memory_space=pltpu.SMEM)
    vmem = pl.BlockSpec(memory_space=pltpu.VMEM)
    anywhere = pl.BlockSpec(memory_space=pl.ANY)

    def permute(x, target):
        return lax.ppermute(x, ("row", "col"), row_major_perm(n_row, n_col, target))

    def relayout(x, m=0, target=at):
        return permute(x, lambda r, c: target((r // inner) ^ m, r % inner, c))

    def inside_permute(x, move, source=inside, target=at):
        return permute(x, lambda r, c: target(*move(*source(r, c))))

    def share(x):
        return inside_permute(x, lambda o, h, g: (o, h ^ 1, g))

    def after(x, done):
        return lax.optimization_barrier((x, done))[0]

    def to_plane(x, m):
        return inside_permute(x, lambda o, h, g: (o ^ m, h, g))

    def share_all(pieces):
        return {m: share(piece) for m, piece in pieces.items()}

    def listed(pieces, shared):
        return [pieces[m] for m in range(outer)] + [shared[m] for m in range(outer)]

    def mirror(x, target):
        moved = inside_permute(x, lambda o, h, g: (g, h, o), inside_spread, target)
        return [moved, share(moved)]

    def exchange(outs):
        return [outs[0]] + [
            inside_permute(outs[d], lambda o, h, g, d=d: (o, h, g ^ d))
            for d in range(len(outs) - 1, 0, -1)
        ]

    def total_of(parts):
        value = parts[0]
        for part in parts[1:]:
            value = value + part.astype(f32)
        return value.astype(bf16)

    block_shape = (blocks, side, side)
    out_shapes = tuple(
        jax.ShapeDtypeStruct(block_shape, bf16 if d else f32) for d in range(n_col)
    )
    params = pltpu.CompilerParams(vmem_limit_bytes=14 * 2**20)

    def held(count):
        return pltpu.VMEM((count, side, side), bf16)

    def dma(count):
        return pltpu.SemaphoreType.DMA((count,))

    tail_shape = jax.ShapeDtypeStruct((16, side), bf16)
    long_shape = jax.ShapeDtypeStruct((blocks * side + tail_shape.shape[0], side), bf16)
    long_sums = [
        pltpu.VMEM(block_shape, f32),
        pltpu.VMEM((n_col - 1,) + long_shape.shape, bf16),
    ]
    sums = [pltpu.VMEM(block_shape, f32), pltpu.VMEM((n_col - 1,) + block_shape, bf16)]
    cost = pl.CostEstimate(
        flops=2 * n_col * blocks * slots * side**3,
        bytes_accessed=4 * 2**20,
        transcendentals=0,
    )

    flat = lambda x: x.reshape(block_shape)
    inter, dens, kohn = flat(intersection), flat(density), flat(kohn_sham)

    far_from = range(2, outer, 2)
    near = [*far_from, 1]

    inter_near = {m: relayout(inter, m) for m in near}
    inter_early = {0: relayout(inter)} | inter_near
    step = relayout(flat(step_dir))
    dens_own = relayout(dens)
    inter_far = {m + 1: to_plane(inter_near[m], 1) for m in far_from}
    dens_behind = after(dens_own, inter_near)
    dens_near = {m: to_plane(dens_behind, m) for m in far_from}
    dens_behind, kohn = after((dens_own, kohn), (inter_near, inter_far))
    dens_near[1] = to_plane(dens_behind, 1)
    kohn_own = relayout(kohn)
    inter_all = listed(inter_early | inter_far, share_all(inter_early) | share_all(inter_far))
    outs = pl.pallas_call(
        functools.partial(first_kernel, rows, slots, n_row, 0, first_at),
        out_shape=out_shapes,
        in_specs=[smem] + [anywhere] * (1 + n_row),
        out_specs=(anywhere,) * n_col,
        scratch_shapes=[held(n_row * blocks + 1), held(blocks), *sums, dma(n_row + 1), dma(n_col)],
        compiler_params=params,
        cost_estimate=cost,
        name="scaled_step_product",
    )(tables, step, *inter_all)
    parts = exchange(outs)

    dens_beside = {0: share(dens_own)}
    dens_far = {m + 1: to_plane(after(dens_near[m], outs), 1) for m in far_from}
    kohn_behind = after(kohn_own, (dens_near, outs))
    kohn_pieces = {m: to_plane(kohn_behind, m) for m in far_from}
    dens_near = after(dens_near, parts[1:])
    dens_beside |= share_all(dens_near) | share_all(dens_far)
    dens_all = listed({0: dens_own} | dens_near | dens_far, dens_beside)
    outs = pl.pallas_call(
        functools.partial(second_kernel, rows, slots, n_row, n_col, later_at),
        out_shape=out_shapes,
        in_specs=[smem] + [anywhere] * (n_row + n_col),
        out_specs=(anywhere,) * n_col,
        scratch_shapes=[
            held(n_row * blocks + 1),
            held(blocks),
            *sums,
            *sums,
            dma(n_row + n_col),
            dma(n_col),
        ],
        compiler_params=params,
        cost_estimate=cost,
        name="change_product",
    )(tables, *dens_all, *parts)
    second_outs = outs
    total = total_of(exchange(outs))

    mirrored = mirror(total, at)
    own = inside_permute(total, lambda o, h, g: (o, h, g), inside_spread)
    kohn_pieces = {0: kohn_own} | after(kohn_pieces, second_outs)
    kohn_beside = share_all(kohn_pieces)
    kohn_last = {m + 1: to_plane(kohn_pieces[m], 1) for m in range(0, outer, 2)}
    kohn_last = after(kohn_last, total)
    kohn_all = listed(kohn_pieces | kohn_last, kohn_beside | share_all(kohn_last))
    *outs, trace = pl.pallas_call(
        functools.partial(third_kernel, rows, slots, n_row, inner, later_at, mirror_at),
        out_shape=out_shapes[:1] + (long_shape,) * (n_col - 1) + (tail_shape,),
        in_specs=[smem] + [anywhere] * (1 + n_row + inner),
        out_specs=(anywhere,) * n_col + (vmem,),
        scratch_shapes=[
            held(n_row * blocks + 1),
            held(inner * blocks + 1),
            held(blocks),
            held(blocks),
            *long_sums,
            dma(n_row + inner + 1),
            dma(n_col),
        ],
        compiler_params=params,
        cost_estimate=cost,
        name="commutator_product",
    )(tables, own, *kohn_all, *mirrored)
    own, *parts = exchange(outs)
    total = pl.pallas_call(
        functools.partial(sum_kernel, n_col),
        out_shape=long_shape,
        in_specs=[vmem] + [anywhere] * n_col,
        out_specs=anywhere,
        scratch_shapes=[*long_sums, pltpu.VMEM(long_shape.shape, bf16), dma(n_col), dma(1)],
        compiler_params=params,
        name="plane_sum",
    )(trace, own, *parts)
    mirrored = mirror(total, at_spread)

    commutator = pl.pallas_call(
        functools.partial(last_kernel, inner, blocks, last_mirror_at),
        out_shape=jax.ShapeDtypeStruct(block_shape, bf16),
        in_specs=[smem] + [anywhere] * (1 + inner),
        out_specs=anywhere,
        scratch_shapes=[
            pltpu.VMEM(((inner * blocks + 1) * side, side), bf16),
            pltpu.VMEM((blocks * side, side), bf16),
            held(blocks),
            dma(inner + 1),
            dma(1),
        ],
        compiler_params=params,
        name="commutator_difference",
    )(tables, total, *mirrored)
    commutator = inside_permute(
        commutator, lambda o, h, g: (o, h, g), inside_spread, lambda o, h, g: (o * inner + h, g)
    )

    plane_trace = tree_sum([one_part(piece[blocks * side :]) for piece in mirrored])
    trace = tree_sum(
        [plane_trace]
        + [
            inside_permute(plane_trace, lambda o, h, g, d=d: (o, h, g ^ d))
            for d in range(1, n_col)
        ]
    )
    trace_value = trace.sum() / (blocks_total * side * side)
    return commutator.reshape(step_dir.shape), trace_value


def solution(mesh):
    in_specs = (P(),) + (P("row", "col", None, None),) * 4
    out_specs = (P("row", "col", None, None), P())
    return jax.shard_map(
        functools.partial(per_device, mesh.shape["row"], mesh.shape["col"]),
        mesh=mesh,
        in_specs=in_specs,
        out_specs=out_specs,
        check_vma=False,
    )
```

```python
import functools

import jax
import jax.numpy as jnp
from jax import lax
from jax.experimental import pallas as pl
from jax.experimental.pallas import tpu as pltpu
from jax.sharding import PartitionSpec as P

CORES = 2


def row_major_perm(n_row, n_col, target):
    pairs = []
    for r in range(n_row):
        for c in range(n_col):
            to_r, to_c = target(r, c)
            pairs.append((r * n_col + c, to_r * n_col + to_c))
    return pairs


def start_copies(pairs, sems):
    copies = [pltpu.make_async_copy(*pair, sems.at[i]) for i, pair in enumerate(pairs)]
    for copy in copies:
        copy.start()
    return copies


def wait_for(copies):
    for copy in copies:
        copy.wait()


def into(pieces, scratch, count):
    scratch[len(pieces) * count] = jnp.zeros(scratch.shape[1:], scratch.dtype)
    return [
        (piece, scratch.at[pl.ds(index * count, count)]) for index, piece in enumerate(pieces)
    ]


def multiply(index_ref, index_at, left_of, right, results, outs, sems, rows, slots, contract):
    copies = []
    for d in range(len(outs) - 1, -1, -1):
        for i in range(rows):
            left = left_of(i)
            for s in range(slots):
                base = index_at + ((d * rows + i) * slots + s) * slots
                blocks = jnp.concatenate(
                    [right[index_ref[base + a]] for a in range(slots)], axis=1
                )
                value = lax.dot_general(
                    blocks,
                    left,
                    (((1,), (contract,)), ((), ())),
                    preferred_element_type=jnp.float32,
                ).astype(results[d].dtype)
                if len(results[d].shape) == 3:
                    results[d][i * slots + s] = value
                else:
                    side = value.shape[0]
                    results[d][pl.ds((i * slots + s) * side, side)] = value
        copy = pltpu.make_async_copy(results[d], outs[d], sems.at[d])
        copy.start()
        copies.append(copy)
    wait_for(copies)


def split_results(first, others):
    return [first] + [others.at[d] for d in range(others.shape[0])]


def first_kernel(rows, slots, n_pieces, n_early, index_at, index_ref, left_ref, *refs):
    pieces, outs = refs[:n_pieces], refs[n_pieces + n_early : -6]
    right, left, first, others, sems, out_sems = refs[-6:]
    wait_for(start_copies(into(pieces, right, rows * slots) + [(left_ref, left)], sems))

    def left_of(i):
        return jnp.concatenate([left[i * slots + a] for a in range(slots)], axis=1)

    results = split_results(first, others)
    multiply(index_ref, index_at, left_of, right, results, outs, out_sems, rows, slots, 1)


def second_kernel(rows, slots, n_pieces, n_out, index_at, index_ref, *refs):
    pieces, parts = refs[:n_pieces], refs[n_pieces : n_pieces + n_out]
    right, left, part_first, part_others, first, others, sems, out_sems = refs[-8:]
    outs = refs[n_pieces + n_out : -8]
    held = split_results(part_first, part_others)
    wait_for(start_copies(list(zip(parts, held)) + into(pieces, right, rows * slots), sems))
    for b in range(rows * slots):
        value = held[0][b]
        for part in held[1:]:
            value = value + part[b].astype(jnp.float32)
        left[b] = value.astype(jnp.bfloat16)

    def left_of(i):
        return jnp.concatenate([left[i * slots + a] for a in range(slots)], axis=0)

    results = split_results(first, others)
    multiply(index_ref, index_at, left_of, right, results, outs, out_sems, rows, slots, 0)


def two_parts(x):
    high = x.astype(jnp.bfloat16)
    low = (x - high.astype(jnp.float32)).astype(jnp.bfloat16)
    return jnp.concatenate([high, low], axis=0)


def one_part(x):
    x = x.astype(jnp.float32)
    half = x.shape[0] // 2
    return x[:half] + x[half:]


def tree_sum(values):
    while len(values) > 1:
        values = [values[i] + values[i + 1] for i in range(0, len(values), 2)]
    return values[0]


def third_kernel(rows, slots, n_pieces, n_mirror, index_at, mirror_at, index_ref, own_ref, *refs):
    pieces, mirrored = refs[:n_pieces], refs[n_pieces : n_pieces + n_mirror]
    *outs, trace = refs[n_pieces + n_mirror : -8]
    right, mirror, own, left, first, others, sems, out_sems = refs[-8:]
    pairs = into(pieces, right, rows * slots) + into(mirrored, mirror, rows * slots) + [(own_ref, own)]
    wait_for(start_copies(pairs, sems))
    blocks, side = rows * slots, right.shape[1]
    part_rows = trace.shape[0] // 2
    total_trace = jnp.zeros((part_rows, side), jnp.float32)
    for b in range(blocks):
        other = mirror[index_ref[mirror_at + b]].astype(jnp.float32).T
        value = (-(own[b].astype(jnp.float32) + other)).astype(jnp.bfloat16)
        left[b] = value
        product = value.astype(jnp.float32) * right[b].astype(jnp.float32).T
        total_trace = total_trace + product.reshape(-1, part_rows, side).sum(0)
    total_trace = two_parts(total_trace)
    trace[...] = total_trace
    results = split_results(first, others)
    for result in results[1:]:
        result[pl.ds(blocks * side, 2 * part_rows)] = total_trace

    def left_of(i):
        return jnp.concatenate([left[i * slots + a] for a in range(slots)], axis=0)

    multiply(index_ref, index_at, left_of, right, results, outs, out_sems, rows, slots, 0)


def sum_kernel(n_out, trace_ref, own_ref, *refs):
    parts, (out, own, others, result, sems, out_sems) = refs[: n_out - 1], refs[n_out - 1 :]
    pairs = [(part, others.at[n_out - 2 - i]) for i, part in enumerate(parts)]
    wait_for(start_copies([(own_ref, own)] + pairs, sems))
    blocks, side = own.shape[:2]
    for b in range(blocks):
        value = own[b]
        for d in range(n_out - 1):
            value = value + others[d, pl.ds(b * side, side)].astype(jnp.float32)
        result[pl.ds(b * side, side)] = value.astype(result.dtype)
    tail = pl.ds(blocks * side, trace_ref.shape[0])
    tiles = [trace_ref[...]] + [others[d, tail] for d in range(n_out - 1)]
    result[tail] = two_parts(tree_sum([one_part(tile) for tile in tiles]))
    wait_for(start_copies([(result, out)], out_sems))


def last_kernel(n_mirror, blocks, mirror_at, index_ref, own_ref, *refs):
    mirrored, (out, mirror, own, result, sems, out_sems) = refs[:n_mirror], refs[n_mirror:]
    side = own.shape[1]
    count = blocks * side
    body = pl.ds(0, count)
    pairs = [(own_ref.at[body], own)] + [
        (piece.at[body], mirror.at[pl.ds(t * count, count)]) for t, piece in enumerate(mirrored)
    ]
    copies = start_copies(pairs, sems)
    mirror[pl.ds(n_mirror * count, side)] = jnp.zeros((side, side), mirror.dtype)
    wait_for(copies)
    for b in range(blocks):
        start = pl.multiple_of(index_ref[mirror_at + b] * side, side)
        other = mirror[pl.ds(start, side)].astype(jnp.float32)
        value = other - own[pl.ds(b * side, side)].astype(jnp.float32).T
        result[b] = value.astype(result.dtype)
    wait_for(start_copies([(result, out)], out_sems))


def per_device(n_row, n_col, block_cols, step_dir, intersection, density, kohn_sham):
    rows, slots, side = step_dir.shape[:3]
    blocks = rows * slots
    blocks_total = block_cols.shape[0]
    inner = n_row // n_col
    outer = n_row // inner
    assert inner == CORES and outer == n_col and outer & (outer - 1) == 0
    row_index = lax.axis_index("row")
    col_index = lax.axis_index("col")
    bf16, f32 = jnp.bfloat16, jnp.float32

    def at(o, h, g):
        return o * inner + g % inner, (g // inner) * CORES + h

    def inside(r, c):
        return r // inner, c % CORES, (c // CORES) * inner + r % inner

    def spread(o, g):
        bits = (n_col - 1).bit_length()
        return g ^ sum(((o >> b) & 1) << (bits - 1 - b) for b in range(bits))

    def at_spread(o, h, g):
        return at(o, h, spread(o, g))

    def inside_spread(r, c):
        o, h, p = inside(r, c)
        return o, h, spread(o, p)

    o_in, h_in, g_in = inside(row_index, col_index)

    by_group = block_cols.reshape(blocks_total, n_col, slots)
    mirror_cols = lax.dynamic_slice_in_dim(by_group, o_in, 1, 1)[:, 0]

    def rows_of(o, h):
        return lax.dynamic_slice_in_dim(by_group, (o * inner + h) * rows, rows, 0)

    def group_cols_of(cols, g):
        return lax.dynamic_slice_in_dim(cols, g, 1, 1)[:, 0]

    own_rows = rows_of(o_in, h_in)

    def index_table(group, first_out):
        own_cols, group_cols = group_cols_of(own_rows, group), group_cols_of(by_group, group)
        wanted = own_rows[:, first_out ^ jnp.arange(n_col)].transpose(1, 0, 2)
        safe = jnp.clip(wanted, 0, blocks_total - 1)
        matched = (
            (group_cols[safe][..., None, :] == own_cols[None, :, None, :, None])
            & (wanted >= 0)[..., None, None]
            & (own_cols >= 0)[None, :, None, :, None]
        )
        piece = ((safe // rows % inner) ^ h_in) * outer + (safe // rows // inner ^ o_in)
        slot = ((piece * rows + safe % rows) * slots)[..., None] + jnp.argmax(matched, axis=-1)
        return jnp.where(matched.any(-1), slot, n_row * blocks).astype(jnp.int32).reshape(-1)

    spread_in = spread(o_in, g_in)
    all_tables = [index_table(g_in, g_in), index_table(g_in, spread_in)]

    def mirror_table(h, cols):
        own_ids = (o_in * inner + h) * rows + jnp.arange(rows)
        safe_own = jnp.clip(cols, 0, blocks_total - 1)
        found = mirror_cols[safe_own] == own_ids[:, None, None]
        source = (safe_own // rows % inner) ^ h
        return jnp.where(
            cols >= 0,
            (source * rows + safe_own % rows) * slots + jnp.argmax(found, axis=-1),
            inner * blocks,
        ).astype(jnp.int32).reshape(-1)

    all_tables += [mirror_table(h_in, group_cols_of(own_rows, g)) for g in (g_in, spread_in)]
    starts = [sum(table.size for table in all_tables[:t]) for t in range(len(all_tables))]
    first_at, later_at, mirror_at, last_mirror_at = starts
    tables = jnp.concatenate(all_tables)

    smem = pl.BlockSpec(memory_space=pltpu.SMEM)
    vmem = pl.BlockSpec(memory_space=pltpu.VMEM)
    anywhere = pl.BlockSpec(memory_space=pl.ANY)

    def permute(x, target):
        return lax.ppermute(x, ("row", "col"), row_major_perm(n_row, n_col, target))

    def relayout(x, m=0, target=at):
        return permute(x, lambda r, c: target((r // inner) ^ m, r % inner, c))

    def inside_permute(x, move, source=inside, target=at):
        return permute(x, lambda r, c: target(*move(*source(r, c))))

    def share(x):
        return inside_permute(x, lambda o, h, g: (o, h ^ 1, g))

    def after(x, done):
        return lax.optimization_barrier((x, done))[0]

    def to_plane(x, m):
        return inside_permute(x, lambda o, h, g: (o ^ m, h, g))

    def share_all(pieces):
        return {m: share(piece) for m, piece in pieces.items()}

    def listed(pieces, shared):
        return [pieces[m] for m in range(outer)] + [shared[m] for m in range(outer)]

    def mirror(x, target, done=()):
        moved = inside_permute(x, lambda o, h, g: (g, h, o), inside_spread, target)
        return [moved, share(after(moved, done))]

    def exchange(outs):
        return [outs[0]] + [
            inside_permute(outs[d], lambda o, h, g, d=d: (o, h, g ^ d))
            for d in range(len(outs) - 1, 0, -1)
        ]

    def total_of(parts):
        value = parts[0]
        for part in parts[1:]:
            value = value + part.astype(f32)
        return value.astype(bf16)

    block_shape = (blocks, side, side)
    out_shapes = tuple(
        jax.ShapeDtypeStruct(block_shape, bf16 if d else f32) for d in range(n_col)
    )
    params = pltpu.CompilerParams(vmem_limit_bytes=14 * 2**20)

    def held(count):
        return pltpu.VMEM((count, side, side), bf16)

    def dma(count):
        return pltpu.SemaphoreType.DMA((count,))

    tail_shape = jax.ShapeDtypeStruct((16, side), bf16)
    long_shape = jax.ShapeDtypeStruct((blocks * side + tail_shape.shape[0], side), bf16)
    long_sums = [
        pltpu.VMEM(block_shape, f32),
        pltpu.VMEM((n_col - 1,) + long_shape.shape, bf16),
    ]
    sums = [pltpu.VMEM(block_shape, f32), pltpu.VMEM((n_col - 1,) + block_shape, bf16)]
    cost = pl.CostEstimate(
        flops=2 * n_col * blocks * slots * side**3,
        bytes_accessed=4 * 2**20,
        transcendentals=0,
    )

    flat = lambda x: x.reshape(block_shape)
    inter, dens, kohn = flat(intersection), flat(density), flat(kohn_sham)

    far_from = range(2, outer, 2)
    near = [*far_from, 1]

    inter_near = {m: relayout(inter, m) for m in near}
    inter_early = {0: relayout(inter)} | inter_near
    step = relayout(flat(step_dir))
    dens_own = relayout(dens)
    inter_far = {m + 1: to_plane(inter_near[m], 1) for m in far_from}
    dens_behind = after(dens_own, inter_near)
    dens_near = {m: to_plane(dens_behind, m) for m in far_from}
    dens_behind, kohn = after((dens_own, kohn), (inter_near, inter_far))
    dens_near[1] = to_plane(dens_behind, 1)
    kohn_own = relayout(kohn)
    inter_all = listed(inter_early | inter_far, share_all(inter_early) | share_all(inter_far))
    outs = pl.pallas_call(
        functools.partial(first_kernel, rows, slots, n_row, 0, first_at),
        out_shape=out_shapes,
        in_specs=[smem] + [anywhere] * (1 + n_row),
        out_specs=(anywhere,) * n_col,
        scratch_shapes=[held(n_row * blocks + 1), held(blocks), *sums, dma(n_row + 1), dma(n_col)],
        compiler_params=params,
        cost_estimate=cost,
        name="scaled_step_product",
    )(tables, step, *inter_all)
    parts = exchange(outs)

    dens_beside = {0: share(dens_own)}
    dens_far = {m + 1: to_plane(after(dens_near[m], outs), 1) for m in far_from}
    kohn_behind = after(kohn_own, (dens_near, outs))
    kohn_pieces = {m: to_plane(kohn_behind, m) for m in near}
    dens_near = after(dens_near, parts[1:])
    dens_beside |= share_all(dens_near) | share_all(dens_far)
    dens_all = listed({0: dens_own} | dens_near | dens_far, dens_beside)
    outs = pl.pallas_call(
        functools.partial(second_kernel, rows, slots, n_row, n_col, later_at),
        out_shape=out_shapes,
        in_specs=[smem] + [anywhere] * (n_row + n_col),
        out_specs=(anywhere,) * n_col,
        scratch_shapes=[
            held(n_row * blocks + 1),
            held(blocks),
            *sums,
            *sums,
            dma(n_row + n_col),
            dma(n_col),
        ],
        compiler_params=params,
        cost_estimate=cost,
        name="change_product",
    )(tables, *dens_all, *parts)
    second_outs = outs
    total = total_of(exchange(outs))

    own = inside_permute(total, lambda o, h, g: (o, h, g), inside_spread)
    mirrored = mirror(total, at, own)
    kohn_pieces = {0: kohn_own} | after(kohn_pieces, second_outs)
    kohn_beside = share_all(kohn_pieces)
    kohn_last = {m + 1: to_plane(kohn_pieces[m], 1) for m in far_from}
    kohn_last = after(kohn_last, total)
    kohn_all = listed(kohn_pieces | kohn_last, kohn_beside | share_all(kohn_last))
    *outs, trace = pl.pallas_call(
        functools.partial(third_kernel, rows, slots, n_row, inner, later_at, mirror_at),
        out_shape=out_shapes[:1] + (long_shape,) * (n_col - 1) + (tail_shape,),
        in_specs=[smem] + [anywhere] * (1 + n_row + inner),
        out_specs=(anywhere,) * n_col + (vmem,),
        scratch_shapes=[
            held(n_row * blocks + 1),
            held(inner * blocks + 1),
            held(blocks),
            held(blocks),
            *long_sums,
            dma(n_row + inner + 1),
            dma(n_col),
        ],
        compiler_params=params,
        cost_estimate=cost,
        name="commutator_product",
    )(tables, own, *kohn_all, *mirrored)
    own, *parts = exchange(outs)
    total = pl.pallas_call(
        functools.partial(sum_kernel, n_col),
        out_shape=long_shape,
        in_specs=[vmem] + [anywhere] * n_col,
        out_specs=anywhere,
        scratch_shapes=[*long_sums, pltpu.VMEM(long_shape.shape, bf16), dma(n_col), dma(1)],
        compiler_params=params,
        name="plane_sum",
    )(trace, own, *parts)
    mirrored = mirror(total, at_spread)

    commutator = pl.pallas_call(
        functools.partial(last_kernel, inner, blocks, last_mirror_at),
        out_shape=jax.ShapeDtypeStruct(block_shape, bf16),
        in_specs=[smem] + [anywhere] * (1 + inner),
        out_specs=anywhere,
        scratch_shapes=[
            pltpu.VMEM(((inner * blocks + 1) * side, side), bf16),
            pltpu.VMEM((blocks * side, side), bf16),
            held(blocks),
            dma(inner + 1),
            dma(1),
        ],
        compiler_params=params,
        name="commutator_difference",
    )(tables, total, *mirrored)
    commutator = inside_permute(
        commutator, lambda o, h, g: (o, h, g), inside_spread, lambda o, h, g: (o * inner + h, g)
    )

    plane_trace = tree_sum([one_part(piece[blocks * side :]) for piece in mirrored])
    trace = tree_sum(
        [plane_trace]
        + [
            inside_permute(plane_trace, lambda o, h, g, d=d: (o, h, g ^ d))
            for d in range(1, n_col)
        ]
    )
    trace_value = trace.sum() / (blocks_total * side * side)
    return commutator.reshape(step_dir.shape), trace_value


def solution(mesh):
    in_specs = (P(),) + (P("row", "col", None, None),) * 4
    out_specs = (P("row", "col", None, None), P())
    return jax.shard_map(
        functools.partial(per_device, mesh.shape["row"], mesh.shape["col"]),
        mesh=mesh,
        in_specs=in_specs,
        out_specs=out_specs,
        check_vma=False,
    )
```

```python
import functools

import jax
import jax.numpy as jnp
from jax import lax
from jax.experimental import pallas as pl
from jax.experimental.pallas import tpu as pltpu
from jax.sharding import PartitionSpec as P

CORES = 2


def row_major_perm(n_row, n_col, target):
    pairs = []
    for r in range(n_row):
        for c in range(n_col):
            to_r, to_c = target(r, c)
            pairs.append((r * n_col + c, to_r * n_col + to_c))
    return pairs


def start_copies(pairs, sems):
    copies = [pltpu.make_async_copy(*pair, sems.at[i]) for i, pair in enumerate(pairs)]
    for copy in copies:
        copy.start()
    return copies


def wait_for(copies):
    for copy in copies:
        copy.wait()


def into(pieces, scratch, count):
    scratch[len(pieces) * count] = jnp.zeros(scratch.shape[1:], scratch.dtype)
    return [
        (piece, scratch.at[pl.ds(index * count, count)]) for index, piece in enumerate(pieces)
    ]


def multiply(index_ref, index_at, left_of, right, results, outs, sems, rows, slots, contract):
    copies = []
    for d in range(len(outs) - 1, -1, -1):
        for i in range(rows):
            left = left_of(i)
            for s in range(slots):
                base = index_at + ((d * rows + i) * slots + s) * slots
                blocks = jnp.concatenate(
                    [right[index_ref[base + a]] for a in range(slots)], axis=1
                )
                value = lax.dot_general(
                    blocks,
                    left,
                    (((1,), (contract,)), ((), ())),
                    preferred_element_type=jnp.float32,
                ).astype(results[d].dtype)
                if len(results[d].shape) == 3:
                    results[d][i * slots + s] = value
                else:
                    side = value.shape[0]
                    results[d][pl.ds((i * slots + s) * side, side)] = value
        copy = pltpu.make_async_copy(results[d], outs[d], sems.at[d])
        copy.start()
        copies.append(copy)
    wait_for(copies)


def split_results(first, others):
    return [first] + [others.at[d] for d in range(others.shape[0])]


def first_kernel(rows, slots, n_pieces, n_early, index_at, index_ref, left_ref, *refs):
    pieces, outs = refs[:n_pieces], refs[n_pieces + n_early : -6]
    right, left, first, others, sems, out_sems = refs[-6:]
    wait_for(start_copies(into(pieces, right, rows * slots) + [(left_ref, left)], sems))

    def left_of(i):
        return jnp.concatenate([left[i * slots + a] for a in range(slots)], axis=1)

    results = split_results(first, others)
    multiply(index_ref, index_at, left_of, right, results, outs, out_sems, rows, slots, 1)


def second_kernel(rows, slots, n_pieces, n_out, index_at, index_ref, *refs):
    pieces, parts = refs[:n_pieces], refs[n_pieces : n_pieces + n_out]
    right, left, part_first, part_others, first, others, sems, out_sems = refs[-8:]
    outs = refs[n_pieces + n_out : -8]
    held = split_results(part_first, part_others)
    wait_for(start_copies(list(zip(parts, held)) + into(pieces, right, rows * slots), sems))
    for b in range(rows * slots):
        value = held[0][b]
        for part in held[1:]:
            value = value + part[b].astype(jnp.float32)
        left[b] = value.astype(jnp.bfloat16)

    def left_of(i):
        return jnp.concatenate([left[i * slots + a] for a in range(slots)], axis=0)

    results = split_results(first, others)
    multiply(index_ref, index_at, left_of, right, results, outs, out_sems, rows, slots, 0)


def two_parts(x):
    high = x.astype(jnp.bfloat16)
    low = (x - high.astype(jnp.float32)).astype(jnp.bfloat16)
    return jnp.concatenate([high, low], axis=0)


def one_part(x):
    x = x.astype(jnp.float32)
    half = x.shape[0] // 2
    return x[:half] + x[half:]


def tree_sum(values):
    while len(values) > 1:
        values = [values[i] + values[i + 1] for i in range(0, len(values), 2)]
    return values[0]


def third_kernel(rows, slots, n_pieces, n_mirror, index_at, mirror_at, index_ref, own_ref, *refs):
    pieces, mirrored = refs[:n_pieces], refs[n_pieces : n_pieces + n_mirror]
    *outs, trace = refs[n_pieces + n_mirror : -8]
    right, mirror, own, left, first, others, sems, out_sems = refs[-8:]
    pairs = into(pieces, right, rows * slots) + into(mirrored, mirror, rows * slots) + [(own_ref, own)]
    wait_for(start_copies(pairs, sems))
    blocks, side = rows * slots, right.shape[1]
    part_rows = trace.shape[0] // 2
    total_trace = jnp.zeros((part_rows, side), jnp.float32)
    for b in range(blocks):
        other = mirror[index_ref[mirror_at + b]].astype(jnp.float32).T
        value = (-(own[b].astype(jnp.float32) + other)).astype(jnp.bfloat16)
        left[b] = value
        product = value.astype(jnp.float32) * right[b].astype(jnp.float32).T
        total_trace = total_trace + product.reshape(-1, part_rows, side).sum(0)
    total_trace = two_parts(total_trace)
    trace[...] = total_trace
    results = split_results(first, others)
    for result in results[1:]:
        result[pl.ds(blocks * side, 2 * part_rows)] = total_trace

    def left_of(i):
        return jnp.concatenate([left[i * slots + a] for a in range(slots)], axis=0)

    multiply(index_ref, index_at, left_of, right, results, outs, out_sems, rows, slots, 0)


def sum_kernel(n_out, trace_ref, own_ref, *refs):
    parts, (out, own, others, result, sems, out_sems) = refs[: n_out - 1], refs[n_out - 1 :]
    pairs = [(part, others.at[n_out - 2 - i]) for i, part in enumerate(parts)]
    wait_for(start_copies([(own_ref, own)] + pairs, sems))
    blocks, side = own.shape[:2]
    for b in range(blocks):
        value = own[b]
        for d in range(n_out - 1):
            value = value + others[d, pl.ds(b * side, side)].astype(jnp.float32)
        result[pl.ds(b * side, side)] = value.astype(result.dtype)
    tail = pl.ds(blocks * side, trace_ref.shape[0])
    tiles = [trace_ref[...]] + [others[d, tail] for d in range(n_out - 1)]
    result[tail] = two_parts(tree_sum([one_part(tile) for tile in tiles]))
    wait_for(start_copies([(result, out)], out_sems))


def last_kernel(n_mirror, blocks, mirror_at, index_ref, own_ref, *refs):
    mirrored, (out, mirror, own, result, sems, out_sems) = refs[:n_mirror], refs[n_mirror:]
    side = own.shape[1]
    count = blocks * side
    body = pl.ds(0, count)
    pairs = [(own_ref.at[body], own)] + [
        (piece.at[body], mirror.at[pl.ds(t * count, count)]) for t, piece in enumerate(mirrored)
    ]
    copies = start_copies(pairs, sems)
    mirror[pl.ds(n_mirror * count, side)] = jnp.zeros((side, side), mirror.dtype)
    wait_for(copies)
    for b in range(blocks):
        start = pl.multiple_of(index_ref[mirror_at + b] * side, side)
        other = mirror[pl.ds(start, side)].astype(jnp.float32)
        value = other - own[pl.ds(b * side, side)].astype(jnp.float32).T
        result[b] = value.astype(result.dtype)
    wait_for(start_copies([(result, out)], out_sems))


def per_device(n_row, n_col, block_cols, step_dir, intersection, density, kohn_sham):
    rows, slots, side = step_dir.shape[:3]
    blocks = rows * slots
    blocks_total = block_cols.shape[0]
    inner = n_row // n_col
    outer = n_row // inner
    assert inner == CORES and outer == n_col and outer & (outer - 1) == 0
    row_index = lax.axis_index("row")
    col_index = lax.axis_index("col")
    bf16, f32 = jnp.bfloat16, jnp.float32

    def at(o, h, g):
        return o * inner + g % inner, (g // inner) * CORES + h

    def inside(r, c):
        return r // inner, c % CORES, (c // CORES) * inner + r % inner

    def spread(o, g):
        bits = (n_col - 1).bit_length()
        return g ^ sum(((o >> b) & 1) << (bits - 1 - b) for b in range(bits))

    def at_spread(o, h, g):
        return at(o, h, spread(o, g))

    def inside_spread(r, c):
        o, h, p = inside(r, c)
        return o, h, spread(o, p)

    o_in, h_in, g_in = inside(row_index, col_index)

    by_group = block_cols.reshape(blocks_total, n_col, slots)
    mirror_cols = lax.dynamic_slice_in_dim(by_group, o_in, 1, 1)[:, 0]

    def rows_of(o, h):
        return lax.dynamic_slice_in_dim(by_group, (o * inner + h) * rows, rows, 0)

    def group_cols_of(cols, g):
        return lax.dynamic_slice_in_dim(cols, g, 1, 1)[:, 0]

    own_rows = rows_of(o_in, h_in)

    def index_table(group, first_out):
        own_cols, group_cols = group_cols_of(own_rows, group), group_cols_of(by_group, group)
        wanted = own_rows[:, first_out ^ jnp.arange(n_col)].transpose(1, 0, 2)
        safe = jnp.clip(wanted, 0, blocks_total - 1)
        matched = (
            (group_cols[safe][..., None, :] == own_cols[None, :, None, :, None])
            & (wanted >= 0)[..., None, None]
            & (own_cols >= 0)[None, :, None, :, None]
        )
        piece = ((safe // rows % inner) ^ h_in) * outer + (safe // rows // inner ^ o_in)
        slot = ((piece * rows + safe % rows) * slots)[..., None] + jnp.argmax(matched, axis=-1)
        return jnp.where(matched.any(-1), slot, n_row * blocks).astype(jnp.int32).reshape(-1)

    spread_in = spread(o_in, g_in)
    all_tables = [index_table(g_in, g_in), index_table(g_in, spread_in)]

    def mirror_table(h, cols):
        own_ids = (o_in * inner + h) * rows + jnp.arange(rows)
        safe_own = jnp.clip(cols, 0, blocks_total - 1)
        found = mirror_cols[safe_own] == own_ids[:, None, None]
        source = (safe_own // rows % inner) ^ h
        return jnp.where(
            cols >= 0,
            (source * rows + safe_own % rows) * slots + jnp.argmax(found, axis=-1),
            inner * blocks,
        ).astype(jnp.int32).reshape(-1)

    all_tables += [mirror_table(h_in, group_cols_of(own_rows, g)) for g in (g_in, spread_in)]
    starts = [sum(table.size for table in all_tables[:t]) for t in range(len(all_tables))]
    first_at, later_at, mirror_at, last_mirror_at = starts
    tables = jnp.concatenate(all_tables)

    smem = pl.BlockSpec(memory_space=pltpu.SMEM)
    vmem = pl.BlockSpec(memory_space=pltpu.VMEM)
    anywhere = pl.BlockSpec(memory_space=pl.ANY)

    def permute(x, target):
        return lax.ppermute(x, ("row", "col"), row_major_perm(n_row, n_col, target))

    def relayout(x, m=0, target=at):
        return permute(x, lambda r, c: target((r // inner) ^ m, r % inner, c))

    def inside_permute(x, move, source=inside, target=at):
        return permute(x, lambda r, c: target(*move(*source(r, c))))

    def share(x):
        return inside_permute(x, lambda o, h, g: (o, h ^ 1, g))

    def after(x, done):
        return lax.optimization_barrier((x, done))[0]

    def to_plane(x, m):
        return inside_permute(x, lambda o, h, g: (o ^ m, h, g))

    def share_all(pieces):
        return {m: share(piece) for m, piece in pieces.items()}

    def listed(pieces, shared):
        return [pieces[m] for m in range(outer)] + [shared[m] for m in range(outer)]

    def mirror(x, target):
        moved = inside_permute(x, lambda o, h, g: (g, h, o), inside_spread, target)
        return [moved, share(moved)]

    def exchange(outs):
        return [outs[0]] + [
            inside_permute(outs[d], lambda o, h, g, d=d: (o, h, g ^ d))
            for d in range(len(outs) - 1, 0, -1)
        ]

    def total_of(parts):
        value = parts[0]
        for part in parts[1:]:
            value = value + part.astype(f32)
        return value.astype(bf16)

    block_shape = (blocks, side, side)
    out_shapes = tuple(
        jax.ShapeDtypeStruct(block_shape, bf16 if d else f32) for d in range(n_col)
    )
    params = pltpu.CompilerParams(vmem_limit_bytes=14 * 2**20)

    def held(count):
        return pltpu.VMEM((count, side, side), bf16)

    def dma(count):
        return pltpu.SemaphoreType.DMA((count,))

    tail_shape = jax.ShapeDtypeStruct((16, side), bf16)
    long_shape = jax.ShapeDtypeStruct((blocks * side + tail_shape.shape[0], side), bf16)
    long_sums = [
        pltpu.VMEM(block_shape, f32),
        pltpu.VMEM((n_col - 1,) + long_shape.shape, bf16),
    ]
    sums = [pltpu.VMEM(block_shape, f32), pltpu.VMEM((n_col - 1,) + block_shape, bf16)]
    cost = pl.CostEstimate(
        flops=2 * n_col * blocks * slots * side**3,
        bytes_accessed=4 * 2**20,
        transcendentals=0,
    )

    flat = lambda x: x.reshape(block_shape)
    inter, dens, kohn = flat(intersection), flat(density), flat(kohn_sham)

    far_from = range(2, outer, 2)
    near = [*far_from, 1]

    inter_near = {m: relayout(inter, m) for m in near}
    inter_early = {0: relayout(inter)} | inter_near
    step = relayout(flat(step_dir))
    dens_own = relayout(dens)
    inter_far = {m + 1: to_plane(inter_near[m], 1) for m in far_from}
    dens_behind = after(dens_own, inter_near)
    dens_near = {m: to_plane(dens_behind, m) for m in far_from}
    dens_behind, kohn = after((dens_own, kohn), (inter_near, inter_far))
    dens_near[1] = to_plane(dens_behind, 1)
    kohn_own = relayout(kohn)
    inter_all = listed(inter_early | inter_far, share_all(inter_early) | share_all(inter_far))
    outs = pl.pallas_call(
        functools.partial(first_kernel, rows, slots, n_row, 0, first_at),
        out_shape=out_shapes,
        in_specs=[smem] + [anywhere] * (1 + n_row),
        out_specs=(anywhere,) * n_col,
        scratch_shapes=[held(n_row * blocks + 1), held(blocks), *sums, dma(n_row + 1), dma(n_col)],
        compiler_params=params,
        cost_estimate=cost,
        name="scaled_step_product",
    )(tables, step, *inter_all)
    parts = exchange(outs)

    dens_beside = {0: share(dens_own)}
    dens_far = {m + 1: to_plane(after(dens_near[m], outs), 1) for m in far_from}
    kohn_behind = after(kohn_own, (dens_near, outs))
    kohn_pieces = {m: to_plane(kohn_behind, m) for m in far_from}
    dens_near = after(dens_near, parts[1:])
    dens_beside |= share_all(dens_near) | share_all(dens_far)
    dens_all = listed({0: dens_own} | dens_near | dens_far, dens_beside)
    outs = pl.pallas_call(
        functools.partial(second_kernel, rows, slots, n_row, n_col, later_at),
        out_shape=out_shapes,
        in_specs=[smem] + [anywhere] * (n_row + n_col),
        out_specs=(anywhere,) * n_col,
        scratch_shapes=[
            held(n_row * blocks + 1),
            held(blocks),
            *sums,
            *sums,
            dma(n_row + n_col),
            dma(n_col),
        ],
        compiler_params=params,
        cost_estimate=cost,
        name="change_product",
    )(tables, *dens_all, *parts)
    second_outs = outs
    total = total_of(exchange(outs))

    mirrored = mirror(total, at)
    own = inside_permute(total, lambda o, h, g: (o, h, g), inside_spread)
    kohn_pieces = {0: kohn_own} | after(kohn_pieces, second_outs)
    kohn_beside = share_all(kohn_pieces)
    kohn_last = {m + 1: to_plane(kohn_pieces[m], 1) for m in range(0, outer, 2)}
    kohn_last = after(kohn_last, total)
    kohn_all = listed(kohn_pieces | kohn_last, kohn_beside | share_all(kohn_last))
    *outs, trace = pl.pallas_call(
        functools.partial(third_kernel, rows, slots, n_row, inner, later_at, mirror_at),
        out_shape=out_shapes[:1] + (long_shape,) * (n_col - 1) + (tail_shape,),
        in_specs=[smem] + [anywhere] * (1 + n_row + inner),
        out_specs=(anywhere,) * n_col + (vmem,),
        scratch_shapes=[
            held(n_row * blocks + 1),
            held(inner * blocks + 1),
            held(blocks),
            held(blocks),
            *long_sums,
            dma(n_row + inner + 1),
            dma(n_col),
        ],
        compiler_params=params,
        cost_estimate=cost,
        name="commutator_product",
    )(tables, own, *kohn_all, *mirrored)
    own, *parts = exchange(outs)
    total = pl.pallas_call(
        functools.partial(sum_kernel, n_col),
        out_shape=long_shape,
        in_specs=[vmem] + [anywhere] * n_col,
        out_specs=anywhere,
        scratch_shapes=[*long_sums, pltpu.VMEM(long_shape.shape, bf16), dma(n_col), dma(1)],
        compiler_params=params,
        name="plane_sum",
    )(trace, own, *parts)
    mirrored = mirror(total, at_spread)

    commutator = pl.pallas_call(
        functools.partial(last_kernel, inner, blocks, last_mirror_at),
        out_shape=jax.ShapeDtypeStruct(block_shape, bf16),
        in_specs=[smem] + [anywhere] * (1 + inner),
        out_specs=anywhere,
        scratch_shapes=[
            pltpu.VMEM(((inner * blocks + 1) * side, side), bf16),
            pltpu.VMEM((blocks * side, side), bf16),
            held(blocks),
            dma(inner + 1),
            dma(1),
        ],
        compiler_params=params,
        name="commutator_difference",
    )(tables, total, *mirrored)
    plane_trace = tree_sum([one_part(piece[blocks * side :]) for piece in mirrored])
    trace = tree_sum(
        [plane_trace]
        + [
            inside_permute(plane_trace, lambda o, h, g, d=d: (o, h, g ^ d))
            for d in range(1, n_col)
        ]
    )

    commutator = inside_permute(
        after(commutator, trace), lambda o, h, g: (o, h, g), inside_spread, lambda o, h, g: (o * inner + h, g)
    )
    trace_value = trace.sum() / (blocks_total * side * side)
    return commutator.reshape(step_dir.shape), trace_value


def solution(mesh):
    in_specs = (P(),) + (P("row", "col", None, None),) * 4
    out_specs = (P("row", "col", None, None), P())
    return jax.shard_map(
        functools.partial(per_device, mesh.shape["row"], mesh.shape["col"]),
        mesh=mesh,
        in_specs=in_specs,
        out_specs=out_specs,
        check_vma=False,
    )
```

```python
import functools

import jax
import jax.numpy as jnp
from jax import lax
from jax.experimental import pallas as pl
from jax.experimental.pallas import tpu as pltpu
from jax.sharding import PartitionSpec as P

CORES = 2


def row_major_perm(n_row, n_col, target):
    pairs = []
    for r in range(n_row):
        for c in range(n_col):
            to_r, to_c = target(r, c)
            pairs.append((r * n_col + c, to_r * n_col + to_c))
    return pairs


def start_copies(pairs, sems):
    copies = [pltpu.make_async_copy(*pair, sems.at[i]) for i, pair in enumerate(pairs)]
    for copy in copies:
        copy.start()
    return copies


def wait_for(copies):
    for copy in copies:
        copy.wait()


def into(pieces, scratch, count):
    scratch[len(pieces) * count] = jnp.zeros(scratch.shape[1:], scratch.dtype)
    return [
        (piece, scratch.at[pl.ds(index * count, count)]) for index, piece in enumerate(pieces)
    ]


def multiply(index_ref, index_at, left_of, right, results, outs, sems, rows, slots, contract):
    copies = []
    for d in range(len(outs) - 1, -1, -1):
        for i in range(rows):
            left = left_of(i)
            for s in range(slots):
                base = index_at + ((d * rows + i) * slots + s) * slots
                blocks = jnp.concatenate(
                    [right[index_ref[base + a]] for a in range(slots)], axis=1
                )
                value = lax.dot_general(
                    blocks,
                    left,
                    (((1,), (contract,)), ((), ())),
                    preferred_element_type=jnp.float32,
                ).astype(results[d].dtype)
                if len(results[d].shape) == 3:
                    results[d][i * slots + s] = value
                else:
                    side = value.shape[0]
                    results[d][pl.ds((i * slots + s) * side, side)] = value
        copy = pltpu.make_async_copy(results[d], outs[d], sems.at[d])
        copy.start()
        copies.append(copy)
    wait_for(copies)


def split_results(first, others):
    return [first] + [others.at[d] for d in range(others.shape[0])]


def first_kernel(rows, slots, n_pieces, n_early, index_at, index_ref, left_ref, *refs):
    pieces, outs = refs[:n_pieces], refs[n_pieces + n_early : -6]
    right, left, first, others, sems, out_sems = refs[-6:]
    wait_for(start_copies(into(pieces, right, rows * slots) + [(left_ref, left)], sems))

    def left_of(i):
        return jnp.concatenate([left[i * slots + a] for a in range(slots)], axis=1)

    results = split_results(first, others)
    multiply(index_ref, index_at, left_of, right, results, outs, out_sems, rows, slots, 1)


def second_kernel(rows, slots, n_pieces, n_out, index_at, index_ref, *refs):
    pieces, parts = refs[:n_pieces], refs[n_pieces : n_pieces + n_out]
    right, left, part_first, part_others, first, others, sems, out_sems = refs[-8:]
    outs = refs[n_pieces + n_out : -8]
    held = split_results(part_first, part_others)
    wait_for(start_copies(list(zip(parts, held)) + into(pieces, right, rows * slots), sems))
    for b in range(rows * slots):
        value = held[0][b]
        for part in held[1:]:
            value = value + part[b].astype(jnp.float32)
        left[b] = value.astype(jnp.bfloat16)

    def left_of(i):
        return jnp.concatenate([left[i * slots + a] for a in range(slots)], axis=0)

    results = split_results(first, others)
    multiply(index_ref, index_at, left_of, right, results, outs, out_sems, rows, slots, 0)


def two_parts(x):
    high = x.astype(jnp.bfloat16)
    low = (x - high.astype(jnp.float32)).astype(jnp.bfloat16)
    return jnp.concatenate([high, low], axis=0)


def one_part(x):
    x = x.astype(jnp.float32)
    half = x.shape[0] // 2
    return x[:half] + x[half:]


def tree_sum(values):
    while len(values) > 1:
        values = [values[i] + values[i + 1] for i in range(0, len(values), 2)]
    return values[0]


def third_kernel(rows, slots, n_pieces, n_mirror, index_at, mirror_at, index_ref, own_ref, *refs):
    pieces, mirrored = refs[:n_pieces], refs[n_pieces : n_pieces + n_mirror]
    *outs, trace = refs[n_pieces + n_mirror : -8]
    right, mirror, own, left, first, others, sems, out_sems = refs[-8:]
    pairs = into(pieces, right, rows * slots) + into(mirrored, mirror, rows * slots) + [(own_ref, own)]
    wait_for(start_copies(pairs, sems))
    blocks, side = rows * slots, right.shape[1]
    part_rows = trace.shape[0] // 2
    total_trace = jnp.zeros((part_rows, side), jnp.float32)
    for b in range(blocks):
        other = mirror[index_ref[mirror_at + b]].astype(jnp.float32).T
        value = (-(own[b].astype(jnp.float32) + other)).astype(jnp.bfloat16)
        left[b] = value
        product = value.astype(jnp.float32) * right[b].astype(jnp.float32).T
        total_trace = total_trace + product.reshape(-1, part_rows, side).sum(0)
    total_trace = two_parts(total_trace)
    trace[...] = total_trace
    results = split_results(first, others)
    for result in results[1:]:
        result[pl.ds(blocks * side, 2 * part_rows)] = total_trace

    def left_of(i):
        return jnp.concatenate([left[i * slots + a] for a in range(slots)], axis=0)

    multiply(index_ref, index_at, left_of, right, results, outs, out_sems, rows, slots, 0)


def sum_kernel(n_out, trace_ref, own_ref, *refs):
    parts, (out, own, others, result, sems, out_sems) = refs[: n_out - 1], refs[n_out - 1 :]
    pairs = [(part, others.at[n_out - 2 - i]) for i, part in enumerate(parts)]
    wait_for(start_copies([(own_ref, own)] + pairs, sems))
    blocks, side = own.shape[:2]
    for b in range(blocks):
        value = own[b]
        for d in range(n_out - 1):
            value = value + others[d, pl.ds(b * side, side)].astype(jnp.float32)
        result[pl.ds(b * side, side)] = value.astype(result.dtype)
    tail = pl.ds(blocks * side, trace_ref.shape[0])
    tiles = [trace_ref[...]] + [others[d, tail] for d in range(n_out - 1)]
    result[tail] = two_parts(tree_sum([one_part(tile) for tile in tiles]))
    wait_for(start_copies([(result, out)], out_sems))


def last_kernel(n_mirror, blocks, mirror_at, index_ref, own_ref, *refs):
    mirrored, (out, mirror, own, result, sems, out_sems) = refs[:n_mirror], refs[n_mirror:]
    side = own.shape[1]
    count = blocks * side
    body = pl.ds(0, count)
    pairs = [(own_ref.at[body], own)] + [
        (piece.at[body], mirror.at[pl.ds(t * count, count)]) for t, piece in enumerate(mirrored)
    ]
    copies = start_copies(pairs, sems)
    mirror[pl.ds(n_mirror * count, side)] = jnp.zeros((side, side), mirror.dtype)
    wait_for(copies)
    for b in range(blocks):
        start = pl.multiple_of(index_ref[mirror_at + b] * side, side)
        other = mirror[pl.ds(start, side)].astype(jnp.float32)
        value = other - own[pl.ds(b * side, side)].astype(jnp.float32).T
        result[b] = value.astype(result.dtype)
    wait_for(start_copies([(result, out)], out_sems))


def per_device(n_row, n_col, block_cols, step_dir, intersection, density, kohn_sham):
    rows, slots, side = step_dir.shape[:3]
    blocks = rows * slots
    blocks_total = block_cols.shape[0]
    inner = n_row // n_col
    outer = n_row // inner
    assert inner == CORES and outer == n_col and outer & (outer - 1) == 0
    row_index = lax.axis_index("row")
    col_index = lax.axis_index("col")
    bf16, f32 = jnp.bfloat16, jnp.float32

    def at(o, h, g):
        return o * inner + g % inner, (g // inner) * CORES + h

    def inside(r, c):
        return r // inner, c % CORES, (c // CORES) * inner + r % inner

    def spread(o, g):
        return g ^ (o % 2)

    def at_spread(o, h, g):
        return at(o, h, spread(o, g))

    def inside_spread(r, c):
        o, h, p = inside(r, c)
        return o, h, spread(o, p)

    o_in, h_in, g_in = inside(row_index, col_index)

    by_group = block_cols.reshape(blocks_total, n_col, slots)
    mirror_cols = lax.dynamic_slice_in_dim(by_group, o_in, 1, 1)[:, 0]

    def rows_of(o, h):
        return lax.dynamic_slice_in_dim(by_group, (o * inner + h) * rows, rows, 0)

    def group_cols_of(cols, g):
        return lax.dynamic_slice_in_dim(cols, g, 1, 1)[:, 0]

    own_rows = rows_of(o_in, h_in)

    def index_table(group, first_out):
        own_cols, group_cols = group_cols_of(own_rows, group), group_cols_of(by_group, group)
        wanted = own_rows[:, first_out ^ jnp.arange(n_col)].transpose(1, 0, 2)
        safe = jnp.clip(wanted, 0, blocks_total - 1)
        matched = (
            (group_cols[safe][..., None, :] == own_cols[None, :, None, :, None])
            & (wanted >= 0)[..., None, None]
            & (own_cols >= 0)[None, :, None, :, None]
        )
        piece = ((safe // rows % inner) ^ h_in) * outer + (safe // rows // inner ^ o_in)
        slot = ((piece * rows + safe % rows) * slots)[..., None] + jnp.argmax(matched, axis=-1)
        return jnp.where(matched.any(-1), slot, n_row * blocks).astype(jnp.int32).reshape(-1)

    spread_in = spread(o_in, g_in)
    all_tables = [index_table(g_in, g_in), index_table(g_in, spread_in)]

    def mirror_table(h, cols):
        own_ids = (o_in * inner + h) * rows + jnp.arange(rows)
        safe_own = jnp.clip(cols, 0, blocks_total - 1)
        found = mirror_cols[safe_own] == own_ids[:, None, None]
        source = (safe_own // rows % inner) ^ h
        return jnp.where(
            cols >= 0,
            (source * rows + safe_own % rows) * slots + jnp.argmax(found, axis=-1),
            inner * blocks,
        ).astype(jnp.int32).reshape(-1)

    all_tables += [mirror_table(h_in, group_cols_of(own_rows, g)) for g in (g_in, spread_in)]
    starts = [sum(table.size for table in all_tables[:t]) for t in range(len(all_tables))]
    first_at, later_at, mirror_at, last_mirror_at = starts
    tables = jnp.concatenate(all_tables)

    smem = pl.BlockSpec(memory_space=pltpu.SMEM)
    vmem = pl.BlockSpec(memory_space=pltpu.VMEM)
    anywhere = pl.BlockSpec(memory_space=pl.ANY)

    def permute(x, target):
        return lax.ppermute(x, ("row", "col"), row_major_perm(n_row, n_col, target))

    def relayout(x, m=0, target=at):
        return permute(x, lambda r, c: target((r // inner) ^ m, r % inner, c))

    def inside_permute(x, move, source=inside, target=at):
        return permute(x, lambda r, c: target(*move(*source(r, c))))

    def share(x):
        return inside_permute(x, lambda o, h, g: (o, h ^ 1, g))

    def after(x, done):
        return lax.optimization_barrier((x, done))[0]

    def to_plane(x, m):
        return inside_permute(x, lambda o, h, g: (o ^ m, h, g))

    def share_all(pieces):
        return {m: share(piece) for m, piece in pieces.items()}

    def listed(pieces, shared):
        return [pieces[m] for m in range(outer)] + [shared[m] for m in range(outer)]

    def mirror(x, target):
        moved = inside_permute(x, lambda o, h, g: (g, h, o), inside_spread, target)
        return [moved, share(moved)]

    def exchange(outs):
        return [outs[0]] + [
            inside_permute(outs[d], lambda o, h, g, d=d: (o, h, g ^ d))
            for d in range(len(outs) - 1, 0, -1)
        ]

    def total_of(parts):
        value = parts[0]
        for part in parts[1:]:
            value = value + part.astype(f32)
        return value.astype(bf16)

    block_shape = (blocks, side, side)
    out_shapes = tuple(
        jax.ShapeDtypeStruct(block_shape, bf16 if d else f32) for d in range(n_col)
    )
    params = pltpu.CompilerParams(vmem_limit_bytes=14 * 2**20)

    def held(count):
        return pltpu.VMEM((count, side, side), bf16)

    def dma(count):
        return pltpu.SemaphoreType.DMA((count,))

    tail_shape = jax.ShapeDtypeStruct((16, side), bf16)
    long_shape = jax.ShapeDtypeStruct((blocks * side + tail_shape.shape[0], side), bf16)
    long_sums = [
        pltpu.VMEM(block_shape, f32),
        pltpu.VMEM((n_col - 1,) + long_shape.shape, bf16),
    ]
    sums = [pltpu.VMEM(block_shape, f32), pltpu.VMEM((n_col - 1,) + block_shape, bf16)]
    cost = pl.CostEstimate(
        flops=2 * n_col * blocks * slots * side**3,
        bytes_accessed=4 * 2**20,
        transcendentals=0,
    )

    flat = lambda x: x.reshape(block_shape)
    inter, dens, kohn = flat(intersection), flat(density), flat(kohn_sham)

    far_from = range(2, outer, 2)
    near = [*far_from, 1]

    inter_near = {m: relayout(inter, m) for m in near}
    inter_early = {0: relayout(inter)} | inter_near
    step = relayout(flat(step_dir))
    dens_own = relayout(dens)
    inter_far = {m + 1: to_plane(inter_near[m], 1) for m in far_from}
    dens_behind = after(dens_own, inter_near)
    dens_near = {m: to_plane(dens_behind, m) for m in far_from}
    dens_behind, kohn = after((dens_own, kohn), (inter_near, inter_far))
    dens_near[1] = to_plane(dens_behind, 1)
    kohn_own = relayout(kohn)
    inter_all = listed(inter_early | inter_far, share_all(inter_early) | share_all(inter_far))
    outs = pl.pallas_call(
        functools.partial(first_kernel, rows, slots, n_row, 0, first_at),
        out_shape=out_shapes,
        in_specs=[smem] + [anywhere] * (1 + n_row),
        out_specs=(anywhere,) * n_col,
        scratch_shapes=[held(n_row * blocks + 1), held(blocks), *sums, dma(n_row + 1), dma(n_col)],
        compiler_params=params,
        cost_estimate=cost,
        name="scaled_step_product",
    )(tables, step, *inter_all)
    parts = exchange(outs)

    dens_beside = {0: share(dens_own)}
    dens_far = {m + 1: to_plane(after(dens_near[m], outs), 1) for m in far_from}
    kohn_behind = after(kohn_own, (dens_near, outs))
    kohn_pieces = {m: to_plane(kohn_behind, m) for m in far_from}
    dens_near = after(dens_near, parts[1:])
    dens_beside |= share_all(dens_near) | share_all(dens_far)
    dens_all = listed({0: dens_own} | dens_near | dens_far, dens_beside)
    outs = pl.pallas_call(
        functools.partial(second_kernel, rows, slots, n_row, n_col, later_at),
        out_shape=out_shapes,
        in_specs=[smem] + [anywhere] * (n_row + n_col),
        out_specs=(anywhere,) * n_col,
        scratch_shapes=[
            held(n_row * blocks + 1),
            held(blocks),
            *sums,
            *sums,
            dma(n_row + n_col),
            dma(n_col),
        ],
        compiler_params=params,
        cost_estimate=cost,
        name="change_product",
    )(tables, *dens_all, *parts)
    second_outs = outs
    total = total_of(exchange(outs))

    mirrored = mirror(total, at)
    own = inside_permute(total, lambda o, h, g: (o, h, g), inside_spread)
    kohn_pieces = {0: kohn_own} | after(kohn_pieces, second_outs)
    kohn_beside = share_all(kohn_pieces)
    kohn_last = {m + 1: to_plane(kohn_pieces[m], 1) for m in range(0, outer, 2)}
    kohn_last = after(kohn_last, total)
    kohn_all = listed(kohn_pieces | kohn_last, kohn_beside | share_all(kohn_last))
    *outs, trace = pl.pallas_call(
        functools.partial(third_kernel, rows, slots, n_row, inner, later_at, mirror_at),
        out_shape=out_shapes[:1] + (long_shape,) * (n_col - 1) + (tail_shape,),
        in_specs=[smem] + [anywhere] * (1 + n_row + inner),
        out_specs=(anywhere,) * n_col + (vmem,),
        scratch_shapes=[
            held(n_row * blocks + 1),
            held(inner * blocks + 1),
            held(blocks),
            held(blocks),
            *long_sums,
            dma(n_row + inner + 1),
            dma(n_col),
        ],
        compiler_params=params,
        cost_estimate=cost,
        name="commutator_product",
    )(tables, own, *kohn_all, *mirrored)
    own, *parts = exchange(outs)
    total = pl.pallas_call(
        functools.partial(sum_kernel, n_col),
        out_shape=long_shape,
        in_specs=[vmem] + [anywhere] * n_col,
        out_specs=anywhere,
        scratch_shapes=[*long_sums, pltpu.VMEM(long_shape.shape, bf16), dma(n_col), dma(1)],
        compiler_params=params,
        name="plane_sum",
    )(trace, own, *parts)
    mirrored = mirror(total, at_spread)

    commutator = pl.pallas_call(
        functools.partial(last_kernel, inner, blocks, last_mirror_at),
        out_shape=jax.ShapeDtypeStruct(block_shape, bf16),
        in_specs=[smem] + [anywhere] * (1 + inner),
        out_specs=anywhere,
        scratch_shapes=[
            pltpu.VMEM(((inner * blocks + 1) * side, side), bf16),
            pltpu.VMEM((blocks * side, side), bf16),
            held(blocks),
            dma(inner + 1),
            dma(1),
        ],
        compiler_params=params,
        name="commutator_difference",
    )(tables, total, *mirrored)
    commutator = inside_permute(
        commutator, lambda o, h, g: (o, h, g), inside_spread, lambda o, h, g: (o * inner + h, g)
    )

    plane_trace = tree_sum([one_part(piece[blocks * side :]) for piece in mirrored])
    trace = tree_sum(
        [plane_trace]
        + [
            inside_permute(plane_trace, lambda o, h, g, d=d: (o, h, g ^ d))
            for d in range(1, n_col)
        ]
    )
    trace_value = trace.sum() / (blocks_total * side * side)
    return commutator.reshape(step_dir.shape), trace_value


def solution(mesh):
    in_specs = (P(),) + (P("row", "col", None, None),) * 4
    out_specs = (P("row", "col", None, None), P())
    return jax.shard_map(
        functools.partial(per_device, mesh.shape["row"], mesh.shape["col"]),
        mesh=mesh,
        in_specs=in_specs,
        out_specs=out_specs,
        check_vma=False,
    )
```

```python
import functools

import jax
import jax.numpy as jnp
from jax import lax
from jax.experimental import pallas as pl
from jax.experimental.pallas import tpu as pltpu
from jax.sharding import PartitionSpec as P

CORES = 2


def row_major_perm(n_row, n_col, target):
    pairs = []
    for r in range(n_row):
        for c in range(n_col):
            to_r, to_c = target(r, c)
            pairs.append((r * n_col + c, to_r * n_col + to_c))
    return pairs


def start_copies(pairs, sems):
    copies = [pltpu.make_async_copy(*pair, sems.at[i]) for i, pair in enumerate(pairs)]
    for copy in copies:
        copy.start()
    return copies


def wait_for(copies):
    for copy in copies:
        copy.wait()


def into(pieces, scratch, count):
    scratch[len(pieces) * count] = jnp.zeros(scratch.shape[1:], scratch.dtype)
    return [
        (piece, scratch.at[pl.ds(index * count, count)]) for index, piece in enumerate(pieces)
    ]


def multiply(index_ref, index_at, left_of, right, results, outs, sems, rows, slots, contract):
    copies = []
    for d in range(len(outs) - 1, -1, -1):
        for i in range(rows):
            left = left_of(i)
            for s in range(slots):
                base = index_at + ((d * rows + i) * slots + s) * slots
                blocks = jnp.concatenate(
                    [right[index_ref[base + a]] for a in range(slots)], axis=1
                )
                value = lax.dot_general(
                    blocks,
                    left,
                    (((1,), (contract,)), ((), ())),
                    preferred_element_type=jnp.float32,
                ).astype(results[d].dtype)
                if len(results[d].shape) == 3:
                    results[d][i * slots + s] = value
                else:
                    side = value.shape[0]
                    results[d][pl.ds((i * slots + s) * side, side)] = value
        copy = pltpu.make_async_copy(results[d], outs[d], sems.at[d])
        copy.start()
        copies.append(copy)
    wait_for(copies)


def split_results(first, others):
    return [first] + [others.at[d] for d in range(others.shape[0])]


def first_kernel(rows, slots, n_pieces, n_early, index_at, index_ref, left_ref, *refs):
    pieces, outs = refs[:n_pieces], refs[n_pieces + n_early : -6]
    right, left, first, others, sems, out_sems = refs[-6:]
    wait_for(start_copies(into(pieces, right, rows * slots) + [(left_ref, left)], sems))

    def left_of(i):
        return jnp.concatenate([left[i * slots + a] for a in range(slots)], axis=1)

    results = split_results(first, others)
    multiply(index_ref, index_at, left_of, right, results, outs, out_sems, rows, slots, 1)


def second_kernel(rows, slots, n_pieces, n_out, index_at, index_ref, *refs):
    pieces, parts = refs[:n_pieces], refs[n_pieces : n_pieces + n_out]
    right, left, part_first, part_others, first, others, sems, out_sems = refs[-8:]
    outs = refs[n_pieces + n_out : -8]
    held = split_results(part_first, part_others)
    wait_for(start_copies(list(zip(parts, held)) + into(pieces, right, rows * slots), sems))
    for b in range(rows * slots):
        value = held[0][b]
        for part in held[1:]:
            value = value + part[b].astype(jnp.float32)
        left[b] = value.astype(jnp.bfloat16)

    def left_of(i):
        return jnp.concatenate([left[i * slots + a] for a in range(slots)], axis=0)

    results = split_results(first, others)
    multiply(index_ref, index_at, left_of, right, results, outs, out_sems, rows, slots, 0)


def two_parts(x):
    high = x.astype(jnp.bfloat16)
    low = (x - high.astype(jnp.float32)).astype(jnp.bfloat16)
    return jnp.concatenate([high, low], axis=0)


def one_part(x):
    x = x.astype(jnp.float32)
    half = x.shape[0] // 2
    return x[:half] + x[half:]


def tree_sum(values):
    while len(values) > 1:
        values = [values[i] + values[i + 1] for i in range(0, len(values), 2)]
    return values[0]


def third_kernel(rows, slots, n_pieces, n_mirror, index_at, mirror_at, index_ref, own_ref, *refs):
    pieces, mirrored = refs[:n_pieces], refs[n_pieces : n_pieces + n_mirror]
    *outs, trace = refs[n_pieces + n_mirror : -8]
    right, mirror, own, left, first, others, sems, out_sems = refs[-8:]
    pairs = into(pieces, right, rows * slots) + into(mirrored, mirror, rows * slots) + [(own_ref, own)]
    wait_for(start_copies(pairs, sems))
    blocks, side = rows * slots, right.shape[1]
    part_rows = trace.shape[0] // 2
    total_trace = jnp.zeros((part_rows, side), jnp.float32)
    for b in range(blocks):
        other = mirror[index_ref[mirror_at + b]].astype(jnp.float32).T
        value = (-(own[b].astype(jnp.float32) + other)).astype(jnp.bfloat16)
        left[b] = value
        product = value.astype(jnp.float32) * right[b].astype(jnp.float32).T
        total_trace = total_trace + product.reshape(-1, part_rows, side).sum(0)
    total_trace = two_parts(total_trace)
    trace[...] = total_trace
    results = split_results(first, others)
    for result in results[1:]:
        result[pl.ds(blocks * side, 2 * part_rows)] = total_trace

    def left_of(i):
        return jnp.concatenate([left[i * slots + a] for a in range(slots)], axis=0)

    multiply(index_ref, index_at, left_of, right, results, outs, out_sems, rows, slots, 0)


def sum_kernel(n_out, trace_ref, own_ref, *refs):
    parts, (out, own, others, result, sems, out_sems) = refs[: n_out - 1], refs[n_out - 1 :]
    pairs = [(part, others.at[n_out - 2 - i]) for i, part in enumerate(parts)]
    wait_for(start_copies([(own_ref, own)] + pairs, sems))
    blocks, side = own.shape[:2]
    for b in range(blocks):
        value = own[b]
        for d in range(n_out - 1):
            value = value + others[d, pl.ds(b * side, side)].astype(jnp.float32)
        result[pl.ds(b * side, side)] = value.astype(result.dtype)
    tail = pl.ds(blocks * side, trace_ref.shape[0])
    tiles = [trace_ref[...]] + [others[d, tail] for d in range(n_out - 1)]
    result[tail] = two_parts(tree_sum([one_part(tile) for tile in tiles]))
    wait_for(start_copies([(result, out)], out_sems))


def last_kernel(n_mirror, blocks, mirror_at, index_ref, own_ref, *refs):
    mirrored, (out, mirror, own, result, sems, out_sems) = refs[:n_mirror], refs[n_mirror:]
    side = own.shape[1]
    count = blocks * side
    body = pl.ds(0, count)
    pairs = [(own_ref.at[body], own)] + [
        (piece.at[body], mirror.at[pl.ds(t * count, count)]) for t, piece in enumerate(mirrored)
    ]
    copies = start_copies(pairs, sems)
    mirror[pl.ds(n_mirror * count, side)] = jnp.zeros((side, side), mirror.dtype)
    wait_for(copies)
    for b in range(blocks):
        start = pl.multiple_of(index_ref[mirror_at + b] * side, side)
        other = mirror[pl.ds(start, side)].astype(jnp.float32)
        value = other - own[pl.ds(b * side, side)].astype(jnp.float32).T
        result[b] = value.astype(result.dtype)
    wait_for(start_copies([(result, out)], out_sems))


def per_device(n_row, n_col, block_cols, step_dir, intersection, density, kohn_sham):
    rows, slots, side = step_dir.shape[:3]
    blocks = rows * slots
    blocks_total = block_cols.shape[0]
    inner = n_row // n_col
    outer = n_row // inner
    assert inner == CORES and outer == n_col and outer & (outer - 1) == 0
    row_index = lax.axis_index("row")
    col_index = lax.axis_index("col")
    bf16, f32 = jnp.bfloat16, jnp.float32

    def at(o, h, g):
        return o * inner + g % inner, (g // inner) * CORES + h

    def inside(r, c):
        return r // inner, c % CORES, (c // CORES) * inner + r % inner

    def spread(o, g):
        bits = (n_col - 1).bit_length()
        return g ^ sum(((o >> b) & 1) << (bits - 1 - b) for b in range(bits))

    def at_spread(o, h, g):
        return at(o, h, spread(o, g))

    def inside_spread(r, c):
        o, h, p = inside(r, c)
        return o, h, spread(o, p)

    o_in, h_in, g_in = inside(row_index, col_index)

    by_group = block_cols.reshape(blocks_total, n_col, slots)
    mirror_cols = lax.dynamic_slice_in_dim(by_group, o_in, 1, 1)[:, 0]

    def rows_of(o, h):
        return lax.dynamic_slice_in_dim(by_group, (o * inner + h) * rows, rows, 0)

    def group_cols_of(cols, g):
        return lax.dynamic_slice_in_dim(cols, g, 1, 1)[:, 0]

    own_rows = rows_of(o_in, h_in)

    def index_table(group, first_out):
        own_cols, group_cols = group_cols_of(own_rows, group), group_cols_of(by_group, group)
        wanted = own_rows[:, first_out ^ jnp.arange(n_col)].transpose(1, 0, 2)
        safe = jnp.clip(wanted, 0, blocks_total - 1)
        matched = (
            (group_cols[safe][..., None, :] == own_cols[None, :, None, :, None])
            & (wanted >= 0)[..., None, None]
            & (own_cols >= 0)[None, :, None, :, None]
        )
        piece = ((safe // rows % inner) ^ h_in) * outer + (safe // rows // inner ^ o_in)
        slot = ((piece * rows + safe % rows) * slots)[..., None] + jnp.argmax(matched, axis=-1)
        return jnp.where(matched.any(-1), slot, n_row * blocks).astype(jnp.int32).reshape(-1)

    spread_in = spread(o_in, g_in)
    all_tables = [index_table(g_in, g_in), index_table(g_in, spread_in)]

    def mirror_table(h, cols):
        own_ids = (o_in * inner + h) * rows + jnp.arange(rows)
        safe_own = jnp.clip(cols, 0, blocks_total - 1)
        found = mirror_cols[safe_own] == own_ids[:, None, None]
        source = (safe_own // rows % inner) ^ h
        return jnp.where(
            cols >= 0,
            (source * rows + safe_own % rows) * slots + jnp.argmax(found, axis=-1),
            inner * blocks,
        ).astype(jnp.int32).reshape(-1)

    all_tables += [mirror_table(h_in, group_cols_of(own_rows, g)) for g in (g_in, spread_in)]
    starts = [sum(table.size for table in all_tables[:t]) for t in range(len(all_tables))]
    first_at, later_at, mirror_at, last_mirror_at = starts
    tables = jnp.concatenate(all_tables)

    smem = pl.BlockSpec(memory_space=pltpu.SMEM)
    vmem = pl.BlockSpec(memory_space=pltpu.VMEM)
    anywhere = pl.BlockSpec(memory_space=pl.ANY)

    def permute(x, target):
        return lax.ppermute(x, ("row", "col"), row_major_perm(n_row, n_col, target))

    def relayout(x, m=0, target=at):
        return permute(x, lambda r, c: target((r // inner) ^ m, r % inner, c))

    def inside_permute(x, move, source=inside, target=at):
        return permute(x, lambda r, c: target(*move(*source(r, c))))

    def share(x):
        return inside_permute(x, lambda o, h, g: (o, h ^ 1, g))

    def after(x, done):
        return lax.optimization_barrier((x, done))[0]

    def to_plane(x, m):
        return inside_permute(x, lambda o, h, g: (o ^ m, h, g))

    def share_all(pieces):
        return {m: share(piece) for m, piece in pieces.items()}

    def listed(pieces, shared):
        return [pieces[m] for m in range(outer)] + [shared[m] for m in range(outer)]

    def mirror(x, target):
        moved = inside_permute(x, lambda o, h, g: (g, h, o), inside_spread, target)
        return [moved, share(moved)]

    def exchange(outs):
        return [outs[0]] + [
            inside_permute(outs[d], lambda o, h, g, d=d: (o, h, g ^ d))
            for d in range(len(outs) - 1, 0, -1)
        ]

    def total_of(parts):
        value = parts[0]
        for part in parts[1:]:
            value = value + part.astype(f32)
        return value.astype(bf16)

    block_shape = (blocks, side, side)
    out_shapes = tuple(
        jax.ShapeDtypeStruct(block_shape, bf16 if d else f32) for d in range(n_col)
    )
    params = pltpu.CompilerParams(vmem_limit_bytes=14 * 2**20)

    def held(count):
        return pltpu.VMEM((count, side, side), bf16)

    def dma(count):
        return pltpu.SemaphoreType.DMA((count,))

    tail_shape = jax.ShapeDtypeStruct((16, side), bf16)
    long_shape = jax.ShapeDtypeStruct((blocks * side + tail_shape.shape[0], side), bf16)
    long_sums = [
        pltpu.VMEM(block_shape, f32),
        pltpu.VMEM((n_col - 1,) + long_shape.shape, bf16),
    ]
    sums = [pltpu.VMEM(block_shape, f32), pltpu.VMEM((n_col - 1,) + block_shape, bf16)]
    cost = pl.CostEstimate(
        flops=2 * n_col * blocks * slots * side**3,
        bytes_accessed=4 * 2**20,
        transcendentals=0,
    )

    flat = lambda x: x.reshape(block_shape)
    inter, dens, kohn = flat(intersection), flat(density), flat(kohn_sham)

    far_from = range(2, outer, 2)
    near = [*far_from, 1]

    inter_near = {m: relayout(inter, m) for m in near}
    inter_early = {0: relayout(inter)} | inter_near
    step = relayout(flat(step_dir))
    dens_own = relayout(dens)
    inter_far = {m + 1: to_plane(inter_near[m], 1) for m in far_from}
    dens_behind = after(dens_own, inter_near)
    dens_near = {m: to_plane(dens_behind, m) for m in far_from}
    dens_behind, kohn = after((dens_own, kohn), (inter_near, inter_far))
    dens_near[1] = to_plane(dens_behind, 1)
    kohn_own = relayout(kohn)
    inter_all = listed(inter_early | inter_far, share_all(inter_early) | share_all(inter_far))
    outs = pl.pallas_call(
        functools.partial(first_kernel, rows, slots, n_row, 0, first_at),
        out_shape=out_shapes,
        in_specs=[smem] + [anywhere] * (1 + n_row),
        out_specs=(anywhere,) * n_col,
        scratch_shapes=[held(n_row * blocks + 1), held(blocks), *sums, dma(n_row + 1), dma(n_col)],
        compiler_params=params,
        cost_estimate=cost,
        name="scaled_step_product",
    )(tables, step, *inter_all)
    parts = exchange(outs)

    dens_beside = {0: share(dens_own)}
    dens_far = {m + 1: to_plane(after(dens_near[m], outs), 1) for m in far_from}
    kohn_behind = after(kohn_own, (dens_near, outs))
    kohn_pieces = {m: to_plane(kohn_behind, m) for m in near}
    dens_near = after(dens_near, parts[1:])
    dens_beside |= share_all(dens_near) | share_all(dens_far)
    dens_all = listed({0: dens_own} | dens_near | dens_far, dens_beside)
    outs = pl.pallas_call(
        functools.partial(second_kernel, rows, slots, n_row, n_col, later_at),
        out_shape=out_shapes,
        in_specs=[smem] + [anywhere] * (n_row + n_col),
        out_specs=(anywhere,) * n_col,
        scratch_shapes=[
            held(n_row * blocks + 1),
            held(blocks),
            *sums,
            *sums,
            dma(n_row + n_col),
            dma(n_col),
        ],
        compiler_params=params,
        cost_estimate=cost,
        name="change_product",
    )(tables, *dens_all, *parts)
    second_outs = outs
    total = total_of(exchange(outs))

    mirrored = mirror(total, at)
    own = inside_permute(total, lambda o, h, g: (o, h, g), inside_spread)
    kohn_pieces = {0: kohn_own} | kohn_pieces
    kohn_beside = share_all(after(kohn_pieces, second_outs))
    kohn_last = {m + 1: to_plane(kohn_pieces[m], 1) for m in far_from}
    kohn_last = after(kohn_last, total)
    kohn_all = listed(kohn_pieces | kohn_last, kohn_beside | share_all(kohn_last))
    *outs, trace = pl.pallas_call(
        functools.partial(third_kernel, rows, slots, n_row, inner, later_at, mirror_at),
        out_shape=out_shapes[:1] + (long_shape,) * (n_col - 1) + (tail_shape,),
        in_specs=[smem] + [anywhere] * (1 + n_row + inner),
        out_specs=(anywhere,) * n_col + (vmem,),
        scratch_shapes=[
            held(n_row * blocks + 1),
            held(inner * blocks + 1),
            held(blocks),
            held(blocks),
            *long_sums,
            dma(n_row + inner + 1),
            dma(n_col),
        ],
        compiler_params=params,
        cost_estimate=cost,
        name="commutator_product",
    )(tables, own, *kohn_all, *mirrored)
    own, *parts = exchange(outs)
    total = pl.pallas_call(
        functools.partial(sum_kernel, n_col),
        out_shape=long_shape,
        in_specs=[vmem] + [anywhere] * n_col,
        out_specs=anywhere,
        scratch_shapes=[*long_sums, pltpu.VMEM(long_shape.shape, bf16), dma(n_col), dma(1)],
        compiler_params=params,
        name="plane_sum",
    )(trace, own, *parts)
    mirrored = mirror(total, at_spread)

    commutator = pl.pallas_call(
        functools.partial(last_kernel, inner, blocks, last_mirror_at),
        out_shape=jax.ShapeDtypeStruct(block_shape, bf16),
        in_specs=[smem] + [anywhere] * (1 + inner),
        out_specs=anywhere,
        scratch_shapes=[
            pltpu.VMEM(((inner * blocks + 1) * side, side), bf16),
            pltpu.VMEM((blocks * side, side), bf16),
            held(blocks),
            dma(inner + 1),
            dma(1),
        ],
        compiler_params=params,
        name="commutator_difference",
    )(tables, total, *mirrored)
    commutator = inside_permute(
        commutator, lambda o, h, g: (o, h, g), inside_spread, lambda o, h, g: (o * inner + h, g)
    )

    plane_trace = tree_sum([one_part(piece[blocks * side :]) for piece in mirrored])
    trace = tree_sum(
        [plane_trace]
        + [
            inside_permute(plane_trace, lambda o, h, g, d=d: (o, h, g ^ d))
            for d in range(1, n_col)
        ]
    )
    trace_value = trace.sum() / (blocks_total * side * side)
    return commutator.reshape(step_dir.shape), trace_value


def solution(mesh):
    in_specs = (P(),) + (P("row", "col", None, None),) * 4
    out_specs = (P("row", "col", None, None), P())
    return jax.shard_map(
        functools.partial(per_device, mesh.shape["row"], mesh.shape["col"]),
        mesh=mesh,
        in_specs=in_specs,
        out_specs=out_specs,
        check_vma=False,
    )
```
